32 devices in a mesh: dev: 32 (over z, y, x, core).
Axes of the slice: x: 2, y: 2, z: 4, core: 2. Of those that a mesh axis runs over, the one named last changes fastest.
Arguments:
- gaussians: float32 [59, 262144], P(None, 'dev'), may hold values from -6 to 3
- view_angles: float32 [3], replicated, may hold values from -4 to 4
- tile_order: int32 [512], P('dev'), may hold values from 0 to 511, as said below
- tile_owners: int32 [512, 512], P('dev'), may hold values from 0 to 31, as said below
- tile_locals: int32 [512, 512], P('dev'), may hold values from 0 to 8191
- list_counts: int32 [512], P('dev'), may hold values from 1 to 512, as said below
- image_cotangent: float32 [3, 131072], P(None, 'dev'), may hold values from -6 to 6
Outputs:
- rendered: float32 [3, 131072], P(None, 'dev')
- gradients: float32 [59, 262144], P(None, 'dev')
The draws below stay inside these ranges and needn't reach their ends.
Inputs may be any that keep to these rules, and one draw needn't show every extreme that they name: `tile_order`: each image tile once. `tile_owners`: the 16 x 512 slots of the tiles of one device name every owner exactly 256 times. Slots from list_counts[i] on are padding.
All inputs are finite; a program needn't handle non-finite values.
Results may differ from the reference program's by a relative error of at most 0.0003.
Values sent between devices are 32-bit elements; how exact they have to be, the bound alone decides.
No kernel may reach another device: no remote copies, remote signals or barrier semaphores. Data moves between devices by JAX's collectives and lax.ppermute only.
A program may use at most 64 MiB of HBM per device.

```python
import jax
import jax.numpy as jnp
from jax import lax

PROJ = 9
PIX = 256
TX = 32
SLOTS = 512
G_DEV = 8192
TILE_DEV = 16
GAUSS = 262144
TILES = 512


def layout(key):
    keys = [jax.random.fold_in(key, 101 + index) for index in range(8)]
    angles = jax.random.uniform(keys[0], (3,), jnp.float32, -3.14159, 3.14159)
    cos_a = jnp.cos(angles[0])
    sin_a = jnp.sin(angles[0])
    cos_b = jnp.cos(angles[1])
    sin_b = jnp.sin(angles[1])
    cos_c = jnp.cos(angles[2])
    sin_c = jnp.sin(angles[2])
    row_zero = [cos_c * cos_b, cos_c * sin_b * sin_a - sin_c * cos_a, cos_c * sin_b * cos_a + sin_c * sin_a]
    row_one = [sin_c * cos_b, sin_c * sin_b * sin_a + cos_c * cos_a, sin_c * sin_b * cos_a - cos_c * sin_a]
    row_two = [-sin_b, cos_b * sin_a, cos_b * cos_a]
    order = jax.random.permutation(keys[1], jnp.arange(TILES, dtype=jnp.int32)).astype(jnp.int32)
    devices = TILES // TILE_DEV
    per_device = TILE_DEV * SLOTS
    base = jnp.arange(per_device, dtype=jnp.int32) % devices
    owner_keys = jax.random.split(keys[2], devices)
    owners = jax.vmap(lambda one_key: jax.random.permutation(one_key, base))(owner_keys).reshape(TILES, SLOTS).astype(jnp.int32)
    target = order[:, None]
    moved = jax.random.randint(keys[3], (TILES, SLOTS), -2, 3, dtype=jnp.int32)
    column = jnp.clip(target % TX + moved, 0, TX - 1)
    near = target // TX * TX + column
    anchor_rank = (near - owners * TILE_DEV) % TILES
    spread = max(G_DEV // TILES, 1)
    locals_drawn = anchor_rank * G_DEV // TILES + jax.random.randint(keys[4], (TILES, SLOTS), 0, spread, dtype=jnp.int32)
    locals_drawn = locals_drawn.at[0, 0].set(G_DEV - 1).at[0, 1].set(0).astype(jnp.int32)
    levels = jax.random.randint(keys[5], (GAUSS,), 0, 4096, dtype=jnp.int32)
    slot_levels = jnp.take(levels, owners * G_DEV + locals_drawn)
    ranks = jnp.argsort(slot_levels, axis=1, stable=True)
    owners = jnp.take_along_axis(owners, ranks, axis=1).astype(jnp.int32)
    locals_drawn = jnp.take_along_axis(locals_drawn, ranks, axis=1).astype(jnp.int32)
    index = jnp.arange(GAUSS, dtype=jnp.int32)
    anchor = (index % G_DEV * TILES // G_DEV + index // G_DEV * TILE_DEV) % TILES
    tiles_y = TILES // TX
    jitter = jax.random.uniform(keys[6], (2, GAUSS), jnp.float32, -16.0, 16.0)
    screen_x = jnp.clip(16.0 * (anchor % TX).astype(jnp.float32) + 8.0 + jitter[0], 0.0, 16.0 * TX)
    screen_y = jnp.clip(16.0 * (anchor // TX).astype(jnp.float32) + 8.0 + jitter[1], 0.0, 16.0 * tiles_y)
    view_x = (screen_x - 8.0 * TX) / (4.0 * TX)
    view_y = (screen_y - 8.0 * tiles_y) / (4.0 * tiles_y)
    depth = (levels.astype(jnp.float32) + 0.5) / 2048.0 - 1.0
    positions = jnp.stack([row_zero[j] * view_x + row_one[j] * view_y + row_two[j] * depth for j in range(3)])
    return (angles, order, owners, locals_drawn, positions)


def draw_view_angles(key, part):
    return layout(key)[0].astype(jnp.float32)


def draw_tile_order(key, part):
    return layout(key)[1]


def draw_tile_owners(key, part):
    return layout(key)[2]


def draw_tile_locals(key, part):
    return layout(key)[3]


def draw_gaussians(key, part):
    positions = layout(key)[4]
    keys = jax.random.split(jax.random.fold_in(key, 7), 5)
    harmonic_scale = jnp.where(jnp.arange(16) == 0, 0.5, 0.15).astype(jnp.float32)[None, :, None]
    log_scales = jax.random.uniform(keys[1], (3, GAUSS), jnp.float32, -2.3, -0.5)
    quats = jax.random.normal(keys[2], (4, GAUSS), jnp.float32) * 0.6
    opacity_logits = jax.random.uniform(keys[3], (1, GAUSS), jnp.float32, -5.5, -4.0)
    harmonic = jax.random.normal(keys[4], (3, 16, GAUSS), jnp.float32) * harmonic_scale
    stacked = jnp.concatenate([positions, log_scales, quats, opacity_logits, harmonic.reshape(48, GAUSS)], axis=0)
    return jnp.clip(stacked, -6.0, 3.0).astype(jnp.float32)


def draw_list_counts(key, part):
    keys = jax.random.split(jax.random.fold_in(key, 23), 2)
    counts = jax.random.randint(keys[0], (TILES,), SLOTS * 3 // 8, SLOTS + 1, dtype=jnp.int32)
    chosen = jax.random.randint(keys[1], (), 0, TILES, dtype=jnp.int32)
    return counts.at[chosen].set(SLOTS).at[(chosen + 1) % TILES].set(1).astype(jnp.int32)


def steps_of(key, extent, cuts, low, high):
    def one(position, shards_of):
        draws = jax.random.uniform(jax.random.fold_in(jax.random.fold_in(key, 6), position), (shards_of,), jnp.float32, low / len(cuts), high / len(cuts))
        return jnp.repeat(jnp.exp(draws), extent[position] // shards_of).reshape((-1,) + (1,) * (len(extent) - position - 1))

    gain = one(*cuts[0])
    for cut in cuts[1:]:
        gain = gain * one(*cut)
    return gain


def scatter_about(key, extent, scale, most, cuts=(), kind=jnp.bfloat16):
    gain = steps_of(key, extent, cuts, -0.22, 0.18) if cuts else 1.0
    values = jax.random.normal(key, extent, jnp.float32) * scale * gain
    return jnp.minimum(jnp.maximum(values, -most), most).astype(kind)


def setup_inputs(seed: int = 0) -> dict:
    key_of = jax.random.split(jax.random.key(seed), 8)
    return {
        "gaussians": draw_gaussians(jax.random.fold_in(key_of[7], 71), 0),
        "view_angles": draw_view_angles(jax.random.fold_in(key_of[7], 71), 0),
        "tile_order": draw_tile_order(jax.random.fold_in(key_of[7], 71), 0),
        "tile_owners": draw_tile_owners(jax.random.fold_in(key_of[7], 71), 0),
        "tile_locals": draw_tile_locals(jax.random.fold_in(key_of[7], 71), 0),
        "list_counts": draw_list_counts(jax.random.fold_in(key_of[7], 71), 0),
        "image_cotangent": scatter_about(key_of[6], (3, TILES * PIX), 1.0, 6.0, ((1, 32),), jnp.float32),
    }


highest = lax.Precision.HIGHEST

def rotation_of(view_angles):
    cos_a = jnp.cos(view_angles[0])
    sin_a = jnp.sin(view_angles[0])
    cos_b = jnp.cos(view_angles[1])
    sin_b = jnp.sin(view_angles[1])
    cos_c = jnp.cos(view_angles[2])
    sin_c = jnp.sin(view_angles[2])
    zero_val = jnp.zeros((), jnp.float32)
    one_val = jnp.ones((), jnp.float32)
    turn_x = jnp.stack([jnp.stack([one_val, zero_val, zero_val]), jnp.stack([zero_val, cos_a, -sin_a]), jnp.stack([zero_val, sin_a, cos_a])])
    turn_y = jnp.stack([jnp.stack([cos_b, zero_val, sin_b]), jnp.stack([zero_val, one_val, zero_val]), jnp.stack([-sin_b, zero_val, cos_b])])
    turn_z = jnp.stack([jnp.stack([cos_c, -sin_c, zero_val]), jnp.stack([sin_c, cos_c, zero_val]), jnp.stack([zero_val, zero_val, one_val])])
    return jnp.dot(turn_z, jnp.dot(turn_y, turn_x, precision=highest), precision=highest)

def harmonics(along_x, along_y, along_z):
    sq_x = along_x * along_x
    sq_y = along_y * along_y
    sq_z = along_z * along_z
    return jnp.stack([0.28209479177387814 + 0.0 * along_x, -0.4886025119029199 * along_y, 0.4886025119029199 * along_z, -0.4886025119029199 * along_x, 1.0925484305920792 * along_x * along_y, -1.0925484305920792 * along_y * along_z, 0.31539156525252005 * (2.0 * sq_z - sq_x - sq_y), -1.0925484305920792 * along_x * along_z, 0.5462742152960396 * (sq_x - sq_y), -0.5900435899266435 * along_y * (3.0 * sq_x - sq_y), 2.890611442640554 * along_x * along_y * along_z, -0.4570457994644658 * along_y * (4.0 * sq_z - sq_x - sq_y), 0.3731763325901154 * along_z * (2.0 * sq_z - 3.0 * sq_x - 3.0 * sq_y), -0.4570457994644658 * along_x * (4.0 * sq_z - sq_x - sq_y), 1.445305721320277 * along_z * (sq_x - sq_y), -0.5900435899266435 * along_x * (sq_x - 3.0 * sq_y)])

def project(columns, view_angles, camera_frame):
    focal_x, focal_y, centre_x, centre_y = camera_frame
    rotation = rotation_of(view_angles)
    positions = columns[0:3]
    cam_first = rotation[0, 0] * positions[0] + rotation[0, 1] * positions[1] + rotation[0, 2] * positions[2]
    cam_second = rotation[1, 0] * positions[0] + rotation[1, 1] * positions[1] + rotation[1, 2] * positions[2]
    mean_x = centre_x + focal_x * cam_first
    mean_y = centre_y + focal_y * cam_second
    scales = jnp.exp(columns[3:6])
    quat_w = columns[6]
    quat_x = columns[7]
    quat_y = columns[8]
    quat_z = columns[9]
    norm_sq = jnp.maximum(quat_w * quat_w + quat_x * quat_x + quat_y * quat_y + quat_z * quat_z, 1.0)
    turned = [[1.0 - 2.0 * (quat_y * quat_y + quat_z * quat_z) / norm_sq, 2.0 * (quat_x * quat_y - quat_w * quat_z) / norm_sq, 2.0 * (quat_x * quat_z + quat_w * quat_y) / norm_sq], [2.0 * (quat_x * quat_y + quat_w * quat_z) / norm_sq, 1.0 - 2.0 * (quat_x * quat_x + quat_z * quat_z) / norm_sq, 2.0 * (quat_y * quat_z - quat_w * quat_x) / norm_sq], [2.0 * (quat_x * quat_z - quat_w * quat_y) / norm_sq, 2.0 * (quat_y * quat_z + quat_w * quat_x) / norm_sq, 1.0 - 2.0 * (quat_x * quat_x + quat_y * quat_y) / norm_sq]]
    first_row = []
    second_row = []
    for column_index in range(3):
        first_row.append(focal_x * (rotation[0, 0] * turned[0][column_index] + rotation[0, 1] * turned[1][column_index] + rotation[0, 2] * turned[2][column_index]) * scales[column_index])
        second_row.append(focal_y * (rotation[1, 0] * turned[0][column_index] + rotation[1, 1] * turned[1][column_index] + rotation[1, 2] * turned[2][column_index]) * scales[column_index])
    cov_a = first_row[0] * first_row[0] + first_row[1] * first_row[1] + first_row[2] * first_row[2] + 0.3
    cov_b = first_row[0] * second_row[0] + first_row[1] * second_row[1] + first_row[2] * second_row[2]
    cov_c = second_row[0] * second_row[0] + second_row[1] * second_row[1] + second_row[2] * second_row[2] + 0.3
    determinant = cov_a * cov_c - cov_b * cov_b
    opacity = 1.0 / (1.0 + jnp.exp(-columns[10]))
    basis = harmonics(rotation[2, 0], rotation[2, 1], rotation[2, 2])
    coeffs = columns[11:59].reshape(3, 16, columns.shape[1])
    colours = 0.5 + jnp.einsum('k,ckn->cn', basis, coeffs, precision=highest)
    return jnp.stack([mean_x, mean_y, cov_c / determinant, -cov_b / determinant, cov_a / determinant, opacity, colours[0], colours[1], colours[2]])

def render_tile(tile_rows, live_count, tile_id):
    pixels = jnp.arange(PIX, dtype=jnp.int32)
    pixel_x = (tile_id % TX * 16 + pixels % 16).astype(jnp.float32) + 0.5
    pixel_y = (tile_id // TX * 16 + pixels // 16).astype(jnp.float32) + 0.5
    offset_x = pixel_x[:, None] - tile_rows[0][None, :]
    offset_y = pixel_y[:, None] - tile_rows[1][None, :]
    powers = -0.5 * (tile_rows[2][None, :] * offset_x * offset_x + tile_rows[4][None, :] * offset_y * offset_y) - tile_rows[3][None, :] * offset_x * offset_y
    slot_live = jnp.arange(SLOTS, dtype=jnp.int32) < live_count
    alphas = jnp.where(slot_live[None, :], tile_rows[5][None, :] * jnp.exp(powers), 0.0)
    logs = jnp.log1p(-alphas)
    trans = jnp.exp(jnp.cumsum(logs, axis=1) - logs)
    return jnp.einsum('ck,pk->cp', tile_rows[6:9], trans * alphas, precision=highest)

def reference(gaussians, view_angles, tile_order, tile_owners, tile_locals, list_counts, image_cotangent):
    tiles_y = TILES // TX
    camera_frame = (4.0 * TX, 4.0 * tiles_y, 8.0 * TX, 8.0 * tiles_y)
    indices = (tile_owners * G_DEV + tile_locals).reshape(-1).astype(jnp.int32)

    def shaded(table):
        return project(jnp.take(table, indices, axis=1), view_angles, camera_frame)
    projected, pullback = jax.vjp(shaded, gaussians)
    tile_rows = projected.reshape(PROJ, TILES, SLOTS).transpose(1, 0, 2)
    cotangents = image_cotangent.reshape(3, TILES, PIX).transpose(1, 0, 2)

    def one_tile(tile_item):
        columns, live_count, tile_id, tile_cot = tile_item
        tile_image, tile_back = jax.vjp(lambda values: render_tile(values, live_count, tile_id), columns)
        return (tile_image, tile_back(tile_cot)[0])
    images, slot_grads = lax.map(one_tile, (tile_rows, list_counts, tile_order, cotangents))
    rendered = images.transpose(1, 0, 2).reshape(3, TILES * PIX)
    gradients = pullback(slot_grads.transpose(1, 0, 2).reshape(PROJ, TILES * SLOTS))[0]
    return (rendered, gradients)
```

```python
from functools import partial

import jax
import jax.numpy as jnp
from jax import lax
from jax.experimental import pallas as pl
from jax.experimental.pallas import tpu as pltpu
from jax.sharding import PartitionSpec as P

PIX = 256
TX = 32
LANES = 128
PROJ = 9
GROUP = 8
STEP = LANES // GROUP
LOG2E = 1.4426950408889634
VMEM_BYTES = 52 * 1024 * 1024

f32 = jnp.float32
bf16 = jnp.bfloat16
i32 = jnp.int32


def iota(shape, dim):
    return lax.broadcasted_iota(i32, shape, dim)


def lane_pick(row, lanes):
    source = jnp.broadcast_to(row, lanes.shape)
    return jnp.take_along_axis(source, lanes, axis=1, mode="promise_in_bounds")


def split_two(values):
    first = values.astype(bf16).astype(f32)
    return first, values - first


def split_three(values):
    first, rest = split_two(values)
    second, third = split_two(rest)
    return first, second, third


def dot(lhs, rhs):
    return lax.dot_general(lhs, rhs, (((1,), (0,)), ((), ())), preferred_element_type=f32)


def dot_nt(lhs, rhs):
    return lax.dot_general(lhs, rhs, (((1,), (1,)), ((), ())), preferred_element_type=f32)


def dot_tn(lhs, rhs):
    return lax.dot_general(lhs, rhs, (((0,), (0,)), ((), ())), preferred_element_type=f32)


class Rows:
    def __init__(self, devices, per_owner):
        self.halves = per_owner // LANES if per_owner % LANES == 0 else 0
        self.count = devices * per_owner // LANES

    def ids(self, ref, block):
        halves = self.halves
        if halves <= 1:
            return ref[pl.ds(8 * block, 8), :]
        return ref[pl.ds(block // halves * 8 * halves + block % halves, 8, stride=halves), :]

    def natural(self, ref, block):
        halves = self.halves
        if halves <= 1:
            return ref[pl.ds(8 * block, 8), :]
        start = block // halves * 8
        return ref[start : start + 8, block % halves * LANES : (block % halves + 1) * LANES]

    def block(self, channel, block):
        halves = self.halves
        if halves == 0:
            return pl.ds(channel * self.count + 8 * block, 8)
        start = block // halves * 8 * PROJ * halves + channel * halves + block % halves
        return pl.ds(start, 8, stride=PROJ * halves)

    def row(self, channel, major, minor):
        halves = self.halves
        if halves == 0:
            return channel * self.count + major
        return major * (PROJ * halves) + channel * halves + minor

    def minors(self):
        return max(self.halves, 1)


def gather_rows(ref, place, majors, minors, slots):
    rows = slots // LANES
    lanes = slots % LANES

    def step(major, found):
        for minor in range(minors):
            here = rows == major * minors + minor
            found = tuple(
                jnp.where(here, lane_pick(ref[pl.ds(place(channel, major, minor), 1), :], lanes), value)
                for channel, value in enumerate(found)
            )
        return found

    start = tuple(jnp.zeros(slots.shape, f32) for _ in range(PROJ))
    return lax.fori_loop(0, majors, step, start, unroll=4)


def route_kernel(devices, per_owner, own_ref, loc_ref, want_ref, back_ref, pos_ref, own_s, loc_s, rank_s):
    rows = own_s.shape[0]
    blocks = own_ref.shape[1] // LANES
    lane = iota((8, LANES), 1)
    from_slot = iota((8, LANES), 0) * STEP + lane // GROUP
    tile_of = lane % GROUP
    for group in range(own_ref.shape[0] // GROUP):
        for block in range(blocks):
            for source, target in ((own_ref, own_s), (loc_ref, loc_s)):
                part = source[group * GROUP : (group + 1) * GROUP, block * LANES : (block + 1) * LANES]
                out = jnp.zeros((8, LANES), i32)
                for tile in range(GROUP):
                    out = jnp.where(tile_of == tile, lane_pick(part[tile : tile + 1], from_slot), out)
                start = (group * blocks + block) * 8
                target[start : start + 8, :] = out
    owner = own_s[...]
    left = (iota((LANES, 2 * LANES), 0) < iota((LANES, 2 * LANES), 1)) | (iota((LANES, 2 * LANES), 1) >= LANES)
    above = iota((rows, rows), 1) < iota((rows, rows), 0)
    hits = jnp.concatenate([jnp.where(owner == one, 1.0, 0.0).astype(bf16) for one in range(devices)], axis=0)
    sums = dot(hits, jnp.where(left, 1.0, 0.0).astype(bf16))
    totals = jnp.concatenate(
        [sums[one * rows : (one + 1) * rows, LANES:].astype(bf16) for one in range(devices)], axis=1
    )
    base = dot(jnp.where(above, 1.0, 0.0).astype(bf16), totals)
    rank = jnp.zeros((rows, LANES), f32)
    for one in range(devices):
        here = sums[one * rows : (one + 1) * rows, :LANES] + base[:, one * LANES : (one + 1) * LANES]
        rank = jnp.where(owner == one, here, rank)
    rank = rank.astype(i32)
    pos_ref[...] = owner * per_owner + rank
    rank_s[...] = rank

    owner_id = iota((devices, LANES), 0)
    rank_id = iota((per_owner, LANES), 0)
    slot_lane = iota((devices, LANES), 1).astype(f32)

    def place(index, total):
        start = pl.multiple_of(index * 8, 8)
        own_rows = own_s[pl.ds(start, 8), :]
        loc_rows = loc_s[pl.ds(start, 8), :]
        rank_rows = rank_s[pl.ds(start, 8), :]
        high_rows = (loc_rows // LANES).astype(f32)
        low_rows = (loc_rows % LANES).astype(f32)
        lhs = []
        rhs = []
        for row in range(8):
            mine = own_rows[row : row + 1] == owner_id
            number = (start + row).astype(f32)
            lhs.append(
                jnp.concatenate(
                    [
                        jnp.where(mine, high_rows[row : row + 1], 0.0),
                        jnp.where(mine, low_rows[row : row + 1], 0.0),
                        jnp.where(mine, number, 0.0),
                        jnp.where(mine, slot_lane, 0.0),
                    ],
                    axis=0,
                ).astype(bf16)
            )
            rhs.append(jnp.where(rank_rows[row : row + 1] == rank_id, 1.0, 0.0).astype(bf16))
        return total + dot_nt(jnp.concatenate(lhs, axis=1), jnp.concatenate(rhs, axis=1))

    total = lax.fori_loop(0, rows // 8, place, jnp.zeros((4 * devices, per_owner), f32)).astype(i32)
    want = total[:devices] * LANES + total[devices : 2 * devices]
    halves = per_owner // LANES
    if per_owner % LANES == 0 and halves > 1:
        for half in range(halves):
            want_ref[pl.ds(half, devices, stride=halves), :] = want[:, half * LANES : (half + 1) * LANES]
    else:
        want_ref[...] = want
    back_ref[...] = total[2 * devices : 3 * devices] * LANES + total[3 * devices :]


def view(angles_ref):
    angle = [jnp.full((1, LANES), angles_ref[index], f32) for index in range(3)]
    (cos_a, cos_b, cos_c) = [jnp.cos(one) for one in angle]
    (sin_a, sin_b, sin_c) = [jnp.sin(one) for one in angle]
    return [
        [cos_c * cos_b, cos_c * sin_b * sin_a - sin_c * cos_a, cos_c * sin_b * cos_a + sin_c * sin_a],
        [sin_c * cos_b, sin_c * sin_b * sin_a + cos_c * cos_a, sin_c * sin_b * cos_a - cos_c * sin_a],
        [-sin_b, cos_b * sin_a, cos_b * cos_a],
    ]


def harmonics(along_x, along_y, along_z):
    sq_x = along_x * along_x
    sq_y = along_y * along_y
    sq_z = along_z * along_z
    return [
        0.28209479177387814 + 0.0 * along_x,
        -0.4886025119029199 * along_y,
        0.4886025119029199 * along_z,
        -0.4886025119029199 * along_x,
        1.0925484305920792 * along_x * along_y,
        -1.0925484305920792 * along_y * along_z,
        0.31539156525252005 * (2.0 * sq_z - sq_x - sq_y),
        -1.0925484305920792 * along_x * along_z,
        0.5462742152960396 * (sq_x - sq_y),
        -0.5900435899266435 * along_y * (3.0 * sq_x - sq_y),
        2.890611442640554 * along_x * along_y * along_z,
        -0.4570457994644658 * along_y * (4.0 * sq_z - sq_x - sq_y),
        0.3731763325901154 * along_z * (2.0 * sq_z - 3.0 * sq_x - 3.0 * sq_y),
        -0.4570457994644658 * along_x * (4.0 * sq_z - sq_x - sq_y),
        1.445305721320277 * along_z * (sq_x - sq_y),
        -0.5900435899266435 * along_x * (sq_x - 3.0 * sq_y),
    ]


def basis_rows(basis, eighth):
    sub = iota((8, LANES), 0)
    found = []
    for colour in range(3):
        out = None
        for inner in range(8):
            index = 8 * eighth + inner - 11 - 16 * colour
            if 0 <= index < 16:
                out = jnp.zeros((8, LANES), f32) if out is None else out
                out = jnp.where(sub == inner, basis[index], out)
        found.append(out)
    return found


def shape_of(columns, rotation, camera_frame):
    focal_x, focal_y, centre_x, centre_y = camera_frame
    positions = columns[0:3]
    cam_first = rotation[0][0] * positions[0] + rotation[0][1] * positions[1] + rotation[0][2] * positions[2]
    cam_second = rotation[1][0] * positions[0] + rotation[1][1] * positions[1] + rotation[1][2] * positions[2]
    mean_x = centre_x + focal_x * cam_first
    mean_y = centre_y + focal_y * cam_second
    scales = [jnp.exp(one) for one in columns[3:6]]
    quat_w, quat_x, quat_y, quat_z = columns[6:10]
    norm_sq = jnp.maximum(quat_w * quat_w + quat_x * quat_x + quat_y * quat_y + quat_z * quat_z, 1.0)
    twice = 2.0 / norm_sq
    turned = [
        [
            1.0 - twice * (quat_y * quat_y + quat_z * quat_z),
            twice * (quat_x * quat_y - quat_w * quat_z),
            twice * (quat_x * quat_z + quat_w * quat_y),
        ],
        [
            twice * (quat_x * quat_y + quat_w * quat_z),
            1.0 - twice * (quat_x * quat_x + quat_z * quat_z),
            twice * (quat_y * quat_z - quat_w * quat_x),
        ],
        [
            twice * (quat_x * quat_z - quat_w * quat_y),
            twice * (quat_y * quat_z + quat_w * quat_x),
            1.0 - twice * (quat_x * quat_x + quat_y * quat_y),
        ],
    ]
    rows = []
    for focal, turn in ((focal_x, rotation[0]), (focal_y, rotation[1])):
        rows.append(
            [
                focal * (turn[0] * turned[0][k] + turn[1] * turned[1][k] + turn[2] * turned[2][k]) * scales[k]
                for k in range(3)
            ]
        )
    first, second = rows
    cov_a = first[0] * first[0] + first[1] * first[1] + first[2] * first[2] + 0.3
    cov_b = first[0] * second[0] + first[1] * second[1] + first[2] * second[2]
    cov_c = second[0] * second[0] + second[1] * second[1] + second[2] * second[2] + 0.3
    determinant = cov_a * cov_c - cov_b * cov_b
    opacity = 1.0 / (1.0 + jnp.exp(-columns[10]))
    return mean_x, mean_y, cov_c / determinant, -cov_b / determinant, cov_a / determinant, opacity


def spread_columns(gauss_ref, dense_s):
    rows = gauss_ref.shape[1] // LANES
    for row in range(rows):
        for eighth in range(2):
            dense_s[pl.ds(8 * eighth * rows + row, 8, stride=rows), :] = gauss_ref[
                8 * eighth : 8 * eighth + 8, row * LANES : (row + 1) * LANES
            ]


def shade_kernel(camera_frame, angles_ref, gauss_ref, table_ref, dense_s, tint_s):
    rows = gauss_ref.shape[1] // LANES
    spread_columns(gauss_ref, dense_s)
    rotation = view(angles_ref)
    basis = harmonics(*rotation[2])
    patterns = [basis_rows(basis, eighth) for eighth in range(7)]
    for row in range(rows):
        lanes = slice(row * LANES, (row + 1) * LANES)
        tints = [None] * 3
        for eighth in range(1, 7):
            block = gauss_ref[8 * eighth : 8 * eighth + 8, lanes]
            for colour in range(3):
                pattern = patterns[eighth][colour]
                if pattern is not None:
                    term = block * pattern
                    tints[colour] = term if tints[colour] is None else tints[colour] + term
        for colour in range(3):
            tint_s[pl.ds(8 * colour * rows + row, 8, stride=rows), :] = tints[colour]
        tint_s[pl.ds(24 * rows + row, 3, stride=rows), :] = gauss_ref[56:59, lanes]
    columns = [dense_s[index * rows : (index + 1) * rows, :] for index in range(11)]
    shaped = shape_of(columns, rotation, camera_frame)
    for index, value in enumerate(shaped):
        table_ref[index * rows : (index + 1) * rows, :] = value
    for colour in range(3):
        total = 0.5
        for inner in range(8):
            start = (8 * colour + inner) * rows
            total = total + tint_s[start : start + rows, :]
        if colour == 2:
            for inner in range(3):
                start = (24 + inner) * rows
                total = total + basis[13 + inner] * tint_s[start : start + rows, :]
        table_ref[(6 + colour) * rows : (7 + colour) * rows, :] = total


def pick_kernel(layout, table_ref, asked_ref, out_ref):
    rows = table_ref.shape[0] // PROJ
    for block in range(layout.count // 8):
        slots = layout.ids(asked_ref, block)
        found = gather_rows(table_ref, lambda channel, major, minor: channel * rows + major, rows, 1, slots)
        for channel in range(PROJ):
            out_ref[layout.block(channel, block), :] = found[channel]


def render_kernel(
    layout,
    count_ref,
    order_ref,
    rows_ref,
    pos_ref,
    back_ref,
    cot_ref,
    image_ref,
    out_ref,
    raw_s,
    coef_s,
    cot_s,
    rhs_s,
    tint_s,
    alpha_s,
    shade_s,
    weight_s,
    delta_s,
    sums_s,
):
    slot_rows = pos_ref.shape[0]
    groups = cot_ref.shape[1] // (GROUP * PIX)
    chunks = slot_rows // groups
    sub = iota((8, LANES), 0)
    lane = iota((8, LANES), 1)
    tile_of = lane % GROUP
    blocks = slot_rows // 8
    middles = []
    for group in range(groups):
        middle_x = jnp.zeros((8, LANES), f32)
        middle_y = jnp.zeros((8, LANES), f32)
        live = jnp.zeros((8, LANES), i32)
        for tile in range(GROUP):
            shown = order_ref[group * GROUP + tile]
            here = tile_of == tile
            middle_x = jnp.where(here, (shown % TX * 16 + 8).astype(f32), middle_x)
            middle_y = jnp.where(here, (shown // TX * 16 + 8).astype(f32), middle_y)
            live = jnp.where(here, count_ref[group * GROUP + tile], live)
        middles.append((middle_x, middle_y, live))

    for block in range(blocks):
        group = block * 8 // chunks
        middle_x, middle_y, live = middles[group]
        found = gather_rows(
            rows_ref, layout.row, layout.count // layout.minors(), layout.minors(), pos_ref[8 * block : 8 * block + 8, :]
        )
        for channel in range(PROJ):
            raw_s[channel * slot_rows + 8 * block : channel * slot_rows + 8 * block + 8, :] = found[channel]
        at_x = found[0] - middle_x
        at_y = found[1] - middle_y
        quad_a = -0.5 * found[2]
        quad_b = -found[3]
        quad_c = -0.5 * found[4]
        flat = quad_a * at_x * at_x + quad_c * at_y * at_y + quad_b * at_x * at_y + jnp.log(found[5])
        place = (8 * block - group * chunks + sub) * STEP + lane // GROUP
        terms = (
            quad_a * LOG2E,
            quad_b * LOG2E,
            quad_c * LOG2E,
            (-2.0 * quad_a * at_x - quad_b * at_y) * LOG2E,
            (-2.0 * quad_c * at_y - quad_b * at_x) * LOG2E,
            jnp.where(place < live, flat * LOG2E, -1e30),
        )
        for index, term in enumerate(terms):
            for part, value in enumerate(split_three(term)):
                coef_s[pl.ds(8 * block * 24 + 6 * part + index, 8, stride=24), :] = value
        for colour in range(3):
            for part, value in enumerate(split_two(found[6 + colour])):
                coef_s[pl.ds(8 * block * 24 + 18 + 3 * part + colour, 8, stride=24), :] = value

    pixel = iota((24, PIX), 1)
    row = iota((24, PIX), 0)
    pix_x = (pixel % 16).astype(f32) - 7.5
    pix_y = (pixel // 16).astype(f32) - 7.5
    kind = row % 6
    monomials = jnp.where(kind == 0, pix_x * pix_x, jnp.where(kind == 1, pix_x * pix_y, 1.0))
    monomials = jnp.where(kind == 2, pix_y * pix_y, monomials)
    monomials = jnp.where(kind == 3, pix_x, jnp.where(kind == 4, pix_y, monomials))
    moments = jnp.where(iota((8, PIX), 0) < 6, monomials[0:8], 0.0).astype(bf16)
    monomials = jnp.where(row < 18, monomials, 0.0)
    nothing = jnp.zeros((24, PIX), f32)
    for group in range(groups):
        for colour in range(3):
            for tile in range(GROUP):
                start = (group * GROUP + tile) * PIX
                cot_s[group * 24 + colour * GROUP + tile, :] = cot_ref[colour, start : start + PIX]
    cots = []
    for group in range(groups):
        first, second = split_two(cot_s[group * 24 : (group + 1) * 24, :])
        cots.append((jnp.concatenate([first, second], axis=0).astype(bf16), first.astype(bf16)))
        rhs_s[group] = jnp.concatenate(
            [
                jnp.concatenate([monomials, nothing], axis=1),
                jnp.concatenate([nothing, first], axis=1),
                jnp.concatenate([nothing, first], axis=1),
                jnp.concatenate([nothing, second], axis=1),
            ],
            axis=0,
        ).astype(bf16)

    own_tile = sub == tile_of

    def evaluate(index, _):
        for group in range(groups):
            chunk = group * chunks + index
            coefs = coef_s[pl.ds(pl.multiple_of(chunk * 24, 8), 24), :]
            tints = [jnp.where(own_tile, coefs[18 + one : 19 + one], 0.0) for one in range(6)]
            lhs = jnp.concatenate([coefs] + tints + tints[:3], axis=0).astype(bf16)
            tint_s[chunk] = lhs[24:72]
            both = dot_tn(lhs, rhs_s[group])
            start = pl.multiple_of(chunk * LANES, LANES)
            alpha_s[pl.ds(start, LANES), :] = jnp.exp2(both[:, :PIX])
            shade_s[pl.ds(start, LANES), :] = both[:, PIX:]
        return 0

    lax.fori_loop(0, chunks, evaluate, 0)

    def forward(index, state):
        out = []
        for group in range(groups):
            trans, image = state[group]
            chunk = group * chunks + index
            start = pl.multiple_of(chunk * LANES, LANES)
            for step in range(STEP):
                alpha = alpha_s[pl.ds(start + step * GROUP, GROUP), :]
                weight = trans * alpha
                trans = trans - weight
                weight_s[pl.ds(start + step * GROUP, GROUP), :] = weight
            first, second = split_two(weight_s[pl.ds(start, LANES), :])
            first = first.astype(bf16)
            second = second.astype(bf16)
            tints = tint_s[chunk]
            by_first = dot(tints, first)
            image = image + by_first[:24] + by_first[24:] + dot(tints[:24], second)
            both, leading = cots[group]
            by_first = dot_nt(both, first)
            tint_grad = by_first[:24] + by_first[24:] + dot_nt(leading, second)
            for colour in range(3):
                own = jnp.where(own_tile, tint_grad[colour * GROUP : (colour + 1) * GROUP], 0.0)
                sums_s[pl.ds(chunk * 16 + 8 + colour, 1), :] = jnp.sum(own, axis=0, keepdims=True)
            out.append((trans, image))
        return tuple(out)

    start = tuple((jnp.ones((GROUP, PIX), f32), jnp.zeros((24, PIX), f32)) for _ in range(groups))
    state = lax.fori_loop(0, chunks, forward, start)
    for group in range(groups):
        for colour in range(3):
            for tile in range(GROUP):
                at = (group * GROUP + tile) * PIX
                image_ref[colour, at : at + PIX] = state[group][1][colour * GROUP + tile]

    def backward(index, state):
        out = []
        for group in range(groups):
            behind = state[group]
            chunk = group * chunks + chunks - 1 - index
            start = pl.multiple_of(chunk * LANES, LANES)
            for step in reversed(range(STEP)):
                at = pl.ds(start + step * GROUP, GROUP)
                ahead = shade_s[at, :] - behind
                delta_s[group, step * GROUP : (step + 1) * GROUP, :] = weight_s[at, :] * ahead
                behind = behind + alpha_s[at, :] * ahead
            first, second = split_two(delta_s[group])
            found = dot_nt(moments, first.astype(bf16)) + dot_nt(moments, second.astype(bf16))
            sums_s[pl.ds(pl.multiple_of(chunk * 16, 8), 8), :] = found
            out.append(behind)
        return tuple(out)

    lax.fori_loop(0, chunks, backward, tuple(jnp.zeros((GROUP, PIX), f32) for _ in range(groups)))

    slot_s = coef_s
    for block in range(blocks):
        middle_x, middle_y, _ = middles[block * 8 // chunks]
        at = slice(8 * block, 8 * block + 8)
        raw = [raw_s[channel * slot_rows + 8 * block : channel * slot_rows + 8 * block + 8, :] for channel in range(6)]
        (sum_xx, sum_xy, sum_yy, sum_x, sum_y, sum_one) = [
            sums_s[pl.ds(8 * block * 16 + index, 8, stride=16), :] for index in range(6)
        ]
        at_x = raw[0] - middle_x
        at_y = raw[1] - middle_y
        off_x = sum_x - at_x * sum_one
        off_y = sum_y - at_y * sum_one
        grads = [
            raw[2] * off_x + raw[3] * off_y,
            raw[4] * off_y + raw[3] * off_x,
            -0.5 * (sum_xx - at_x * (sum_x + off_x)),
            -(sum_xy - at_y * sum_x - at_x * off_y),
            -0.5 * (sum_yy - at_y * (sum_y + off_y)),
            sum_one / raw[5],
        ] + [sums_s[pl.ds(8 * block * 16 + 8 + colour, 8, stride=16), :] for colour in range(3)]
        for channel, value in enumerate(grads):
            slot_s[channel * slot_rows + 8 * block : channel * slot_rows + 8 * block + 8, :] = value
    for block in range(layout.count // 8):
        slots = layout.natural(back_ref, block)
        found = gather_rows(slot_s, lambda channel, major, minor: channel * slot_rows + major, slot_rows, 1, slots)
        for channel in range(PROJ):
            out_ref[layout.block(channel, block), :] = found[channel]


def collect_kernel(layout, camera_frame, angles_ref, gauss_ref, asked_ref, terms_ref, grad_ref, lhs_s, rhs_s, total_s, dense_s, out_s):
    rows = gauss_ref.shape[1] // LANES
    wide = 2 * LANES
    lows = gauss_ref.shape[1] // wide
    low_id = iota((lows, LANES), 0)
    high_id = iota((wide, LANES), 0)
    minors = layout.minors()
    total_s[...] = jnp.zeros(total_s.shape, f32)

    def add(index, _):
        start = pl.multiple_of(index * 8, 8)
        asked = asked_ref[pl.ds(start, 8), :]
        low = asked // wide
        high = asked % wide
        for row in range(8):
            lanes = slice(row * LANES, (row + 1) * LANES)
            mine = low[row : row + 1] == low_id
            rhs_s[:, lanes] = jnp.where(high[row : row + 1] == high_id, 1.0, 0.0).astype(bf16)
            for channel in range(PROJ):
                at = layout.row(channel, index * (8 // minors) + row // minors, row % minors)
                for part, value in enumerate(split_two(terms_ref[pl.ds(at, 1), :])):
                    first = (part * PROJ + channel) * lows
                    lhs_s[first : first + lows, lanes] = jnp.where(mine, value, 0.0).astype(bf16)
        total_s[...] += dot_nt(lhs_s[...], rhs_s[...])
        return 0

    lax.fori_loop(0, layout.count // 8, add, 0)
    spread_columns(gauss_ref, dense_s)
    rotation = view(angles_ref)
    basis = harmonics(*rotation[2])
    for half in range(2):
        lanes = slice(half * LANES, (half + 1) * LANES)
        sums = [
            total_s[channel * lows : (channel + 1) * lows, lanes]
            + total_s[(PROJ + channel) * lows : (PROJ + channel + 1) * lows, lanes]
            for channel in range(PROJ)
        ]
        columns = tuple(dense_s[pl.ds(index * rows + half, lows, stride=2), :] for index in range(11))
        _, pullback = jax.vjp(lambda *values: shape_of(values, rotation, camera_frame), *columns)
        grads = pullback(tuple(sums[:6]))
        for index, value in enumerate(tuple(grads) + tuple(sums[6:])):
            out_s[pl.ds(index * rows + half, lows, stride=2), :] = value
    sub = iota((8, LANES), 0)
    patterns = [basis_rows(basis, eighth) for eighth in range(8)]
    for row in range(rows):
        lanes = slice(row * LANES, (row + 1) * LANES)
        grad_ref[0:8, lanes] = out_s[pl.ds(row, 8, stride=rows), :]
        tints = [out_s[(11 + colour) * rows + row : (11 + colour) * rows + row + 1, :] for colour in range(3)]
        for eighth in range(1, 8):
            value = None
            for colour in range(3):
                pattern = patterns[eighth][colour]
                if pattern is not None:
                    term = pattern * tints[colour]
                    value = term if value is None else value + term
            if eighth == 1:
                value = jnp.where(sub < 3, out_s[pl.ds(8 * rows + row, 8, stride=rows), :], value)
            if eighth == 7:
                grad_ref[56:59, lanes] = value[0:3]
            else:
                grad_ref[8 * eighth : 8 * eighth + 8, lanes] = value


VMEM = pl.BlockSpec(memory_space=pltpu.VMEM)
SMEM = pl.BlockSpec(memory_space=pltpu.SMEM)


def call(kernel, specs, outs, scratch, flops, name):
    return pl.pallas_call(
        kernel,
        in_specs=specs,
        out_specs=[VMEM] * len(outs),
        out_shape=[jax.ShapeDtypeStruct(shape, dtype) for shape, dtype in outs],
        scratch_shapes=[pltpu.VMEM(shape, dtype) for shape, dtype in scratch],
        compiler_params=pltpu.CompilerParams(vmem_limit_bytes=VMEM_BYTES),
        cost_estimate=pl.CostEstimate(flops=flops, bytes_accessed=4 << 20, transcendentals=0),
        name=name,
    )


def route(devices, owners, locals_):
    slots = owners.size
    per_owner = slots // devices
    rows = slots // LANES
    halves = per_owner // LANES if per_owner % LANES == 0 else 0
    asked = (devices * halves, LANES) if halves else (devices, per_owner)
    return call(
        partial(route_kernel, devices, per_owner),
        [VMEM, VMEM],
        [(asked, i32), ((devices, per_owner), i32), ((rows, LANES), i32)],
        [((rows, LANES), i32)] * 3,
        1 << 30,
        "route",
    )(owners, locals_)


def shade(camera_frame, view_angles, gaussians):
    rows = gaussians.shape[1] // LANES
    return call(
        partial(shade_kernel, camera_frame),
        [SMEM, VMEM],
        [((PROJ * rows, LANES), f32)],
        [((16 * rows, LANES), f32), ((27 * rows, LANES), f32)],
        1 << 30,
        "shade",
    )(view_angles, gaussians)[0]


def pick(layout, table, asked):
    return call(
        partial(pick_kernel, layout),
        [VMEM, VMEM],
        [((PROJ * layout.count, LANES), f32)],
        [],
        1 << 30,
        "pick",
    )(table, asked)[0]


def render(layout, list_counts, tile_order, rows, pos, back, cotangent):
    slot_rows = pos.shape[0]
    groups = tile_order.shape[0] // GROUP
    slots = slot_rows * LANES
    return call(
        partial(render_kernel, layout),
        [SMEM, SMEM, VMEM, VMEM, VMEM, VMEM],
        [(cotangent.shape, f32), ((PROJ * layout.count, LANES), f32)],
        [
            ((PROJ * slot_rows, LANES), f32),
            ((24 * slot_rows, LANES), f32),
            ((24 * groups, PIX), f32),
            ((groups, 96, 2 * PIX), bf16),
            ((slot_rows, 48, LANES), bf16),
            ((slots, PIX), f32),
            ((slots, PIX), f32),
            ((slots, PIX), f32),
            ((groups, LANES, PIX), f32),
            ((16 * slot_rows, LANES), f32),
        ],
        1 << 34,
        "render",
    )(list_counts, tile_order, rows, pos, back, cotangent)


def collect(layout, camera_frame, view_angles, gaussians, asked, terms):
    rows = gaussians.shape[1] // LANES
    lows = gaussians.shape[1] // (2 * LANES)
    return call(
        partial(collect_kernel, layout, camera_frame),
        [SMEM, VMEM, VMEM, VMEM],
        [(gaussians.shape, f32)],
        [
            ((2 * PROJ * lows, 8 * LANES), bf16),
            ((2 * LANES, 8 * LANES), bf16),
            ((2 * PROJ * lows, 2 * LANES), f32),
            ((16 * rows, LANES), f32),
            ((16 * rows, LANES), f32),
        ],
        1 << 32,
        "collect",
    )(view_angles, gaussians, asked, terms)[0]


def swap_rows(layout, devices, rows):
    if layout.halves:
        return lax.all_to_all(rows, "dev", split_axis=0, concat_axis=0, tiled=True)
    apart = rows.reshape(PROJ, devices, layout.count * LANES // devices)
    return lax.all_to_all(apart, "dev", split_axis=1, concat_axis=1, tiled=True).reshape(rows.shape)


def shards(gaussians, view_angles, tile_order, tile_owners, tile_locals, list_counts, image_cotangent):
    devices = lax.axis_size("dev")
    tiles_y = devices * tile_order.shape[0] // TX
    camera_frame = (4.0 * TX, 4.0 * tiles_y, 8.0 * TX, 8.0 * tiles_y)
    layout = Rows(devices, tile_owners.size // devices)
    want, back, pos = route(devices, tile_owners, tile_locals)
    asked = lax.all_to_all(want, "dev", split_axis=0, concat_axis=0, tiled=True)
    table = shade(camera_frame, view_angles, gaussians)
    if not layout.halves:
        asked = asked.reshape(layout.count, LANES)
        back = back.reshape(layout.count, LANES)
    arrived = swap_rows(layout, devices, pick(layout, table, asked))
    rendered, slot_grads = render(layout, list_counts, tile_order, arrived, pos, back, image_cotangent)
    terms = swap_rows(layout, devices, slot_grads)
    gradients = collect(layout, camera_frame, view_angles, gaussians, asked, terms)
    return (rendered, gradients)


def solution(mesh):
    return jax.shard_map(
        shards,
        mesh=mesh,
        in_specs=(
            P(None, "dev"),
            P(),
            P("dev"),
            P("dev", None),
            P("dev", None),
            P("dev"),
            P(None, "dev"),
        ),
        out_specs=(P(None, "dev"), P(None, "dev")),
        check_vma=False,
    )
```

```python
from functools import partial

import jax
import jax.numpy as jnp
from jax import lax
from jax.experimental import pallas as pl
from jax.experimental.pallas import tpu as pltpu
from jax.sharding import PartitionSpec as P

PIX = 256
TX = 32
LANES = 128
PROJ = 9
GROUP = 8
STEP = LANES // GROUP
LOG2E = 1.4426950408889634
VMEM_BYTES = 52 * 1024 * 1024

f32 = jnp.float32
bf16 = jnp.bfloat16
i32 = jnp.int32


def iota(shape, dim):
    return lax.broadcasted_iota(i32, shape, dim)


def lane_pick(row, lanes):
    source = jnp.broadcast_to(row, lanes.shape)
    return jnp.take_along_axis(source, lanes, axis=1, mode="promise_in_bounds")


def split_two(values):
    first = values.astype(bf16).astype(f32)
    return first, values - first


def split_three(values):
    first, rest = split_two(values)
    second, third = split_two(rest)
    return first, second, third


def dot(lhs, rhs):
    return lax.dot_general(lhs, rhs, (((1,), (0,)), ((), ())), preferred_element_type=f32)


def dot_nt(lhs, rhs):
    return lax.dot_general(lhs, rhs, (((1,), (1,)), ((), ())), preferred_element_type=f32)


def dot_tn(lhs, rhs):
    return lax.dot_general(lhs, rhs, (((0,), (0,)), ((), ())), preferred_element_type=f32)


class Rows:
    def __init__(self, devices, per_owner):
        self.halves = per_owner // LANES if per_owner % LANES == 0 else 0
        self.count = devices * per_owner // LANES

    def ids(self, ref, block):
        halves = self.halves
        if halves <= 1:
            return ref[pl.ds(8 * block, 8), :]
        return ref[pl.ds(block // halves * 8 * halves + block % halves, 8, stride=halves), :]

    def natural(self, ref, block):
        halves = self.halves
        if halves <= 1:
            return ref[pl.ds(8 * block, 8), :]
        start = block // halves * 8
        return ref[start : start + 8, block % halves * LANES : (block % halves + 1) * LANES]

    def block(self, channel, block):
        halves = self.halves
        if halves == 0:
            return pl.ds(channel * self.count + 8 * block, 8)
        start = block // halves * 8 * PROJ * halves + channel * halves + block % halves
        return pl.ds(start, 8, stride=PROJ * halves)

    def row(self, channel, major, minor):
        halves = self.halves
        if halves == 0:
            return channel * self.count + major
        return major * (PROJ * halves) + channel * halves + minor

    def minors(self):
        return max(self.halves, 1)


def gather_rows(ref, place, majors, minors, slots, put):
    rows = [one // LANES for one in slots]
    lanes = [one % LANES for one in slots]
    batch = 3
    for first in range(0, PROJ, batch):

        def step(major, found):
            for minor in range(minors):
                here = [one == major * minors + minor for one in rows]
                out = []
                for channel in range(batch):
                    row = ref[pl.ds(place(first + channel, major, minor), 1), :]
                    source = jnp.broadcast_to(row, (8, LANES))
                    out.append(
                        tuple(
                            jnp.where(mask, lane_pick(source, lane), value)
                            for mask, lane, value in zip(here, lanes, found[channel])
                        )
                    )
                found = tuple(out)
            return found

        nothing = tuple(jnp.zeros((8, LANES), f32) for _ in slots)
        found = lax.fori_loop(0, majors, step, (nothing,) * batch, unroll=2)
        for channel in range(batch):
            for block, value in enumerate(found[channel]):
                put(first + channel, block, value)


def route_kernel(devices, per_owner, own_ref, loc_ref, want_ref, back_ref, pos_ref, own_s, loc_s, rank_s):
    rows = own_s.shape[0]
    blocks = own_ref.shape[1] // LANES
    lane = iota((8, LANES), 1)
    from_slot = iota((8, LANES), 0) * STEP + lane // GROUP
    tile_of = lane % GROUP
    for group in range(own_ref.shape[0] // GROUP):
        for block in range(blocks):
            for source, target in ((own_ref, own_s), (loc_ref, loc_s)):
                part = source[group * GROUP : (group + 1) * GROUP, block * LANES : (block + 1) * LANES]
                out = jnp.zeros((8, LANES), i32)
                for tile in range(GROUP):
                    out = jnp.where(tile_of == tile, lane_pick(part[tile : tile + 1], from_slot), out)
                start = (group * blocks + block) * 8
                target[start : start + 8, :] = out
    owner = own_s[...]
    left = (iota((LANES, 2 * LANES), 0) < iota((LANES, 2 * LANES), 1)) | (iota((LANES, 2 * LANES), 1) >= LANES)
    above = iota((rows, rows), 1) < iota((rows, rows), 0)
    hits = jnp.concatenate([jnp.where(owner == one, 1.0, 0.0).astype(bf16) for one in range(devices)], axis=0)
    sums = dot(hits, jnp.where(left, 1.0, 0.0).astype(bf16))
    totals = jnp.concatenate(
        [sums[one * rows : (one + 1) * rows, LANES:].astype(bf16) for one in range(devices)], axis=1
    )
    base = dot(jnp.where(above, 1.0, 0.0).astype(bf16), totals)
    rank = jnp.zeros((rows, LANES), f32)
    for one in range(devices):
        here = sums[one * rows : (one + 1) * rows, :LANES] + base[:, one * LANES : (one + 1) * LANES]
        rank = jnp.where(owner == one, here, rank)
    rank = rank.astype(i32)
    pos_ref[...] = owner * per_owner + rank
    rank_s[...] = rank

    owner_id = iota((devices, LANES), 0)
    rank_id = iota((per_owner, LANES), 0)
    slot_lane = iota((devices, LANES), 1).astype(f32)

    def place(index, total):
        start = pl.multiple_of(index * 8, 8)
        own_rows = own_s[pl.ds(start, 8), :]
        loc_rows = loc_s[pl.ds(start, 8), :]
        rank_rows = rank_s[pl.ds(start, 8), :]
        high_rows = (loc_rows // LANES).astype(f32)
        low_rows = (loc_rows % LANES).astype(f32)
        lhs = []
        rhs = []
        for row in range(8):
            mine = own_rows[row : row + 1] == owner_id
            number = (start + row).astype(f32)
            lhs.append(
                jnp.concatenate(
                    [
                        jnp.where(mine, high_rows[row : row + 1], 0.0),
                        jnp.where(mine, low_rows[row : row + 1], 0.0),
                        jnp.where(mine, number, 0.0),
                        jnp.where(mine, slot_lane, 0.0),
                    ],
                    axis=0,
                ).astype(bf16)
            )
            rhs.append(jnp.where(rank_rows[row : row + 1] == rank_id, 1.0, 0.0).astype(bf16))
        return total + dot_nt(jnp.concatenate(lhs, axis=1), jnp.concatenate(rhs, axis=1))

    total = lax.fori_loop(0, rows // 8, place, jnp.zeros((4 * devices, per_owner), f32)).astype(i32)
    want = total[:devices] * LANES + total[devices : 2 * devices]
    halves = per_owner // LANES
    if per_owner % LANES == 0 and halves > 1:
        for half in range(halves):
            want_ref[pl.ds(half, devices, stride=halves), :] = want[:, half * LANES : (half + 1) * LANES]
    else:
        want_ref[...] = want
    back_ref[...] = total[2 * devices : 3 * devices] * LANES + total[3 * devices :]


def view(angles_ref):
    angle = [jnp.full((1, LANES), angles_ref[index], f32) for index in range(3)]
    (cos_a, cos_b, cos_c) = [jnp.cos(one) for one in angle]
    (sin_a, sin_b, sin_c) = [jnp.sin(one) for one in angle]
    return [
        [cos_c * cos_b, cos_c * sin_b * sin_a - sin_c * cos_a, cos_c * sin_b * cos_a + sin_c * sin_a],
        [sin_c * cos_b, sin_c * sin_b * sin_a + cos_c * cos_a, sin_c * sin_b * cos_a - cos_c * sin_a],
        [-sin_b, cos_b * sin_a, cos_b * cos_a],
    ]


def harmonics(along_x, along_y, along_z):
    sq_x = along_x * along_x
    sq_y = along_y * along_y
    sq_z = along_z * along_z
    return [
        0.28209479177387814 + 0.0 * along_x,
        -0.4886025119029199 * along_y,
        0.4886025119029199 * along_z,
        -0.4886025119029199 * along_x,
        1.0925484305920792 * along_x * along_y,
        -1.0925484305920792 * along_y * along_z,
        0.31539156525252005 * (2.0 * sq_z - sq_x - sq_y),
        -1.0925484305920792 * along_x * along_z,
        0.5462742152960396 * (sq_x - sq_y),
        -0.5900435899266435 * along_y * (3.0 * sq_x - sq_y),
        2.890611442640554 * along_x * along_y * along_z,
        -0.4570457994644658 * along_y * (4.0 * sq_z - sq_x - sq_y),
        0.3731763325901154 * along_z * (2.0 * sq_z - 3.0 * sq_x - 3.0 * sq_y),
        -0.4570457994644658 * along_x * (4.0 * sq_z - sq_x - sq_y),
        1.445305721320277 * along_z * (sq_x - sq_y),
        -0.5900435899266435 * along_x * (sq_x - 3.0 * sq_y),
    ]


def basis_rows(basis, eighth):
    sub = iota((8, LANES), 0)
    found = []
    for colour in range(3):
        out = None
        for inner in range(8):
            index = 8 * eighth + inner - 11 - 16 * colour
            if 0 <= index < 16:
                out = jnp.zeros((8, LANES), f32) if out is None else out
                out = jnp.where(sub == inner, basis[index], out)
        found.append(out)
    return found


def shape_of(columns, rotation, camera_frame):
    focal_x, focal_y, centre_x, centre_y = camera_frame
    positions = columns[0:3]
    cam_first = rotation[0][0] * positions[0] + rotation[0][1] * positions[1] + rotation[0][2] * positions[2]
    cam_second = rotation[1][0] * positions[0] + rotation[1][1] * positions[1] + rotation[1][2] * positions[2]
    mean_x = centre_x + focal_x * cam_first
    mean_y = centre_y + focal_y * cam_second
    scales = [jnp.exp(one) for one in columns[3:6]]
    quat_w, quat_x, quat_y, quat_z = columns[6:10]
    norm_sq = jnp.maximum(quat_w * quat_w + quat_x * quat_x + quat_y * quat_y + quat_z * quat_z, 1.0)
    twice = 2.0 / norm_sq
    turned = [
        [
            1.0 - twice * (quat_y * quat_y + quat_z * quat_z),
            twice * (quat_x * quat_y - quat_w * quat_z),
            twice * (quat_x * quat_z + quat_w * quat_y),
        ],
        [
            twice * (quat_x * quat_y + quat_w * quat_z),
            1.0 - twice * (quat_x * quat_x + quat_z * quat_z),
            twice * (quat_y * quat_z - quat_w * quat_x),
        ],
        [
            twice * (quat_x * quat_z - quat_w * quat_y),
            twice * (quat_y * quat_z + quat_w * quat_x),
            1.0 - twice * (quat_x * quat_x + quat_y * quat_y),
        ],
    ]
    rows = []
    for focal, turn in ((focal_x, rotation[0]), (focal_y, rotation[1])):
        rows.append(
            [
                focal * (turn[0] * turned[0][k] + turn[1] * turned[1][k] + turn[2] * turned[2][k]) * scales[k]
                for k in range(3)
            ]
        )
    first, second = rows
    cov_a = first[0] * first[0] + first[1] * first[1] + first[2] * first[2] + 0.3
    cov_b = first[0] * second[0] + first[1] * second[1] + first[2] * second[2]
    cov_c = second[0] * second[0] + second[1] * second[1] + second[2] * second[2] + 0.3
    determinant = cov_a * cov_c - cov_b * cov_b
    opacity = 1.0 / (1.0 + jnp.exp(-columns[10]))
    return mean_x, mean_y, cov_c / determinant, -cov_b / determinant, cov_a / determinant, opacity


def spread_columns(gauss_ref, dense_s):
    rows = gauss_ref.shape[1] // LANES
    for row in range(rows):
        for eighth in range(2):
            dense_s[pl.ds(8 * eighth * rows + row, 8, stride=rows), :] = gauss_ref[
                8 * eighth : 8 * eighth + 8, row * LANES : (row + 1) * LANES
            ]


def shade_kernel(camera_frame, angles_ref, gauss_ref, parts_ref, dense_s, tint_s):
    rows = gauss_ref.shape[1] // LANES
    spread_columns(gauss_ref, dense_s)
    rotation = view(angles_ref)
    basis = harmonics(*rotation[2])
    patterns = [basis_rows(basis, eighth) for eighth in range(7)]
    for row in range(rows):
        lanes = slice(row * LANES, (row + 1) * LANES)
        tints = [None] * 3
        for eighth in range(1, 7):
            block = gauss_ref[8 * eighth : 8 * eighth + 8, lanes]
            for colour in range(3):
                pattern = patterns[eighth][colour]
                if pattern is not None:
                    term = block * pattern
                    tints[colour] = term if tints[colour] is None else tints[colour] + term
        for colour in range(3):
            tint_s[pl.ds(8 * colour * rows + row, 8, stride=rows), :] = tints[colour]
        tint_s[pl.ds(24 * rows + row, 3, stride=rows), :] = gauss_ref[56:59, lanes]
    columns = [dense_s[index * rows : (index + 1) * rows, :] for index in range(11)]
    shaped = shape_of(columns, rotation, camera_frame)

    def put(channel, value):
        parts = jnp.concatenate(split_three(value), axis=0)
        parts_ref[channel * LANES : (channel + 1) * LANES, :] = parts.T.astype(bf16)

    for index, value in enumerate(shaped):
        put(index, value)
    for colour in range(3):
        total = 0.5
        for inner in range(8):
            start = (8 * colour + inner) * rows
            total = total + tint_s[start : start + rows, :]
        if colour == 2:
            for inner in range(3):
                start = (24 + inner) * rows
                total = total + basis[13 + inner] * tint_s[start : start + rows, :]
        put(6 + colour, total)


def pick_kernel(layout, parts_ref, asked_ref, out_ref):
    rows = parts_ref.shape[1] // 3
    pair = 2 * LANES
    row_id = iota((rows, pair), 0)
    lane_id = iota((LANES, pair), 0)
    minors = layout.minors()

    def pick_some(index, _):
        asked = asked_ref[pl.ds(pl.multiple_of(index * 8, 8), 8), :]
        for two in range(4):
            slots = jnp.concatenate([asked[2 * two : 2 * two + 1], asked[2 * two + 1 : 2 * two + 2]], axis=1)
            here = jnp.where(slots // LANES == row_id, 1.0, 0.0).astype(bf16)
            found = dot(parts_ref[...], jnp.concatenate([here, here, here], axis=0))
            mine = slots % LANES == lane_id
            for channel in range(PROJ):
                value = jnp.where(mine, found[channel * LANES : (channel + 1) * LANES], 0.0)
                value = jnp.sum(value, axis=0, keepdims=True)
                for one in range(2):
                    row = 2 * two + one
                    at = layout.row(channel, index * (8 // minors) + row // minors, row % minors)
                    out_ref[pl.ds(at, 1), :] = value[:, one * LANES : (one + 1) * LANES]
        return 0

    lax.fori_loop(0, layout.count // 8, pick_some, 0)


def render_kernel(
    layout,
    count_ref,
    order_ref,
    rows_ref,
    pos_ref,
    back_ref,
    cot_ref,
    image_ref,
    out_ref,
    raw_s,
    coef_s,
    cot_s,
    rhs_s,
    tint_s,
    alpha_s,
    shade_s,
    weight_s,
    delta_s,
    sums_s,
):
    slot_rows = pos_ref.shape[0]
    groups = cot_ref.shape[1] // (GROUP * PIX)
    chunks = slot_rows // groups
    sub = iota((8, LANES), 0)
    lane = iota((8, LANES), 1)
    tile_of = lane % GROUP
    blocks = slot_rows // 8
    middles = []
    for group in range(groups):
        middle_x = jnp.zeros((8, LANES), f32)
        middle_y = jnp.zeros((8, LANES), f32)
        live = jnp.zeros((8, LANES), i32)
        for tile in range(GROUP):
            shown = order_ref[group * GROUP + tile]
            here = tile_of == tile
            middle_x = jnp.where(here, (shown % TX * 16 + 8).astype(f32), middle_x)
            middle_y = jnp.where(here, (shown // TX * 16 + 8).astype(f32), middle_y)
            live = jnp.where(here, count_ref[group * GROUP + tile], live)
        middles.append((middle_x, middle_y, live))

    def put_raw(channel, block, value):
        raw_s[channel * slot_rows + 8 * block : channel * slot_rows + 8 * block + 8, :] = value

    slots = [pos_ref[8 * block : 8 * block + 8, :] for block in range(blocks)]
    gather_rows(rows_ref, layout.row, layout.count // layout.minors(), layout.minors(), slots, put_raw)
    for block in range(blocks):
        group = block * 8 // chunks
        middle_x, middle_y, live = middles[group]
        found = [
            raw_s[channel * slot_rows + 8 * block : channel * slot_rows + 8 * block + 8, :] for channel in range(PROJ)
        ]
        at_x = found[0] - middle_x
        at_y = found[1] - middle_y
        quad_a = -0.5 * found[2]
        quad_b = -found[3]
        quad_c = -0.5 * found[4]
        flat = quad_a * at_x * at_x + quad_c * at_y * at_y + quad_b * at_x * at_y + jnp.log(found[5])
        place = (8 * block - group * chunks + sub) * STEP + lane // GROUP
        terms = (
            quad_a * LOG2E,
            quad_b * LOG2E,
            quad_c * LOG2E,
            (-2.0 * quad_a * at_x - quad_b * at_y) * LOG2E,
            (-2.0 * quad_c * at_y - quad_b * at_x) * LOG2E,
            jnp.where(place < live, flat * LOG2E, -1e30),
        )
        for index, term in enumerate(terms):
            for part, value in enumerate(split_three(term)):
                coef_s[pl.ds(8 * block * 24 + 6 * part + index, 8, stride=24), :] = value
        for colour in range(3):
            for part, value in enumerate(split_two(found[6 + colour])):
                coef_s[pl.ds(8 * block * 24 + 18 + 3 * part + colour, 8, stride=24), :] = value

    pixel = iota((24, PIX), 1)
    row = iota((24, PIX), 0)
    pix_x = (pixel % 16).astype(f32) - 7.5
    pix_y = (pixel // 16).astype(f32) - 7.5
    kind = row % 6
    monomials = jnp.where(kind == 0, pix_x * pix_x, jnp.where(kind == 1, pix_x * pix_y, 1.0))
    monomials = jnp.where(kind == 2, pix_y * pix_y, monomials)
    monomials = jnp.where(kind == 3, pix_x, jnp.where(kind == 4, pix_y, monomials))
    moments = jnp.where(iota((8, PIX), 0) < 6, monomials[0:8], 0.0).astype(bf16)
    monomials = jnp.where(row < 18, monomials, 0.0)
    nothing = jnp.zeros((24, PIX), f32)
    for group in range(groups):
        for colour in range(3):
            for tile in range(GROUP):
                start = (group * GROUP + tile) * PIX
                cot_s[group * 24 + colour * GROUP + tile, :] = cot_ref[colour, start : start + PIX]
    cots = []
    for group in range(groups):
        first, second = split_two(cot_s[group * 24 : (group + 1) * 24, :])
        cots.append((jnp.concatenate([first, second], axis=0).astype(bf16), first.astype(bf16)))
        rhs_s[group] = jnp.concatenate(
            [
                jnp.concatenate([monomials, nothing], axis=1),
                jnp.concatenate([nothing, first], axis=1),
                jnp.concatenate([nothing, first], axis=1),
                jnp.concatenate([nothing, second], axis=1),
            ],
            axis=0,
        ).astype(bf16)

    own_tile = sub == tile_of

    def evaluate(index, _):
        for group in range(groups):
            chunk = group * chunks + index
            coefs = coef_s[pl.ds(pl.multiple_of(chunk * 24, 8), 24), :]
            tints = [jnp.where(own_tile, coefs[18 + one : 19 + one], 0.0) for one in range(6)]
            lhs = jnp.concatenate([coefs] + tints + tints[:3], axis=0).astype(bf16)
            tint_s[chunk] = lhs[24:72]
            both = dot_tn(lhs, rhs_s[group])
            start = pl.multiple_of(chunk * LANES, LANES)
            alpha_s[pl.ds(start, LANES), :] = jnp.exp2(both[:, :PIX])
            shade_s[pl.ds(start, LANES), :] = both[:, PIX:]
        return 0

    lax.fori_loop(0, chunks, evaluate, 0)

    def forward(index, state):
        out = []
        for group in range(groups):
            trans, image = state[group]
            chunk = group * chunks + index
            start = pl.multiple_of(chunk * LANES, LANES)
            for step in range(STEP):
                alpha = alpha_s[pl.ds(start + step * GROUP, GROUP), :]
                weight = trans * alpha
                trans = trans - weight
                weight_s[pl.ds(start + step * GROUP, GROUP), :] = weight
            first, second = split_two(weight_s[pl.ds(start, LANES), :])
            first = first.astype(bf16)
            second = second.astype(bf16)
            tints = tint_s[chunk]
            by_first = dot(tints, first)
            image = image + by_first[:24] + by_first[24:] + dot(tints[:24], second)
            both, leading = cots[group]
            by_first = dot_nt(both, first)
            tint_grad = by_first[:24] + by_first[24:] + dot_nt(leading, second)
            for colour in range(3):
                own = jnp.where(own_tile, tint_grad[colour * GROUP : (colour + 1) * GROUP], 0.0)
                sums_s[pl.ds(chunk * 16 + 8 + colour, 1), :] = jnp.sum(own, axis=0, keepdims=True)
            out.append((trans, image))
        return tuple(out)

    start = tuple((jnp.ones((GROUP, PIX), f32), jnp.zeros((24, PIX), f32)) for _ in range(groups))
    state = lax.fori_loop(0, chunks, forward, start)
    for group in range(groups):
        for colour in range(3):
            for tile in range(GROUP):
                at = (group * GROUP + tile) * PIX
                image_ref[colour, at : at + PIX] = state[group][1][colour * GROUP + tile]

    def backward(index, state):
        out = []
        for group in range(groups):
            behind = state[group]
            chunk = group * chunks + chunks - 1 - index
            start = pl.multiple_of(chunk * LANES, LANES)
            for step in reversed(range(STEP)):
                at = pl.ds(start + step * GROUP, GROUP)
                ahead = shade_s[at, :] - behind
                delta_s[group, step * GROUP : (step + 1) * GROUP, :] = weight_s[at, :] * ahead
                behind = behind + alpha_s[at, :] * ahead
            first, second = split_two(delta_s[group])
            found = dot_nt(moments, first.astype(bf16)) + dot_nt(moments, second.astype(bf16))
            sums_s[pl.ds(pl.multiple_of(chunk * 16, 8), 8), :] = found
            out.append(behind)
        return tuple(out)

    lax.fori_loop(0, chunks, backward, tuple(jnp.zeros((GROUP, PIX), f32) for _ in range(groups)))

    slot_s = coef_s
    for block in range(blocks):
        middle_x, middle_y, _ = middles[block * 8 // chunks]
        at = slice(8 * block, 8 * block + 8)
        raw = [raw_s[channel * slot_rows + 8 * block : channel * slot_rows + 8 * block + 8, :] for channel in range(6)]
        (sum_xx, sum_xy, sum_yy, sum_x, sum_y, sum_one) = [
            sums_s[pl.ds(8 * block * 16 + index, 8, stride=16), :] for index in range(6)
        ]
        at_x = raw[0] - middle_x
        at_y = raw[1] - middle_y
        off_x = sum_x - at_x * sum_one
        off_y = sum_y - at_y * sum_one
        grads = [
            raw[2] * off_x + raw[3] * off_y,
            raw[4] * off_y + raw[3] * off_x,
            -0.5 * (sum_xx - at_x * (sum_x + off_x)),
            -(sum_xy - at_y * sum_x - at_x * off_y),
            -0.5 * (sum_yy - at_y * (sum_y + off_y)),
            sum_one / raw[5],
        ] + [sums_s[pl.ds(8 * block * 16 + 8 + colour, 8, stride=16), :] for colour in range(3)]
        for channel, value in enumerate(grads):
            slot_s[channel * slot_rows + 8 * block : channel * slot_rows + 8 * block + 8, :] = value

    def put_out(channel, block, value):
        out_ref[layout.block(channel, block), :] = value

    slots = [layout.natural(back_ref, block) for block in range(layout.count // 8)]
    gather_rows(slot_s, lambda channel, major, minor: channel * slot_rows + major, slot_rows, 1, slots, put_out)


def collect_kernel(layout, camera_frame, angles_ref, gauss_ref, asked_ref, terms_ref, grad_ref, lhs_s, rhs_s, total_s, dense_s, out_s):
    rows = gauss_ref.shape[1] // LANES
    wide = 2 * LANES
    lows = gauss_ref.shape[1] // wide
    low_id = iota((lows, LANES), 0)
    high_id = iota((wide, LANES), 0)
    minors = layout.minors()
    total_s[...] = jnp.zeros(total_s.shape, f32)

    def add(index, _):
        start = pl.multiple_of(index * 8, 8)
        asked = asked_ref[pl.ds(start, 8), :]
        low = asked // wide
        high = asked % wide
        for row in range(8):
            lanes = slice(row * LANES, (row + 1) * LANES)
            mine = low[row : row + 1] == low_id
            rhs_s[:, lanes] = jnp.where(high[row : row + 1] == high_id, 1.0, 0.0).astype(bf16)
            for channel in range(PROJ):
                at = layout.row(channel, index * (8 // minors) + row // minors, row % minors)
                for part, value in enumerate(split_two(terms_ref[pl.ds(at, 1), :])):
                    first = (part * PROJ + channel) * lows
                    lhs_s[first : first + lows, lanes] = jnp.where(mine, value, 0.0).astype(bf16)
        total_s[...] += dot_nt(lhs_s[...], rhs_s[...])
        return 0

    lax.fori_loop(0, layout.count // 8, add, 0)
    spread_columns(gauss_ref, dense_s)
    rotation = view(angles_ref)
    basis = harmonics(*rotation[2])
    for half in range(2):
        lanes = slice(half * LANES, (half + 1) * LANES)
        sums = [
            total_s[channel * lows : (channel + 1) * lows, lanes]
            + total_s[(PROJ + channel) * lows : (PROJ + channel + 1) * lows, lanes]
            for channel in range(PROJ)
        ]
        columns = tuple(dense_s[pl.ds(index * rows + half, lows, stride=2), :] for index in range(11))
        _, pullback = jax.vjp(lambda *values: shape_of(values, rotation, camera_frame), *columns)
        grads = pullback(tuple(sums[:6]))
        for index, value in enumerate(tuple(grads) + tuple(sums[6:])):
            out_s[pl.ds(index * rows + half, lows, stride=2), :] = value
    sub = iota((8, LANES), 0)
    patterns = [basis_rows(basis, eighth) for eighth in range(8)]
    for row in range(rows):
        lanes = slice(row * LANES, (row + 1) * LANES)
        grad_ref[0:8, lanes] = out_s[pl.ds(row, 8, stride=rows), :]
        tints = [out_s[(11 + colour) * rows + row : (11 + colour) * rows + row + 1, :] for colour in range(3)]
        for eighth in range(1, 8):
            value = None
            for colour in range(3):
                pattern = patterns[eighth][colour]
                if pattern is not None:
                    term = pattern * tints[colour]
                    value = term if value is None else value + term
            if eighth == 1:
                value = jnp.where(sub < 3, out_s[pl.ds(8 * rows + row, 8, stride=rows), :], value)
            if eighth == 7:
                grad_ref[56:59, lanes] = value[0:3]
            else:
                grad_ref[8 * eighth : 8 * eighth + 8, lanes] = value


VMEM = pl.BlockSpec(memory_space=pltpu.VMEM)
SMEM = pl.BlockSpec(memory_space=pltpu.SMEM)


def call(kernel, specs, outs, scratch, flops, name):
    return pl.pallas_call(
        kernel,
        in_specs=specs,
        out_specs=[VMEM] * len(outs),
        out_shape=[jax.ShapeDtypeStruct(shape, dtype) for shape, dtype in outs],
        scratch_shapes=[pltpu.VMEM(shape, dtype) for shape, dtype in scratch],
        compiler_params=pltpu.CompilerParams(vmem_limit_bytes=VMEM_BYTES),
        cost_estimate=pl.CostEstimate(flops=flops, bytes_accessed=4 << 20, transcendentals=0),
        name=name,
    )


def route(devices, owners, locals_):
    slots = owners.size
    per_owner = slots // devices
    rows = slots // LANES
    halves = per_owner // LANES if per_owner % LANES == 0 else 0
    asked = (devices * halves, LANES) if halves else (devices, per_owner)
    return call(
        partial(route_kernel, devices, per_owner),
        [VMEM, VMEM],
        [(asked, i32), ((devices, per_owner), i32), ((rows, LANES), i32)],
        [((rows, LANES), i32)] * 3,
        1 << 30,
        "route",
    )(owners, locals_)


def shade(camera_frame, view_angles, gaussians):
    rows = gaussians.shape[1] // LANES
    return call(
        partial(shade_kernel, camera_frame),
        [SMEM, VMEM],
        [((PROJ * LANES, 3 * rows), bf16)],
        [((16 * rows, LANES), f32), ((27 * rows, LANES), f32)],
        1 << 30,
        "shade",
    )(view_angles, gaussians)[0]


def pick(layout, table, asked):
    return call(
        partial(pick_kernel, layout),
        [VMEM, VMEM],
        [((PROJ * layout.count, LANES), f32)],
        [],
        1 << 30,
        "pick",
    )(table, asked)[0]


def render(layout, list_counts, tile_order, rows, pos, back, cotangent):
    slot_rows = pos.shape[0]
    groups = tile_order.shape[0] // GROUP
    slots = slot_rows * LANES
    return call(
        partial(render_kernel, layout),
        [SMEM, SMEM, VMEM, VMEM, VMEM, VMEM],
        [(cotangent.shape, f32), ((PROJ * layout.count, LANES), f32)],
        [
            ((PROJ * slot_rows, LANES), f32),
            ((24 * slot_rows, LANES), f32),
            ((24 * groups, PIX), f32),
            ((groups, 96, 2 * PIX), bf16),
            ((slot_rows, 48, LANES), bf16),
            ((slots, PIX), f32),
            ((slots, PIX), f32),
            ((slots, PIX), f32),
            ((groups, LANES, PIX), f32),
            ((16 * slot_rows, LANES), f32),
        ],
        1 << 34,
        "render",
    )(list_counts, tile_order, rows, pos, back, cotangent)


def collect(layout, camera_frame, view_angles, gaussians, asked, terms):
    rows = gaussians.shape[1] // LANES
    lows = gaussians.shape[1] // (2 * LANES)
    return call(
        partial(collect_kernel, layout, camera_frame),
        [SMEM, VMEM, VMEM, VMEM],
        [(gaussians.shape, f32)],
        [
            ((2 * PROJ * lows, 8 * LANES), bf16),
            ((2 * LANES, 8 * LANES), bf16),
            ((2 * PROJ * lows, 2 * LANES), f32),
            ((16 * rows, LANES), f32),
            ((16 * rows, LANES), f32),
        ],
        1 << 32,
        "collect",
    )(view_angles, gaussians, asked, terms)[0]


def swap_rows(layout, devices, rows):
    if layout.halves:
        return lax.all_to_all(rows, "dev", split_axis=0, concat_axis=0, tiled=True)
    apart = rows.reshape(PROJ, devices, layout.count * LANES // devices)
    return lax.all_to_all(apart, "dev", split_axis=1, concat_axis=1, tiled=True).reshape(rows.shape)


def shards(gaussians, view_angles, tile_order, tile_owners, tile_locals, list_counts, image_cotangent):
    devices = lax.axis_size("dev")
    tiles_y = devices * tile_order.shape[0] // TX
    camera_frame = (4.0 * TX, 4.0 * tiles_y, 8.0 * TX, 8.0 * tiles_y)
    layout = Rows(devices, tile_owners.size // devices)
    want, back, pos = route(devices, tile_owners, tile_locals)
    asked = lax.all_to_all(want, "dev", split_axis=0, concat_axis=0, tiled=True)
    table = shade(camera_frame, view_angles, gaussians)
    if not layout.halves:
        asked = asked.reshape(layout.count, LANES)
        back = back.reshape(layout.count, LANES)
    arrived = swap_rows(layout, devices, pick(layout, table, asked))
    rendered, slot_grads = render(layout, list_counts, tile_order, arrived, pos, back, image_cotangent)
    terms = swap_rows(layout, devices, slot_grads)
    gradients = collect(layout, camera_frame, view_angles, gaussians, asked, terms)
    return (rendered, gradients)


def solution(mesh):
    return jax.shard_map(
        shards,
        mesh=mesh,
        in_specs=(
            P(None, "dev"),
            P(),
            P("dev"),
            P("dev", None),
            P("dev", None),
            P("dev"),
            P(None, "dev"),
        ),
        out_specs=(P(None, "dev"), P(None, "dev")),
        check_vma=False,
    )
```

```python
from functools import partial

import jax
import jax.numpy as jnp
from jax import lax
from jax.experimental import pallas as pl
from jax.experimental.pallas import tpu as pltpu
from jax.sharding import PartitionSpec as P

PIX = 256
TX = 32
LANES = 128
PROJ = 9
GROUP = 8
WIDE = 2 * LANES
PARTS = (3, 3, 3, 3, 3, 2, 2, 2, 2)
STEP = LANES // GROUP
LOG2E = 1.4426950408889634
VMEM_BYTES = 52 * 1024 * 1024

f32 = jnp.float32
bf16 = jnp.bfloat16
i32 = jnp.int32


def iota(shape, dim):
    return lax.broadcasted_iota(i32, shape, dim)


def lane_pick(row, lanes):
    source = jnp.broadcast_to(row, lanes.shape)
    return jnp.take_along_axis(source, lanes, axis=1, mode="promise_in_bounds")


def split_two(values):
    first = values.astype(bf16).astype(f32)
    return first, values - first


def split_three(values):
    first, rest = split_two(values)
    second, third = split_two(rest)
    return first, second, third


def dot(lhs, rhs):
    return lax.dot_general(lhs, rhs, (((1,), (0,)), ((), ())), preferred_element_type=f32)


def dot_nt(lhs, rhs):
    return lax.dot_general(lhs, rhs, (((1,), (1,)), ((), ())), preferred_element_type=f32)


def dot_tn(lhs, rhs):
    return lax.dot_general(lhs, rhs, (((0,), (0,)), ((), ())), preferred_element_type=f32)


class Rows:
    def __init__(self, devices, per_owner):
        self.halves = per_owner // LANES if per_owner % LANES == 0 else 0
        self.count = devices * per_owner // LANES

    def row(self, channel, major, minor):
        halves = self.halves
        if halves == 0:
            return channel * self.count + major
        return major * (PROJ * halves) + channel * halves + minor

    def half(self, ref, channel, half):
        halves = self.halves
        if halves == 0:
            return ref[pl.ds(channel * self.count + half, self.count // 2, stride=2), :]
        return jnp.concatenate(
            [ref[pl.ds(self.row(channel, one // halves, one % halves), 1), :] for one in range(half, self.count, 2)], axis=0
        ) if halves != 2 else ref[pl.ds(channel * 2 + half, self.count // 2, stride=2 * PROJ), :]

    def minors(self):
        return max(self.halves, 1)


def pick_slots(parts, slots, low_id, high_id, put):
    here = jnp.where(slots % WIDE == high_id, 1.0, 0.0).astype(bf16)
    found = dot(parts, here)
    mine = slots // WIDE == low_id
    lows = low_id.shape[0]
    first = 0
    for channel, count in enumerate(PARTS if parts.shape[0] == sum(PARTS) * lows else (2,) * PROJ):
        value = found[first * lows : (first + 1) * lows]
        for part in range(1, count):
            value = value + found[(first + part) * lows : (first + part + 1) * lows]
        first += count
        put(channel, jnp.sum(jnp.where(mine, value, 0.0), axis=0, keepdims=True))


def put_parts(parts_ref, channel, half, value, counts):
    lows = value.shape[0]
    first = sum(counts[:channel])
    parts = split_three(value) if counts[channel] == 3 else split_two(value)
    for part, one in enumerate(parts):
        at = (first + part) * lows
        parts_ref[at : at + lows, half * LANES : (half + 1) * LANES] = one.astype(bf16)


def route_kernel(devices, per_owner, own_hbm, loc_hbm, want_ref, back_ref, pos_ref, own_ref, loc_ref, own_s, loc_s, rank_s, sems):
    copies = [pltpu.make_async_copy(own_hbm, own_ref, sems.at[0]), pltpu.make_async_copy(loc_hbm, loc_ref, sems.at[1])]
    for copy in copies:
        copy.start()
    for copy in copies:
        copy.wait()
    rows = own_s.shape[0]
    blocks = own_ref.shape[1] // LANES
    lane = iota((8, LANES), 1)
    from_slot = iota((8, LANES), 0) * STEP + lane // GROUP
    tile_of = lane % GROUP
    for group in range(own_ref.shape[0] // GROUP):
        for block in range(blocks):
            for source, target in ((own_ref, own_s), (loc_ref, loc_s)):
                part = source[group * GROUP : (group + 1) * GROUP, block * LANES : (block + 1) * LANES]
                out = jnp.zeros((8, LANES), i32)
                for tile in range(GROUP):
                    out = jnp.where(tile_of == tile, lane_pick(part[tile : tile + 1], from_slot), out)
                start = (group * blocks + block) * 8
                target[start : start + 8, :] = out
    owner = own_s[...]
    left = (iota((LANES, 2 * LANES), 0) < iota((LANES, 2 * LANES), 1)) | (iota((LANES, 2 * LANES), 1) >= LANES)
    above = iota((rows, rows), 1) < iota((rows, rows), 0)
    hits = jnp.concatenate([jnp.where(owner == one, 1.0, 0.0).astype(bf16) for one in range(devices)], axis=0)
    sums = dot(hits, jnp.where(left, 1.0, 0.0).astype(bf16))
    totals = jnp.concatenate(
        [sums[one * rows : (one + 1) * rows, LANES:].astype(bf16) for one in range(devices)], axis=1
    )
    base = dot(jnp.where(above, 1.0, 0.0).astype(bf16), totals)
    rank = jnp.zeros((rows, LANES), f32)
    for one in range(devices):
        here = sums[one * rows : (one + 1) * rows, :LANES] + base[:, one * LANES : (one + 1) * LANES]
        rank = jnp.where(owner == one, here, rank)
    rank = rank.astype(i32)
    pos_ref[...] = owner * per_owner + rank
    rank_s[...] = rank

    owner_id = iota((devices, LANES), 0)
    rank_id = iota((per_owner, LANES), 0)
    slot_lane = iota((devices, LANES), 1).astype(f32)

    def place(index, total):
        start = pl.multiple_of(index * 8, 8)
        own_rows = own_s[pl.ds(start, 8), :]
        loc_rows = loc_s[pl.ds(start, 8), :]
        rank_rows = rank_s[pl.ds(start, 8), :]
        high_rows = (loc_rows // LANES).astype(f32)
        low_rows = (loc_rows % LANES).astype(f32)
        lhs = []
        rhs = []
        for row in range(8):
            mine = own_rows[row : row + 1] == owner_id
            number = (start + row).astype(f32)
            lhs.append(
                jnp.concatenate(
                    [
                        jnp.where(mine, high_rows[row : row + 1], 0.0),
                        jnp.where(mine, low_rows[row : row + 1], 0.0),
                        jnp.where(mine, number, 0.0),
                        jnp.where(mine, slot_lane, 0.0),
                    ],
                    axis=0,
                ).astype(bf16)
            )
            rhs.append(jnp.where(rank_rows[row : row + 1] == rank_id, 1.0, 0.0).astype(bf16))
        return total + dot_nt(jnp.concatenate(lhs, axis=1), jnp.concatenate(rhs, axis=1))

    total = lax.fori_loop(0, rows // 8, place, jnp.zeros((4 * devices, per_owner), f32)).astype(i32)
    want = total[:devices] * LANES + total[devices : 2 * devices]
    halves = per_owner // LANES
    if per_owner % LANES == 0 and halves > 1:
        for half in range(halves):
            want_ref[pl.ds(half, devices, stride=halves), :] = want[:, half * LANES : (half + 1) * LANES]
    else:
        want_ref[...] = want
    back_ref[...] = total[2 * devices : 3 * devices] * LANES + total[3 * devices :]


def view(angles_ref):
    angle = [jnp.full((1, LANES), angles_ref[index], f32) for index in range(3)]
    (cos_a, cos_b, cos_c) = [jnp.cos(one) for one in angle]
    (sin_a, sin_b, sin_c) = [jnp.sin(one) for one in angle]
    return [
        [cos_c * cos_b, cos_c * sin_b * sin_a - sin_c * cos_a, cos_c * sin_b * cos_a + sin_c * sin_a],
        [sin_c * cos_b, sin_c * sin_b * sin_a + cos_c * cos_a, sin_c * sin_b * cos_a - cos_c * sin_a],
        [-sin_b, cos_b * sin_a, cos_b * cos_a],
    ]


def harmonics(along_x, along_y, along_z):
    sq_x = along_x * along_x
    sq_y = along_y * along_y
    sq_z = along_z * along_z
    return [
        0.28209479177387814 + 0.0 * along_x,
        -0.4886025119029199 * along_y,
        0.4886025119029199 * along_z,
        -0.4886025119029199 * along_x,
        1.0925484305920792 * along_x * along_y,
        -1.0925484305920792 * along_y * along_z,
        0.31539156525252005 * (2.0 * sq_z - sq_x - sq_y),
        -1.0925484305920792 * along_x * along_z,
        0.5462742152960396 * (sq_x - sq_y),
        -0.5900435899266435 * along_y * (3.0 * sq_x - sq_y),
        2.890611442640554 * along_x * along_y * along_z,
        -0.4570457994644658 * along_y * (4.0 * sq_z - sq_x - sq_y),
        0.3731763325901154 * along_z * (2.0 * sq_z - 3.0 * sq_x - 3.0 * sq_y),
        -0.4570457994644658 * along_x * (4.0 * sq_z - sq_x - sq_y),
        1.445305721320277 * along_z * (sq_x - sq_y),
        -0.5900435899266435 * along_x * (sq_x - 3.0 * sq_y),
    ]


def basis_rows(basis, eighth):
    sub = iota((8, LANES), 0)
    found = []
    for colour in range(3):
        out = None
        for inner in range(8):
            index = 8 * eighth + inner - 11 - 16 * colour
            if 0 <= index < 16:
                out = jnp.zeros((8, LANES), f32) if out is None else out
                out = jnp.where(sub == inner, basis[index], out)
        found.append(out)
    return found


def shape_of(columns, rotation, camera_frame):
    focal_x, focal_y, centre_x, centre_y = camera_frame
    positions = columns[0:3]
    cam_first = rotation[0][0] * positions[0] + rotation[0][1] * positions[1] + rotation[0][2] * positions[2]
    cam_second = rotation[1][0] * positions[0] + rotation[1][1] * positions[1] + rotation[1][2] * positions[2]
    mean_x = centre_x + focal_x * cam_first
    mean_y = centre_y + focal_y * cam_second
    scales = [jnp.exp(one) for one in columns[3:6]]
    quat_w, quat_x, quat_y, quat_z = columns[6:10]
    norm_sq = jnp.maximum(quat_w * quat_w + quat_x * quat_x + quat_y * quat_y + quat_z * quat_z, 1.0)
    twice = 2.0 / norm_sq
    turned = [
        [
            1.0 - twice * (quat_y * quat_y + quat_z * quat_z),
            twice * (quat_x * quat_y - quat_w * quat_z),
            twice * (quat_x * quat_z + quat_w * quat_y),
        ],
        [
            twice * (quat_x * quat_y + quat_w * quat_z),
            1.0 - twice * (quat_x * quat_x + quat_z * quat_z),
            twice * (quat_y * quat_z - quat_w * quat_x),
        ],
        [
            twice * (quat_x * quat_z - quat_w * quat_y),
            twice * (quat_y * quat_z + quat_w * quat_x),
            1.0 - twice * (quat_x * quat_x + quat_y * quat_y),
        ],
    ]
    rows = []
    for focal, turn in ((focal_x, rotation[0]), (focal_y, rotation[1])):
        rows.append(
            [
                focal * (turn[0] * turned[0][k] + turn[1] * turned[1][k] + turn[2] * turned[2][k]) * scales[k]
                for k in range(3)
            ]
        )
    first, second = rows
    cov_a = first[0] * first[0] + first[1] * first[1] + first[2] * first[2] + 0.3
    cov_b = first[0] * second[0] + first[1] * second[1] + first[2] * second[2]
    cov_c = second[0] * second[0] + second[1] * second[1] + second[2] * second[2] + 0.3
    determinant = cov_a * cov_c - cov_b * cov_b
    opacity = 1.0 / (1.0 + jnp.exp(-columns[10]))
    return mean_x, mean_y, cov_c / determinant, -cov_b / determinant, cov_a / determinant, opacity


def spread_columns(gauss_ref, dense_s):
    rows = gauss_ref.shape[1] // LANES
    for row in range(rows):
        for eighth in range(2):
            dense_s[pl.ds(8 * eighth * rows + row, 8, stride=rows), :] = gauss_ref[
                8 * eighth : 8 * eighth + 8, row * LANES : (row + 1) * LANES
            ]


def shade_kernel(camera_frame, angles_ref, gauss_ref, parts_ref, dense_s, tint_s):
    rows = gauss_ref.shape[1] // LANES
    spread_columns(gauss_ref, dense_s)
    rotation = view(angles_ref)
    basis = harmonics(*rotation[2])
    patterns = [basis_rows(basis, eighth) for eighth in range(7)]
    for row in range(rows):
        lanes = slice(row * LANES, (row + 1) * LANES)
        tints = [None] * 3
        for eighth in range(1, 7):
            block = gauss_ref[8 * eighth : 8 * eighth + 8, lanes]
            for colour in range(3):
                pattern = patterns[eighth][colour]
                if pattern is not None:
                    term = block * pattern
                    tints[colour] = term if tints[colour] is None else tints[colour] + term
        for colour in range(3):
            tint_s[pl.ds(8 * colour * rows + row, 8, stride=rows), :] = tints[colour]
        tint_s[pl.ds(24 * rows + row, 3, stride=rows), :] = gauss_ref[56:59, lanes]
    for half in range(2):
        at = [pl.ds(index * rows + half, rows // 2, stride=2) for index in range(27)]
        columns = [dense_s[one, :] for one in at[:11]]
        for index, value in enumerate(shape_of(columns, rotation, camera_frame)):
            put_parts(parts_ref, index, half, value, PARTS)
        for colour in range(3):
            total = 0.5
            for inner in range(8):
                total = total + tint_s[at[8 * colour + inner], :]
            if colour == 2:
                for inner in range(3):
                    total = total + basis[13 + inner] * tint_s[at[24 + inner], :]
            put_parts(parts_ref, 6 + colour, half, total, PARTS)


def pick_kernel(layout, parts_ref, asked_ref, out_ref):
    low_id = iota((parts_ref.shape[0] // sum(PARTS), WIDE), 0)
    high_id = iota((WIDE, WIDE), 0)
    minors = layout.minors()

    def pick_some(index, _):
        slots = jnp.concatenate([asked_ref[pl.ds(2 * index + one, 1), :] for one in range(2)], axis=1)

        def put(channel, value):
            for one in range(2):
                at = layout.row(channel, (2 * index + one) // minors, (2 * index + one) % minors)
                out_ref[pl.ds(at, 1), :] = value[:, one * LANES : (one + 1) * LANES]

        pick_slots(parts_ref[...], slots, low_id, high_id, put)
        return 0

    lax.fori_loop(0, layout.count // 2, pick_some, 0, unroll=2)


def render_kernel(
    layout,
    count_ref,
    order_ref,
    rows_ref,
    pos_ref,
    back_ref,
    cot_ref,
    image_ref,
    out_ref,
    in_s,
    out_s,
    raw_s,
    coef_s,
    cot_s,
    rhs_s,
    tint_s,
    alpha_s,
    shade_s,
    weight_s,
    delta_s,
    sums_s,
):
    slot_rows = pos_ref.shape[0]
    groups = cot_ref.shape[1] // (GROUP * PIX)
    chunks = slot_rows // groups
    sub = iota((8, LANES), 0)
    lane = iota((8, LANES), 1)
    tile_of = lane % GROUP
    blocks = slot_rows // 8
    middles = []
    for group in range(groups):
        middle_x = jnp.zeros((8, LANES), f32)
        middle_y = jnp.zeros((8, LANES), f32)
        live = jnp.zeros((8, LANES), i32)
        for tile in range(GROUP):
            shown = order_ref[group * GROUP + tile]
            here = tile_of == tile
            middle_x = jnp.where(here, (shown % TX * 16 + 8).astype(f32), middle_x)
            middle_y = jnp.where(here, (shown // TX * 16 + 8).astype(f32), middle_y)
            live = jnp.where(here, count_ref[group * GROUP + tile], live)
        middles.append((middle_x, middle_y, live))

    for half in range(2):
        for channel in range(PROJ):
            put_parts(in_s, channel, half, layout.half(rows_ref, channel, half), PARTS)
    low_id = iota((slot_rows // 2, WIDE), 0)
    high_id = iota((WIDE, WIDE), 0)

    def pick_in(index, _):
        slots = jnp.concatenate([pos_ref[pl.ds(2 * index + one, 1), :] for one in range(2)], axis=1)

        def put(channel, value):
            for one in range(2):
                raw_s[pl.ds(channel * slot_rows + 2 * index + one, 1), :] = value[:, one * LANES : (one + 1) * LANES]

        pick_slots(in_s[...], slots, low_id, high_id, put)
        return 0

    lax.fori_loop(0, slot_rows // 2, pick_in, 0, unroll=2)
    for block in range(blocks):
        group = block * 8 // chunks
        middle_x, middle_y, live = middles[group]
        found = [
            raw_s[channel * slot_rows + 8 * block : channel * slot_rows + 8 * block + 8, :] for channel in range(PROJ)
        ]
        at_x = found[0] - middle_x
        at_y = found[1] - middle_y
        quad_a = -0.5 * found[2]
        quad_b = -found[3]
        quad_c = -0.5 * found[4]
        flat = quad_a * at_x * at_x + quad_c * at_y * at_y + quad_b * at_x * at_y + jnp.log(found[5])
        place = (8 * block - group * chunks + sub) * STEP + lane // GROUP
        terms = (
            quad_a * LOG2E,
            quad_b * LOG2E,
            quad_c * LOG2E,
            (-2.0 * quad_a * at_x - quad_b * at_y) * LOG2E,
            (-2.0 * quad_c * at_y - quad_b * at_x) * LOG2E,
            jnp.where(place < live, flat * LOG2E, -1e30),
        )
        for index, term in enumerate(terms):
            for part, value in enumerate(split_three(term)):
                coef_s[pl.ds(8 * block * 24 + 6 * part + index, 8, stride=24), :] = value
        for colour in range(3):
            for part, value in enumerate(split_two(found[6 + colour])):
                coef_s[pl.ds(8 * block * 24 + 18 + 3 * part + colour, 8, stride=24), :] = value

    pixel = iota((24, PIX), 1)
    row = iota((24, PIX), 0)
    pix_x = (pixel % 16).astype(f32) - 7.5
    pix_y = (pixel // 16).astype(f32) - 7.5
    kind = row % 6
    monomials = jnp.where(kind == 0, pix_x * pix_x, jnp.where(kind == 1, pix_x * pix_y, 1.0))
    monomials = jnp.where(kind == 2, pix_y * pix_y, monomials)
    monomials = jnp.where(kind == 3, pix_x, jnp.where(kind == 4, pix_y, monomials))
    moments = jnp.where(iota((8, PIX), 0) < 6, monomials[0:8], 0.0).astype(bf16)
    monomials = jnp.where(row < 18, monomials, 0.0)
    nothing = jnp.zeros((24, PIX), f32)
    for group in range(groups):
        for colour in range(3):
            for tile in range(GROUP):
                start = (group * GROUP + tile) * PIX
                cot_s[group * 24 + colour * GROUP + tile, :] = cot_ref[colour, start : start + PIX]
    cots = []
    spare = jnp.zeros((8, PIX), f32)
    for group in range(groups):
        first, second = split_two(cot_s[group * 24 : (group + 1) * 24, :])
        cots.append(jnp.concatenate([first, spare, second, spare], axis=0).astype(bf16))
        rhs_s[group] = jnp.concatenate(
            [
                jnp.concatenate([jnp.concatenate([nothing, monomials[8 * one : 8 * one + 8]], axis=0) for one in range(3)], axis=0),
                jnp.concatenate([first, spare, first, spare, second, spare], axis=0),
            ],
            axis=1,
        ).astype(bf16)

    own_tile = sub == tile_of

    def evaluate(index, _):
        for group in range(groups):
            chunk = group * chunks + index
            coefs = coef_s[pl.ds(pl.multiple_of(chunk * 24, 8), 24), :]
            tints = [jnp.where(own_tile, coefs[18 + one : 19 + one], 0.0) for one in range(6)]
            lhs = jnp.concatenate(
                tints[:3] + [coefs[0:8]] + tints[3:] + [coefs[8:16]] + tints[:3] + [coefs[16:24]], axis=0
            ).astype(bf16)
            tint_s[chunk] = lhs[0:64]
            both = dot_tn(lhs, rhs_s[group])
            start = pl.multiple_of(chunk * LANES, LANES)
            alpha_s[pl.ds(start, LANES), :] = jnp.exp2(both[:, :PIX])
            shade_s[pl.ds(start, LANES), :] = both[:, PIX:]
        return 0

    lax.fori_loop(0, chunks, evaluate, 0, unroll=2)

    def scan(index, trans):
        out = []
        for group in range(groups):
            one = trans[group]
            start = pl.multiple_of((group * chunks + index) * LANES, LANES)
            for step in range(STEP):
                alpha = alpha_s[pl.ds(start + step * GROUP, GROUP), :]
                weight = one * alpha
                one = one - weight
                weight_s[pl.ds(start + step * GROUP, GROUP), :] = weight
            out.append(one)
        return tuple(out)

    def paint(index, images):
        out = []
        for group in range(groups):
            chunk = group * chunks + index
            start = pl.multiple_of(chunk * LANES, LANES)
            first, second = split_two(weight_s[pl.ds(start, LANES), :])
            first = first.astype(bf16)
            second = second.astype(bf16)
            tints = tint_s[chunk]
            by_first = dot(tints, first)
            out.append(images[group] + by_first[0:24] + by_first[32:56] + dot(tints[0:32], second)[0:24])
            by_first = dot_nt(cots[group], first)
            tint_grad = by_first[0:24] + by_first[32:56] + dot_nt(cots[group][0:32], second)[0:24]
            for colour in range(3):
                own = jnp.where(own_tile, tint_grad[colour * GROUP : (colour + 1) * GROUP], 0.0)
                sums_s[pl.ds(chunk * 16 + 8 + colour, 1), :] = jnp.sum(own, axis=0, keepdims=True)
        return tuple(out)

    def forward(index, state):
        trans, images = state
        images = paint(index - 1, images)
        return scan(index, trans), images

    trans = scan(0, tuple(jnp.ones((GROUP, PIX), f32) for _ in range(groups)))
    images = tuple(jnp.zeros((24, PIX), f32) for _ in range(groups))
    trans, images = lax.fori_loop(1, chunks, forward, (trans, images))
    images = paint(chunks - 1, images)
    for group in range(groups):
        for colour in range(3):
            for tile in range(GROUP):
                at = (group * GROUP + tile) * PIX
                image_ref[colour, at : at + PIX] = images[group][colour * GROUP + tile]

    def moment(index):
        for group in range(groups):
            chunk = group * chunks + index
            first, second = split_two(delta_s[group])
            found = dot_nt(moments, first.astype(bf16)) + dot_nt(moments, second.astype(bf16))
            sums_s[pl.ds(pl.multiple_of(chunk * 16, 8), 8), :] = found

    def rescan(index, behinds):
        out = []
        for group in range(groups):
            behind = behinds[group]
            start = pl.multiple_of((group * chunks + index) * LANES, LANES)
            for step in reversed(range(STEP)):
                at = pl.ds(start + step * GROUP, GROUP)
                ahead = shade_s[at, :] - behind
                delta_s[group, step * GROUP : (step + 1) * GROUP, :] = weight_s[at, :] * ahead
                behind = behind + alpha_s[at, :] * ahead
            out.append(behind)
        return tuple(out)

    def backward(index, behinds):
        moment(chunks - index)
        return rescan(chunks - 1 - index, behinds)

    behinds = rescan(chunks - 1, tuple(jnp.zeros((GROUP, PIX), f32) for _ in range(groups)))
    lax.fori_loop(1, chunks, backward, behinds)
    moment(0)

    slot_s = coef_s
    for block in range(blocks):
        middle_x, middle_y, _ = middles[block * 8 // chunks]
        at = slice(8 * block, 8 * block + 8)
        raw = [raw_s[channel * slot_rows + 8 * block : channel * slot_rows + 8 * block + 8, :] for channel in range(6)]
        (sum_xx, sum_xy, sum_yy, sum_x, sum_y, sum_one) = [
            sums_s[pl.ds(8 * block * 16 + index, 8, stride=16), :] for index in range(6)
        ]
        at_x = raw[0] - middle_x
        at_y = raw[1] - middle_y
        off_x = sum_x - at_x * sum_one
        off_y = sum_y - at_y * sum_one
        grads = [
            raw[2] * off_x + raw[3] * off_y,
            raw[4] * off_y + raw[3] * off_x,
            -0.5 * (sum_xx - at_x * (sum_x + off_x)),
            -(sum_xy - at_y * sum_x - at_x * off_y),
            -0.5 * (sum_yy - at_y * (sum_y + off_y)),
            sum_one / raw[5],
        ] + [sums_s[pl.ds(8 * block * 16 + 8 + colour, 8, stride=16), :] for colour in range(3)]
        for channel, value in enumerate(grads):
            slot_s[channel * slot_rows + 8 * block : channel * slot_rows + 8 * block + 8, :] = value

    for half in range(2):
        for channel in range(PROJ):
            value = slot_s[pl.ds(channel * slot_rows + half, slot_rows // 2, stride=2), :]
            put_parts(out_s, channel, half, value, (2,) * PROJ)
    minors = layout.minors()

    def pick_out(index, _):
        if layout.halves == 2:
            slots = back_ref[pl.ds(index, 1), :]
        else:
            slots = jnp.concatenate([back_ref[pl.ds(2 * index + one, 1), :] for one in range(2)], axis=1)

        def put(channel, value):
            for one in range(2):
                at = layout.row(channel, (2 * index + one) // minors, (2 * index + one) % minors)
                out_ref[pl.ds(at, 1), :] = value[:, one * LANES : (one + 1) * LANES]

        pick_slots(out_s[...], slots, low_id, high_id, put)
        return 0

    lax.fori_loop(0, layout.count // 2, pick_out, 0, unroll=2)


def collect_kernel(layout, camera_frame, angles_ref, gauss_ref, asked_ref, terms_ref, grad_ref, lhs_s, rhs_s, total_s, dense_s, out_s):
    rows = gauss_ref.shape[1] // LANES
    wide = 2 * LANES
    lows = gauss_ref.shape[1] // wide
    low_id = iota((lows, LANES), 0)
    high_id = iota((wide, LANES), 0)
    minors = layout.minors()
    total_s[...] = jnp.zeros(total_s.shape, f32)

    def add(index, _):
        start = pl.multiple_of(index * 8, 8)
        asked = asked_ref[pl.ds(start, 8), :]
        low = asked // wide
        high = asked % wide
        for row in range(8):
            lanes = slice(row * LANES, (row + 1) * LANES)
            mine = low[row : row + 1] == low_id
            rhs_s[:, lanes] = jnp.where(high[row : row + 1] == high_id, 1.0, 0.0).astype(bf16)
            for channel in range(PROJ):
                at = layout.row(channel, index * (8 // minors) + row // minors, row % minors)
                for part, value in enumerate(split_two(terms_ref[pl.ds(at, 1), :])):
                    first = (part * PROJ + channel) * lows
                    lhs_s[first : first + lows, lanes] = jnp.where(mine, value, 0.0).astype(bf16)
        total_s[...] += dot_nt(lhs_s[...], rhs_s[...])
        return 0

    lax.fori_loop(0, layout.count // 8, add, 0)
    spread_columns(gauss_ref, dense_s)
    rotation = view(angles_ref)
    basis = harmonics(*rotation[2])
    for half in range(2):
        lanes = slice(half * LANES, (half + 1) * LANES)
        sums = [
            total_s[channel * lows : (channel + 1) * lows, lanes]
            + total_s[(PROJ + channel) * lows : (PROJ + channel + 1) * lows, lanes]
            for channel in range(PROJ)
        ]
        columns = tuple(dense_s[pl.ds(index * rows + half, lows, stride=2), :] for index in range(11))
        _, pullback = jax.vjp(lambda *values: shape_of(values, rotation, camera_frame), *columns)
        grads = pullback(tuple(sums[:6]))
        for index, value in enumerate(tuple(grads) + tuple(sums[6:])):
            out_s[pl.ds(index * rows + half, lows, stride=2), :] = value
    sub = iota((8, LANES), 0)
    patterns = [basis_rows(basis, eighth) for eighth in range(8)]
    for row in range(rows):
        lanes = slice(row * LANES, (row + 1) * LANES)
        grad_ref[0:8, lanes] = out_s[pl.ds(row, 8, stride=rows), :]
        tints = [out_s[(11 + colour) * rows + row : (11 + colour) * rows + row + 1, :] for colour in range(3)]
        for eighth in range(1, 8):
            value = None
            for colour in range(3):
                pattern = patterns[eighth][colour]
                if pattern is not None:
                    term = pattern * tints[colour]
                    value = term if value is None else value + term
            if eighth == 1:
                value = jnp.where(sub < 3, out_s[pl.ds(8 * rows + row, 8, stride=rows), :], value)
            if eighth == 7:
                grad_ref[56:59, lanes] = value[0:3]
            else:
                grad_ref[8 * eighth : 8 * eighth + 8, lanes] = value


VMEM = pl.BlockSpec(memory_space=pltpu.VMEM)
ANY = pl.BlockSpec(memory_space=pl.ANY)
SMEM = pl.BlockSpec(memory_space=pltpu.SMEM)


def call(kernel, specs, outs, scratch, flops, name):
    return pl.pallas_call(
        kernel,
        in_specs=specs,
        out_specs=[VMEM] * len(outs),
        out_shape=[jax.ShapeDtypeStruct(shape, dtype) for shape, dtype in outs],
        scratch_shapes=[pltpu.VMEM(*one) if isinstance(one, tuple) else one for one in scratch],
        compiler_params=pltpu.CompilerParams(vmem_limit_bytes=VMEM_BYTES),
        cost_estimate=pl.CostEstimate(flops=flops, bytes_accessed=4 << 20, transcendentals=0),
        name=name,
    )


def route(devices, owners, locals_):
    slots = owners.size
    per_owner = slots // devices
    rows = slots // LANES
    halves = per_owner // LANES if per_owner % LANES == 0 else 0
    asked = (devices * halves, LANES) if halves else (devices, per_owner)
    return call(
        partial(route_kernel, devices, per_owner),
        [ANY, ANY],
        [(asked, i32), ((devices, per_owner), i32), ((rows, LANES), i32)],
        [(owners.shape, i32)] * 2 + [((rows, LANES), i32)] * 3 + [pltpu.SemaphoreType.DMA((2,))],
        1 << 30,
        "route",
    )(owners, locals_)


def shade(camera_frame, view_angles, gaussians):
    rows = gaussians.shape[1] // LANES
    return call(
        partial(shade_kernel, camera_frame),
        [SMEM, VMEM],
        [((sum(PARTS) * rows // 2, WIDE), bf16)],
        [((16 * rows, LANES), f32), ((27 * rows, LANES), f32)],
        1 << 30,
        "shade",
    )(view_angles, gaussians)[0]


def pick(layout, table, asked):
    return call(
        partial(pick_kernel, layout),
        [VMEM, VMEM],
        [((PROJ * layout.count, LANES), f32)],
        [],
        1 << 30,
        "pick",
    )(table, asked)[0]


def render(layout, list_counts, tile_order, rows, pos, back, cotangent):
    slot_rows = pos.shape[0]
    groups = tile_order.shape[0] // GROUP
    slots = slot_rows * LANES
    return call(
        partial(render_kernel, layout),
        [SMEM, SMEM, VMEM, VMEM, VMEM, VMEM],
        [(cotangent.shape, f32), ((PROJ * layout.count, LANES), f32)],
        [
            ((sum(PARTS) * slot_rows // 2, WIDE), bf16),
            ((2 * PROJ * slot_rows // 2, WIDE), bf16),
            ((PROJ * slot_rows, LANES), f32),
            ((24 * slot_rows, LANES), f32),
            ((24 * groups, PIX), f32),
            ((groups, 96, 2 * PIX), bf16),
            ((slot_rows, 64, LANES), bf16),
            ((slots, PIX), f32),
            ((slots, PIX), f32),
            ((slots, PIX), f32),
            ((groups, LANES, PIX), f32),
            ((16 * slot_rows, LANES), f32),
        ],
        1 << 34,
        "render",
    )(list_counts, tile_order, rows, pos, back, cotangent)


def collect(layout, camera_frame, view_angles, gaussians, asked, terms):
    rows = gaussians.shape[1] // LANES
    lows = gaussians.shape[1] // (2 * LANES)
    return call(
        partial(collect_kernel, layout, camera_frame),
        [SMEM, VMEM, VMEM, VMEM],
        [(gaussians.shape, f32)],
        [
            ((2 * PROJ * lows, 8 * LANES), bf16),
            ((2 * LANES, 8 * LANES), bf16),
            ((2 * PROJ * lows, 2 * LANES), f32),
            ((16 * rows, LANES), f32),
            ((16 * rows, LANES), f32),
        ],
        1 << 32,
        "collect",
    )(view_angles, gaussians, asked, terms)[0]


def swap_rows(layout, devices, rows):
    if layout.halves:
        apart = rows.reshape(devices * PROJ, layout.halves, LANES)
        return lax.all_to_all(apart, "dev", split_axis=0, concat_axis=0, tiled=True).reshape(rows.shape)
    apart = rows.reshape(PROJ, devices, layout.count * LANES // devices)
    return lax.all_to_all(apart, "dev", split_axis=1, concat_axis=1, tiled=True).reshape(rows.shape)


def shards(gaussians, view_angles, tile_order, tile_owners, tile_locals, list_counts, image_cotangent):
    devices = lax.axis_size("dev")
    tiles_y = devices * tile_order.shape[0] // TX
    camera_frame = (4.0 * TX, 4.0 * tiles_y, 8.0 * TX, 8.0 * tiles_y)
    layout = Rows(devices, tile_owners.size // devices)
    want, back, pos = route(devices, tile_owners, tile_locals)
    asked = lax.all_to_all(want, "dev", split_axis=0, concat_axis=0, tiled=True)
    table = shade(camera_frame, view_angles, gaussians)
    if not layout.halves:
        asked = asked.reshape(layout.count, LANES)
    if layout.halves != 2:
        back = back.reshape(layout.count, LANES)
    arrived = swap_rows(layout, devices, pick(layout, table, asked))
    rendered, slot_grads = render(layout, list_counts, tile_order, arrived, pos, back, image_cotangent)
    terms = swap_rows(layout, devices, slot_grads)
    gradients = collect(layout, camera_frame, view_angles, gaussians, asked, terms)
    return (rendered, gradients)


def solution(mesh):
    return jax.shard_map(
        shards,
        mesh=mesh,
        in_specs=(
            P(None, "dev"),
            P(),
            P("dev"),
            P("dev", None),
            P("dev", None),
            P("dev"),
            P(None, "dev"),
        ),
        out_specs=(P(None, "dev"), P(None, "dev")),
        check_vma=False,
    )
```

```python
from functools import partial

import jax
import jax.numpy as jnp
from jax import lax
from jax.experimental import pallas as pl
from jax.experimental.pallas import tpu as pltpu
from jax.sharding import PartitionSpec as P

PIX = 256
TX = 32
LANES = 128
PROJ = 9
GROUP = 8
WIDE = 2 * LANES
PARTS = (3, 3, 3, 3, 3, 2, 2, 2, 2)
STEP = LANES // GROUP
LOG2E = 1.4426950408889634
BATCH = 4
VMEM_BYTES = 52 * 1024 * 1024

f32 = jnp.float32
bf16 = jnp.bfloat16
i32 = jnp.int32


def iota(shape, dim):
    return lax.broadcasted_iota(i32, shape, dim)


def lane_pick(row, lanes):
    source = jnp.broadcast_to(row, lanes.shape)
    return jnp.take_along_axis(source, lanes, axis=1, mode="promise_in_bounds")


def split_two(values):
    first = values.astype(bf16).astype(f32)
    return first, values - first


def split_three(values):
    first, rest = split_two(values)
    second, third = split_two(rest)
    return first, second, third


def dot(lhs, rhs):
    return lax.dot_general(lhs, rhs, (((1,), (0,)), ((), ())), preferred_element_type=f32)


def dot_nt(lhs, rhs):
    return lax.dot_general(lhs, rhs, (((1,), (1,)), ((), ())), preferred_element_type=f32)


def dot_tn(lhs, rhs):
    return lax.dot_general(lhs, rhs, (((0,), (0,)), ((), ())), preferred_element_type=f32)


class Rows:
    def __init__(self, devices, per_owner):
        self.halves = per_owner // LANES if per_owner % LANES == 0 else 0
        self.count = devices * per_owner // LANES

    def row(self, channel, major, minor):
        halves = self.halves
        if halves == 0:
            return channel * self.count + major
        return major * (PROJ * halves) + channel * halves + minor

    def half(self, ref, channel, half):
        halves = self.halves
        if halves == 0:
            return ref[pl.ds(channel * self.count + half, self.count // 2, stride=2), :]
        return jnp.concatenate(
            [ref[pl.ds(self.row(channel, one // halves, one % halves), 1), :] for one in range(half, self.count, 2)], axis=0
        ) if halves != 2 else ref[pl.ds(channel * 2 + half, self.count // 2, stride=2 * PROJ), :]

    def minors(self):
        return max(self.halves, 1)


def pick_slots(parts, slots, low_id, high_id, put):
    here = jnp.where(slots % WIDE == high_id, 1.0, 0.0).astype(bf16)
    found = dot(parts, here)
    mine = slots // WIDE == low_id
    lows = low_id.shape[0]
    first = 0
    for channel, count in enumerate(PARTS if parts.shape[0] == sum(PARTS) * lows else (2,) * PROJ):
        value = found[first * lows : (first + 1) * lows]
        for part in range(1, count):
            value = value + found[(first + part) * lows : (first + part + 1) * lows]
        first += count
        put(channel, jnp.sum(jnp.where(mine, value, 0.0), axis=0, keepdims=True))


def put_parts(parts_ref, channel, half, value, counts):
    lows = value.shape[0]
    first = sum(counts[:channel])
    parts = split_three(value) if counts[channel] == 3 else split_two(value)
    for part, one in enumerate(parts):
        at = (first + part) * lows
        parts_ref[at : at + lows, half * LANES : (half + 1) * LANES] = one.astype(bf16)


def route_kernel(devices, per_owner, own_hbm, loc_hbm, want_ref, back_ref, pos_ref, own_ref, loc_ref, own_s, loc_s, rank_s, sems):
    copies = [pltpu.make_async_copy(own_hbm, own_ref, sems.at[0]), pltpu.make_async_copy(loc_hbm, loc_ref, sems.at[1])]
    for copy in copies:
        copy.start()
    for copy in copies:
        copy.wait()
    rows = own_s.shape[0]
    blocks = own_ref.shape[1] // LANES
    lane = iota((8, LANES), 1)
    from_slot = iota((8, LANES), 0) * STEP + lane // GROUP
    tile_of = lane % GROUP
    for group in range(own_ref.shape[0] // GROUP):
        for block in range(blocks):
            for source, target in ((own_ref, own_s), (loc_ref, loc_s)):
                part = source[group * GROUP : (group + 1) * GROUP, block * LANES : (block + 1) * LANES]
                out = jnp.zeros((8, LANES), i32)
                for tile in range(GROUP):
                    out = jnp.where(tile_of == tile, lane_pick(part[tile : tile + 1], from_slot), out)
                start = (group * blocks + block) * 8
                target[start : start + 8, :] = out
    owner = own_s[...]
    left = (iota((LANES, 2 * LANES), 0) < iota((LANES, 2 * LANES), 1)) | (iota((LANES, 2 * LANES), 1) >= LANES)
    above = iota((rows, rows), 1) < iota((rows, rows), 0)
    hits = jnp.concatenate([jnp.where(owner == one, 1.0, 0.0).astype(bf16) for one in range(devices)], axis=0)
    sums = dot(hits, jnp.where(left, 1.0, 0.0).astype(bf16))
    totals = jnp.concatenate(
        [sums[one * rows : (one + 1) * rows, LANES:].astype(bf16) for one in range(devices)], axis=1
    )
    base = dot(jnp.where(above, 1.0, 0.0).astype(bf16), totals)
    rank = jnp.zeros((rows, LANES), f32)
    for one in range(devices):
        here = sums[one * rows : (one + 1) * rows, :LANES] + base[:, one * LANES : (one + 1) * LANES]
        rank = jnp.where(owner == one, here, rank)
    rank = rank.astype(i32)
    pos_ref[...] = owner * per_owner + rank
    rank_s[...] = rank

    owner_id = iota((devices, LANES), 0)
    rank_id = iota((per_owner, LANES), 0)
    slot_lane = iota((devices, LANES), 1).astype(f32)

    def place(index, total):
        start = pl.multiple_of(index * 8, 8)
        own_rows = own_s[pl.ds(start, 8), :]
        loc_rows = loc_s[pl.ds(start, 8), :]
        rank_rows = rank_s[pl.ds(start, 8), :]
        high_rows = (loc_rows // LANES).astype(f32)
        low_rows = (loc_rows % LANES).astype(f32)
        lhs = []
        rhs = []
        for row in range(8):
            mine = own_rows[row : row + 1] == owner_id
            number = (start + row).astype(f32)
            lhs.append(
                jnp.concatenate(
                    [
                        jnp.where(mine, high_rows[row : row + 1], 0.0),
                        jnp.where(mine, low_rows[row : row + 1], 0.0),
                        jnp.where(mine, number, 0.0),
                        jnp.where(mine, slot_lane, 0.0),
                    ],
                    axis=0,
                ).astype(bf16)
            )
            rhs.append(jnp.where(rank_rows[row : row + 1] == rank_id, 1.0, 0.0).astype(bf16))
        return total + dot_nt(jnp.concatenate(lhs, axis=1), jnp.concatenate(rhs, axis=1))

    total = lax.fori_loop(0, rows // 8, place, jnp.zeros((4 * devices, per_owner), f32)).astype(i32)
    want = total[:devices] * LANES + total[devices : 2 * devices]
    halves = per_owner // LANES
    if per_owner % LANES == 0 and halves > 1:
        for half in range(halves):
            want_ref[pl.ds(half, devices, stride=halves), :] = want[:, half * LANES : (half + 1) * LANES]
    else:
        want_ref[...] = want
    back_ref[...] = total[2 * devices : 3 * devices] * LANES + total[3 * devices :]


def view(angles_ref):
    angle = [jnp.full((1, LANES), angles_ref[index], f32) for index in range(3)]
    (cos_a, cos_b, cos_c) = [jnp.cos(one) for one in angle]
    (sin_a, sin_b, sin_c) = [jnp.sin(one) for one in angle]
    return [
        [cos_c * cos_b, cos_c * sin_b * sin_a - sin_c * cos_a, cos_c * sin_b * cos_a + sin_c * sin_a],
        [sin_c * cos_b, sin_c * sin_b * sin_a + cos_c * cos_a, sin_c * sin_b * cos_a - cos_c * sin_a],
        [-sin_b, cos_b * sin_a, cos_b * cos_a],
    ]


def harmonics(along_x, along_y, along_z):
    sq_x = along_x * along_x
    sq_y = along_y * along_y
    sq_z = along_z * along_z
    return [
        0.28209479177387814 + 0.0 * along_x,
        -0.4886025119029199 * along_y,
        0.4886025119029199 * along_z,
        -0.4886025119029199 * along_x,
        1.0925484305920792 * along_x * along_y,
        -1.0925484305920792 * along_y * along_z,
        0.31539156525252005 * (2.0 * sq_z - sq_x - sq_y),
        -1.0925484305920792 * along_x * along_z,
        0.5462742152960396 * (sq_x - sq_y),
        -0.5900435899266435 * along_y * (3.0 * sq_x - sq_y),
        2.890611442640554 * along_x * along_y * along_z,
        -0.4570457994644658 * along_y * (4.0 * sq_z - sq_x - sq_y),
        0.3731763325901154 * along_z * (2.0 * sq_z - 3.0 * sq_x - 3.0 * sq_y),
        -0.4570457994644658 * along_x * (4.0 * sq_z - sq_x - sq_y),
        1.445305721320277 * along_z * (sq_x - sq_y),
        -0.5900435899266435 * along_x * (sq_x - 3.0 * sq_y),
    ]


def basis_rows(basis, eighth):
    sub = iota((8, LANES), 0)
    found = []
    for colour in range(3):
        out = None
        for inner in range(8):
            index = 8 * eighth + inner - 11 - 16 * colour
            if 0 <= index < 16:
                out = jnp.zeros((8, LANES), f32) if out is None else out
                out = jnp.where(sub == inner, basis[index], out)
        found.append(out)
    return found


def shape_of(columns, rotation, camera_frame):
    focal_x, focal_y, centre_x, centre_y = camera_frame
    positions = columns[0:3]
    cam_first = rotation[0][0] * positions[0] + rotation[0][1] * positions[1] + rotation[0][2] * positions[2]
    cam_second = rotation[1][0] * positions[0] + rotation[1][1] * positions[1] + rotation[1][2] * positions[2]
    mean_x = centre_x + focal_x * cam_first
    mean_y = centre_y + focal_y * cam_second
    scales = [jnp.exp(one) for one in columns[3:6]]
    quat_w, quat_x, quat_y, quat_z = columns[6:10]
    norm_sq = jnp.maximum(quat_w * quat_w + quat_x * quat_x + quat_y * quat_y + quat_z * quat_z, 1.0)
    twice = 2.0 / norm_sq
    turned = [
        [
            1.0 - twice * (quat_y * quat_y + quat_z * quat_z),
            twice * (quat_x * quat_y - quat_w * quat_z),
            twice * (quat_x * quat_z + quat_w * quat_y),
        ],
        [
            twice * (quat_x * quat_y + quat_w * quat_z),
            1.0 - twice * (quat_x * quat_x + quat_z * quat_z),
            twice * (quat_y * quat_z - quat_w * quat_x),
        ],
        [
            twice * (quat_x * quat_z - quat_w * quat_y),
            twice * (quat_y * quat_z + quat_w * quat_x),
            1.0 - twice * (quat_x * quat_x + quat_y * quat_y),
        ],
    ]
    rows = []
    for focal, turn in ((focal_x, rotation[0]), (focal_y, rotation[1])):
        rows.append(
            [
                focal * (turn[0] * turned[0][k] + turn[1] * turned[1][k] + turn[2] * turned[2][k]) * scales[k]
                for k in range(3)
            ]
        )
    first, second = rows
    cov_a = first[0] * first[0] + first[1] * first[1] + first[2] * first[2] + 0.3
    cov_b = first[0] * second[0] + first[1] * second[1] + first[2] * second[2]
    cov_c = second[0] * second[0] + second[1] * second[1] + second[2] * second[2] + 0.3
    determinant = cov_a * cov_c - cov_b * cov_b
    opacity = 1.0 / (1.0 + jnp.exp(-columns[10]))
    return mean_x, mean_y, cov_c / determinant, -cov_b / determinant, cov_a / determinant, opacity


def spread_columns(gauss_ref, dense_s):
    rows = gauss_ref.shape[1] // LANES
    for row in range(rows):
        for eighth in range(2):
            dense_s[pl.ds(8 * eighth * rows + row, 8, stride=rows), :] = gauss_ref[
                8 * eighth : 8 * eighth + 8, row * LANES : (row + 1) * LANES
            ]


def shade_kernel(camera_frame, angles_ref, gauss_ref, parts_ref, dense_s, tint_s):
    rows = gauss_ref.shape[1] // LANES
    spread_columns(gauss_ref, dense_s)
    rotation = view(angles_ref)
    basis = harmonics(*rotation[2])
    patterns = [basis_rows(basis, eighth) for eighth in range(7)]
    for row in range(rows):
        lanes = slice(row * LANES, (row + 1) * LANES)
        tints = [None] * 3
        for eighth in range(1, 7):
            block = gauss_ref[8 * eighth : 8 * eighth + 8, lanes]
            for colour in range(3):
                pattern = patterns[eighth][colour]
                if pattern is not None:
                    term = block * pattern
                    tints[colour] = term if tints[colour] is None else tints[colour] + term
        for colour in range(3):
            tint_s[pl.ds(8 * colour * rows + row, 8, stride=rows), :] = tints[colour]
        tint_s[pl.ds(24 * rows + row, 3, stride=rows), :] = gauss_ref[56:59, lanes]
    for half in range(2):
        at = [pl.ds(index * rows + half, rows // 2, stride=2) for index in range(27)]
        columns = [dense_s[one, :] for one in at[:11]]
        for index, value in enumerate(shape_of(columns, rotation, camera_frame)):
            put_parts(parts_ref, index, half, value, PARTS)
        for colour in range(3):
            total = 0.5
            for inner in range(8):
                total = total + tint_s[at[8 * colour + inner], :]
            if colour == 2:
                for inner in range(3):
                    total = total + basis[13 + inner] * tint_s[at[24 + inner], :]
            put_parts(parts_ref, 6 + colour, half, total, PARTS)


def pick_kernel(layout, parts_ref, asked_ref, out_ref):
    low_id = iota((parts_ref.shape[0] // sum(PARTS), WIDE), 0)
    high_id = iota((WIDE, WIDE), 0)
    minors = layout.minors()

    def pick_some(index, _):
        slots = jnp.concatenate([asked_ref[pl.ds(2 * index + one, 1), :] for one in range(2)], axis=1)

        def put(channel, value):
            for one in range(2):
                at = layout.row(channel, (2 * index + one) // minors, (2 * index + one) % minors)
                out_ref[pl.ds(at, 1), :] = value[:, one * LANES : (one + 1) * LANES]

        pick_slots(parts_ref[...], slots, low_id, high_id, put)
        return 0

    lax.fori_loop(0, layout.count // 2, pick_some, 0, unroll=4)


def render_kernel(
    layout,
    count_ref,
    order_ref,
    rows_ref,
    pos_ref,
    back_ref,
    cot_ref,
    image_ref,
    out_ref,
    in_s,
    out_s,
    raw_s,
    coef_s,
    cot_s,
    rhs_s,
    tint_s,
    alpha_s,
    shade_s,
    weight_s,
    sums_s,
):
    slot_rows = pos_ref.shape[0]
    groups = cot_ref.shape[1] // (GROUP * PIX)
    chunks = slot_rows // groups
    sub = iota((8, LANES), 0)
    lane = iota((8, LANES), 1)
    tile_of = lane % GROUP
    blocks = slot_rows // 8
    middles = []
    for group in range(groups):
        middle_x = jnp.zeros((8, LANES), f32)
        middle_y = jnp.zeros((8, LANES), f32)
        live = jnp.zeros((8, LANES), i32)
        for tile in range(GROUP):
            shown = order_ref[group * GROUP + tile]
            here = tile_of == tile
            middle_x = jnp.where(here, (shown % TX * 16 + 8).astype(f32), middle_x)
            middle_y = jnp.where(here, (shown // TX * 16 + 8).astype(f32), middle_y)
            live = jnp.where(here, count_ref[group * GROUP + tile], live)
        middles.append((middle_x, middle_y, live))

    for half in range(2):
        for channel in range(PROJ):
            put_parts(in_s, channel, half, layout.half(rows_ref, channel, half), PARTS)
    low_id = iota((slot_rows // 2, WIDE), 0)
    high_id = iota((WIDE, WIDE), 0)

    def pick_in(index, _):
        slots = jnp.concatenate([pos_ref[pl.ds(2 * index + one, 1), :] for one in range(2)], axis=1)

        def put(channel, value):
            for one in range(2):
                raw_s[pl.ds(channel * slot_rows + 2 * index + one, 1), :] = value[:, one * LANES : (one + 1) * LANES]

        pick_slots(in_s[...], slots, low_id, high_id, put)
        return 0

    lax.fori_loop(0, slot_rows // 2, pick_in, 0, unroll=4)
    for block in range(blocks):
        group = block * 8 // chunks
        middle_x, middle_y, live = middles[group]
        found = [
            raw_s[channel * slot_rows + 8 * block : channel * slot_rows + 8 * block + 8, :] for channel in range(PROJ)
        ]
        at_x = found[0] - middle_x
        at_y = found[1] - middle_y
        quad_a = -0.5 * found[2]
        quad_b = -found[3]
        quad_c = -0.5 * found[4]
        flat = quad_a * at_x * at_x + quad_c * at_y * at_y + quad_b * at_x * at_y + jnp.log(found[5])
        place = (8 * block - group * chunks + sub) * STEP + lane // GROUP
        terms = (
            quad_a * LOG2E,
            quad_b * LOG2E,
            quad_c * LOG2E,
            (-2.0 * quad_a * at_x - quad_b * at_y) * LOG2E,
            (-2.0 * quad_c * at_y - quad_b * at_x) * LOG2E,
            jnp.where(place < live, flat * LOG2E, -1e30),
        )
        for index, term in enumerate(terms):
            for part, value in enumerate(split_three(term)):
                coef_s[pl.ds(8 * block * 24 + 6 * part + index, 8, stride=24), :] = value
        for colour in range(3):
            for part, value in enumerate(split_two(found[6 + colour])):
                coef_s[pl.ds(8 * block * 24 + 18 + 3 * part + colour, 8, stride=24), :] = value

    pixel = iota((24, PIX), 1)
    row = iota((24, PIX), 0)
    pix_x = (pixel % 16).astype(f32) - 7.5
    pix_y = (pixel // 16).astype(f32) - 7.5
    kind = row % 6
    monomials = jnp.where(kind == 0, pix_x * pix_x, jnp.where(kind == 1, pix_x * pix_y, 1.0))
    monomials = jnp.where(kind == 2, pix_y * pix_y, monomials)
    monomials = jnp.where(kind == 3, pix_x, jnp.where(kind == 4, pix_y, monomials))
    moments = jnp.where(iota((8, PIX), 0) < 6, monomials[0:8], 0.0).astype(bf16)
    monomials = jnp.where(row < 18, monomials, 0.0)
    nothing = jnp.zeros((24, PIX), f32)
    for group in range(groups):
        for colour in range(3):
            for tile in range(GROUP):
                start = (group * GROUP + tile) * PIX
                cot_s[group * 24 + colour * GROUP + tile, :] = cot_ref[colour, start : start + PIX]
    cots = []
    spare = jnp.zeros((8, PIX), f32)
    for group in range(groups):
        first, second = split_two(cot_s[group * 24 : (group + 1) * 24, :])
        cots.append(jnp.concatenate([first, spare, second, spare], axis=0).astype(bf16))
        rhs_s[group] = jnp.concatenate(
            [
                jnp.concatenate([jnp.concatenate([nothing, monomials[8 * one : 8 * one + 8]], axis=0) for one in range(3)], axis=0),
                jnp.concatenate([first, spare, first, spare, second, spare], axis=0),
            ],
            axis=1,
        ).astype(bf16)

    own_tile = sub == tile_of

    def evaluate(index, _):
        for group in range(groups):
            chunk = group * chunks + index
            coefs = coef_s[pl.ds(pl.multiple_of(chunk * 24, 8), 24), :]
            tints = [jnp.where(own_tile, coefs[18 + one : 19 + one], 0.0) for one in range(6)]
            lhs = jnp.concatenate(
                tints[:3] + [coefs[0:8]] + tints[3:] + [coefs[8:16]] + tints[:3] + [coefs[16:24]], axis=0
            ).astype(bf16)
            tint_s[chunk] = lhs[0:64]
            both = dot_tn(lhs, rhs_s[group])
            start = pl.multiple_of(chunk * LANES, LANES)
            alpha_s[pl.ds(start, LANES), :] = jnp.exp2(both[:, :PIX])
            shade_s[pl.ds(start, LANES), :] = both[:, PIX:]
        return 0

    lax.fori_loop(0, chunks, evaluate, 0, unroll=BATCH)

    def scan(index, trans):
        out = []
        for group in range(groups):
            one = trans[group]
            start = pl.multiple_of((group * chunks + index) * LANES, LANES)
            for step in range(STEP):
                alpha = alpha_s[pl.ds(start + step * GROUP, GROUP), :]
                weight = one * alpha
                one = one - weight
                weight_s[pl.ds(start + step * GROUP, GROUP), :] = weight
            out.append(one)
        return tuple(out)

    def paint(index, images):
        out = []
        for group in range(groups):
            chunk = group * chunks + index
            start = pl.multiple_of(chunk * LANES, LANES)
            first, second = split_two(weight_s[pl.ds(start, LANES), :])
            first = first.astype(bf16)
            second = second.astype(bf16)
            tints = tint_s[chunk]
            by_first = dot(tints, first)
            out.append(images[group] + by_first[0:24] + by_first[32:56] + dot(tints[0:32], second)[0:24])
            by_first = dot_nt(cots[group], first)
            tint_grad = by_first[0:24] + by_first[32:56] + dot_nt(cots[group][0:32], second)[0:24]
            for colour in range(3):
                own = jnp.where(own_tile, tint_grad[colour * GROUP : (colour + 1) * GROUP], 0.0)
                sums_s[pl.ds(chunk * 16 + 8 + colour, 1), :] = jnp.sum(own, axis=0, keepdims=True)
        return tuple(out)

    def scan_batch(batch, trans):
        for one in range(BATCH):
            trans = scan(batch * BATCH + one, trans)
        return trans

    def paint_batch(batch, images):
        for one in range(BATCH):
            images = paint(batch * BATCH + one, images)
        return images

    def forward(batch, state):
        trans, images = state
        images = paint_batch(batch - 1, images)
        return scan_batch(batch, trans), images

    batches = chunks // BATCH
    trans = scan_batch(0, tuple(jnp.ones((GROUP, PIX), f32) for _ in range(groups)))
    images = tuple(jnp.zeros((24, PIX), f32) for _ in range(groups))
    trans, images = lax.fori_loop(1, batches, forward, (trans, images))
    images = paint_batch(batches - 1, images)
    for group in range(groups):
        for colour in range(3):
            for tile in range(GROUP):
                at = (group * GROUP + tile) * PIX
                image_ref[colour, at : at + PIX] = images[group][colour * GROUP + tile]

    def moment(index):
        for group in range(groups):
            chunk = group * chunks + index
            first, second = split_two(shade_s[pl.ds(pl.multiple_of(chunk * LANES, LANES), LANES), :])
            found = dot_nt(moments, first.astype(bf16)) + dot_nt(moments, second.astype(bf16))
            sums_s[pl.ds(pl.multiple_of(chunk * 16, 8), 8), :] = found

    def rescan(index, behinds):
        out = []
        for group in range(groups):
            behind = behinds[group]
            start = pl.multiple_of((group * chunks + index) * LANES, LANES)
            for step in reversed(range(STEP)):
                at = pl.ds(start + step * GROUP, GROUP)
                ahead = shade_s[at, :] - behind
                shade_s[at, :] = weight_s[at, :] * ahead
                behind = behind + alpha_s[at, :] * ahead
            out.append(behind)
        return tuple(out)

    def moment_batch(batch):
        for one in range(BATCH):
            moment(batch * BATCH + one)

    def rescan_batch(batch, behinds):
        for one in reversed(range(BATCH)):
            behinds = rescan(batch * BATCH + one, behinds)
        return behinds

    def backward(index, behinds):
        moment_batch(batches - index)
        return rescan_batch(batches - 1 - index, behinds)

    behinds = rescan_batch(batches - 1, tuple(jnp.zeros((GROUP, PIX), f32) for _ in range(groups)))
    lax.fori_loop(1, batches, backward, behinds)
    moment_batch(0)

    slot_s = coef_s
    for block in range(blocks):
        middle_x, middle_y, _ = middles[block * 8 // chunks]
        at = slice(8 * block, 8 * block + 8)
        raw = [raw_s[channel * slot_rows + 8 * block : channel * slot_rows + 8 * block + 8, :] for channel in range(6)]
        (sum_xx, sum_xy, sum_yy, sum_x, sum_y, sum_one) = [
            sums_s[pl.ds(8 * block * 16 + index, 8, stride=16), :] for index in range(6)
        ]
        at_x = raw[0] - middle_x
        at_y = raw[1] - middle_y
        off_x = sum_x - at_x * sum_one
        off_y = sum_y - at_y * sum_one
        grads = [
            raw[2] * off_x + raw[3] * off_y,
            raw[4] * off_y + raw[3] * off_x,
            -0.5 * (sum_xx - at_x * (sum_x + off_x)),
            -(sum_xy - at_y * sum_x - at_x * off_y),
            -0.5 * (sum_yy - at_y * (sum_y + off_y)),
            sum_one / raw[5],
        ] + [sums_s[pl.ds(8 * block * 16 + 8 + colour, 8, stride=16), :] for colour in range(3)]
        for channel, value in enumerate(grads):
            slot_s[channel * slot_rows + 8 * block : channel * slot_rows + 8 * block + 8, :] = value

    for half in range(2):
        for channel in range(PROJ):
            value = slot_s[pl.ds(channel * slot_rows + half, slot_rows // 2, stride=2), :]
            put_parts(out_s, channel, half, value, (2,) * PROJ)
    minors = layout.minors()

    def pick_out(index, _):
        if layout.halves == 2:
            slots = back_ref[pl.ds(index, 1), :]
        else:
            slots = jnp.concatenate([back_ref[pl.ds(2 * index + one, 1), :] for one in range(2)], axis=1)

        def put(channel, value):
            for one in range(2):
                at = layout.row(channel, (2 * index + one) // minors, (2 * index + one) % minors)
                out_ref[pl.ds(at, 1), :] = value[:, one * LANES : (one + 1) * LANES]

        pick_slots(out_s[...], slots, low_id, high_id, put)
        return 0

    lax.fori_loop(0, layout.count // 2, pick_out, 0, unroll=4)


def collect_kernel(layout, camera_frame, angles_ref, gauss_ref, asked_ref, terms_ref, grad_ref, lhs_s, rhs_s, total_s, dense_s, out_s):
    rows = gauss_ref.shape[1] // LANES
    wide = 2 * LANES
    lows = gauss_ref.shape[1] // wide
    low_id = iota((lows, LANES), 0)
    high_id = iota((wide, LANES), 0)
    minors = layout.minors()
    total_s[...] = jnp.zeros(total_s.shape, f32)

    def add(index, _):
        start = pl.multiple_of(index * 8, 8)
        asked = asked_ref[pl.ds(start, 8), :]
        low = asked // wide
        high = asked % wide
        for row in range(8):
            lanes = slice(row * LANES, (row + 1) * LANES)
            mine = low[row : row + 1] == low_id
            rhs_s[:, lanes] = jnp.where(high[row : row + 1] == high_id, 1.0, 0.0).astype(bf16)
            for channel in range(PROJ):
                at = layout.row(channel, index * (8 // minors) + row // minors, row % minors)
                for part, value in enumerate(split_two(terms_ref[pl.ds(at, 1), :])):
                    first = (part * PROJ + channel) * lows
                    lhs_s[first : first + lows, lanes] = jnp.where(mine, value, 0.0).astype(bf16)
        total_s[...] += dot_nt(lhs_s[...], rhs_s[...])
        return 0

    lax.fori_loop(0, layout.count // 8, add, 0)
    spread_columns(gauss_ref, dense_s)
    rotation = view(angles_ref)
    basis = harmonics(*rotation[2])
    for half in range(2):
        lanes = slice(half * LANES, (half + 1) * LANES)
        sums = [
            total_s[channel * lows : (channel + 1) * lows, lanes]
            + total_s[(PROJ + channel) * lows : (PROJ + channel + 1) * lows, lanes]
            for channel in range(PROJ)
        ]
        columns = tuple(dense_s[pl.ds(index * rows + half, lows, stride=2), :] for index in range(11))
        _, pullback = jax.vjp(lambda *values: shape_of(values, rotation, camera_frame), *columns)
        grads = pullback(tuple(sums[:6]))
        for index, value in enumerate(tuple(grads) + tuple(sums[6:])):
            out_s[pl.ds(index * rows + half, lows, stride=2), :] = value
    sub = iota((8, LANES), 0)
    patterns = [basis_rows(basis, eighth) for eighth in range(8)]
    for row in range(rows):
        lanes = slice(row * LANES, (row + 1) * LANES)
        grad_ref[0:8, lanes] = out_s[pl.ds(row, 8, stride=rows), :]
        tints = [out_s[(11 + colour) * rows + row : (11 + colour) * rows + row + 1, :] for colour in range(3)]
        for eighth in range(1, 8):
            value = None
            for colour in range(3):
                pattern = patterns[eighth][colour]
                if pattern is not None:
                    term = pattern * tints[colour]
                    value = term if value is None else value + term
            if eighth == 1:
                value = jnp.where(sub < 3, out_s[pl.ds(8 * rows + row, 8, stride=rows), :], value)
            if eighth == 7:
                grad_ref[56:59, lanes] = value[0:3]
            else:
                grad_ref[8 * eighth : 8 * eighth + 8, lanes] = value


VMEM = pl.BlockSpec(memory_space=pltpu.VMEM)
ANY = pl.BlockSpec(memory_space=pl.ANY)
SMEM = pl.BlockSpec(memory_space=pltpu.SMEM)


def call(kernel, specs, outs, scratch, flops, name):
    return pl.pallas_call(
        kernel,
        in_specs=specs,
        out_specs=[VMEM] * len(outs),
        out_shape=[jax.ShapeDtypeStruct(shape, dtype) for shape, dtype in outs],
        scratch_shapes=[pltpu.VMEM(*one) if isinstance(one, tuple) else one for one in scratch],
        compiler_params=pltpu.CompilerParams(vmem_limit_bytes=VMEM_BYTES),
        cost_estimate=pl.CostEstimate(flops=flops, bytes_accessed=4 << 20, transcendentals=0),
        name=name,
    )


def route(devices, owners, locals_):
    slots = owners.size
    per_owner = slots // devices
    rows = slots // LANES
    halves = per_owner // LANES if per_owner % LANES == 0 else 0
    asked = (devices * halves, LANES) if halves else (devices, per_owner)
    return call(
        partial(route_kernel, devices, per_owner),
        [ANY, ANY],
        [(asked, i32), ((devices, per_owner), i32), ((rows, LANES), i32)],
        [(owners.shape, i32)] * 2 + [((rows, LANES), i32)] * 3 + [pltpu.SemaphoreType.DMA((2,))],
        1 << 30,
        "route",
    )(owners, locals_)


def shade(camera_frame, view_angles, gaussians):
    rows = gaussians.shape[1] // LANES
    return call(
        partial(shade_kernel, camera_frame),
        [SMEM, VMEM],
        [((sum(PARTS) * rows // 2, WIDE), bf16)],
        [((16 * rows, LANES), f32), ((27 * rows, LANES), f32)],
        1 << 30,
        "shade",
    )(view_angles, gaussians)[0]


def pick(layout, table, asked):
    return call(
        partial(pick_kernel, layout),
        [VMEM, VMEM],
        [((PROJ * layout.count, LANES), f32)],
        [],
        1 << 30,
        "pick",
    )(table, asked)[0]


def render(layout, list_counts, tile_order, rows, pos, back, cotangent):
    slot_rows = pos.shape[0]
    groups = tile_order.shape[0] // GROUP
    slots = slot_rows * LANES
    return call(
        partial(render_kernel, layout),
        [SMEM, SMEM, VMEM, VMEM, VMEM, VMEM],
        [(cotangent.shape, f32), ((PROJ * layout.count, LANES), f32)],
        [
            ((sum(PARTS) * slot_rows // 2, WIDE), bf16),
            ((2 * PROJ * slot_rows // 2, WIDE), bf16),
            ((PROJ * slot_rows, LANES), f32),
            ((24 * slot_rows, LANES), f32),
            ((24 * groups, PIX), f32),
            ((groups, 96, 2 * PIX), bf16),
            ((slot_rows, 64, LANES), bf16),
            ((slots, PIX), f32),
            ((slots, PIX), f32),
            ((slots, PIX), f32),
            ((16 * slot_rows, LANES), f32),
        ],
        1 << 34,
        "render",
    )(list_counts, tile_order, rows, pos, back, cotangent)


def collect(layout, camera_frame, view_angles, gaussians, asked, terms):
    rows = gaussians.shape[1] // LANES
    lows = gaussians.shape[1] // (2 * LANES)
    return call(
        partial(collect_kernel, layout, camera_frame),
        [SMEM, VMEM, VMEM, VMEM],
        [(gaussians.shape, f32)],
        [
            ((2 * PROJ * lows, 8 * LANES), bf16),
            ((2 * LANES, 8 * LANES), bf16),
            ((2 * PROJ * lows, 2 * LANES), f32),
            ((16 * rows, LANES), f32),
            ((16 * rows, LANES), f32),
        ],
        1 << 32,
        "collect",
    )(view_angles, gaussians, asked, terms)[0]


def swap_rows(layout, devices, rows):
    if layout.halves:
        apart = rows.reshape(devices * PROJ, layout.halves, LANES)
        return lax.all_to_all(apart, "dev", split_axis=0, concat_axis=0, tiled=True).reshape(rows.shape)
    apart = rows.reshape(PROJ, devices, layout.count * LANES // devices)
    return lax.all_to_all(apart, "dev", split_axis=1, concat_axis=1, tiled=True).reshape(rows.shape)


def shards(gaussians, view_angles, tile_order, tile_owners, tile_locals, list_counts, image_cotangent):
    devices = lax.axis_size("dev")
    tiles_y = devices * tile_order.shape[0] // TX
    camera_frame = (4.0 * TX, 4.0 * tiles_y, 8.0 * TX, 8.0 * tiles_y)
    layout = Rows(devices, tile_owners.size // devices)
    want, back, pos = route(devices, tile_owners, tile_locals)
    asked = lax.all_to_all(want, "dev", split_axis=0, concat_axis=0, tiled=True)
    table = shade(camera_frame, view_angles, gaussians)
    if not layout.halves:
        asked = asked.reshape(layout.count, LANES)
    if layout.halves != 2:
        back = back.reshape(layout.count, LANES)
    arrived = swap_rows(layout, devices, pick(layout, table, asked))
    rendered, slot_grads = render(layout, list_counts, tile_order, arrived, pos, back, image_cotangent)
    terms = swap_rows(layout, devices, slot_grads)
    gradients = collect(layout, camera_frame, view_angles, gaussians, asked, terms)
    return (rendered, gradients)


def solution(mesh):
    return jax.shard_map(
        shards,
        mesh=mesh,
        in_specs=(
            P(None, "dev"),
            P(),
            P("dev"),
            P("dev", None),
            P("dev", None),
            P("dev"),
            P(None, "dev"),
        ),
        out_specs=(P(None, "dev"), P(None, "dev")),
        check_vma=False,
    )
```

```python
from functools import partial

import jax
import jax.numpy as jnp
from jax import lax
from jax.experimental import pallas as pl
from jax.experimental.pallas import tpu as pltpu
from jax.sharding import PartitionSpec as P

PIX = 256
TX = 32
LANES = 128
PROJ = 9
GROUP = 8
WIDE = 2 * LANES
PARTS = (3, 3, 3, 3, 3, 2, 2, 2, 2)
STEP = LANES // GROUP
LOG2E = 1.4426950408889634
BATCH = 8
VMEM_BYTES = 52 * 1024 * 1024

f32 = jnp.float32
bf16 = jnp.bfloat16
i32 = jnp.int32


def iota(shape, dim):
    return lax.broadcasted_iota(i32, shape, dim)


def lane_pick(row, lanes):
    source = jnp.broadcast_to(row, lanes.shape)
    return jnp.take_along_axis(source, lanes, axis=1, mode="promise_in_bounds")


def split_two(values):
    first = values.astype(bf16).astype(f32)
    return first, values - first


def split_three(values):
    first, rest = split_two(values)
    second, third = split_two(rest)
    return first, second, third


def dot(lhs, rhs):
    return lax.dot_general(lhs, rhs, (((1,), (0,)), ((), ())), preferred_element_type=f32)


def dot_nt(lhs, rhs):
    return lax.dot_general(lhs, rhs, (((1,), (1,)), ((), ())), preferred_element_type=f32)


def dot_tn(lhs, rhs):
    return lax.dot_general(lhs, rhs, (((0,), (0,)), ((), ())), preferred_element_type=f32)


class Rows:
    def __init__(self, devices, per_owner):
        self.halves = per_owner // LANES if per_owner % LANES == 0 else 0
        self.count = devices * per_owner // LANES

    def row(self, channel, major, minor):
        halves = self.halves
        if halves == 0:
            return channel * self.count + major
        return major * (PROJ * halves) + channel * halves + minor

    def half(self, ref, channel, half):
        halves = self.halves
        if halves == 0:
            return ref[pl.ds(channel * self.count + half, self.count // 2, stride=2), :]
        return jnp.concatenate(
            [ref[pl.ds(self.row(channel, one // halves, one % halves), 1), :] for one in range(half, self.count, 2)], axis=0
        ) if halves != 2 else ref[pl.ds(channel * 2 + half, self.count // 2, stride=2 * PROJ), :]

    def minors(self):
        return max(self.halves, 1)


def pick_slots(parts, slots, low_id, high_id, put):
    here = jnp.where(slots % WIDE == high_id, 1.0, 0.0).astype(bf16)
    found = dot(parts, here)
    mine = slots // WIDE == low_id
    lows = low_id.shape[0]
    first = 0
    for channel, count in enumerate(PARTS if parts.shape[0] == sum(PARTS) * lows else (2,) * PROJ):
        value = found[first * lows : (first + 1) * lows]
        for part in range(1, count):
            value = value + found[(first + part) * lows : (first + part + 1) * lows]
        first += count
        put(channel, jnp.sum(jnp.where(mine, value, 0.0), axis=0, keepdims=True))


def put_parts(parts_ref, channel, half, value, counts, lows=None, low=0):
    lows = lows or value.shape[0]
    first = sum(counts[:channel])
    parts = split_three(value) if counts[channel] == 3 else split_two(value)
    for part, one in enumerate(parts):
        at = (first + part) * lows + low
        parts_ref[at : at + value.shape[0], half * LANES : (half + 1) * LANES] = one.astype(bf16)


def route_kernel(devices, per_owner, own_hbm, loc_hbm, want_ref, back_ref, pos_ref, own_ref, loc_ref, own_s, loc_s, rank_s, sems):
    copies = [pltpu.make_async_copy(own_hbm, own_ref, sems.at[0]), pltpu.make_async_copy(loc_hbm, loc_ref, sems.at[1])]
    for copy in copies:
        copy.start()
    for copy in copies:
        copy.wait()
    rows = own_s.shape[0]
    blocks = own_ref.shape[1] // LANES
    lane = iota((8, LANES), 1)
    from_slot = iota((8, LANES), 0) * STEP + lane // GROUP
    tile_of = lane % GROUP
    for group in range(own_ref.shape[0] // GROUP):
        for block in range(blocks):
            for source, target in ((own_ref, own_s), (loc_ref, loc_s)):
                part = source[group * GROUP : (group + 1) * GROUP, block * LANES : (block + 1) * LANES]
                out = jnp.zeros((8, LANES), i32)
                for tile in range(GROUP):
                    out = jnp.where(tile_of == tile, lane_pick(part[tile : tile + 1], from_slot), out)
                start = (group * blocks + block) * 8
                target[start : start + 8, :] = out
    owner = own_s[...]
    left = (iota((LANES, 2 * LANES), 0) < iota((LANES, 2 * LANES), 1)) | (iota((LANES, 2 * LANES), 1) >= LANES)
    above = iota((rows, rows), 1) < iota((rows, rows), 0)
    hits = jnp.concatenate([jnp.where(owner == one, 1.0, 0.0).astype(bf16) for one in range(devices)], axis=0)
    sums = dot(hits, jnp.where(left, 1.0, 0.0).astype(bf16))
    totals = jnp.concatenate(
        [sums[one * rows : (one + 1) * rows, LANES:].astype(bf16) for one in range(devices)], axis=1
    )
    base = dot(jnp.where(above, 1.0, 0.0).astype(bf16), totals)
    rank = jnp.zeros((rows, LANES), f32)
    for one in range(devices):
        here = sums[one * rows : (one + 1) * rows, :LANES] + base[:, one * LANES : (one + 1) * LANES]
        rank = jnp.where(owner == one, here, rank)
    rank = rank.astype(i32)
    pos_ref[...] = owner * per_owner + rank
    rank_s[...] = rank

    owner_id = iota((devices, LANES), 0)
    rank_id = iota((per_owner, LANES), 0)
    slot_lane = iota((devices, LANES), 1).astype(f32)

    def place(index, total):
        start = pl.multiple_of(index * 8, 8)
        own_rows = own_s[pl.ds(start, 8), :]
        loc_rows = loc_s[pl.ds(start, 8), :]
        rank_rows = rank_s[pl.ds(start, 8), :]
        high_rows = (loc_rows // LANES).astype(f32)
        low_rows = (loc_rows % LANES).astype(f32)
        lhs = []
        rhs = []
        for row in range(8):
            mine = own_rows[row : row + 1] == owner_id
            number = (start + row).astype(f32)
            lhs.append(
                jnp.concatenate(
                    [
                        jnp.where(mine, high_rows[row : row + 1], 0.0),
                        jnp.where(mine, low_rows[row : row + 1], 0.0),
                        jnp.where(mine, number, 0.0),
                        jnp.where(mine, slot_lane, 0.0),
                    ],
                    axis=0,
                ).astype(bf16)
            )
            rhs.append(jnp.where(rank_rows[row : row + 1] == rank_id, 1.0, 0.0).astype(bf16))
        return total + dot_nt(jnp.concatenate(lhs, axis=1), jnp.concatenate(rhs, axis=1))

    total = lax.fori_loop(0, rows // 8, place, jnp.zeros((4 * devices, per_owner), f32)).astype(i32)
    want = total[:devices] * LANES + total[devices : 2 * devices]
    halves = per_owner // LANES
    if per_owner % LANES == 0 and halves > 1:
        for half in range(halves):
            want_ref[pl.ds(half, devices, stride=halves), :] = want[:, half * LANES : (half + 1) * LANES]
    else:
        want_ref[...] = want
    back_ref[...] = total[2 * devices : 3 * devices] * LANES + total[3 * devices :]


def view(angles_ref):
    angle = [jnp.full((1, LANES), angles_ref[index], f32) for index in range(3)]
    (cos_a, cos_b, cos_c) = [jnp.cos(one) for one in angle]
    (sin_a, sin_b, sin_c) = [jnp.sin(one) for one in angle]
    return [
        [cos_c * cos_b, cos_c * sin_b * sin_a - sin_c * cos_a, cos_c * sin_b * cos_a + sin_c * sin_a],
        [sin_c * cos_b, sin_c * sin_b * sin_a + cos_c * cos_a, sin_c * sin_b * cos_a - cos_c * sin_a],
        [-sin_b, cos_b * sin_a, cos_b * cos_a],
    ]


def harmonics(along_x, along_y, along_z):
    sq_x = along_x * along_x
    sq_y = along_y * along_y
    sq_z = along_z * along_z
    return [
        0.28209479177387814 + 0.0 * along_x,
        -0.4886025119029199 * along_y,
        0.4886025119029199 * along_z,
        -0.4886025119029199 * along_x,
        1.0925484305920792 * along_x * along_y,
        -1.0925484305920792 * along_y * along_z,
        0.31539156525252005 * (2.0 * sq_z - sq_x - sq_y),
        -1.0925484305920792 * along_x * along_z,
        0.5462742152960396 * (sq_x - sq_y),
        -0.5900435899266435 * along_y * (3.0 * sq_x - sq_y),
        2.890611442640554 * along_x * along_y * along_z,
        -0.4570457994644658 * along_y * (4.0 * sq_z - sq_x - sq_y),
        0.3731763325901154 * along_z * (2.0 * sq_z - 3.0 * sq_x - 3.0 * sq_y),
        -0.4570457994644658 * along_x * (4.0 * sq_z - sq_x - sq_y),
        1.445305721320277 * along_z * (sq_x - sq_y),
        -0.5900435899266435 * along_x * (sq_x - 3.0 * sq_y),
    ]


def basis_rows(basis, eighth):
    sub = iota((8, LANES), 0)
    found = []
    for colour in range(3):
        out = None
        for inner in range(8):
            index = 8 * eighth + inner - 11 - 16 * colour
            if 0 <= index < 16:
                out = jnp.zeros((8, LANES), f32) if out is None else out
                out = jnp.where(sub == inner, basis[index], out)
        found.append(out)
    return found


def shape_of(columns, rotation, camera_frame):
    focal_x, focal_y, centre_x, centre_y = camera_frame
    positions = columns[0:3]
    cam_first = rotation[0][0] * positions[0] + rotation[0][1] * positions[1] + rotation[0][2] * positions[2]
    cam_second = rotation[1][0] * positions[0] + rotation[1][1] * positions[1] + rotation[1][2] * positions[2]
    mean_x = centre_x + focal_x * cam_first
    mean_y = centre_y + focal_y * cam_second
    scales = [jnp.exp(one) for one in columns[3:6]]
    quat_w, quat_x, quat_y, quat_z = columns[6:10]
    norm_sq = jnp.maximum(quat_w * quat_w + quat_x * quat_x + quat_y * quat_y + quat_z * quat_z, 1.0)
    twice = 2.0 / norm_sq
    turned = [
        [
            1.0 - twice * (quat_y * quat_y + quat_z * quat_z),
            twice * (quat_x * quat_y - quat_w * quat_z),
            twice * (quat_x * quat_z + quat_w * quat_y),
        ],
        [
            twice * (quat_x * quat_y + quat_w * quat_z),
            1.0 - twice * (quat_x * quat_x + quat_z * quat_z),
            twice * (quat_y * quat_z - quat_w * quat_x),
        ],
        [
            twice * (quat_x * quat_z - quat_w * quat_y),
            twice * (quat_y * quat_z + quat_w * quat_x),
            1.0 - twice * (quat_x * quat_x + quat_y * quat_y),
        ],
    ]
    rows = []
    for focal, turn in ((focal_x, rotation[0]), (focal_y, rotation[1])):
        rows.append(
            [
                focal * (turn[0] * turned[0][k] + turn[1] * turned[1][k] + turn[2] * turned[2][k]) * scales[k]
                for k in range(3)
            ]
        )
    first, second = rows
    cov_a = first[0] * first[0] + first[1] * first[1] + first[2] * first[2] + 0.3
    cov_b = first[0] * second[0] + first[1] * second[1] + first[2] * second[2]
    cov_c = second[0] * second[0] + second[1] * second[1] + second[2] * second[2] + 0.3
    determinant = cov_a * cov_c - cov_b * cov_b
    opacity = 1.0 / (1.0 + jnp.exp(-columns[10]))
    return mean_x, mean_y, cov_c / determinant, -cov_b / determinant, cov_a / determinant, opacity


def spread_columns(gauss_ref, dense_s):
    rows = gauss_ref.shape[1] // LANES
    for row in range(rows):
        for eighth in range(2):
            dense_s[pl.ds(8 * eighth * rows + row, 8, stride=rows), :] = gauss_ref[
                8 * eighth : 8 * eighth + 8, row * LANES : (row + 1) * LANES
            ]


def shade_kernel(camera_frame, angles_ref, gauss_ref, parts_ref, dense_s, tint_s):
    rows = gauss_ref.shape[1] // LANES
    spread_columns(gauss_ref, dense_s)
    rotation = view(angles_ref)
    basis = harmonics(*rotation[2])
    patterns = [basis_rows(basis, eighth) for eighth in range(7)]
    for row in range(rows):
        lanes = slice(row * LANES, (row + 1) * LANES)
        tints = [None] * 3
        for eighth in range(1, 7):
            block = gauss_ref[8 * eighth : 8 * eighth + 8, lanes]
            for colour in range(3):
                pattern = patterns[eighth][colour]
                if pattern is not None:
                    term = block * pattern
                    tints[colour] = term if tints[colour] is None else tints[colour] + term
        for colour in range(3):
            tint_s[pl.ds(8 * colour * rows + row, 8, stride=rows), :] = tints[colour]
        tint_s[pl.ds(24 * rows + row, 3, stride=rows), :] = gauss_ref[56:59, lanes]
    for part in range(rows // 16):
        half = part % 2
        low = part // 2 * 16
        at = [pl.ds(index * rows + 2 * low + half, 16, stride=2) for index in range(27)]
        columns = [dense_s[one, :] for one in at[:11]]
        for index, value in enumerate(shape_of(columns, rotation, camera_frame)):
            put_parts(parts_ref, index, half, value, PARTS, rows // 2, low)
        for colour in range(3):
            total = 0.5
            for inner in range(8):
                total = total + tint_s[at[8 * colour + inner], :]
            if colour == 2:
                for inner in range(3):
                    total = total + basis[13 + inner] * tint_s[at[24 + inner], :]
            put_parts(parts_ref, 6 + colour, half, total, PARTS, rows // 2, low)


def pick_kernel(layout, parts_ref, asked_ref, out_ref):
    low_id = iota((parts_ref.shape[0] // sum(PARTS), WIDE), 0)
    high_id = iota((WIDE, WIDE), 0)
    minors = layout.minors()

    def pick_some(index, _):
        slots = jnp.concatenate([asked_ref[pl.ds(2 * index + one, 1), :] for one in range(2)], axis=1)

        def put(channel, value):
            for one in range(2):
                at = layout.row(channel, (2 * index + one) // minors, (2 * index + one) % minors)
                out_ref[pl.ds(at, 1), :] = value[:, one * LANES : (one + 1) * LANES]

        pick_slots(parts_ref[...], slots, low_id, high_id, put)
        return 0

    lax.fori_loop(0, layout.count // 2, pick_some, 0, unroll=8)


def render_kernel(
    layout,
    count_ref,
    order_ref,
    rows_ref,
    pos_ref,
    back_ref,
    cot_ref,
    image_ref,
    out_ref,
    in_s,
    out_s,
    raw_s,
    coef_s,
    cot_s,
    rhs_s,
    tint_s,
    alpha_s,
    shade_s,
    weight_s,
    sums_s,
):
    slot_rows = pos_ref.shape[0]
    groups = cot_ref.shape[1] // (GROUP * PIX)
    chunks = slot_rows // groups
    sub = iota((8, LANES), 0)
    lane = iota((8, LANES), 1)
    tile_of = lane % GROUP
    blocks = slot_rows // 8
    middles = []
    for group in range(groups):
        middle_x = jnp.zeros((8, LANES), f32)
        middle_y = jnp.zeros((8, LANES), f32)
        live = jnp.zeros((8, LANES), i32)
        for tile in range(GROUP):
            shown = order_ref[group * GROUP + tile]
            here = tile_of == tile
            middle_x = jnp.where(here, (shown % TX * 16 + 8).astype(f32), middle_x)
            middle_y = jnp.where(here, (shown // TX * 16 + 8).astype(f32), middle_y)
            live = jnp.where(here, count_ref[group * GROUP + tile], live)
        middles.append((middle_x, middle_y, live))

    for half in range(2):
        for channel in range(PROJ):
            put_parts(in_s, channel, half, layout.half(rows_ref, channel, half), PARTS)
    low_id = iota((slot_rows // 2, WIDE), 0)
    high_id = iota((WIDE, WIDE), 0)

    def pick_in(index, _):
        slots = jnp.concatenate([pos_ref[pl.ds(2 * index + one, 1), :] for one in range(2)], axis=1)

        def put(channel, value):
            for one in range(2):
                raw_s[pl.ds(channel * slot_rows + 2 * index + one, 1), :] = value[:, one * LANES : (one + 1) * LANES]

        pick_slots(in_s[...], slots, low_id, high_id, put)
        return 0

    lax.fori_loop(0, slot_rows // 2, pick_in, 0, unroll=8)
    for block in range(blocks):
        group = block * 8 // chunks
        middle_x, middle_y, live = middles[group]
        found = [
            raw_s[channel * slot_rows + 8 * block : channel * slot_rows + 8 * block + 8, :] for channel in range(PROJ)
        ]
        at_x = found[0] - middle_x
        at_y = found[1] - middle_y
        quad_a = -0.5 * found[2]
        quad_b = -found[3]
        quad_c = -0.5 * found[4]
        flat = quad_a * at_x * at_x + quad_c * at_y * at_y + quad_b * at_x * at_y + jnp.log(found[5])
        place = (8 * block - group * chunks + sub) * STEP + lane // GROUP
        terms = (
            quad_a * LOG2E,
            quad_b * LOG2E,
            quad_c * LOG2E,
            (-2.0 * quad_a * at_x - quad_b * at_y) * LOG2E,
            (-2.0 * quad_c * at_y - quad_b * at_x) * LOG2E,
            jnp.where(place < live, flat * LOG2E, -1e30),
        )
        for index, term in enumerate(terms):
            for part, value in enumerate(split_three(term)):
                coef_s[pl.ds(8 * block * 24 + 6 * part + index, 8, stride=24), :] = value
        for colour in range(3):
            for part, value in enumerate(split_two(found[6 + colour])):
                coef_s[pl.ds(8 * block * 24 + 18 + 3 * part + colour, 8, stride=24), :] = value

    pixel = iota((24, PIX), 1)
    row = iota((24, PIX), 0)
    pix_x = (pixel % 16).astype(f32) - 7.5
    pix_y = (pixel // 16).astype(f32) - 7.5
    kind = row % 6
    monomials = jnp.where(kind == 0, pix_x * pix_x, jnp.where(kind == 1, pix_x * pix_y, 1.0))
    monomials = jnp.where(kind == 2, pix_y * pix_y, monomials)
    monomials = jnp.where(kind == 3, pix_x, jnp.where(kind == 4, pix_y, monomials))
    moments = jnp.where(iota((8, PIX), 0) < 6, monomials[0:8], 0.0).astype(bf16)
    monomials = jnp.where(row < 18, monomials, 0.0)
    nothing = jnp.zeros((24, PIX), f32)
    for group in range(groups):
        for colour in range(3):
            for tile in range(GROUP):
                start = (group * GROUP + tile) * PIX
                cot_s[group * 24 + colour * GROUP + tile, :] = cot_ref[colour, start : start + PIX]
    cots = []
    spare = jnp.zeros((8, PIX), f32)
    for group in range(groups):
        first, second = split_two(cot_s[group * 24 : (group + 1) * 24, :])
        cots.append(jnp.concatenate([first, spare, second, spare], axis=0).astype(bf16))
        rhs_s[group] = jnp.concatenate(
            [
                jnp.concatenate([jnp.concatenate([nothing, monomials[8 * one : 8 * one + 8]], axis=0) for one in range(3)], axis=0),
                jnp.concatenate([first, spare, first, spare, second, spare], axis=0),
            ],
            axis=1,
        ).astype(bf16)

    own_tile = sub == tile_of

    def evaluate(index, _):
        for group in range(groups):
            chunk = group * chunks + index
            coefs = coef_s[pl.ds(pl.multiple_of(chunk * 24, 8), 24), :]
            tints = [jnp.where(own_tile, coefs[18 + one : 19 + one], 0.0) for one in range(6)]
            lhs = jnp.concatenate(
                tints[:3] + [coefs[0:8]] + tints[3:] + [coefs[8:16]] + tints[:3] + [coefs[16:24]], axis=0
            ).astype(bf16)
            tint_s[chunk] = lhs[0:64]
            both = dot_tn(lhs, rhs_s[group])
            start = pl.multiple_of(chunk * LANES, LANES)
            alpha_s[pl.ds(start, LANES), :] = jnp.exp2(both[:, :PIX])
            shade_s[pl.ds(start, LANES), :] = both[:, PIX:]
        return 0

    lax.fori_loop(0, chunks, evaluate, 0, unroll=BATCH)

    def scan(index, trans):
        out = []
        for group in range(groups):
            one = trans[group]
            start = pl.multiple_of((group * chunks + index) * LANES, LANES)
            for step in range(STEP):
                alpha = alpha_s[pl.ds(start + step * GROUP, GROUP), :]
                weight = one * alpha
                one = one - weight
                weight_s[pl.ds(start + step * GROUP, GROUP), :] = weight
            out.append(one)
        return tuple(out)

    def paint(index, images):
        out = []
        for group in range(groups):
            chunk = group * chunks + index
            start = pl.multiple_of(chunk * LANES, LANES)
            first, second = split_two(weight_s[pl.ds(start, LANES), :])
            first = first.astype(bf16)
            second = second.astype(bf16)
            tints = tint_s[chunk]
            by_first = dot(tints, first)
            out.append(images[group] + by_first[0:24] + by_first[32:56] + dot(tints[0:32], second)[0:24])
            by_first = dot_nt(cots[group], first)
            tint_grad = by_first[0:24] + by_first[32:56] + dot_nt(cots[group][0:32], second)[0:24]
            for colour in range(3):
                own = jnp.where(own_tile, tint_grad[colour * GROUP : (colour + 1) * GROUP], 0.0)
                sums_s[pl.ds(chunk * 16 + 8 + colour, 1), :] = jnp.sum(own, axis=0, keepdims=True)
        return tuple(out)

    def scan_batch(batch, trans):
        for one in range(BATCH):
            trans = scan(batch * BATCH + one, trans)
        return trans

    def paint_batch(batch, images):
        for one in range(BATCH):
            images = paint(batch * BATCH + one, images)
        return images

    def forward(batch, state):
        trans, images = state
        images = paint_batch(batch - 1, images)
        return scan_batch(batch, trans), images

    batches = chunks // BATCH
    trans = scan_batch(0, tuple(jnp.ones((GROUP, PIX), f32) for _ in range(groups)))
    images = tuple(jnp.zeros((24, PIX), f32) for _ in range(groups))
    trans, images = lax.fori_loop(1, batches, forward, (trans, images))
    images = paint_batch(batches - 1, images)
    for group in range(groups):
        for colour in range(3):
            for tile in range(GROUP):
                at = (group * GROUP + tile) * PIX
                image_ref[colour, at : at + PIX] = images[group][colour * GROUP + tile]

    def moment(index):
        for group in range(groups):
            chunk = group * chunks + index
            first, second = split_two(shade_s[pl.ds(pl.multiple_of(chunk * LANES, LANES), LANES), :])
            found = dot_nt(moments, first.astype(bf16)) + dot_nt(moments, second.astype(bf16))
            sums_s[pl.ds(pl.multiple_of(chunk * 16, 8), 8), :] = found

    def rescan(index, behinds):
        out = []
        for group in range(groups):
            behind = behinds[group]
            start = pl.multiple_of((group * chunks + index) * LANES, LANES)
            for step in reversed(range(STEP)):
                at = pl.ds(start + step * GROUP, GROUP)
                ahead = shade_s[at, :] - behind
                shade_s[at, :] = weight_s[at, :] * ahead
                behind = behind + alpha_s[at, :] * ahead
            out.append(behind)
        return tuple(out)

    def moment_batch(batch):
        for one in range(BATCH):
            moment(batch * BATCH + one)

    def rescan_batch(batch, behinds):
        for one in reversed(range(BATCH)):
            behinds = rescan(batch * BATCH + one, behinds)
        return behinds

    def backward(index, behinds):
        moment_batch(batches - index)
        return rescan_batch(batches - 1 - index, behinds)

    behinds = rescan_batch(batches - 1, tuple(jnp.zeros((GROUP, PIX), f32) for _ in range(groups)))
    lax.fori_loop(1, batches, backward, behinds)
    moment_batch(0)

    slot_s = coef_s
    for block in range(blocks):
        middle_x, middle_y, _ = middles[block * 8 // chunks]
        at = slice(8 * block, 8 * block + 8)
        raw = [raw_s[channel * slot_rows + 8 * block : channel * slot_rows + 8 * block + 8, :] for channel in range(6)]
        (sum_xx, sum_xy, sum_yy, sum_x, sum_y, sum_one) = [
            sums_s[pl.ds(8 * block * 16 + index, 8, stride=16), :] for index in range(6)
        ]
        at_x = raw[0] - middle_x
        at_y = raw[1] - middle_y
        off_x = sum_x - at_x * sum_one
        off_y = sum_y - at_y * sum_one
        grads = [
            raw[2] * off_x + raw[3] * off_y,
            raw[4] * off_y + raw[3] * off_x,
            -0.5 * (sum_xx - at_x * (sum_x + off_x)),
            -(sum_xy - at_y * sum_x - at_x * off_y),
            -0.5 * (sum_yy - at_y * (sum_y + off_y)),
            sum_one / raw[5],
        ] + [sums_s[pl.ds(8 * block * 16 + 8 + colour, 8, stride=16), :] for colour in range(3)]
        for channel, value in enumerate(grads):
            slot_s[channel * slot_rows + 8 * block : channel * slot_rows + 8 * block + 8, :] = value

    for half in range(2):
        for channel in range(PROJ):
            value = slot_s[pl.ds(channel * slot_rows + half, slot_rows // 2, stride=2), :]
            put_parts(out_s, channel, half, value, (2,) * PROJ)
    minors = layout.minors()

    def pick_out(index, _):
        if layout.halves == 2:
            slots = back_ref[pl.ds(index, 1), :]
        else:
            slots = jnp.concatenate([back_ref[pl.ds(2 * index + one, 1), :] for one in range(2)], axis=1)

        def put(channel, value):
            for one in range(2):
                at = layout.row(channel, (2 * index + one) // minors, (2 * index + one) % minors)
                out_ref[pl.ds(at, 1), :] = value[:, one * LANES : (one + 1) * LANES]

        pick_slots(out_s[...], slots, low_id, high_id, put)
        return 0

    lax.fori_loop(0, layout.count // 2, pick_out, 0, unroll=8)


def collect_kernel(
    layout, camera_frame, angles_ref, dense_ref, asked_ref, terms_ref, grad_hbm, lhs_a, lhs_b, rhs_a, rhs_b, total_s, out_s, grad_ref, sems
):
    gauss = grad_ref.shape[1]
    rows = gauss // LANES
    lows = gauss // WIDE
    low_id = iota((lows, LANES), 0)
    high_id = iota((WIDE, LANES), 0)
    minors = layout.minors()

    def build(index, lhs_s, rhs_s):
        asked = asked_ref[pl.ds(pl.multiple_of(index * 8, 8), 8), :]
        low = asked // WIDE
        high = asked % WIDE
        for row in range(8):
            lanes = slice(row * LANES, (row + 1) * LANES)
            mine = low[row : row + 1] == low_id
            rhs_s[:, lanes] = jnp.where(high[row : row + 1] == high_id, 1.0, 0.0).astype(bf16)
            for channel in range(PROJ):
                at = layout.row(channel, index * (8 // minors) + row // minors, row % minors)
                for part, value in enumerate(split_two(terms_ref[pl.ds(at, 1), :])):
                    first = (part * PROJ + channel) * lows
                    lhs_s[first : first + lows, lanes] = jnp.where(mine, value, 0.0).astype(bf16)

    last = layout.count // 8 - 1
    build(0, lhs_a, rhs_a)
    total_s[...] = jnp.zeros(total_s.shape, f32)

    def add(index, _):
        build(2 * index + 1, lhs_b, rhs_b)
        total_s[...] += dot_nt(lhs_a[...], rhs_a[...])
        build(jnp.minimum(2 * index + 2, last), lhs_a, rhs_a)
        total_s[...] += dot_nt(lhs_b[...], rhs_b[...])
        return 0

    lax.fori_loop(0, layout.count // 16, add, 0)
    rotation = view(angles_ref)
    basis = harmonics(*rotation[2])
    for part in range(rows // 8):
        half = part % 2
        low = part // 2 * 8
        lanes = slice(half * LANES, (half + 1) * LANES)
        sums = [
            total_s[channel * lows + low : channel * lows + low + 8, lanes]
            + total_s[(PROJ + channel) * lows + low : (PROJ + channel) * lows + low + 8, lanes]
            for channel in range(PROJ)
        ]
        columns = tuple(dense_ref[pl.ds(index * rows + 2 * low + half, 8, stride=2), :] for index in range(11))
        _, pullback = jax.vjp(lambda *values: shape_of(values, rotation, camera_frame), *columns)
        grads = pullback(tuple(sums[:6]))
        for index, value in enumerate(tuple(grads) + tuple(sums[6:])):
            out_s[pl.ds(index * rows + 2 * low + half, 8, stride=2), :] = value
    sub = iota((8, LANES), 0)
    patterns = [basis_rows(basis, eighth) for eighth in range(8)]
    copies = []
    pieces = sems.shape[0]
    wide = gauss // pieces
    for row in range(rows):
        lanes = slice(row * LANES, (row + 1) * LANES)
        grad_ref[0:8, lanes] = out_s[pl.ds(row, 8, stride=rows), :]
        tints = [out_s[(11 + colour) * rows + row : (11 + colour) * rows + row + 1, :] for colour in range(3)]
        for eighth in range(1, 8):
            value = None
            for colour in range(3):
                pattern = patterns[eighth][colour]
                if pattern is not None:
                    term = pattern * tints[colour]
                    value = term if value is None else value + term
            if eighth == 1:
                value = jnp.where(sub < 3, out_s[pl.ds(8 * rows + row, 8, stride=rows), :], value)
            if eighth == 7:
                grad_ref[56:59, lanes] = value[0:3]
            else:
                grad_ref[8 * eighth : 8 * eighth + 8, lanes] = value
        if (row + 1) * LANES % wide == 0:
            piece = len(copies)
            span = slice(piece * wide, (piece + 1) * wide)
            copies.append(pltpu.make_async_copy(grad_ref.at[:, span], grad_hbm.at[:, span], sems.at[piece]))
            copies[-1].start()
    for copy in copies:
        copy.wait()


VMEM = pl.BlockSpec(memory_space=pltpu.VMEM)
HBM = pl.BlockSpec(memory_space=pltpu.HBM)
SMEM = pl.BlockSpec(memory_space=pltpu.SMEM)


def call(kernel, specs, outs, scratch, flops, name, out_spec=VMEM, vmem=VMEM_BYTES):
    return pl.pallas_call(
        kernel,
        in_specs=specs,
        out_specs=[out_spec] * len(outs),
        out_shape=[jax.ShapeDtypeStruct(shape, dtype) for shape, dtype in outs],
        scratch_shapes=[pltpu.VMEM(*one) if isinstance(one, tuple) else one for one in scratch],
        compiler_params=pltpu.CompilerParams(vmem_limit_bytes=vmem),
        cost_estimate=pl.CostEstimate(flops=flops, bytes_accessed=4 << 20, transcendentals=0),
        name=name,
    )


def route(devices, owners, locals_):
    slots = owners.size
    per_owner = slots // devices
    rows = slots // LANES
    halves = per_owner // LANES if per_owner % LANES == 0 else 0
    asked = (devices * halves, LANES) if halves else (devices, per_owner)
    return call(
        partial(route_kernel, devices, per_owner),
        [HBM, HBM],
        [(asked, i32), ((devices, per_owner), i32), ((rows, LANES), i32)],
        [(owners.shape, i32)] * 2 + [((rows, LANES), i32)] * 3 + [pltpu.SemaphoreType.DMA((2,))],
        1 << 30,
        "route",
        vmem=63 << 20,
    )(owners, locals_)


def shade(camera_frame, view_angles, gaussians):
    rows = gaussians.shape[1] // LANES
    return call(
        partial(shade_kernel, camera_frame),
        [SMEM, VMEM],
        [((sum(PARTS) * rows // 2, WIDE), bf16), ((16 * rows, LANES), f32)],
        [((27 * rows, LANES), f32)],
        1 << 30,
        "shade",
    )(view_angles, gaussians)


def pick(layout, table, asked):
    return call(
        partial(pick_kernel, layout),
        [VMEM, VMEM],
        [((PROJ * layout.count, LANES), f32)],
        [],
        1 << 30,
        "pick",
    )(table, asked)[0]


def render(layout, list_counts, tile_order, rows, pos, back, cotangent):
    slot_rows = pos.shape[0]
    groups = tile_order.shape[0] // GROUP
    slots = slot_rows * LANES
    return call(
        partial(render_kernel, layout),
        [SMEM, SMEM, VMEM, VMEM, VMEM, VMEM],
        [(cotangent.shape, f32), ((PROJ * layout.count, LANES), f32)],
        [
            ((sum(PARTS) * slot_rows // 2, WIDE), bf16),
            ((2 * PROJ * slot_rows // 2, WIDE), bf16),
            ((PROJ * slot_rows, LANES), f32),
            ((24 * slot_rows, LANES), f32),
            ((24 * groups, PIX), f32),
            ((groups, 96, 2 * PIX), bf16),
            ((slot_rows, 64, LANES), bf16),
            ((slots, PIX), f32),
            ((slots, PIX), f32),
            ((slots, PIX), f32),
            ((16 * slot_rows, LANES), f32),
        ],
        1 << 34,
        "render",
    )(list_counts, tile_order, rows, pos, back, cotangent)


def collect(layout, camera_frame, view_angles, shape, dense, asked, terms):
    rows = shape[1] // LANES
    lows = shape[1] // WIDE
    lhs = ((2 * PROJ * lows, 8 * LANES), bf16)
    rhs = ((WIDE, 8 * LANES), bf16)
    return call(
        partial(collect_kernel, layout, camera_frame),
        [SMEM, VMEM, VMEM, VMEM],
        [(shape, f32)],
        [
            lhs,
            lhs,
            rhs,
            rhs,
            ((2 * PROJ * lows, WIDE), f32),
            ((16 * rows, LANES), f32),
            (shape, f32),
            pltpu.SemaphoreType.DMA((8,)),
        ],
        1 << 32,
        "collect",
        out_spec=HBM,
    )(view_angles, dense, asked, terms)[0]


def swap_rows(layout, devices, rows):
    if layout.halves:
        apart = rows.reshape(devices * PROJ, layout.halves, LANES)
        return lax.all_to_all(apart, "dev", split_axis=0, concat_axis=0, tiled=True).reshape(rows.shape)
    apart = rows.reshape(PROJ, devices, layout.count * LANES // devices)
    return lax.all_to_all(apart, "dev", split_axis=1, concat_axis=1, tiled=True).reshape(rows.shape)


def shards(gaussians, view_angles, tile_order, tile_owners, tile_locals, list_counts, image_cotangent):
    devices = lax.axis_size("dev")
    tiles_y = devices * tile_order.shape[0] // TX
    camera_frame = (4.0 * TX, 4.0 * tiles_y, 8.0 * TX, 8.0 * tiles_y)
    layout = Rows(devices, tile_owners.size // devices)
    want, back, pos = route(devices, tile_owners, tile_locals)
    asked = lax.all_to_all(want, "dev", split_axis=0, concat_axis=0, tiled=True)
    table, dense = shade(camera_frame, view_angles, gaussians)
    if not layout.halves:
        asked = asked.reshape(layout.count, LANES)
    if layout.halves != 2:
        back = back.reshape(layout.count, LANES)
    arrived = swap_rows(layout, devices, pick(layout, table, asked))
    rendered, slot_grads = render(layout, list_counts, tile_order, arrived, pos, back, image_cotangent)
    terms = swap_rows(layout, devices, slot_grads)
    gradients = collect(layout, camera_frame, view_angles, gaussians.shape, dense, asked, terms)
    return (rendered, gradients)


def solution(mesh):
    return jax.shard_map(
        shards,
        mesh=mesh,
        in_specs=(
            P(None, "dev"),
            P(),
            P("dev"),
            P("dev", None),
            P("dev", None),
            P("dev"),
            P(None, "dev"),
        ),
        out_specs=(P(None, "dev"), P(None, "dev")),
        check_vma=False,
    )
```

```python
from functools import partial

import jax
import jax.numpy as jnp
from jax import lax
from jax.experimental import pallas as pl
from jax.experimental.pallas import tpu as pltpu
from jax.sharding import PartitionSpec as P

PIX = 256
TX = 32
LANES = 128
PROJ = 9
GROUP = 8
WIDE = 2 * LANES
PARTS = (3, 3, 3, 3, 3, 2, 2, 2, 2)
STEP = LANES // GROUP
LOG2E = 1.4426950408889634
BATCH = 8
VMEM_BYTES = 52 * 1024 * 1024

f32 = jnp.float32
bf16 = jnp.bfloat16
i32 = jnp.int32


def iota(shape, dim):
    return lax.broadcasted_iota(i32, shape, dim)


def lane_pick(row, lanes):
    source = jnp.broadcast_to(row, lanes.shape)
    return jnp.take_along_axis(source, lanes, axis=1, mode="promise_in_bounds")


def split_two(values):
    first = values.astype(bf16).astype(f32)
    return first, values - first


def split_three(values):
    first, rest = split_two(values)
    second, third = split_two(rest)
    return first, second, third


def dot(lhs, rhs):
    return lax.dot_general(lhs, rhs, (((1,), (0,)), ((), ())), preferred_element_type=f32)


def dot_nt(lhs, rhs):
    return lax.dot_general(lhs, rhs, (((1,), (1,)), ((), ())), preferred_element_type=f32)


def dot_tn(lhs, rhs):
    return lax.dot_general(lhs, rhs, (((0,), (0,)), ((), ())), preferred_element_type=f32)


class Rows:
    def __init__(self, devices, per_owner):
        self.halves = per_owner // LANES if per_owner % LANES == 0 else 0
        self.count = devices * per_owner // LANES

    def row(self, channel, major, minor):
        halves = self.halves
        if halves == 0:
            return channel * self.count + major
        return major * (PROJ * halves) + channel * halves + minor

    def half(self, ref, channel, half):
        halves = self.halves
        if halves == 0:
            return ref[pl.ds(channel * self.count + half, self.count // 2, stride=2), :]
        return jnp.concatenate(
            [ref[pl.ds(self.row(channel, one // halves, one % halves), 1), :] for one in range(half, self.count, 2)], axis=0
        ) if halves != 2 else ref[pl.ds(channel * 2 + half, self.count // 2, stride=2 * PROJ), :]

    def minors(self):
        return max(self.halves, 1)


def narrow(ids):
    return ids.astype(f32).astype(bf16)


def one_hot(ids, every):
    return jnp.where(narrow(ids) == every, jnp.ones((), bf16), jnp.zeros((), bf16))


def pick_slots(parts, slots, low_id, high_id, put):
    found = dot(parts, one_hot(slots % WIDE, high_id))
    mine = slots // WIDE == low_id
    lows = low_id.shape[0]
    first = 0
    for channel, count in enumerate(PARTS if parts.shape[0] == sum(PARTS) * lows else (2,) * PROJ):
        value = found[first * lows : (first + 1) * lows]
        for part in range(1, count):
            value = value + found[(first + part) * lows : (first + part + 1) * lows]
        first += count
        put(channel, jnp.sum(jnp.where(mine, value, 0.0), axis=0, keepdims=True))


def put_parts(parts_ref, channel, half, value, counts, lows=None, low=0):
    lows = lows or value.shape[0]
    first = sum(counts[:channel])
    parts = split_three(value) if counts[channel] == 3 else split_two(value)
    for part, one in enumerate(parts):
        at = (first + part) * lows + low
        parts_ref[at : at + value.shape[0], half * LANES : (half + 1) * LANES] = one.astype(bf16)


def route_kernel(devices, per_owner, own_hbm, loc_hbm, want_ref, back_ref, pos_ref, own_ref, loc_ref, own_s, loc_s, rank_s, sems):
    copies = [pltpu.make_async_copy(own_hbm, own_ref, sems.at[0]), pltpu.make_async_copy(loc_hbm, loc_ref, sems.at[1])]
    for copy in copies:
        copy.start()
    for copy in copies:
        copy.wait()
    rows = own_s.shape[0]
    blocks = own_ref.shape[1] // LANES
    lane = iota((8, LANES), 1)
    from_slot = iota((8, LANES), 0) * STEP + lane // GROUP
    tile_of = lane % GROUP
    for group in range(own_ref.shape[0] // GROUP):
        for block in range(blocks):
            for source, target in ((own_ref, own_s), (loc_ref, loc_s)):
                part = source[group * GROUP : (group + 1) * GROUP, block * LANES : (block + 1) * LANES]
                out = jnp.zeros((8, LANES), i32)
                for tile in range(GROUP):
                    out = jnp.where(tile_of == tile, lane_pick(part[tile : tile + 1], from_slot), out)
                start = (group * blocks + block) * 8
                target[start : start + 8, :] = out
    owner = own_s[...]
    left = (iota((LANES, 2 * LANES), 0) < iota((LANES, 2 * LANES), 1)) | (iota((LANES, 2 * LANES), 1) >= LANES)
    above = iota((rows, rows), 1) < iota((rows, rows), 0)
    hits = jnp.concatenate([jnp.where(owner == one, 1.0, 0.0).astype(bf16) for one in range(devices)], axis=0)
    sums = dot(hits, jnp.where(left, 1.0, 0.0).astype(bf16))
    totals = jnp.concatenate(
        [sums[one * rows : (one + 1) * rows, LANES:].astype(bf16) for one in range(devices)], axis=1
    )
    base = dot(jnp.where(above, 1.0, 0.0).astype(bf16), totals)
    rank = jnp.zeros((rows, LANES), f32)
    for one in range(devices):
        here = sums[one * rows : (one + 1) * rows, :LANES] + base[:, one * LANES : (one + 1) * LANES]
        rank = jnp.where(owner == one, here, rank)
    rank = rank.astype(i32)
    pos_ref[...] = owner * per_owner + rank
    rank_s[...] = rank

    owner_id = iota((devices, LANES), 0)
    rank_id = narrow(iota((per_owner, LANES), 0))
    slot_lane = iota((devices, LANES), 1).astype(f32)

    def place(index, total):
        start = pl.multiple_of(index * 8, 8)
        own_rows = own_s[pl.ds(start, 8), :]
        loc_rows = loc_s[pl.ds(start, 8), :]
        rank_rows = rank_s[pl.ds(start, 8), :]
        high_rows = (loc_rows // LANES).astype(f32)
        low_rows = (loc_rows % LANES).astype(f32)
        lhs = []
        rhs = []
        for row in range(8):
            mine = own_rows[row : row + 1] == owner_id
            number = (start + row).astype(f32)
            lhs.append(
                jnp.concatenate(
                    [
                        jnp.where(mine, high_rows[row : row + 1], 0.0),
                        jnp.where(mine, low_rows[row : row + 1], 0.0),
                        jnp.where(mine, number, 0.0),
                        jnp.where(mine, slot_lane, 0.0),
                    ],
                    axis=0,
                ).astype(bf16)
            )
            rhs.append(one_hot(rank_rows[row : row + 1], rank_id))
        return total + dot_nt(jnp.concatenate(lhs, axis=1), jnp.concatenate(rhs, axis=1))

    total = lax.fori_loop(0, rows // 8, place, jnp.zeros((4 * devices, per_owner), f32), unroll=4).astype(i32)
    want = total[:devices] * LANES + total[devices : 2 * devices]
    halves = per_owner // LANES
    if per_owner % LANES == 0 and halves > 1:
        for half in range(halves):
            want_ref[pl.ds(half, devices, stride=halves), :] = want[:, half * LANES : (half + 1) * LANES]
    else:
        want_ref[...] = want
    back_ref[...] = total[2 * devices : 3 * devices] * LANES + total[3 * devices :]


def view(angles_ref):
    angle = [jnp.full((1, LANES), angles_ref[index], f32) for index in range(3)]
    (cos_a, cos_b, cos_c) = [jnp.cos(one) for one in angle]
    (sin_a, sin_b, sin_c) = [jnp.sin(one) for one in angle]
    return [
        [cos_c * cos_b, cos_c * sin_b * sin_a - sin_c * cos_a, cos_c * sin_b * cos_a + sin_c * sin_a],
        [sin_c * cos_b, sin_c * sin_b * sin_a + cos_c * cos_a, sin_c * sin_b * cos_a - cos_c * sin_a],
        [-sin_b, cos_b * sin_a, cos_b * cos_a],
    ]


def harmonics(along_x, along_y, along_z):
    sq_x = along_x * along_x
    sq_y = along_y * along_y
    sq_z = along_z * along_z
    return [
        0.28209479177387814 + 0.0 * along_x,
        -0.4886025119029199 * along_y,
        0.4886025119029199 * along_z,
        -0.4886025119029199 * along_x,
        1.0925484305920792 * along_x * along_y,
        -1.0925484305920792 * along_y * along_z,
        0.31539156525252005 * (2.0 * sq_z - sq_x - sq_y),
        -1.0925484305920792 * along_x * along_z,
        0.5462742152960396 * (sq_x - sq_y),
        -0.5900435899266435 * along_y * (3.0 * sq_x - sq_y),
        2.890611442640554 * along_x * along_y * along_z,
        -0.4570457994644658 * along_y * (4.0 * sq_z - sq_x - sq_y),
        0.3731763325901154 * along_z * (2.0 * sq_z - 3.0 * sq_x - 3.0 * sq_y),
        -0.4570457994644658 * along_x * (4.0 * sq_z - sq_x - sq_y),
        1.445305721320277 * along_z * (sq_x - sq_y),
        -0.5900435899266435 * along_x * (sq_x - 3.0 * sq_y),
    ]


def basis_rows(basis, eighth):
    sub = iota((8, LANES), 0)
    found = []
    for colour in range(3):
        out = None
        for inner in range(8):
            index = 8 * eighth + inner - 11 - 16 * colour
            if 0 <= index < 16:
                out = jnp.zeros((8, LANES), f32) if out is None else out
                out = jnp.where(sub == inner, basis[index], out)
        found.append(out)
    return found


def shape_of(columns, rotation, camera_frame):
    focal_x, focal_y, centre_x, centre_y = camera_frame
    positions = columns[0:3]
    cam_first = rotation[0][0] * positions[0] + rotation[0][1] * positions[1] + rotation[0][2] * positions[2]
    cam_second = rotation[1][0] * positions[0] + rotation[1][1] * positions[1] + rotation[1][2] * positions[2]
    mean_x = centre_x + focal_x * cam_first
    mean_y = centre_y + focal_y * cam_second
    scales = [jnp.exp(one) for one in columns[3:6]]
    quat_w, quat_x, quat_y, quat_z = columns[6:10]
    norm_sq = jnp.maximum(quat_w * quat_w + quat_x * quat_x + quat_y * quat_y + quat_z * quat_z, 1.0)
    twice = 2.0 / norm_sq
    turned = [
        [
            1.0 - twice * (quat_y * quat_y + quat_z * quat_z),
            twice * (quat_x * quat_y - quat_w * quat_z),
            twice * (quat_x * quat_z + quat_w * quat_y),
        ],
        [
            twice * (quat_x * quat_y + quat_w * quat_z),
            1.0 - twice * (quat_x * quat_x + quat_z * quat_z),
            twice * (quat_y * quat_z - quat_w * quat_x),
        ],
        [
            twice * (quat_x * quat_z - quat_w * quat_y),
            twice * (quat_y * quat_z + quat_w * quat_x),
            1.0 - twice * (quat_x * quat_x + quat_y * quat_y),
        ],
    ]
    rows = []
    for focal, turn in ((focal_x, rotation[0]), (focal_y, rotation[1])):
        rows.append(
            [
                focal * (turn[0] * turned[0][k] + turn[1] * turned[1][k] + turn[2] * turned[2][k]) * scales[k]
                for k in range(3)
            ]
        )
    first, second = rows
    cov_a = first[0] * first[0] + first[1] * first[1] + first[2] * first[2] + 0.3
    cov_b = first[0] * second[0] + first[1] * second[1] + first[2] * second[2]
    cov_c = second[0] * second[0] + second[1] * second[1] + second[2] * second[2] + 0.3
    determinant = cov_a * cov_c - cov_b * cov_b
    opacity = 1.0 / (1.0 + jnp.exp(-columns[10]))
    return mean_x, mean_y, cov_c / determinant, -cov_b / determinant, cov_a / determinant, opacity


def spread_columns(gauss_ref, dense_s):
    rows = gauss_ref.shape[1] // LANES
    for row in range(rows):
        for eighth in range(2):
            dense_s[pl.ds(8 * eighth * rows + row, 8, stride=rows), :] = gauss_ref[
                8 * eighth : 8 * eighth + 8, row * LANES : (row + 1) * LANES
            ]


def shade_kernel(camera_frame, angles_ref, gauss_ref, parts_ref, dense_s, tint_s):
    rows = gauss_ref.shape[1] // LANES
    spread_columns(gauss_ref, dense_s)
    rotation = view(angles_ref)
    basis = harmonics(*rotation[2])
    patterns = [basis_rows(basis, eighth) for eighth in range(7)]
    for row in range(rows):
        lanes = slice(row * LANES, (row + 1) * LANES)
        tints = [None] * 3
        for eighth in range(1, 7):
            block = gauss_ref[8 * eighth : 8 * eighth + 8, lanes]
            for colour in range(3):
                pattern = patterns[eighth][colour]
                if pattern is not None:
                    term = block * pattern
                    tints[colour] = term if tints[colour] is None else tints[colour] + term
        for colour in range(3):
            tint_s[pl.ds(8 * colour * rows + row, 8, stride=rows), :] = tints[colour]
        tint_s[pl.ds(24 * rows + row, 3, stride=rows), :] = gauss_ref[56:59, lanes]
    for part in range(rows // 16):
        half = part % 2
        low = part // 2 * 16
        at = [pl.ds(index * rows + 2 * low + half, 16, stride=2) for index in range(27)]
        columns = [dense_s[one, :] for one in at[:11]]
        for index, value in enumerate(shape_of(columns, rotation, camera_frame)):
            put_parts(parts_ref, index, half, value, PARTS, rows // 2, low)
        for colour in range(3):
            total = 0.5
            for inner in range(8):
                total = total + tint_s[at[8 * colour + inner], :]
            if colour == 2:
                for inner in range(3):
                    total = total + basis[13 + inner] * tint_s[at[24 + inner], :]
            put_parts(parts_ref, 6 + colour, half, total, PARTS, rows // 2, low)


def pick_kernel(layout, parts_ref, asked_ref, out_ref):
    low_id = iota((parts_ref.shape[0] // sum(PARTS), WIDE), 0)
    high_id = narrow(iota((WIDE, WIDE), 0))
    minors = layout.minors()

    def pick_some(index, _):
        slots = jnp.concatenate([asked_ref[pl.ds(2 * index + one, 1), :] for one in range(2)], axis=1)

        def put(channel, value):
            for one in range(2):
                at = layout.row(channel, (2 * index + one) // minors, (2 * index + one) % minors)
                out_ref[pl.ds(at, 1), :] = value[:, one * LANES : (one + 1) * LANES]

        pick_slots(parts_ref[...], slots, low_id, high_id, put)
        return 0

    lax.fori_loop(0, layout.count // 2, pick_some, 0, unroll=16)


def render_kernel(
    layout,
    count_ref,
    order_ref,
    rows_ref,
    pos_ref,
    back_ref,
    cot_ref,
    image_ref,
    out_ref,
    in_s,
    out_s,
    raw_s,
    coef_s,
    cot_s,
    rhs_s,
    tint_s,
    alpha_s,
    shade_s,
    weight_s,
    sums_s,
):
    slot_rows = pos_ref.shape[0]
    groups = cot_ref.shape[1] // (GROUP * PIX)
    chunks = slot_rows // groups
    sub = iota((8, LANES), 0)
    lane = iota((8, LANES), 1)
    tile_of = lane % GROUP
    blocks = slot_rows // 8
    middles = []
    for group in range(groups):
        middle_x = jnp.zeros((8, LANES), f32)
        middle_y = jnp.zeros((8, LANES), f32)
        live = jnp.zeros((8, LANES), i32)
        for tile in range(GROUP):
            shown = order_ref[group * GROUP + tile]
            here = tile_of == tile
            middle_x = jnp.where(here, (shown % TX * 16 + 8).astype(f32), middle_x)
            middle_y = jnp.where(here, (shown // TX * 16 + 8).astype(f32), middle_y)
            live = jnp.where(here, count_ref[group * GROUP + tile], live)
        middles.append((middle_x, middle_y, live))

    for half in range(2):
        for channel in range(PROJ):
            put_parts(in_s, channel, half, layout.half(rows_ref, channel, half), PARTS)
    low_id = iota((slot_rows // 2, WIDE), 0)
    high_id = narrow(iota((WIDE, WIDE), 0))

    def pick_in(index, _):
        slots = jnp.concatenate([pos_ref[pl.ds(2 * index + one, 1), :] for one in range(2)], axis=1)

        def put(channel, value):
            for one in range(2):
                raw_s[pl.ds(channel * slot_rows + 2 * index + one, 1), :] = value[:, one * LANES : (one + 1) * LANES]

        pick_slots(in_s[...], slots, low_id, high_id, put)
        return 0

    lax.fori_loop(0, slot_rows // 2, pick_in, 0, unroll=16)
    for block in range(blocks):
        group = block * 8 // chunks
        middle_x, middle_y, live = middles[group]
        found = [
            raw_s[channel * slot_rows + 8 * block : channel * slot_rows + 8 * block + 8, :] for channel in range(PROJ)
        ]
        at_x = found[0] - middle_x
        at_y = found[1] - middle_y
        quad_a = -0.5 * found[2]
        quad_b = -found[3]
        quad_c = -0.5 * found[4]
        flat = quad_a * at_x * at_x + quad_c * at_y * at_y + quad_b * at_x * at_y + jnp.log(found[5])
        place = (8 * block - group * chunks + sub) * STEP + lane // GROUP
        terms = (
            quad_a * LOG2E,
            quad_b * LOG2E,
            quad_c * LOG2E,
            (-2.0 * quad_a * at_x - quad_b * at_y) * LOG2E,
            (-2.0 * quad_c * at_y - quad_b * at_x) * LOG2E,
            jnp.where(place < live, flat * LOG2E, -1e30),
        )
        for index, term in enumerate(terms):
            for part, value in enumerate(split_three(term)):
                coef_s[pl.ds(8 * block * 24 + 6 * part + index, 8, stride=24), :] = value
        for colour in range(3):
            for part, value in enumerate(split_two(found[6 + colour])):
                coef_s[pl.ds(8 * block * 24 + 18 + 3 * part + colour, 8, stride=24), :] = value

    pixel = iota((24, PIX), 1)
    row = iota((24, PIX), 0)
    pix_x = (pixel % 16).astype(f32) - 7.5
    pix_y = (pixel // 16).astype(f32) - 7.5
    kind = row % 6
    monomials = jnp.where(kind == 0, pix_x * pix_x, jnp.where(kind == 1, pix_x * pix_y, 1.0))
    monomials = jnp.where(kind == 2, pix_y * pix_y, monomials)
    monomials = jnp.where(kind == 3, pix_x, jnp.where(kind == 4, pix_y, monomials))
    moments = jnp.where(iota((8, PIX), 0) < 6, monomials[0:8], 0.0).astype(bf16)
    monomials = jnp.where(row < 18, monomials, 0.0)
    nothing = jnp.zeros((24, PIX), f32)
    for group in range(groups):
        for colour in range(3):
            for tile in range(GROUP):
                start = (group * GROUP + tile) * PIX
                cot_s[group * 24 + colour * GROUP + tile, :] = cot_ref[colour, start : start + PIX]
    cots = []
    spare = jnp.zeros((8, PIX), f32)
    for group in range(groups):
        first, second = split_two(cot_s[group * 24 : (group + 1) * 24, :])
        cots.append(jnp.concatenate([first, spare, second, spare], axis=0).astype(bf16))
        rhs_s[group] = jnp.concatenate(
            [
                jnp.concatenate([jnp.concatenate([nothing, monomials[8 * one : 8 * one + 8]], axis=0) for one in range(3)], axis=0),
                jnp.concatenate([first, spare, first, spare, second, spare], axis=0),
            ],
            axis=1,
        ).astype(bf16)

    own_tile = sub == tile_of
    own_pair = iota((8, WIDE), 0) == iota((8, WIDE), 1) % GROUP

    def evaluate(index, _):
        for group in range(groups):
            chunk = group * chunks + index
            coefs = coef_s[pl.ds(pl.multiple_of(chunk * 24, 8), 24), :]
            tints = [jnp.where(own_tile, coefs[18 + one : 19 + one], 0.0) for one in range(6)]
            lhs = jnp.concatenate(
                tints[:3] + [coefs[0:8]] + tints[3:] + [coefs[8:16]] + tints[:3] + [coefs[16:24]], axis=0
            ).astype(bf16)
            both = dot_tn(lhs, rhs_s[group])
            start = pl.multiple_of(chunk * LANES, LANES)
            tint_s[:, pl.ds(start, LANES)] = lhs[0:64]
            alpha_s[pl.ds(start, LANES), :] = jnp.exp2(both[:, :PIX])
            shade_s[pl.ds(start, LANES), :] = both[:, PIX:]
        return 0

    lax.fori_loop(0, chunks, evaluate, 0, unroll=BATCH)

    def scan(index, trans):
        out = []
        for group in range(groups):
            one = trans[group]
            start = pl.multiple_of((group * chunks + index) * LANES, LANES)
            for step in range(STEP):
                alpha = alpha_s[pl.ds(start + step * GROUP, GROUP), :]
                weight = one * alpha
                one = one - weight
                weight_s[pl.ds(start + step * GROUP, GROUP), :] = weight
            out.append(one)
        return tuple(out)

    def paint(index, images):
        out = []
        for group in range(groups):
            chunk = group * chunks + index
            both = pl.ds(pl.multiple_of(chunk * LANES, WIDE), WIDE)
            first, second = split_two(weight_s[both, :])
            first = first.astype(bf16)
            second = second.astype(bf16)
            tints = tint_s[:, both]
            by_first = dot(tints, first)
            out.append(images[group] + by_first[0:24] + by_first[32:56] + dot(tints[0:32], second)[0:24])
            by_first = dot_nt(cots[group], first)
            tint_grad = by_first[0:24] + by_first[32:56] + dot_nt(cots[group][0:32], second)[0:24]
            for colour in range(3):
                own = jnp.where(own_pair, tint_grad[colour * GROUP : (colour + 1) * GROUP], 0.0)
                own = jnp.sum(own, axis=0, keepdims=True)
                for one in range(2):
                    sums_s[pl.ds((chunk + one) * 16 + 8 + colour, 1), :] = own[:, one * LANES : (one + 1) * LANES]
        return tuple(out)

    def scan_batch(batch, trans):
        for one in range(BATCH):
            trans = scan(batch * BATCH + one, trans)
        return trans

    def paint_batch(batch, images):
        for one in range(0, BATCH, 2):
            images = paint(batch * BATCH + one, images)
        return images

    def forward(batch, state):
        trans, images = state
        images = paint_batch(batch - 1, images)
        return scan_batch(batch, trans), images

    batches = chunks // BATCH
    trans = scan_batch(0, tuple(jnp.ones((GROUP, PIX), f32) for _ in range(groups)))
    images = tuple(jnp.zeros((24, PIX), f32) for _ in range(groups))
    trans, images = lax.fori_loop(1, batches, forward, (trans, images))
    images = paint_batch(batches - 1, images)
    for group in range(groups):
        for colour in range(3):
            for tile in range(GROUP):
                at = (group * GROUP + tile) * PIX
                image_ref[colour, at : at + PIX] = images[group][colour * GROUP + tile]

    def moment(index):
        for group in range(groups):
            chunk = group * chunks + index
            first, second = split_two(shade_s[pl.ds(pl.multiple_of(chunk * LANES, WIDE), WIDE), :])
            found = dot_nt(moments, first.astype(bf16)) + dot_nt(moments, second.astype(bf16))
            for one in range(2):
                start = pl.multiple_of((chunk + one) * 16, 8)
                sums_s[pl.ds(start, 8), :] = found[:, one * LANES : (one + 1) * LANES]

    def rescan(index, behinds):
        out = []
        for group in range(groups):
            behind = behinds[group]
            start = pl.multiple_of((group * chunks + index) * LANES, LANES)
            for step in reversed(range(STEP)):
                at = pl.ds(start + step * GROUP, GROUP)
                ahead = shade_s[at, :] - behind
                shade_s[at, :] = weight_s[at, :] * ahead
                behind = behind + alpha_s[at, :] * ahead
            out.append(behind)
        return tuple(out)

    def moment_batch(batch):
        for one in range(0, BATCH, 2):
            moment(batch * BATCH + one)

    def rescan_batch(batch, behinds):
        for one in reversed(range(BATCH)):
            behinds = rescan(batch * BATCH + one, behinds)
        return behinds

    def backward(index, behinds):
        moment_batch(batches - index)
        return rescan_batch(batches - 1 - index, behinds)

    behinds = rescan_batch(batches - 1, tuple(jnp.zeros((GROUP, PIX), f32) for _ in range(groups)))
    lax.fori_loop(1, batches, backward, behinds)
    moment_batch(0)

    slot_s = coef_s
    for block in range(blocks):
        middle_x, middle_y, _ = middles[block * 8 // chunks]
        at = slice(8 * block, 8 * block + 8)
        raw = [raw_s[channel * slot_rows + 8 * block : channel * slot_rows + 8 * block + 8, :] for channel in range(6)]
        (sum_xx, sum_xy, sum_yy, sum_x, sum_y, sum_one) = [
            sums_s[pl.ds(8 * block * 16 + index, 8, stride=16), :] for index in range(6)
        ]
        at_x = raw[0] - middle_x
        at_y = raw[1] - middle_y
        off_x = sum_x - at_x * sum_one
        off_y = sum_y - at_y * sum_one
        grads = [
            raw[2] * off_x + raw[3] * off_y,
            raw[4] * off_y + raw[3] * off_x,
            -0.5 * (sum_xx - at_x * (sum_x + off_x)),
            -(sum_xy - at_y * sum_x - at_x * off_y),
            -0.5 * (sum_yy - at_y * (sum_y + off_y)),
            sum_one / raw[5],
        ] + [sums_s[pl.ds(8 * block * 16 + 8 + colour, 8, stride=16), :] for colour in range(3)]
        for channel, value in enumerate(grads):
            slot_s[channel * slot_rows + 8 * block : channel * slot_rows + 8 * block + 8, :] = value

    for half in range(2):
        for channel in range(PROJ):
            value = slot_s[pl.ds(channel * slot_rows + half, slot_rows // 2, stride=2), :]
            put_parts(out_s, channel, half, value, (2,) * PROJ)
    minors = layout.minors()

    def pick_out(index, _):
        if layout.halves == 2:
            slots = back_ref[pl.ds(index, 1), :]
        else:
            slots = jnp.concatenate([back_ref[pl.ds(2 * index + one, 1), :] for one in range(2)], axis=1)

        def put(channel, value):
            for one in range(2):
                at = layout.row(channel, (2 * index + one) // minors, (2 * index + one) % minors)
                out_ref[pl.ds(at, 1), :] = value[:, one * LANES : (one + 1) * LANES]

        pick_slots(out_s[...], slots, low_id, high_id, put)
        return 0

    lax.fori_loop(0, layout.count // 2, pick_out, 0, unroll=16)


def collect_kernel(
    layout, camera_frame, angles_ref, dense_ref, asked_ref, terms_ref, grad_hbm, lhs_a, lhs_b, rhs_a, rhs_b, total_s, out_s, grad_ref, sems
):
    gauss = grad_ref.shape[1]
    rows = gauss // LANES
    lows = gauss // WIDE
    low_id = narrow(iota((lows, LANES), 0))
    high_id = narrow(iota((WIDE, LANES), 0))
    minors = layout.minors()

    def build(index, lhs_s, rhs_s):
        asked = asked_ref[pl.ds(pl.multiple_of(index * 8, 8), 8), :]
        low = asked // WIDE
        high = asked % WIDE
        for row in range(8):
            lanes = slice(row * LANES, (row + 1) * LANES)
            mine = one_hot(low[row : row + 1], low_id)
            rhs_s[:, lanes] = one_hot(high[row : row + 1], high_id)
            for channel in range(PROJ):
                at = layout.row(channel, index * (8 // minors) + row // minors, row % minors)
                for part, value in enumerate(split_two(terms_ref[pl.ds(at, 1), :])):
                    first = (part * PROJ + channel) * lows
                    lhs_s[first : first + lows, lanes] = mine * value.astype(bf16)

    last = layout.count // 8 - 1
    build(0, lhs_a, rhs_a)
    total_s[...] = jnp.zeros(total_s.shape, f32)

    def add(index, _):
        build(2 * index + 1, lhs_b, rhs_b)
        total_s[...] += dot_nt(lhs_a[...], rhs_a[...])
        build(jnp.minimum(2 * index + 2, last), lhs_a, rhs_a)
        total_s[...] += dot_nt(lhs_b[...], rhs_b[...])
        return 0

    lax.fori_loop(0, layout.count // 16, add, 0)
    rotation = view(angles_ref)
    basis = harmonics(*rotation[2])
    for part in range(rows // 8):
        half = part % 2
        low = part // 2 * 8
        lanes = slice(half * LANES, (half + 1) * LANES)
        sums = [
            total_s[channel * lows + low : channel * lows + low + 8, lanes]
            + total_s[(PROJ + channel) * lows + low : (PROJ + channel) * lows + low + 8, lanes]
            for channel in range(PROJ)
        ]
        columns = tuple(dense_ref[pl.ds(index * rows + 2 * low + half, 8, stride=2), :] for index in range(11))
        _, pullback = jax.vjp(lambda *values: shape_of(values, rotation, camera_frame), *columns)
        grads = pullback(tuple(sums[:6]))
        for index, value in enumerate(tuple(grads) + tuple(sums[6:])):
            out_s[pl.ds(index * rows + 2 * low + half, 8, stride=2), :] = value
    sub = iota((8, LANES), 0)
    patterns = [basis_rows(basis, eighth) for eighth in range(8)]
    copies = []
    pieces = sems.shape[0]
    wide = gauss // pieces
    for row in range(rows):
        lanes = slice(row * LANES, (row + 1) * LANES)
        grad_ref[0:8, lanes] = out_s[pl.ds(row, 8, stride=rows), :]
        tints = [out_s[(11 + colour) * rows + row : (11 + colour) * rows + row + 1, :] for colour in range(3)]
        for eighth in range(1, 8):
            value = None
            for colour in range(3):
                pattern = patterns[eighth][colour]
                if pattern is not None:
                    term = pattern * tints[colour]
                    value = term if value is None else value + term
            if eighth == 1:
                value = jnp.where(sub < 3, out_s[pl.ds(8 * rows + row, 8, stride=rows), :], value)
            if eighth == 7:
                grad_ref[56:59, lanes] = value[0:3]
            else:
                grad_ref[8 * eighth : 8 * eighth + 8, lanes] = value
        if (row + 1) * LANES % wide == 0:
            piece = len(copies)
            span = slice(piece * wide, (piece + 1) * wide)
            copies.append(pltpu.make_async_copy(grad_ref.at[:, span], grad_hbm.at[:, span], sems.at[piece]))
            copies[-1].start()
    for copy in copies:
        copy.wait()


VMEM = pl.BlockSpec(memory_space=pltpu.VMEM)
HBM = pl.BlockSpec(memory_space=pltpu.HBM)
SMEM = pl.BlockSpec(memory_space=pltpu.SMEM)


def call(kernel, specs, outs, scratch, flops, name, out_spec=VMEM, vmem=VMEM_BYTES):
    return pl.pallas_call(
        kernel,
        in_specs=specs,
        out_specs=[out_spec] * len(outs),
        out_shape=[jax.ShapeDtypeStruct(shape, dtype) for shape, dtype in outs],
        scratch_shapes=[pltpu.VMEM(*one) if isinstance(one, tuple) else one for one in scratch],
        compiler_params=pltpu.CompilerParams(vmem_limit_bytes=vmem),
        cost_estimate=pl.CostEstimate(flops=flops, bytes_accessed=4 << 20, transcendentals=0),
        name=name,
    )


def route(devices, owners, locals_):
    slots = owners.size
    per_owner = slots // devices
    rows = slots // LANES
    halves = per_owner // LANES if per_owner % LANES == 0 else 0
    asked = (devices * halves, LANES) if halves else (devices, per_owner)
    return call(
        partial(route_kernel, devices, per_owner),
        [HBM, HBM],
        [(asked, i32), ((devices, per_owner), i32), ((rows, LANES), i32)],
        [(owners.shape, i32)] * 2 + [((rows, LANES), i32)] * 3 + [pltpu.SemaphoreType.DMA((2,))],
        1 << 30,
        "route",
        vmem=63 << 20,
    )(owners, locals_)


def shade(camera_frame, view_angles, gaussians):
    rows = gaussians.shape[1] // LANES
    return call(
        partial(shade_kernel, camera_frame),
        [SMEM, VMEM],
        [((sum(PARTS) * rows // 2, WIDE), bf16), ((16 * rows, LANES), f32)],
        [((27 * rows, LANES), f32)],
        1 << 30,
        "shade",
    )(view_angles, gaussians)


def pick(layout, table, asked):
    return call(
        partial(pick_kernel, layout),
        [VMEM, VMEM],
        [((PROJ * layout.count, LANES), f32)],
        [],
        1 << 30,
        "pick",
    )(table, asked)[0]


def render(layout, list_counts, tile_order, rows, pos, back, cotangent):
    slot_rows = pos.shape[0]
    groups = tile_order.shape[0] // GROUP
    slots = slot_rows * LANES
    return call(
        partial(render_kernel, layout),
        [SMEM, SMEM, VMEM, VMEM, VMEM, VMEM],
        [(cotangent.shape, f32), ((PROJ * layout.count, LANES), f32)],
        [
            ((sum(PARTS) * slot_rows // 2, WIDE), bf16),
            ((2 * PROJ * slot_rows // 2, WIDE), bf16),
            ((PROJ * slot_rows, LANES), f32),
            ((24 * slot_rows, LANES), f32),
            ((24 * groups, PIX), f32),
            ((groups, 96, 2 * PIX), bf16),
            ((64, slots), bf16),
            ((slots, PIX), f32),
            ((slots, PIX), f32),
            ((slots, PIX), f32),
            ((16 * slot_rows, LANES), f32),
        ],
        1 << 34,
        "render",
    )(list_counts, tile_order, rows, pos, back, cotangent)


def collect(layout, camera_frame, view_angles, shape, dense, asked, terms):
    rows = shape[1] // LANES
    lows = shape[1] // WIDE
    lhs = ((2 * PROJ * lows, 8 * LANES), bf16)
    rhs = ((WIDE, 8 * LANES), bf16)
    return call(
        partial(collect_kernel, layout, camera_frame),
        [SMEM, VMEM, VMEM, VMEM],
        [(shape, f32)],
        [
            lhs,
            lhs,
            rhs,
            rhs,
            ((2 * PROJ * lows, WIDE), f32),
            ((16 * rows, LANES), f32),
            (shape, f32),
            pltpu.SemaphoreType.DMA((8,)),
        ],
        1 << 32,
        "collect",
        out_spec=HBM,
    )(view_angles, dense, asked, terms)[0]


def swap_rows(layout, devices, rows):
    if layout.halves:
        apart = rows.reshape(devices * PROJ, layout.halves, LANES)
        return lax.all_to_all(apart, "dev", split_axis=0, concat_axis=0, tiled=True).reshape(rows.shape)
    apart = rows.reshape(PROJ, devices, layout.count * LANES // devices)
    return lax.all_to_all(apart, "dev", split_axis=1, concat_axis=1, tiled=True).reshape(rows.shape)


def shards(gaussians, view_angles, tile_order, tile_owners, tile_locals, list_counts, image_cotangent):
    devices = lax.axis_size("dev")
    tiles_y = devices * tile_order.shape[0] // TX
    camera_frame = (4.0 * TX, 4.0 * tiles_y, 8.0 * TX, 8.0 * tiles_y)
    layout = Rows(devices, tile_owners.size // devices)
    want, back, pos = route(devices, tile_owners, tile_locals)
    asked = lax.all_to_all(want, "dev", split_axis=0, concat_axis=0, tiled=True)
    table, dense = shade(camera_frame, view_angles, gaussians)
    if not layout.halves:
        asked = asked.reshape(layout.count, LANES)
    if layout.halves != 2:
        back = back.reshape(layout.count, LANES)
    arrived = swap_rows(layout, devices, pick(layout, table, asked))
    rendered, slot_grads = render(layout, list_counts, tile_order, arrived, pos, back, image_cotangent)
    terms = swap_rows(layout, devices, slot_grads)
    gradients = collect(layout, camera_frame, view_angles, gaussians.shape, dense, asked, terms)
    return (rendered, gradients)


def solution(mesh):
    return jax.shard_map(
        shards,
        mesh=mesh,
        in_specs=(
            P(None, "dev"),
            P(),
            P("dev"),
            P("dev", None),
            P("dev", None),
            P("dev"),
            P(None, "dev"),
        ),
        out_specs=(P(None, "dev"), P(None, "dev")),
        check_vma=False,
    )
```

```python
from functools import partial

import jax
import jax.numpy as jnp
from jax import lax
from jax.experimental import pallas as pl
from jax.experimental.pallas import tpu as pltpu
from jax.sharding import PartitionSpec as P

PIX = 256
TX = 32
LANES = 128
PROJ = 9
GROUP = 8
WIDE = 2 * LANES
PARTS = (3, 3, 3, 3, 3, 2, 2, 2, 2)
STEP = LANES // GROUP
LOG2E = 1.4426950408889634
AHEAD = 2
VMEM_BYTES = 52 * 1024 * 1024

f32 = jnp.float32
bf16 = jnp.bfloat16
i32 = jnp.int32


def iota(shape, dim):
    return lax.broadcasted_iota(i32, shape, dim)


def lane_pick(row, lanes):
    source = jnp.broadcast_to(row, lanes.shape)
    return jnp.take_along_axis(source, lanes, axis=1, mode="promise_in_bounds")


def split_two(values):
    first = values.astype(bf16).astype(f32)
    return first, values - first


def split_three(values):
    first, rest = split_two(values)
    second, third = split_two(rest)
    return first, second, third


def dot(lhs, rhs):
    return lax.dot_general(lhs, rhs, (((1,), (0,)), ((), ())), preferred_element_type=f32)


def dot_nt(lhs, rhs):
    return lax.dot_general(lhs, rhs, (((1,), (1,)), ((), ())), preferred_element_type=f32)


def dot_tn(lhs, rhs):
    return lax.dot_general(lhs, rhs, (((0,), (0,)), ((), ())), preferred_element_type=f32)


class Rows:
    def __init__(self, devices, per_owner):
        self.halves = per_owner // LANES if per_owner % LANES == 0 else 0
        self.count = devices * per_owner // LANES

    def row(self, channel, major, minor):
        halves = self.halves
        if halves == 0:
            return channel * self.count + major
        return major * (PROJ * halves) + channel * halves + minor

    def half(self, ref, channel, half):
        halves = self.halves
        if halves == 0:
            return ref[pl.ds(channel * self.count + half, self.count // 2, stride=2), :]
        return jnp.concatenate(
            [ref[pl.ds(self.row(channel, one // halves, one % halves), 1), :] for one in range(half, self.count, 2)], axis=0
        ) if halves != 2 else ref[pl.ds(channel * 2 + half, self.count // 2, stride=2 * PROJ), :]

    def minors(self):
        return max(self.halves, 1)


def narrow(ids):
    return ids.astype(f32).astype(bf16)


def one_hot(ids, every):
    return jnp.where(narrow(ids) == every, jnp.ones((), bf16), jnp.zeros((), bf16))


def pick_slots(parts, slots, low_id, high_id, put):
    found = dot(parts, one_hot(slots % WIDE, high_id))
    mine = slots // WIDE == low_id
    lows = low_id.shape[0]
    first = 0
    for channel, count in enumerate(PARTS if parts.shape[0] == sum(PARTS) * lows else (2,) * PROJ):
        value = found[first * lows : (first + 1) * lows]
        for part in range(1, count):
            value = value + found[(first + part) * lows : (first + part + 1) * lows]
        first += count
        put(channel, jnp.sum(jnp.where(mine, value, 0.0), axis=0, keepdims=True))


def put_parts(parts_ref, channel, half, value, counts, lows=None, low=0):
    lows = lows or value.shape[0]
    first = sum(counts[:channel])
    parts = split_three(value) if counts[channel] == 3 else split_two(value)
    for part, one in enumerate(parts):
        at = (first + part) * lows + low
        parts_ref[at : at + value.shape[0], half * LANES : (half + 1) * LANES] = one.astype(bf16)


def route_kernel(devices, per_owner, own_hbm, loc_hbm, want_ref, back_ref, pos_ref, own_ref, loc_ref, own_s, loc_s, rank_s, sems):
    copies = [pltpu.make_async_copy(own_hbm, own_ref, sems.at[0]), pltpu.make_async_copy(loc_hbm, loc_ref, sems.at[1])]
    for copy in copies:
        copy.start()
    for copy in copies:
        copy.wait()
    rows = own_s.shape[0]
    blocks = own_ref.shape[1] // LANES
    lane = iota((8, LANES), 1)
    from_slot = iota((8, LANES), 0) * STEP + lane // GROUP
    tile_of = lane % GROUP
    for group in range(own_ref.shape[0] // GROUP):
        for block in range(blocks):
            for source, target in ((own_ref, own_s), (loc_ref, loc_s)):
                part = source[group * GROUP : (group + 1) * GROUP, block * LANES : (block + 1) * LANES]
                out = jnp.zeros((8, LANES), i32)
                for tile in range(GROUP):
                    out = jnp.where(tile_of == tile, lane_pick(part[tile : tile + 1], from_slot), out)
                start = (group * blocks + block) * 8
                target[start : start + 8, :] = out
    owner = own_s[...]
    left = (iota((LANES, 2 * LANES), 0) < iota((LANES, 2 * LANES), 1)) | (iota((LANES, 2 * LANES), 1) >= LANES)
    above = iota((rows, rows), 1) < iota((rows, rows), 0)
    hits = jnp.concatenate([jnp.where(owner == one, 1.0, 0.0).astype(bf16) for one in range(devices)], axis=0)
    sums = dot(hits, jnp.where(left, 1.0, 0.0).astype(bf16))
    totals = jnp.concatenate(
        [sums[one * rows : (one + 1) * rows, LANES:].astype(bf16) for one in range(devices)], axis=1
    )
    base = dot(jnp.where(above, 1.0, 0.0).astype(bf16), totals)
    rank = jnp.zeros((rows, LANES), f32)
    for one in range(devices):
        here = sums[one * rows : (one + 1) * rows, :LANES] + base[:, one * LANES : (one + 1) * LANES]
        rank = jnp.where(owner == one, here, rank)
    rank = rank.astype(i32)
    pos_ref[...] = owner * per_owner + rank
    rank_s[...] = rank

    owner_id = iota((devices, LANES), 0)
    rank_id = narrow(iota((per_owner, LANES), 0))
    slot_lane = iota((devices, LANES), 1).astype(f32)

    def place(index, total):
        start = pl.multiple_of(index * 8, 8)
        own_rows = own_s[pl.ds(start, 8), :]
        loc_rows = loc_s[pl.ds(start, 8), :]
        rank_rows = rank_s[pl.ds(start, 8), :]
        high_rows = (loc_rows // LANES).astype(f32)
        low_rows = (loc_rows % LANES).astype(f32)
        lhs = []
        rhs = []
        for row in range(8):
            mine = own_rows[row : row + 1] == owner_id
            number = (start + row).astype(f32)
            lhs.append(
                jnp.concatenate(
                    [
                        jnp.where(mine, high_rows[row : row + 1], 0.0),
                        jnp.where(mine, low_rows[row : row + 1], 0.0),
                        jnp.where(mine, number, 0.0),
                        jnp.where(mine, slot_lane, 0.0),
                    ],
                    axis=0,
                ).astype(bf16)
            )
            rhs.append(one_hot(rank_rows[row : row + 1], rank_id))
        return total + dot_nt(jnp.concatenate(lhs, axis=1), jnp.concatenate(rhs, axis=1))

    total = lax.fori_loop(0, rows // 8, place, jnp.zeros((4 * devices, per_owner), f32), unroll=True).astype(i32)
    want = total[:devices] * LANES + total[devices : 2 * devices]
    halves = per_owner // LANES
    if per_owner % LANES == 0 and halves > 1:
        for half in range(halves):
            want_ref[pl.ds(half, devices, stride=halves), :] = want[:, half * LANES : (half + 1) * LANES]
    else:
        want_ref[...] = want
    back_ref[...] = total[2 * devices : 3 * devices] * LANES + total[3 * devices :]


def view(angles_ref):
    angle = [jnp.full((1, LANES), angles_ref[index], f32) for index in range(3)]
    (cos_a, cos_b, cos_c) = [jnp.cos(one) for one in angle]
    (sin_a, sin_b, sin_c) = [jnp.sin(one) for one in angle]
    return [
        [cos_c * cos_b, cos_c * sin_b * sin_a - sin_c * cos_a, cos_c * sin_b * cos_a + sin_c * sin_a],
        [sin_c * cos_b, sin_c * sin_b * sin_a + cos_c * cos_a, sin_c * sin_b * cos_a - cos_c * sin_a],
        [-sin_b, cos_b * sin_a, cos_b * cos_a],
    ]


def harmonics(along_x, along_y, along_z):
    sq_x = along_x * along_x
    sq_y = along_y * along_y
    sq_z = along_z * along_z
    return [
        0.28209479177387814 + 0.0 * along_x,
        -0.4886025119029199 * along_y,
        0.4886025119029199 * along_z,
        -0.4886025119029199 * along_x,
        1.0925484305920792 * along_x * along_y,
        -1.0925484305920792 * along_y * along_z,
        0.31539156525252005 * (2.0 * sq_z - sq_x - sq_y),
        -1.0925484305920792 * along_x * along_z,
        0.5462742152960396 * (sq_x - sq_y),
        -0.5900435899266435 * along_y * (3.0 * sq_x - sq_y),
        2.890611442640554 * along_x * along_y * along_z,
        -0.4570457994644658 * along_y * (4.0 * sq_z - sq_x - sq_y),
        0.3731763325901154 * along_z * (2.0 * sq_z - 3.0 * sq_x - 3.0 * sq_y),
        -0.4570457994644658 * along_x * (4.0 * sq_z - sq_x - sq_y),
        1.445305721320277 * along_z * (sq_x - sq_y),
        -0.5900435899266435 * along_x * (sq_x - 3.0 * sq_y),
    ]


def basis_rows(basis, eighth):
    sub = iota((8, LANES), 0)
    found = []
    for colour in range(3):
        out = None
        for inner in range(8):
            index = 8 * eighth + inner - 11 - 16 * colour
            if 0 <= index < 16:
                out = jnp.zeros((8, LANES), f32) if out is None else out
                out = jnp.where(sub == inner, basis[index], out)
        found.append(out)
    return found


def shape_of(columns, rotation, camera_frame):
    focal_x, focal_y, centre_x, centre_y = camera_frame
    positions = columns[0:3]
    cam_first = rotation[0][0] * positions[0] + rotation[0][1] * positions[1] + rotation[0][2] * positions[2]
    cam_second = rotation[1][0] * positions[0] + rotation[1][1] * positions[1] + rotation[1][2] * positions[2]
    mean_x = centre_x + focal_x * cam_first
    mean_y = centre_y + focal_y * cam_second
    scales = [jnp.exp(one) for one in columns[3:6]]
    quat_w, quat_x, quat_y, quat_z = columns[6:10]
    norm_sq = jnp.maximum(quat_w * quat_w + quat_x * quat_x + quat_y * quat_y + quat_z * quat_z, 1.0)
    twice = 2.0 / norm_sq
    turned = [
        [
            1.0 - twice * (quat_y * quat_y + quat_z * quat_z),
            twice * (quat_x * quat_y - quat_w * quat_z),
            twice * (quat_x * quat_z + quat_w * quat_y),
        ],
        [
            twice * (quat_x * quat_y + quat_w * quat_z),
            1.0 - twice * (quat_x * quat_x + quat_z * quat_z),
            twice * (quat_y * quat_z - quat_w * quat_x),
        ],
        [
            twice * (quat_x * quat_z - quat_w * quat_y),
            twice * (quat_y * quat_z + quat_w * quat_x),
            1.0 - twice * (quat_x * quat_x + quat_y * quat_y),
        ],
    ]
    rows = []
    for focal, turn in ((focal_x, rotation[0]), (focal_y, rotation[1])):
        rows.append(
            [
                focal * (turn[0] * turned[0][k] + turn[1] * turned[1][k] + turn[2] * turned[2][k]) * scales[k]
                for k in range(3)
            ]
        )
    first, second = rows
    cov_a = first[0] * first[0] + first[1] * first[1] + first[2] * first[2] + 0.3
    cov_b = first[0] * second[0] + first[1] * second[1] + first[2] * second[2]
    cov_c = second[0] * second[0] + second[1] * second[1] + second[2] * second[2] + 0.3
    determinant = cov_a * cov_c - cov_b * cov_b
    opacity = 1.0 / (1.0 + jnp.exp(-columns[10]))
    return mean_x, mean_y, cov_c / determinant, -cov_b / determinant, cov_a / determinant, opacity


def spread_columns(gauss_ref, dense_s):
    rows = gauss_ref.shape[1] // LANES
    for row in range(rows):
        for eighth in range(2):
            dense_s[pl.ds(8 * eighth * rows + row, 8, stride=rows), :] = gauss_ref[
                8 * eighth : 8 * eighth + 8, row * LANES : (row + 1) * LANES
            ]


def shade_kernel(camera_frame, angles_ref, gauss_ref, parts_ref, dense_s, tint_s):
    rows = gauss_ref.shape[1] // LANES
    spread_columns(gauss_ref, dense_s)
    rotation = view(angles_ref)
    basis = harmonics(*rotation[2])
    patterns = [basis_rows(basis, eighth) for eighth in range(7)]
    for row in range(rows):
        lanes = slice(row * LANES, (row + 1) * LANES)
        tints = [None] * 3
        for eighth in range(1, 7):
            block = gauss_ref[8 * eighth : 8 * eighth + 8, lanes]
            for colour in range(3):
                pattern = patterns[eighth][colour]
                if pattern is not None:
                    term = block * pattern
                    tints[colour] = term if tints[colour] is None else tints[colour] + term
        for colour in range(3):
            tint_s[pl.ds(8 * colour * rows + row, 8, stride=rows), :] = tints[colour]
        tint_s[pl.ds(24 * rows + row, 3, stride=rows), :] = gauss_ref[56:59, lanes]
    for part in range(rows // 16):
        half = part % 2
        low = part // 2 * 16
        at = [pl.ds(index * rows + 2 * low + half, 16, stride=2) for index in range(27)]
        columns = [dense_s[one, :] for one in at[:11]]
        for index, value in enumerate(shape_of(columns, rotation, camera_frame)):
            put_parts(parts_ref, index, half, value, PARTS, rows // 2, low)
        for colour in range(3):
            total = 0.5
            for inner in range(8):
                total = total + tint_s[at[8 * colour + inner], :]
            if colour == 2:
                for inner in range(3):
                    total = total + basis[13 + inner] * tint_s[at[24 + inner], :]
            put_parts(parts_ref, 6 + colour, half, total, PARTS, rows // 2, low)


def pick_kernel(layout, parts_ref, asked_ref, out_ref):
    low_id = iota((parts_ref.shape[0] // sum(PARTS), WIDE), 0)
    high_id = narrow(iota((WIDE, WIDE), 0))
    minors = layout.minors()

    def pick_some(index, _):
        slots = jnp.concatenate([asked_ref[pl.ds(2 * index + one, 1), :] for one in range(2)], axis=1)

        def put(channel, value):
            for one in range(2):
                at = layout.row(channel, (2 * index + one) // minors, (2 * index + one) % minors)
                out_ref[pl.ds(at, 1), :] = value[:, one * LANES : (one + 1) * LANES]

        pick_slots(parts_ref[...], slots, low_id, high_id, put)
        return 0

    lax.fori_loop(0, layout.count // 2, pick_some, 0, unroll=True)


def render_kernel(
    layout,
    count_ref,
    order_ref,
    rows_ref,
    pos_ref,
    back_ref,
    cot_ref,
    image_ref,
    out_ref,
    in_s,
    out_s,
    raw_s,
    coef_s,
    cot_s,
    rhs_s,
    tint_s,
    alpha_s,
    shade_s,
    weight_s,
    sums_s,
):
    slot_rows = pos_ref.shape[0]
    groups = cot_ref.shape[1] // (GROUP * PIX)
    chunks = slot_rows // groups
    sub = iota((8, LANES), 0)
    lane = iota((8, LANES), 1)
    tile_of = lane % GROUP
    blocks = slot_rows // 8
    middles = []
    for group in range(groups):
        middle_x = jnp.zeros((8, LANES), f32)
        middle_y = jnp.zeros((8, LANES), f32)
        live = jnp.zeros((8, LANES), i32)
        for tile in range(GROUP):
            shown = order_ref[group * GROUP + tile]
            here = tile_of == tile
            middle_x = jnp.where(here, (shown % TX * 16 + 8).astype(f32), middle_x)
            middle_y = jnp.where(here, (shown // TX * 16 + 8).astype(f32), middle_y)
            live = jnp.where(here, count_ref[group * GROUP + tile], live)
        middles.append((middle_x, middle_y, live))

    for half in range(2):
        for channel in range(PROJ):
            put_parts(in_s, channel, half, layout.half(rows_ref, channel, half), PARTS)
    low_id = iota((slot_rows // 2, WIDE), 0)
    high_id = narrow(iota((WIDE, WIDE), 0))

    def pick_in(index, _):
        slots = jnp.concatenate([pos_ref[pl.ds(2 * index + one, 1), :] for one in range(2)], axis=1)

        def put(channel, value):
            for one in range(2):
                raw_s[pl.ds(channel * slot_rows + 2 * index + one, 1), :] = value[:, one * LANES : (one + 1) * LANES]

        pick_slots(in_s[...], slots, low_id, high_id, put)
        return 0

    lax.fori_loop(0, slot_rows // 2, pick_in, 0, unroll=True)
    for block in range(blocks):
        group = block * 8 // chunks
        middle_x, middle_y, live = middles[group]
        found = [
            raw_s[channel * slot_rows + 8 * block : channel * slot_rows + 8 * block + 8, :] for channel in range(PROJ)
        ]
        at_x = found[0] - middle_x
        at_y = found[1] - middle_y
        quad_a = -0.5 * found[2]
        quad_b = -found[3]
        quad_c = -0.5 * found[4]
        flat = quad_a * at_x * at_x + quad_c * at_y * at_y + quad_b * at_x * at_y + jnp.log(found[5])
        place = (8 * block - group * chunks + sub) * STEP + lane // GROUP
        terms = (
            quad_a * LOG2E,
            quad_b * LOG2E,
            quad_c * LOG2E,
            (-2.0 * quad_a * at_x - quad_b * at_y) * LOG2E,
            (-2.0 * quad_c * at_y - quad_b * at_x) * LOG2E,
            jnp.where(place < live, flat * LOG2E, -1e30),
        )
        for index, term in enumerate(terms):
            for part, value in enumerate(split_three(term)):
                coef_s[pl.ds(8 * block * 24 + 6 * part + index, 8, stride=24), :] = value
        for colour in range(3):
            for part, value in enumerate(split_two(found[6 + colour])):
                coef_s[pl.ds(8 * block * 24 + 18 + 3 * part + colour, 8, stride=24), :] = value

    pixel = iota((24, PIX), 1)
    row = iota((24, PIX), 0)
    pix_x = (pixel % 16).astype(f32) - 7.5
    pix_y = (pixel // 16).astype(f32) - 7.5
    kind = row % 6
    monomials = jnp.where(kind == 0, pix_x * pix_x, jnp.where(kind == 1, pix_x * pix_y, 1.0))
    monomials = jnp.where(kind == 2, pix_y * pix_y, monomials)
    monomials = jnp.where(kind == 3, pix_x, jnp.where(kind == 4, pix_y, monomials))
    moments = jnp.where(iota((8, PIX), 0) < 6, monomials[0:8], 0.0).astype(bf16)
    monomials = jnp.where(row < 18, monomials, 0.0)
    nothing = jnp.zeros((24, PIX), f32)
    for group in range(groups):
        for colour in range(3):
            for tile in range(GROUP):
                start = (group * GROUP + tile) * PIX
                cot_s[group * 24 + colour * GROUP + tile, :] = cot_ref[colour, start : start + PIX]
    cots = []
    spare = jnp.zeros((8, PIX), f32)
    for group in range(groups):
        first, second = split_two(cot_s[group * 24 : (group + 1) * 24, :])
        cots.append(jnp.concatenate([first, spare, second, spare], axis=0).astype(bf16))
        rhs_s[group] = jnp.concatenate(
            [
                jnp.concatenate([jnp.concatenate([nothing, monomials[8 * one : 8 * one + 8]], axis=0) for one in range(3)], axis=0),
                jnp.concatenate([first, spare, first, spare, second, spare], axis=0),
            ],
            axis=1,
        ).astype(bf16)

    own_tile = sub == tile_of
    own_pair = iota((8, WIDE), 0) == iota((8, WIDE), 1) % GROUP

    def evaluate(index):
        for group in range(groups):
            chunk = group * chunks + index
            coefs = coef_s[chunk * 24 : (chunk + 1) * 24, :]
            tints = [jnp.where(own_tile, coefs[18 + one : 19 + one], 0.0) for one in range(6)]
            lhs = jnp.concatenate(
                tints[:3] + [coefs[0:8]] + tints[3:] + [coefs[8:16]] + tints[:3] + [coefs[16:24]], axis=0
            ).astype(bf16)
            both = dot_tn(lhs, rhs_s[group])
            lanes = slice(chunk * LANES, (chunk + 1) * LANES)
            tint_s[:, lanes] = lhs[0:64]
            alpha_s[lanes, :] = jnp.exp2(both[:, :PIX])
            shade_s[lanes, :] = both[:, PIX:]

    def scan(index, trans):
        out = []
        for group in range(groups):
            one = trans[group]
            start = (group * chunks + index) * LANES
            for step in range(STEP):
                alpha = alpha_s[pl.ds(start + step * GROUP, GROUP), :]
                weight = one * alpha
                one = one - weight
                weight_s[pl.ds(start + step * GROUP, GROUP), :] = weight
            out.append(one)
        return tuple(out)

    def paint(index, images):
        out = []
        for group in range(groups):
            chunk = group * chunks + index
            both = slice(chunk * LANES, chunk * LANES + WIDE)
            first, second = split_two(weight_s[both, :])
            first = first.astype(bf16)
            second = second.astype(bf16)
            tints = tint_s[:, both]
            by_first = dot(tints, first)
            out.append(images[group] + by_first[0:24] + by_first[32:56] + dot(tints[0:32], second)[0:24])
            by_first = dot_nt(cots[group], first)
            tint_grad = by_first[0:24] + by_first[32:56] + dot_nt(cots[group][0:32], second)[0:24]
            for colour in range(3):
                own = jnp.where(own_pair, tint_grad[colour * GROUP : (colour + 1) * GROUP], 0.0)
                own = jnp.sum(own, axis=0, keepdims=True)
                for one in range(2):
                    sums_s[(chunk + one) * 16 + 8 + colour : (chunk + one) * 16 + 9 + colour, :] = own[:, one * LANES : (one + 1) * LANES]
        return tuple(out)

    trans = tuple(jnp.ones((GROUP, PIX), f32) for _ in range(groups))
    images = tuple(jnp.zeros((24, PIX), f32) for _ in range(groups))
    for pair in range(-AHEAD, chunks // 2 + 1):
        for one in range(2):
            if pair + AHEAD < chunks // 2:
                evaluate(2 * (pair + AHEAD) + one)
        for one in range(2):
            if 0 <= pair < chunks // 2:
                trans = scan(2 * pair + one, trans)
        if pair > 0:
            images = paint(2 * (pair - 1), images)
    for group in range(groups):
        for colour in range(3):
            for tile in range(GROUP):
                at = (group * GROUP + tile) * PIX
                image_ref[colour, at : at + PIX] = images[group][colour * GROUP + tile]

    def moment(index):
        for group in range(groups):
            chunk = group * chunks + index
            first, second = split_two(shade_s[slice(chunk * LANES, chunk * LANES + WIDE), :])
            found = dot_nt(moments, first.astype(bf16)) + dot_nt(moments, second.astype(bf16))
            for one in range(2):
                start = (chunk + one) * 16
                sums_s[start : start + 8, :] = found[:, one * LANES : (one + 1) * LANES]

    def rescan(index, behinds):
        out = []
        for group in range(groups):
            behind = behinds[group]
            start = (group * chunks + index) * LANES
            for step in reversed(range(STEP)):
                at = pl.ds(start + step * GROUP, GROUP)
                ahead = shade_s[at, :] - behind
                shade_s[at, :] = weight_s[at, :] * ahead
                behind = behind + alpha_s[at, :] * ahead
            out.append(behind)
        return tuple(out)

    behinds = tuple(jnp.zeros((GROUP, PIX), f32) for _ in range(groups))
    for pair in reversed(range(-1, chunks // 2)):
        for one in reversed(range(2)):
            if pair >= 0:
                behinds = rescan(2 * pair + one, behinds)
        if pair + 1 < chunks // 2:
            moment(2 * (pair + 1))

    slot_s = coef_s
    for block in range(blocks):
        middle_x, middle_y, _ = middles[block * 8 // chunks]
        at = slice(8 * block, 8 * block + 8)
        raw = [raw_s[channel * slot_rows + 8 * block : channel * slot_rows + 8 * block + 8, :] for channel in range(6)]
        (sum_xx, sum_xy, sum_yy, sum_x, sum_y, sum_one) = [
            sums_s[pl.ds(8 * block * 16 + index, 8, stride=16), :] for index in range(6)
        ]
        at_x = raw[0] - middle_x
        at_y = raw[1] - middle_y
        off_x = sum_x - at_x * sum_one
        off_y = sum_y - at_y * sum_one
        grads = [
            raw[2] * off_x + raw[3] * off_y,
            raw[4] * off_y + raw[3] * off_x,
            -0.5 * (sum_xx - at_x * (sum_x + off_x)),
            -(sum_xy - at_y * sum_x - at_x * off_y),
            -0.5 * (sum_yy - at_y * (sum_y + off_y)),
            sum_one / raw[5],
        ] + [sums_s[pl.ds(8 * block * 16 + 8 + colour, 8, stride=16), :] for colour in range(3)]
        for channel, value in enumerate(grads):
            slot_s[channel * slot_rows + 8 * block : channel * slot_rows + 8 * block + 8, :] = value

    for half in range(2):
        for channel in range(PROJ):
            value = slot_s[pl.ds(channel * slot_rows + half, slot_rows // 2, stride=2), :]
            put_parts(out_s, channel, half, value, (2,) * PROJ)
    minors = layout.minors()

    def pick_out(index, _):
        if layout.halves == 2:
            slots = back_ref[pl.ds(index, 1), :]
        else:
            slots = jnp.concatenate([back_ref[pl.ds(2 * index + one, 1), :] for one in range(2)], axis=1)

        def put(channel, value):
            for one in range(2):
                at = layout.row(channel, (2 * index + one) // minors, (2 * index + one) % minors)
                out_ref[pl.ds(at, 1), :] = value[:, one * LANES : (one + 1) * LANES]

        pick_slots(out_s[...], slots, low_id, high_id, put)
        return 0

    lax.fori_loop(0, layout.count // 2, pick_out, 0, unroll=True)


def collect_kernel(
    layout, camera_frame, angles_ref, dense_ref, asked_ref, terms_ref, grad_hbm, lhs_s, rhs_s, total_s, out_s, grad_ref, sems
):
    gauss = grad_ref.shape[1]
    rows = gauss // LANES
    lows = gauss // WIDE
    low_id = narrow(iota((lows, LANES), 0))
    high_id = narrow(iota((WIDE, LANES), 0))
    minors = layout.minors()

    for index in range(layout.count // 8):
        asked = asked_ref[8 * index : 8 * index + 8, :]
        low = asked // WIDE
        high = asked % WIDE
        for row in range(8):
            lanes = slice((8 * index + row) * LANES, (8 * index + row + 1) * LANES)
            mine = one_hot(low[row : row + 1], low_id)
            rhs_s[:, lanes] = one_hot(high[row : row + 1], high_id)
            for channel in range(PROJ):
                at = layout.row(channel, (8 * index + row) // minors, row % minors)
                for part, value in enumerate(split_two(terms_ref[at : at + 1, :])):
                    first = (part * PROJ + channel) * lows
                    lhs_s[first : first + lows, lanes] = mine * value.astype(bf16)
        lanes = slice(8 * index * LANES, 8 * (index + 1) * LANES)
        found = dot_nt(lhs_s[:, lanes], rhs_s[:, lanes])
        total_s[...] = found if index == 0 else total_s[...] + found
    rotation = view(angles_ref)
    basis = harmonics(*rotation[2])
    for part in range(rows // 8):
        half = part % 2
        low = part // 2 * 8
        lanes = slice(half * LANES, (half + 1) * LANES)
        sums = [
            total_s[channel * lows + low : channel * lows + low + 8, lanes]
            + total_s[(PROJ + channel) * lows + low : (PROJ + channel) * lows + low + 8, lanes]
            for channel in range(PROJ)
        ]
        columns = tuple(dense_ref[pl.ds(index * rows + 2 * low + half, 8, stride=2), :] for index in range(11))
        _, pullback = jax.vjp(lambda *values: shape_of(values, rotation, camera_frame), *columns)
        grads = pullback(tuple(sums[:6]))
        for index, value in enumerate(tuple(grads) + tuple(sums[6:])):
            out_s[pl.ds(index * rows + 2 * low + half, 8, stride=2), :] = value
    sub = iota((8, LANES), 0)
    patterns = [basis_rows(basis, eighth) for eighth in range(8)]
    copies = []
    pieces = sems.shape[0]
    wide = gauss // pieces
    for row in range(rows):
        lanes = slice(row * LANES, (row + 1) * LANES)
        grad_ref[0:8, lanes] = out_s[pl.ds(row, 8, stride=rows), :]
        tints = [out_s[(11 + colour) * rows + row : (11 + colour) * rows + row + 1, :] for colour in range(3)]
        for eighth in range(1, 8):
            value = None
            for colour in range(3):
                pattern = patterns[eighth][colour]
                if pattern is not None:
                    term = pattern * tints[colour]
                    value = term if value is None else value + term
            if eighth == 1:
                value = jnp.where(sub < 3, out_s[pl.ds(8 * rows + row, 8, stride=rows), :], value)
            if eighth == 7:
                grad_ref[56:59, lanes] = value[0:3]
            else:
                grad_ref[8 * eighth : 8 * eighth + 8, lanes] = value
        if (row + 1) * LANES % wide == 0:
            piece = len(copies)
            span = slice(piece * wide, (piece + 1) * wide)
            copies.append(pltpu.make_async_copy(grad_ref.at[:, span], grad_hbm.at[:, span], sems.at[piece]))
            copies[-1].start()
    for copy in copies:
        copy.wait()


VMEM = pl.BlockSpec(memory_space=pltpu.VMEM)
HBM = pl.BlockSpec(memory_space=pltpu.HBM)
SMEM = pl.BlockSpec(memory_space=pltpu.SMEM)


def call(kernel, specs, outs, scratch, flops, name, out_spec=VMEM, vmem=VMEM_BYTES):
    return pl.pallas_call(
        kernel,
        in_specs=specs,
        out_specs=[out_spec] * len(outs),
        out_shape=[jax.ShapeDtypeStruct(shape, dtype) for shape, dtype in outs],
        scratch_shapes=[pltpu.VMEM(*one) if isinstance(one, tuple) else one for one in scratch],
        compiler_params=pltpu.CompilerParams(vmem_limit_bytes=vmem),
        cost_estimate=pl.CostEstimate(flops=flops, bytes_accessed=4 << 20, transcendentals=0),
        name=name,
    )


def route(devices, owners, locals_):
    slots = owners.size
    per_owner = slots // devices
    rows = slots // LANES
    halves = per_owner // LANES if per_owner % LANES == 0 else 0
    asked = (devices * halves, LANES) if halves else (devices, per_owner)
    return call(
        partial(route_kernel, devices, per_owner),
        [HBM, HBM],
        [(asked, i32), ((devices, per_owner), i32), ((rows, LANES), i32)],
        [(owners.shape, i32)] * 2 + [((rows, LANES), i32)] * 3 + [pltpu.SemaphoreType.DMA((2,))],
        1 << 30,
        "route",
        vmem=63 << 20,
    )(owners, locals_)


def shade(camera_frame, view_angles, gaussians):
    rows = gaussians.shape[1] // LANES
    return call(
        partial(shade_kernel, camera_frame),
        [SMEM, VMEM],
        [((sum(PARTS) * rows // 2, WIDE), bf16), ((16 * rows, LANES), f32)],
        [((27 * rows, LANES), f32)],
        1 << 30,
        "shade",
    )(view_angles, gaussians)


def pick(layout, table, asked):
    return call(
        partial(pick_kernel, layout),
        [VMEM, VMEM],
        [((PROJ * layout.count, LANES), f32)],
        [],
        1 << 30,
        "pick",
    )(table, asked)[0]


def render(layout, list_counts, tile_order, rows, pos, back, cotangent):
    slot_rows = pos.shape[0]
    groups = tile_order.shape[0] // GROUP
    slots = slot_rows * LANES
    return call(
        partial(render_kernel, layout),
        [SMEM, SMEM, VMEM, VMEM, VMEM, VMEM],
        [(cotangent.shape, f32), ((PROJ * layout.count, LANES), f32)],
        [
            ((sum(PARTS) * slot_rows // 2, WIDE), bf16),
            ((2 * PROJ * slot_rows // 2, WIDE), bf16),
            ((PROJ * slot_rows, LANES), f32),
            ((24 * slot_rows, LANES), f32),
            ((24 * groups, PIX), f32),
            ((groups, 96, 2 * PIX), bf16),
            ((64, slots), bf16),
            ((slots, PIX), f32),
            ((slots, PIX), f32),
            ((slots, PIX), f32),
            ((16 * slot_rows, LANES), f32),
        ],
        1 << 34,
        "render",
    )(list_counts, tile_order, rows, pos, back, cotangent)


def collect(layout, camera_frame, view_angles, shape, dense, asked, terms):
    rows = shape[1] // LANES
    lows = shape[1] // WIDE
    return call(
        partial(collect_kernel, layout, camera_frame),
        [SMEM, VMEM, VMEM, VMEM],
        [(shape, f32)],
        [
            ((2 * PROJ * lows, layout.count * LANES), bf16),
            ((WIDE, layout.count * LANES), bf16),
            ((2 * PROJ * lows, WIDE), f32),
            ((16 * rows, LANES), f32),
            (shape, f32),
            pltpu.SemaphoreType.DMA((8,)),
        ],
        1 << 32,
        "collect",
        out_spec=HBM,
    )(view_angles, dense, asked, terms)[0]


def swap_rows(layout, devices, rows):
    if layout.halves:
        apart = rows.reshape(devices * PROJ, layout.halves, LANES)
        return lax.all_to_all(apart, "dev", split_axis=0, concat_axis=0, tiled=True).reshape(rows.shape)
    apart = rows.reshape(PROJ, devices, layout.count * LANES // devices)
    return lax.all_to_all(apart, "dev", split_axis=1, concat_axis=1, tiled=True).reshape(rows.shape)


def shards(gaussians, view_angles, tile_order, tile_owners, tile_locals, list_counts, image_cotangent):
    devices = lax.axis_size("dev")
    tiles_y = devices * tile_order.shape[0] // TX
    camera_frame = (4.0 * TX, 4.0 * tiles_y, 8.0 * TX, 8.0 * tiles_y)
    layout = Rows(devices, tile_owners.size // devices)
    want, back, pos = route(devices, tile_owners, tile_locals)
    asked = lax.all_to_all(want, "dev", split_axis=0, concat_axis=0, tiled=True)
    table, dense = shade(camera_frame, view_angles, gaussians)
    if not layout.halves:
        asked = asked.reshape(layout.count, LANES)
    if layout.halves != 2:
        back = back.reshape(layout.count, LANES)
    arrived = swap_rows(layout, devices, pick(layout, table, asked))
    rendered, slot_grads = render(layout, list_counts, tile_order, arrived, pos, back, image_cotangent)
    terms = swap_rows(layout, devices, slot_grads)
    gradients = collect(layout, camera_frame, view_angles, gaussians.shape, dense, asked, terms)
    return (rendered, gradients)


def solution(mesh):
    return jax.shard_map(
        shards,
        mesh=mesh,
        in_specs=(
            P(None, "dev"),
            P(),
            P("dev"),
            P("dev", None),
            P("dev", None),
            P("dev"),
            P(None, "dev"),
        ),
        out_specs=(P(None, "dev"), P(None, "dev")),
        check_vma=False,
    )
```

```python
from functools import partial

import jax
import jax.numpy as jnp
from jax import lax
from jax.experimental import pallas as pl
from jax.experimental.pallas import tpu as pltpu
from jax.sharding import PartitionSpec as P

PIX = 256
TX = 32
LANES = 128
PROJ = 9
GROUP = 8
WIDE = 2 * LANES
PARTS = (3, 3, 3, 3, 3, 2, 2, 2, 2)
STEP = LANES // GROUP
LOG2E = 1.4426950408889634
AHEAD = 2
VMEM_BYTES = 52 * 1024 * 1024

f32 = jnp.float32
bf16 = jnp.bfloat16
i32 = jnp.int32


def iota(shape, dim):
    return lax.broadcasted_iota(i32, shape, dim)


def lane_pick(row, lanes):
    source = jnp.broadcast_to(row, lanes.shape)
    return jnp.take_along_axis(source, lanes, axis=1, mode="promise_in_bounds")


def split_two(values):
    first = values.astype(bf16).astype(f32)
    return first, values - first


def split_three(values):
    first, rest = split_two(values)
    second, third = split_two(rest)
    return first, second, third


def dot(lhs, rhs):
    return lax.dot_general(lhs, rhs, (((1,), (0,)), ((), ())), preferred_element_type=f32)


def dot_nt(lhs, rhs):
    return lax.dot_general(lhs, rhs, (((1,), (1,)), ((), ())), preferred_element_type=f32)


def dot_tn(lhs, rhs):
    return lax.dot_general(lhs, rhs, (((0,), (0,)), ((), ())), preferred_element_type=f32)


class Rows:
    def __init__(self, devices, per_owner):
        self.halves = per_owner // LANES if per_owner % LANES == 0 else 0
        self.count = devices * per_owner // LANES

    def row(self, channel, major, minor):
        halves = self.halves
        if halves == 0:
            return channel * self.count + major
        return major * (PROJ * halves) + channel * halves + minor

    def half(self, channel, half):
        if self.halves == 0:
            return pl.ds(channel * self.count + half, self.count // 2, stride=2)
        assert self.halves <= 2
        return pl.ds(self.row(channel, half // self.halves, half % self.halves), self.count // 2, stride=2 * PROJ)

    def minors(self):
        return max(self.halves, 1)


def narrow(ids):
    return ids.astype(f32).astype(bf16)


def one_hot(ids, every):
    return jnp.where(narrow(ids) == every, jnp.ones((), bf16), jnp.zeros((), bf16))


def put_terms(lhs_s, channel, lanes, row, mine):
    lows = mine.shape[0]
    row = jnp.broadcast_to(row, (16, LANES))
    first = row.astype(bf16)
    second = (row - first.astype(f32)).astype(bf16)
    for part, value in enumerate((first, second)):
        for low in range(0, lows, 16):
            start = (part * PROJ + channel) * lows + low
            lhs_s[start : start + 16, lanes] = mine[low : low + 16] * value


def pick_slots(parts, hot, slots, low_id, put):
    found = dot(parts, hot)
    mine = slots // WIDE == low_id
    lows = low_id.shape[0]
    first = 0
    for channel, count in enumerate(PARTS):
        value = found[first * lows : (first + 1) * lows]
        for part in range(1, count):
            value = value + found[(first + part) * lows : (first + part + 1) * lows]
        first += count
        put(channel, jnp.sum(jnp.where(mine, value, 0.0), axis=0, keepdims=True))


def put_parts(parts_ref, channel, half, value, counts, lows=None, low=0):
    lows = lows or value.shape[0]
    first = sum(counts[:channel])
    parts = split_three(value) if counts[channel] == 3 else split_two(value)
    for part, one in enumerate(parts):
        at = (first + part) * lows + low
        parts_ref[at : at + value.shape[0], half * LANES : (half + 1) * LANES] = one.astype(bf16)


def route_kernel(devices, per_owner, own_hbm, loc_hbm, want_ref, pos_ref, own_ref, loc_ref, sems):
    copies = [pltpu.make_async_copy(own_hbm, own_ref, sems.at[0]), pltpu.make_async_copy(loc_hbm, loc_ref, sems.at[1])]
    for copy in copies:
        copy.start()
    for copy in copies:
        copy.wait()
    tiles = own_ref.shape[0]
    blocks = own_ref.shape[1] // LANES
    rows = tiles * blocks
    owner = jnp.concatenate([own_ref[:, block * LANES : (block + 1) * LANES] for block in range(blocks)], axis=0)
    local = jnp.concatenate([loc_ref[:, block * LANES : (block + 1) * LANES] for block in range(blocks)], axis=0)
    left = (iota((LANES, 2 * LANES), 0) < iota((LANES, 2 * LANES), 1)) | (iota((LANES, 2 * LANES), 1) >= LANES)
    above = iota((rows, rows), 1) < iota((rows, rows), 0)
    hits = jnp.concatenate([jnp.where(owner == one, 1.0, 0.0).astype(bf16) for one in range(devices)], axis=0)
    sums = dot(hits, jnp.where(left, 1.0, 0.0).astype(bf16))
    totals = jnp.concatenate(
        [sums[one * rows : (one + 1) * rows, LANES:].astype(bf16) for one in range(devices)], axis=1
    )
    base = dot(jnp.where(above, 1.0, 0.0).astype(bf16), totals)
    rank = jnp.zeros((rows, LANES), f32)
    for one in range(devices):
        here = sums[one * rows : (one + 1) * rows, :LANES] + base[:, one * LANES : (one + 1) * LANES]
        rank = jnp.where(owner == one, here, rank)
    rank = rank.astype(i32)
    place = owner * per_owner + rank

    owner_id = iota((devices, LANES), 0)
    rank_id = narrow(iota((per_owner, LANES), 0))
    high = (local // LANES).astype(f32)
    low = (local % LANES).astype(f32)
    total = jnp.zeros((2 * devices, per_owner), f32)
    for start in range(0, rows, 8):
        lhs = []
        rhs = []
        for row in range(start, start + 8):
            mine = owner[row : row + 1] == owner_id
            lhs.append(
                jnp.concatenate(
                    [jnp.where(mine, high[row : row + 1], 0.0), jnp.where(mine, low[row : row + 1], 0.0)], axis=0
                ).astype(bf16)
            )
            rhs.append(one_hot(rank[row : row + 1], rank_id))
        total = total + dot_nt(jnp.concatenate(lhs, axis=1), jnp.concatenate(rhs, axis=1))
    total = total.astype(i32)
    want = total[:devices] * LANES + total[devices:]
    halves = per_owner // LANES
    if per_owner % LANES == 0 and halves > 1:
        for half in range(halves):
            want_ref[pl.ds(half, devices, stride=halves), :] = want[:, half * LANES : (half + 1) * LANES]
    else:
        want_ref[...] = want

    lane = iota((8, LANES), 1)
    from_slot = iota((8, LANES), 0) * STEP + lane // GROUP
    tile_of = lane % GROUP
    for group in range(tiles // GROUP):
        for block in range(blocks):
            part = place[block * tiles + group * GROUP : block * tiles + (group + 1) * GROUP]
            out = jnp.zeros((8, LANES), i32)
            for tile in range(GROUP):
                out = jnp.where(tile_of == tile, lane_pick(part[tile : tile + 1], from_slot), out)
            start = (group * blocks + block) * 8
            pos_ref[start : start + 8, :] = out


def view(angles_ref):
    angle = [jnp.full((1, LANES), angles_ref[index], f32) for index in range(3)]
    (cos_a, cos_b, cos_c) = [jnp.cos(one) for one in angle]
    (sin_a, sin_b, sin_c) = [jnp.sin(one) for one in angle]
    return [
        [cos_c * cos_b, cos_c * sin_b * sin_a - sin_c * cos_a, cos_c * sin_b * cos_a + sin_c * sin_a],
        [sin_c * cos_b, sin_c * sin_b * sin_a + cos_c * cos_a, sin_c * sin_b * cos_a - cos_c * sin_a],
        [-sin_b, cos_b * sin_a, cos_b * cos_a],
    ]


def harmonics(along_x, along_y, along_z):
    sq_x = along_x * along_x
    sq_y = along_y * along_y
    sq_z = along_z * along_z
    return [
        0.28209479177387814 + 0.0 * along_x,
        -0.4886025119029199 * along_y,
        0.4886025119029199 * along_z,
        -0.4886025119029199 * along_x,
        1.0925484305920792 * along_x * along_y,
        -1.0925484305920792 * along_y * along_z,
        0.31539156525252005 * (2.0 * sq_z - sq_x - sq_y),
        -1.0925484305920792 * along_x * along_z,
        0.5462742152960396 * (sq_x - sq_y),
        -0.5900435899266435 * along_y * (3.0 * sq_x - sq_y),
        2.890611442640554 * along_x * along_y * along_z,
        -0.4570457994644658 * along_y * (4.0 * sq_z - sq_x - sq_y),
        0.3731763325901154 * along_z * (2.0 * sq_z - 3.0 * sq_x - 3.0 * sq_y),
        -0.4570457994644658 * along_x * (4.0 * sq_z - sq_x - sq_y),
        1.445305721320277 * along_z * (sq_x - sq_y),
        -0.5900435899266435 * along_x * (sq_x - 3.0 * sq_y),
    ]


def basis_rows(basis, eighth):
    sub = iota((8, LANES), 0)
    found = []
    for colour in range(3):
        out = None
        for inner in range(8):
            index = 8 * eighth + inner - 11 - 16 * colour
            if 0 <= index < 16:
                out = jnp.zeros((8, LANES), f32) if out is None else out
                out = jnp.where(sub == inner, basis[index], out)
        found.append(out)
    return found


def shape_of(columns, rotation, camera_frame):
    focal_x, focal_y, centre_x, centre_y = camera_frame
    positions = columns[0:3]
    cam_first = rotation[0][0] * positions[0] + rotation[0][1] * positions[1] + rotation[0][2] * positions[2]
    cam_second = rotation[1][0] * positions[0] + rotation[1][1] * positions[1] + rotation[1][2] * positions[2]
    mean_x = centre_x + focal_x * cam_first
    mean_y = centre_y + focal_y * cam_second
    scales = [jnp.exp(one) for one in columns[3:6]]
    quat_w, quat_x, quat_y, quat_z = columns[6:10]
    norm_sq = jnp.maximum(quat_w * quat_w + quat_x * quat_x + quat_y * quat_y + quat_z * quat_z, 1.0)
    twice = 2.0 / norm_sq
    turned = [
        [
            1.0 - twice * (quat_y * quat_y + quat_z * quat_z),
            twice * (quat_x * quat_y - quat_w * quat_z),
            twice * (quat_x * quat_z + quat_w * quat_y),
        ],
        [
            twice * (quat_x * quat_y + quat_w * quat_z),
            1.0 - twice * (quat_x * quat_x + quat_z * quat_z),
            twice * (quat_y * quat_z - quat_w * quat_x),
        ],
        [
            twice * (quat_x * quat_z - quat_w * quat_y),
            twice * (quat_y * quat_z + quat_w * quat_x),
            1.0 - twice * (quat_x * quat_x + quat_y * quat_y),
        ],
    ]
    rows = []
    for focal, turn in ((focal_x, rotation[0]), (focal_y, rotation[1])):
        rows.append(
            [
                focal * (turn[0] * turned[0][k] + turn[1] * turned[1][k] + turn[2] * turned[2][k]) * scales[k]
                for k in range(3)
            ]
        )
    first, second = rows
    cov_a = first[0] * first[0] + first[1] * first[1] + first[2] * first[2] + 0.3
    cov_b = first[0] * second[0] + first[1] * second[1] + first[2] * second[2]
    cov_c = second[0] * second[0] + second[1] * second[1] + second[2] * second[2] + 0.3
    determinant = cov_a * cov_c - cov_b * cov_b
    opacity = 1.0 / (1.0 + jnp.exp(-columns[10]))
    return mean_x, mean_y, cov_c / determinant, -cov_b / determinant, cov_a / determinant, opacity


def spread_columns(gauss_ref, dense_s):
    rows = gauss_ref.shape[1] // LANES
    for row in range(rows):
        for eighth in range(2):
            dense_s[pl.ds(8 * eighth * rows + row, 8, stride=rows), :] = gauss_ref[
                8 * eighth : 8 * eighth + 8, row * LANES : (row + 1) * LANES
            ]


def shade_kernel(camera_frame, angles_ref, gauss_ref, parts_ref, dense_s, tint_s):
    rows = gauss_ref.shape[1] // LANES
    spread_columns(gauss_ref, dense_s)
    rotation = view(angles_ref)
    basis = harmonics(*rotation[2])
    patterns = [basis_rows(basis, eighth) for eighth in range(7)]
    for row in range(rows):
        lanes = slice(row * LANES, (row + 1) * LANES)
        tints = [None] * 3
        for eighth in range(1, 7):
            block = gauss_ref[8 * eighth : 8 * eighth + 8, lanes]
            for colour in range(3):
                pattern = patterns[eighth][colour]
                if pattern is not None:
                    term = block * pattern
                    tints[colour] = term if tints[colour] is None else tints[colour] + term
        for colour in range(3):
            tint_s[pl.ds(8 * colour * rows + row, 8, stride=rows), :] = tints[colour]
        tint_s[pl.ds(24 * rows + row, 3, stride=rows), :] = gauss_ref[56:59, lanes]
    for part in range(rows // 16):
        half = part % 2
        low = part // 2 * 16
        at = [pl.ds(index * rows + 2 * low + half, 16, stride=2) for index in range(27)]
        columns = [dense_s[one, :] for one in at[:11]]
        for index, value in enumerate(shape_of(columns, rotation, camera_frame)):
            put_parts(parts_ref, index, half, value, PARTS, rows // 2, low)
        for colour in range(3):
            total = 0.5
            for inner in range(8):
                total = total + tint_s[at[8 * colour + inner], :]
            if colour == 2:
                for inner in range(3):
                    total = total + basis[13 + inner] * tint_s[at[24 + inner], :]
            put_parts(parts_ref, 6 + colour, half, total, PARTS, rows // 2, low)


def pick_kernel(layout, parts_ref, asked_ref, out_ref):
    low_id = iota((parts_ref.shape[0] // sum(PARTS), WIDE), 0)
    high_id = narrow(iota((WIDE, WIDE), 0))
    minors = layout.minors()

    for index in range(layout.count // 2):
        slots = jnp.concatenate([asked_ref[2 * index + one : 2 * index + one + 1, :] for one in range(2)], axis=1)

        def put(channel, value):
            for one in range(2):
                at = layout.row(channel, (2 * index + one) // minors, (2 * index + one) % minors)
                out_ref[at : at + 1, :] = value[:, one * LANES : (one + 1) * LANES]

        pick_slots(parts_ref[...], one_hot(slots % WIDE, high_id), slots, low_id, put)


def render_kernel(
    layout,
    count_ref,
    order_ref,
    rows_ref,
    pos_ref,
    cot_ref,
    image_ref,
    out_ref,
    in_s,
    hot_s,
    lhs_s,
    total_s,
    raw_s,
    coef_s,
    cot_s,
    rhs_s,
    tint_s,
    alpha_s,
    shade_s,
    weight_s,
    sums_s,
):
    slot_rows = pos_ref.shape[0]
    groups = cot_ref.shape[1] // (GROUP * PIX)
    chunks = slot_rows // groups
    sub = iota((8, LANES), 0)
    lane = iota((8, LANES), 1)
    tile_of = lane % GROUP
    blocks = slot_rows // 8
    middles = []
    for group in range(groups):
        middle_x = jnp.zeros((8, LANES), f32)
        middle_y = jnp.zeros((8, LANES), f32)
        live = jnp.zeros((8, LANES), i32)
        for tile in range(GROUP):
            shown = order_ref[group * GROUP + tile]
            here = tile_of == tile
            middle_x = jnp.where(here, (shown % TX * 16 + 8).astype(f32), middle_x)
            middle_y = jnp.where(here, (shown // TX * 16 + 8).astype(f32), middle_y)
            live = jnp.where(here, count_ref[group * GROUP + tile], live)
        middles.append((middle_x, middle_y, live))

    for half in range(2):
        for channel in range(PROJ):
            put_parts(in_s, channel, half, rows_ref[layout.half(channel, half), :], PARTS)
    low_id = iota((slot_rows // 2, WIDE), 0)
    high_id = narrow(iota((WIDE, WIDE), 0))

    def pick_in(row):
        slots = jnp.concatenate([pos_ref[row + one : row + one + 1, :] for one in range(2)], axis=1)
        hot = one_hot(slots % WIDE, high_id)
        hot_s[:, row * LANES : (row + 2) * LANES] = hot

        def put(channel, value):
            for one in range(2):
                at = channel * slot_rows + row + one
                raw_s[at : at + 1, :] = value[:, one * LANES : (one + 1) * LANES]

        pick_slots(in_s[...], hot, slots, low_id, put)

    def quadratics(block):
        group = block * 8 // chunks
        middle_x, middle_y, live = middles[group]
        found = [
            raw_s[channel * slot_rows + 8 * block : channel * slot_rows + 8 * block + 8, :] for channel in range(PROJ)
        ]
        at_x = found[0] - middle_x
        at_y = found[1] - middle_y
        quad_a = -0.5 * found[2]
        quad_b = -found[3]
        quad_c = -0.5 * found[4]
        flat = quad_a * at_x * at_x + quad_c * at_y * at_y + quad_b * at_x * at_y + jnp.log(found[5])
        place = (8 * block - group * chunks + sub) * STEP + lane // GROUP
        terms = (
            quad_a * LOG2E,
            quad_b * LOG2E,
            quad_c * LOG2E,
            (-2.0 * quad_a * at_x - quad_b * at_y) * LOG2E,
            (-2.0 * quad_c * at_y - quad_b * at_x) * LOG2E,
            jnp.where(place < live, flat * LOG2E, -1e30),
        )
        for index, term in enumerate(terms):
            for part, value in enumerate(split_three(term)):
                coef_s[pl.ds(8 * block * 24 + 6 * part + index, 8, stride=24), :] = value
        for colour in range(3):
            for part, value in enumerate(split_two(found[6 + colour])):
                coef_s[pl.ds(8 * block * 24 + 18 + 3 * part + colour, 8, stride=24), :] = value

    pixel = iota((24, PIX), 1)
    row = iota((24, PIX), 0)
    pix_x = (pixel % 16).astype(f32) - 7.5
    pix_y = (pixel // 16).astype(f32) - 7.5
    kind = row % 6
    monomials = jnp.where(kind == 0, pix_x * pix_x, jnp.where(kind == 1, pix_x * pix_y, 1.0))
    monomials = jnp.where(kind == 2, pix_y * pix_y, monomials)
    monomials = jnp.where(kind == 3, pix_x, jnp.where(kind == 4, pix_y, monomials))
    moments = jnp.where(iota((8, PIX), 0) < 6, monomials[0:8], 0.0).astype(bf16)
    monomials = jnp.where(row < 18, monomials, 0.0)
    nothing = jnp.zeros((24, PIX), f32)
    for group in range(groups):
        for colour in range(3):
            for tile in range(GROUP):
                start = (group * GROUP + tile) * PIX
                cot_s[group * 24 + colour * GROUP + tile, :] = cot_ref[colour, start : start + PIX]
    cots = []
    spare = jnp.zeros((8, PIX), f32)
    for group in range(groups):
        first, second = split_two(cot_s[group * 24 : (group + 1) * 24, :])
        cots.append(jnp.concatenate([first, spare, second, spare], axis=0).astype(bf16))
        rhs_s[group] = jnp.concatenate(
            [
                jnp.concatenate([jnp.concatenate([nothing, monomials[8 * one : 8 * one + 8]], axis=0) for one in range(3)], axis=0),
                jnp.concatenate([first, spare, first, spare, second, spare], axis=0),
            ],
            axis=1,
        ).astype(bf16)

    own_tile = sub == tile_of
    own_pair = iota((8, WIDE), 0) == iota((8, WIDE), 1) % GROUP

    def evaluate(index):
        for group in range(groups):
            chunk = group * chunks + index
            coefs = coef_s[chunk * 24 : (chunk + 1) * 24, :]
            tints = [jnp.where(own_tile, coefs[18 + one : 19 + one], 0.0) for one in range(6)]
            lhs = jnp.concatenate(
                tints[:3] + [coefs[0:8]] + tints[3:] + [coefs[8:16]] + tints[:3] + [coefs[16:24]], axis=0
            ).astype(bf16)
            both = dot_tn(lhs, rhs_s[group])
            lanes = slice(chunk * LANES, (chunk + 1) * LANES)
            tint_s[:, lanes] = lhs[0:64]
            alpha_s[lanes, :] = jnp.exp2(both[:, :PIX])
            shade_s[lanes, :] = both[:, PIX:]

    def scan(index, trans):
        out = []
        for group in range(groups):
            one = trans[group]
            start = (group * chunks + index) * LANES
            for step in range(STEP):
                alpha = alpha_s[pl.ds(start + step * GROUP, GROUP), :]
                weight = one * alpha
                one = one - weight
                weight_s[pl.ds(start + step * GROUP, GROUP), :] = weight
            out.append(one)
        return tuple(out)

    def paint(index, images):
        out = []
        for group in range(groups):
            chunk = group * chunks + index
            both = slice(chunk * LANES, chunk * LANES + WIDE)
            first, second = split_two(weight_s[both, :])
            first = first.astype(bf16)
            second = second.astype(bf16)
            tints = tint_s[:, both]
            by_first = dot(tints, first)
            out.append(images[group] + by_first[0:24] + by_first[32:56] + dot(tints[0:32], second)[0:24])
            by_first = dot_nt(cots[group], first)
            tint_grad = by_first[0:24] + by_first[32:56] + dot_nt(cots[group][0:32], second)[0:24]
            for colour in range(3):
                own = jnp.where(own_pair, tint_grad[colour * GROUP : (colour + 1) * GROUP], 0.0)
                own = jnp.sum(own, axis=0, keepdims=True)
                for one in range(2):
                    sums_s[(chunk + one) * 16 + 8 + colour : (chunk + one) * 16 + 9 + colour, :] = own[:, one * LANES : (one + 1) * LANES]
        return tuple(out)

    trans = tuple(jnp.ones((GROUP, PIX), f32) for _ in range(groups))
    images = tuple(jnp.zeros((24, PIX), f32) for _ in range(groups))
    per_group = chunks // 8
    for block in range(0, blocks, per_group):
        for row in range(0, 8, 2):
            pick_in(8 * block + row)
        quadratics(block)
    for pair in range(-AHEAD, chunks // 2 + 1):
        step = pair + AHEAD + 4
        if 4 <= step < chunks // 2:
            for group in range(groups):
                block = group * per_group + step // 4
                pick_in(8 * block + step % 4 * 2)
                if step % 4 == 3:
                    quadratics(block)
        for one in range(2):
            if pair + AHEAD < chunks // 2:
                evaluate(2 * (pair + AHEAD) + one)
        for one in range(2):
            if 0 <= pair < chunks // 2:
                trans = scan(2 * pair + one, trans)
        if pair > 0:
            images = paint(2 * (pair - 1), images)
    for group in range(groups):
        for colour in range(3):
            for tile in range(GROUP):
                at = (group * GROUP + tile) * PIX
                image_ref[colour, at : at + PIX] = images[group][colour * GROUP + tile]

    def moment(index):
        for group in range(groups):
            chunk = group * chunks + index
            first, second = split_two(shade_s[slice(chunk * LANES, chunk * LANES + WIDE), :])
            found = dot_nt(moments, first.astype(bf16)) + dot_nt(moments, second.astype(bf16))
            for one in range(2):
                start = (chunk + one) * 16
                sums_s[start : start + 8, :] = found[:, one * LANES : (one + 1) * LANES]

    def rescan(index, behinds):
        out = []
        for group in range(groups):
            behind = behinds[group]
            start = (group * chunks + index) * LANES
            for step in reversed(range(STEP)):
                at = pl.ds(start + step * GROUP, GROUP)
                ahead = shade_s[at, :] - behind
                shade_s[at, :] = weight_s[at, :] * ahead
                behind = behind + alpha_s[at, :] * ahead
            out.append(behind)
        return tuple(out)

    slot_s = raw_s
    owner_id = narrow(iota((slot_rows // 2, LANES), 0))

    def send(block):
        middle_x, middle_y, _ = middles[block * 8 // chunks]
        raw = [raw_s[channel * slot_rows + 8 * block : channel * slot_rows + 8 * block + 8, :] for channel in range(6)]
        (sum_xx, sum_xy, sum_yy, sum_x, sum_y, sum_one) = [
            sums_s[pl.ds(8 * block * 16 + index, 8, stride=16), :] for index in range(6)
        ]
        at_x = raw[0] - middle_x
        at_y = raw[1] - middle_y
        off_x = sum_x - at_x * sum_one
        off_y = sum_y - at_y * sum_one
        grads = [
            raw[2] * off_x + raw[3] * off_y,
            raw[4] * off_y + raw[3] * off_x,
            -0.5 * (sum_xx - at_x * (sum_x + off_x)),
            -(sum_xy - at_y * sum_x - at_x * off_y),
            -0.5 * (sum_yy - at_y * (sum_y + off_y)),
            sum_one / raw[5],
        ] + [sums_s[pl.ds(8 * block * 16 + 8 + colour, 8, stride=16), :] for colour in range(3)]
        for channel, value in enumerate(grads):
            slot_s[channel * slot_rows + 8 * block : channel * slot_rows + 8 * block + 8, :] = value

        for row in range(8 * block, 8 * block + 8):
            lanes = slice(row * LANES, (row + 1) * LANES)
            mine = one_hot(pos_ref[row : row + 1, :] // WIDE, owner_id)
            for channel in range(PROJ):
                at = channel * slot_rows + row
                put_terms(lhs_s, channel, lanes, slot_s[at : at + 1, :], mine)
        lanes = slice(8 * block * LANES, 8 * (block + 1) * LANES)
        found = dot_nt(lhs_s[:, lanes], hot_s[:, lanes])
        total_s[...] = found if block == per_group - 1 else total_s[...] + found

    behinds = tuple(jnp.zeros((GROUP, PIX), f32) for _ in range(groups))
    for pair in reversed(range(-1, chunks // 2)):
        for one in reversed(range(2)):
            if pair >= 0:
                behinds = rescan(2 * pair + one, behinds)
        if pair + 1 < chunks // 2:
            moment(2 * (pair + 1))
            if (pair + 1) % 4 == 0:
                for group in range(groups):
                    send(group * per_group + (pair + 1) // 4)

    lows = slot_rows // 2
    for channel in range(PROJ):
        value = total_s[channel * lows : (channel + 1) * lows, :]
        value = value + total_s[(PROJ + channel) * lows : (PROJ + channel + 1) * lows, :]
        for half in range(2):
            out_ref[layout.half(channel, half), :] = value[:, half * LANES : (half + 1) * LANES]


def collect_kernel(
    layout, camera_frame, angles_ref, dense_ref, asked_ref, terms_ref, grad_hbm, lhs_s, rhs_s, total_s, out_s, grad_ref, sems
):
    gauss = grad_ref.shape[1]
    rows = gauss // LANES
    lows = gauss // WIDE
    low_id = narrow(iota((lows, LANES), 0))
    high_id = narrow(iota((WIDE, LANES), 0))
    minors = layout.minors()

    for index in range(layout.count // 8):
        asked = asked_ref[8 * index : 8 * index + 8, :]
        low = asked // WIDE
        high = asked % WIDE
        for row in range(8):
            lanes = slice((8 * index + row) * LANES, (8 * index + row + 1) * LANES)
            mine = one_hot(low[row : row + 1], low_id)
            rhs_s[:, lanes] = one_hot(high[row : row + 1], high_id)
            for channel in range(PROJ):
                at = layout.row(channel, (8 * index + row) // minors, row % minors)
                put_terms(lhs_s, channel, lanes, terms_ref[at : at + 1, :], mine)
        lanes = slice(8 * index * LANES, 8 * (index + 1) * LANES)
        found = dot_nt(lhs_s[:, lanes], rhs_s[:, lanes])
        total_s[...] = found if index == 0 else total_s[...] + found
    rotation = view(angles_ref)
    basis = harmonics(*rotation[2])
    for part in range(rows // 8):
        half = part % 2
        low = part // 2 * 8
        lanes = slice(half * LANES, (half + 1) * LANES)
        sums = [
            total_s[channel * lows + low : channel * lows + low + 8, lanes]
            + total_s[(PROJ + channel) * lows + low : (PROJ + channel) * lows + low + 8, lanes]
            for channel in range(PROJ)
        ]
        columns = tuple(dense_ref[pl.ds(index * rows + 2 * low + half, 8, stride=2), :] for index in range(11))
        _, pullback = jax.vjp(lambda *values: shape_of(values, rotation, camera_frame), *columns)
        grads = pullback(tuple(sums[:6]))
        for index, value in enumerate(tuple(grads) + tuple(sums[6:])):
            out_s[pl.ds(index * rows + 2 * low + half, 8, stride=2), :] = value
    sub = iota((8, LANES), 0)
    patterns = [basis_rows(basis, eighth) for eighth in range(8)]
    copies = []
    pieces = sems.shape[0]
    wide = gauss // pieces
    for row in range(rows):
        lanes = slice(row * LANES, (row + 1) * LANES)
        grad_ref[0:8, lanes] = out_s[pl.ds(row, 8, stride=rows), :]
        tints = [out_s[(11 + colour) * rows + row : (11 + colour) * rows + row + 1, :] for colour in range(3)]
        for eighth in range(1, 8):
            value = None
            for colour in range(3):
                pattern = patterns[eighth][colour]
                if pattern is not None:
                    term = pattern * tints[colour]
                    value = term if value is None else value + term
            if eighth == 1:
                value = jnp.where(sub < 3, out_s[pl.ds(8 * rows + row, 8, stride=rows), :], value)
            if eighth == 7:
                grad_ref[56:59, lanes] = value[0:3]
            else:
                grad_ref[8 * eighth : 8 * eighth + 8, lanes] = value
        if (row + 1) * LANES % wide == 0:
            piece = len(copies)
            span = slice(piece * wide, (piece + 1) * wide)
            copies.append(pltpu.make_async_copy(grad_ref.at[:, span], grad_hbm.at[:, span], sems.at[piece]))
            copies[-1].start()
    for copy in copies:
        copy.wait()


VMEM = pl.BlockSpec(memory_space=pltpu.VMEM)
HBM = pl.BlockSpec(memory_space=pltpu.HBM)
SMEM = pl.BlockSpec(memory_space=pltpu.SMEM)


def call(kernel, specs, outs, scratch, flops, name, out_spec=VMEM, vmem=VMEM_BYTES):
    return pl.pallas_call(
        kernel,
        in_specs=specs,
        out_specs=[out_spec] * len(outs),
        out_shape=[jax.ShapeDtypeStruct(shape, dtype) for shape, dtype in outs],
        scratch_shapes=[pltpu.VMEM(*one) if isinstance(one, tuple) else one for one in scratch],
        compiler_params=pltpu.CompilerParams(vmem_limit_bytes=vmem),
        cost_estimate=pl.CostEstimate(flops=flops, bytes_accessed=4 << 20, transcendentals=0),
        name=name,
    )


def route(devices, owners, locals_):
    slots = owners.size
    per_owner = slots // devices
    rows = slots // LANES
    halves = per_owner // LANES if per_owner % LANES == 0 else 0
    asked = (devices * halves, LANES) if halves else (devices, per_owner)
    return call(
        partial(route_kernel, devices, per_owner),
        [HBM, HBM],
        [(asked, i32), ((rows, LANES), i32)],
        [(owners.shape, i32)] * 2 + [pltpu.SemaphoreType.DMA((2,))],
        1 << 30,
        "route",
        vmem=63 << 20,
    )(owners, locals_)


def shade(camera_frame, view_angles, gaussians):
    rows = gaussians.shape[1] // LANES
    return call(
        partial(shade_kernel, camera_frame),
        [SMEM, VMEM],
        [((sum(PARTS) * rows // 2, WIDE), bf16), ((16 * rows, LANES), f32)],
        [((27 * rows, LANES), f32)],
        1 << 30,
        "shade",
    )(view_angles, gaussians)


def pick(layout, table, asked):
    return call(
        partial(pick_kernel, layout),
        [VMEM, VMEM],
        [((PROJ * layout.count, LANES), f32)],
        [],
        1 << 30,
        "pick",
    )(table, asked)[0]


def render(layout, list_counts, tile_order, rows, pos, cotangent):
    slot_rows = pos.shape[0]
    groups = tile_order.shape[0] // GROUP
    slots = slot_rows * LANES
    return call(
        partial(render_kernel, layout),
        [SMEM, SMEM, VMEM, VMEM, VMEM],
        [(cotangent.shape, f32), ((PROJ * layout.count, LANES), f32)],
        [
            ((sum(PARTS) * slot_rows // 2, WIDE), bf16),
            ((WIDE, slots), bf16),
            ((PROJ * slot_rows, slots), bf16),
            ((PROJ * slot_rows, WIDE), f32),
            ((PROJ * slot_rows, LANES), f32),
            ((24 * slot_rows, LANES), f32),
            ((24 * groups, PIX), f32),
            ((groups, 96, 2 * PIX), bf16),
            ((64, slots), bf16),
            ((slots, PIX), f32),
            ((slots, PIX), f32),
            ((slots, PIX), f32),
            ((16 * slot_rows, LANES), f32),
        ],
        1 << 34,
        "render",
    )(list_counts, tile_order, rows, pos, cotangent)


def collect(layout, camera_frame, view_angles, shape, dense, asked, terms):
    rows = shape[1] // LANES
    lows = shape[1] // WIDE
    return call(
        partial(collect_kernel, layout, camera_frame),
        [SMEM, VMEM, VMEM, VMEM],
        [(shape, f32)],
        [
            ((2 * PROJ * lows, layout.count * LANES), bf16),
            ((WIDE, layout.count * LANES), bf16),
            ((2 * PROJ * lows, WIDE), f32),
            ((16 * rows, LANES), f32),
            (shape, f32),
            pltpu.SemaphoreType.DMA((8,)),
        ],
        1 << 32,
        "collect",
        out_spec=HBM,
    )(view_angles, dense, asked, terms)[0]


def swap_rows(layout, devices, rows):
    if layout.halves:
        apart = rows.reshape(devices * PROJ, layout.halves, LANES)
        return lax.all_to_all(apart, "dev", split_axis=0, concat_axis=0, tiled=True).reshape(rows.shape)
    apart = rows.reshape(PROJ, devices, layout.count * LANES // devices)
    return lax.all_to_all(apart, "dev", split_axis=1, concat_axis=1, tiled=True).reshape(rows.shape)


def shards(gaussians, view_angles, tile_order, tile_owners, tile_locals, list_counts, image_cotangent):
    devices = lax.axis_size("dev")
    tiles_y = devices * tile_order.shape[0] // TX
    camera_frame = (4.0 * TX, 4.0 * tiles_y, 8.0 * TX, 8.0 * tiles_y)
    layout = Rows(devices, tile_owners.size // devices)
    want, pos = route(devices, tile_owners, tile_locals)
    asked = lax.all_to_all(want, "dev", split_axis=0, concat_axis=0, tiled=True)
    table, dense = shade(camera_frame, view_angles, gaussians)
    if not layout.halves:
        asked = asked.reshape(layout.count, LANES)
    arrived = swap_rows(layout, devices, pick(layout, table, asked))
    rendered, slot_grads = render(layout, list_counts, tile_order, arrived, pos, image_cotangent)
    terms = swap_rows(layout, devices, slot_grads)
    gradients = collect(layout, camera_frame, view_angles, gaussians.shape, dense, asked, terms)
    return (rendered, gradients)


def solution(mesh):
    return jax.shard_map(
        shards,
        mesh=mesh,
        in_specs=(
            P(None, "dev"),
            P(),
            P("dev"),
            P("dev", None),
            P("dev", None),
            P("dev"),
            P(None, "dev"),
        ),
        out_specs=(P(None, "dev"), P(None, "dev")),
        check_vma=False,
    )
```

```python
from functools import partial

import jax
import jax.numpy as jnp
from jax import lax
from jax.experimental import pallas as pl
from jax.experimental.pallas import tpu as pltpu
from jax.sharding import PartitionSpec as P

PIX = 256
TX = 32
LANES = 128
PROJ = 9
GROUP = 8
WIDE = 2 * LANES
PARTS = (3, 3, 3, 3, 3, 2, 2, 2, 2)
STEP = LANES // GROUP
LOG2E = 1.4426950408889634
PLANE = 8
AHEAD = 2
VMEM_BYTES = 52 * 1024 * 1024

f32 = jnp.float32
bf16 = jnp.bfloat16
i32 = jnp.int32


def iota(shape, dim):
    return lax.broadcasted_iota(i32, shape, dim)


def lane_pick(row, lanes):
    source = jnp.broadcast_to(row, lanes.shape)
    return jnp.take_along_axis(source, lanes, axis=1, mode="promise_in_bounds")


def split_two(values):
    first = values.astype(bf16).astype(f32)
    return first, values - first


def split_three(values):
    first, rest = split_two(values)
    second, third = split_two(rest)
    return first, second, third


def dot(lhs, rhs):
    return lax.dot_general(lhs, rhs, (((1,), (0,)), ((), ())), preferred_element_type=f32)


def dot_nt(lhs, rhs):
    return lax.dot_general(lhs, rhs, (((1,), (1,)), ((), ())), preferred_element_type=f32)


def dot_tn(lhs, rhs):
    return lax.dot_general(lhs, rhs, (((0,), (0,)), ((), ())), preferred_element_type=f32)


class Rows:
    def __init__(self, devices, per_owner):
        self.halves = per_owner // LANES if per_owner % LANES == 0 else 0
        self.count = devices * per_owner // LANES

    def row(self, channel, major, minor):
        halves = self.halves
        if halves == 0:
            return channel * self.count + major
        return major * (PROJ * halves) + channel * halves + minor

    def half(self, ref, channel, half):
        halves = self.halves
        if halves == 0:
            return ref[pl.ds(channel * self.count + half, self.count // 2, stride=2), :]
        return jnp.concatenate(
            [ref[pl.ds(self.row(channel, one // halves, one % halves), 1), :] for one in range(half, self.count, 2)], axis=0
        ) if halves != 2 else ref[pl.ds(channel * 2 + half, self.count // 2, stride=2 * PROJ), :]

    def minors(self):
        return max(self.halves, 1)


def narrow(ids):
    return ids.astype(f32).astype(bf16)


def one_hot(ids, every):
    return jnp.where(narrow(ids) == every, jnp.ones((), bf16), jnp.zeros((), bf16))


def put_terms(lhs_s, channel, lanes, row, mine):
    lows = mine.shape[0]
    row = jnp.broadcast_to(row, (16, LANES))
    first = row.astype(bf16)
    second = (row - first.astype(f32)).astype(bf16)
    for part, value in enumerate((first, second)):
        for low in range(0, lows, 16):
            start = (part * PROJ + channel) * lows + low
            lhs_s[start : start + 16, lanes] = mine[low : low + 16] * value


def pick_slots(parts, slots, low_id, high_id, put):
    found = dot(parts, one_hot(slots % WIDE, high_id))
    mine = slots // WIDE == low_id
    lows = low_id.shape[0]
    first = 0
    for channel, count in enumerate(PARTS if parts.shape[0] == sum(PARTS) * lows else (2,) * PROJ):
        value = found[first * lows : (first + 1) * lows]
        for part in range(1, count):
            value = value + found[(first + part) * lows : (first + part + 1) * lows]
        first += count
        put(channel, jnp.sum(jnp.where(mine, value, 0.0), axis=0, keepdims=True))


def put_parts(parts_ref, channel, half, value, counts, lows=None, low=0):
    lows = lows or value.shape[0]
    first = sum(counts[:channel])
    parts = split_three(value) if counts[channel] == 3 else split_two(value)
    for part, one in enumerate(parts):
        at = (first + part) * lows + low
        parts_ref[at : at + value.shape[0], half * LANES : (half + 1) * LANES] = one.astype(bf16)


def route_kernel(devices, per_owner, own_hbm, loc_hbm, want_ref, back_ref, pos_ref, own_ref, loc_ref, own_s, loc_s, rank_s, sems):
    copies = [pltpu.make_async_copy(own_hbm, own_ref, sems.at[0]), pltpu.make_async_copy(loc_hbm, loc_ref, sems.at[1])]
    for copy in copies:
        copy.start()
    for copy in copies:
        copy.wait()
    rows = own_s.shape[0]
    blocks = own_ref.shape[1] // LANES
    lane = iota((8, LANES), 1)
    from_slot = iota((8, LANES), 0) * STEP + lane // GROUP
    tile_of = lane % GROUP
    for group in range(own_ref.shape[0] // GROUP):
        for block in range(blocks):
            for source, target in ((own_ref, own_s), (loc_ref, loc_s)):
                part = source[group * GROUP : (group + 1) * GROUP, block * LANES : (block + 1) * LANES]
                out = jnp.zeros((8, LANES), i32)
                for tile in range(GROUP):
                    out = jnp.where(tile_of == tile, lane_pick(part[tile : tile + 1], from_slot), out)
                start = (group * blocks + block) * 8
                target[start : start + 8, :] = out
    owner = own_s[...]
    left = (iota((LANES, 2 * LANES), 0) < iota((LANES, 2 * LANES), 1)) | (iota((LANES, 2 * LANES), 1) >= LANES)
    above = iota((rows, rows), 1) < iota((rows, rows), 0)
    hits = jnp.concatenate([jnp.where(owner == one, 1.0, 0.0).astype(bf16) for one in range(devices)], axis=0)
    sums = dot(hits, jnp.where(left, 1.0, 0.0).astype(bf16))
    totals = jnp.concatenate(
        [sums[one * rows : (one + 1) * rows, LANES:].astype(bf16) for one in range(devices)], axis=1
    )
    base = dot(jnp.where(above, 1.0, 0.0).astype(bf16), totals)
    rank = jnp.zeros((rows, LANES), f32)
    for one in range(devices):
        here = sums[one * rows : (one + 1) * rows, :LANES] + base[:, one * LANES : (one + 1) * LANES]
        rank = jnp.where(owner == one, here, rank)
    rank = rank.astype(i32)
    pos_ref[...] = owner * per_owner + rank
    rank_s[...] = rank

    owner_id = iota((devices, LANES), 0)
    rank_id = narrow(iota((per_owner, LANES), 0))
    slot_lane = iota((devices, LANES), 1).astype(f32)

    def place(index, total):
        start = pl.multiple_of(index * 8, 8)
        own_rows = own_s[pl.ds(start, 8), :]
        loc_rows = loc_s[pl.ds(start, 8), :]
        rank_rows = rank_s[pl.ds(start, 8), :]
        high_rows = (loc_rows // LANES).astype(f32)
        low_rows = (loc_rows % LANES).astype(f32)
        lhs = []
        rhs = []
        for row in range(8):
            mine = own_rows[row : row + 1] == owner_id
            number = (start + row).astype(f32)
            lhs.append(
                jnp.concatenate(
                    [
                        jnp.where(mine, high_rows[row : row + 1], 0.0),
                        jnp.where(mine, low_rows[row : row + 1], 0.0),
                        jnp.where(mine, number, 0.0),
                        jnp.where(mine, slot_lane, 0.0),
                    ],
                    axis=0,
                ).astype(bf16)
            )
            rhs.append(one_hot(rank_rows[row : row + 1], rank_id))
        return total + dot_nt(jnp.concatenate(lhs, axis=1), jnp.concatenate(rhs, axis=1))

    total = lax.fori_loop(0, rows // 8, place, jnp.zeros((4 * devices, per_owner), f32), unroll=devices <= 32).astype(i32)
    want = total[:devices] * LANES + total[devices : 2 * devices]
    halves = per_owner // LANES
    if per_owner % LANES == 0 and halves > 1:
        planes = devices // PLANE
        for plane in range(planes):
            for half in range(halves):
                rows_of = pl.ds(plane * halves + half, PLANE, stride=planes * halves)
                want_ref[rows_of, :] = want[plane * PLANE : (plane + 1) * PLANE, half * LANES : (half + 1) * LANES]
    else:
        want_ref[...] = want
    back_ref[...] = total[2 * devices : 3 * devices] * LANES + total[3 * devices :]


def view(angles_ref):
    angle = [jnp.full((1, LANES), angles_ref[index], f32) for index in range(3)]
    (cos_a, cos_b, cos_c) = [jnp.cos(one) for one in angle]
    (sin_a, sin_b, sin_c) = [jnp.sin(one) for one in angle]
    return [
        [cos_c * cos_b, cos_c * sin_b * sin_a - sin_c * cos_a, cos_c * sin_b * cos_a + sin_c * sin_a],
        [sin_c * cos_b, sin_c * sin_b * sin_a + cos_c * cos_a, sin_c * sin_b * cos_a - cos_c * sin_a],
        [-sin_b, cos_b * sin_a, cos_b * cos_a],
    ]


def harmonics(along_x, along_y, along_z):
    sq_x = along_x * along_x
    sq_y = along_y * along_y
    sq_z = along_z * along_z
    return [
        0.28209479177387814 + 0.0 * along_x,
        -0.4886025119029199 * along_y,
        0.4886025119029199 * along_z,
        -0.4886025119029199 * along_x,
        1.0925484305920792 * along_x * along_y,
        -1.0925484305920792 * along_y * along_z,
        0.31539156525252005 * (2.0 * sq_z - sq_x - sq_y),
        -1.0925484305920792 * along_x * along_z,
        0.5462742152960396 * (sq_x - sq_y),
        -0.5900435899266435 * along_y * (3.0 * sq_x - sq_y),
        2.890611442640554 * along_x * along_y * along_z,
        -0.4570457994644658 * along_y * (4.0 * sq_z - sq_x - sq_y),
        0.3731763325901154 * along_z * (2.0 * sq_z - 3.0 * sq_x - 3.0 * sq_y),
        -0.4570457994644658 * along_x * (4.0 * sq_z - sq_x - sq_y),
        1.445305721320277 * along_z * (sq_x - sq_y),
        -0.5900435899266435 * along_x * (sq_x - 3.0 * sq_y),
    ]


def basis_rows(basis, eighth):
    sub = iota((8, LANES), 0)
    found = []
    for colour in range(3):
        out = None
        for inner in range(8):
            index = 8 * eighth + inner - 11 - 16 * colour
            if 0 <= index < 16:
                out = jnp.zeros((8, LANES), f32) if out is None else out
                out = jnp.where(sub == inner, basis[index], out)
        found.append(out)
    return found


def shape_of(columns, rotation, camera_frame):
    focal_x, focal_y, centre_x, centre_y = camera_frame
    positions = columns[0:3]
    cam_first = rotation[0][0] * positions[0] + rotation[0][1] * positions[1] + rotation[0][2] * positions[2]
    cam_second = rotation[1][0] * positions[0] + rotation[1][1] * positions[1] + rotation[1][2] * positions[2]
    mean_x = centre_x + focal_x * cam_first
    mean_y = centre_y + focal_y * cam_second
    scales = [jnp.exp(one) for one in columns[3:6]]
    quat_w, quat_x, quat_y, quat_z = columns[6:10]
    norm_sq = jnp.maximum(quat_w * quat_w + quat_x * quat_x + quat_y * quat_y + quat_z * quat_z, 1.0)
    twice = 2.0 / norm_sq
    turned = [
        [
            1.0 - twice * (quat_y * quat_y + quat_z * quat_z),
            twice * (quat_x * quat_y - quat_w * quat_z),
            twice * (quat_x * quat_z + quat_w * quat_y),
        ],
        [
            twice * (quat_x * quat_y + quat_w * quat_z),
            1.0 - twice * (quat_x * quat_x + quat_z * quat_z),
            twice * (quat_y * quat_z - quat_w * quat_x),
        ],
        [
            twice * (quat_x * quat_z - quat_w * quat_y),
            twice * (quat_y * quat_z + quat_w * quat_x),
            1.0 - twice * (quat_x * quat_x + quat_y * quat_y),
        ],
    ]
    rows = []
    for focal, turn in ((focal_x, rotation[0]), (focal_y, rotation[1])):
        rows.append(
            [
                focal * (turn[0] * turned[0][k] + turn[1] * turned[1][k] + turn[2] * turned[2][k]) * scales[k]
                for k in range(3)
            ]
        )
    first, second = rows
    cov_a = first[0] * first[0] + first[1] * first[1] + first[2] * first[2] + 0.3
    cov_b = first[0] * second[0] + first[1] * second[1] + first[2] * second[2]
    cov_c = second[0] * second[0] + second[1] * second[1] + second[2] * second[2] + 0.3
    determinant = cov_a * cov_c - cov_b * cov_b
    opacity = 1.0 / (1.0 + jnp.exp(-columns[10]))
    return mean_x, mean_y, cov_c / determinant, -cov_b / determinant, cov_a / determinant, opacity


def spread_columns(gauss_ref, dense_s):
    rows = gauss_ref.shape[1] // LANES
    for row in range(rows):
        for eighth in range(2):
            dense_s[pl.ds(8 * eighth * rows + row, 8, stride=rows), :] = gauss_ref[
                8 * eighth : 8 * eighth + 8, row * LANES : (row + 1) * LANES
            ]


def shade_kernel(camera_frame, angles_ref, gauss_ref, parts_ref, dense_s, tint_s):
    rows = gauss_ref.shape[1] // LANES
    spread_columns(gauss_ref, dense_s)
    rotation = view(angles_ref)
    basis = harmonics(*rotation[2])
    patterns = [basis_rows(basis, eighth) for eighth in range(7)]
    for row in range(rows):
        lanes = slice(row * LANES, (row + 1) * LANES)
        tints = [None] * 3
        for eighth in range(1, 7):
            block = gauss_ref[8 * eighth : 8 * eighth + 8, lanes]
            for colour in range(3):
                pattern = patterns[eighth][colour]
                if pattern is not None:
                    term = block * pattern
                    tints[colour] = term if tints[colour] is None else tints[colour] + term
        for colour in range(3):
            tint_s[pl.ds(8 * colour * rows + row, 8, stride=rows), :] = tints[colour]
        tint_s[pl.ds(24 * rows + row, 3, stride=rows), :] = gauss_ref[56:59, lanes]
    for part in range(rows // 16):
        half = part % 2
        low = part // 2 * 16
        at = [pl.ds(index * rows + 2 * low + half, 16, stride=2) for index in range(27)]
        columns = [dense_s[one, :] for one in at[:11]]
        for index, value in enumerate(shape_of(columns, rotation, camera_frame)):
            put_parts(parts_ref, index, half, value, PARTS, rows // 2, low)
        for colour in range(3):
            total = 0.5
            for inner in range(8):
                total = total + tint_s[at[8 * colour + inner], :]
            if colour == 2:
                for inner in range(3):
                    total = total + basis[13 + inner] * tint_s[at[24 + inner], :]
            put_parts(parts_ref, 6 + colour, half, total, PARTS, rows // 2, low)


def pick_kernel(layout, parts_ref, asked_ref, out_ref):
    low_id = iota((parts_ref.shape[0] // sum(PARTS), WIDE), 0)
    high_id = narrow(iota((WIDE, WIDE), 0))
    minors = layout.minors()

    def pick_some(index, _):
        slots = jnp.concatenate([asked_ref[pl.ds(2 * index + one, 1), :] for one in range(2)], axis=1)

        def put(channel, value):
            for one in range(2):
                at = layout.row(channel, (2 * index + one) // minors, (2 * index + one) % minors)
                out_ref[pl.ds(at, 1), :] = value[:, one * LANES : (one + 1) * LANES]

        pick_slots(parts_ref[...], slots, low_id, high_id, put)
        return 0

    lax.fori_loop(0, layout.count // 2, pick_some, 0, unroll=True)


def render_kernel(
    layout,
    count_ref,
    order_ref,
    rows_ref,
    pos_ref,
    back_ref,
    cot_ref,
    image_ref,
    out_ref,
    in_s,
    out_s,
    raw_s,
    coef_s,
    cot_s,
    rhs_s,
    tint_s,
    alpha_s,
    shade_s,
    weight_s,
    sums_s,
):
    slot_rows = pos_ref.shape[0]
    groups = cot_ref.shape[1] // (GROUP * PIX)
    chunks = slot_rows // groups
    sub = iota((8, LANES), 0)
    lane = iota((8, LANES), 1)
    tile_of = lane % GROUP
    blocks = slot_rows // 8
    middles = []
    for group in range(groups):
        middle_x = jnp.zeros((8, LANES), f32)
        middle_y = jnp.zeros((8, LANES), f32)
        live = jnp.zeros((8, LANES), i32)
        for tile in range(GROUP):
            shown = order_ref[group * GROUP + tile]
            here = tile_of == tile
            middle_x = jnp.where(here, (shown % TX * 16 + 8).astype(f32), middle_x)
            middle_y = jnp.where(here, (shown // TX * 16 + 8).astype(f32), middle_y)
            live = jnp.where(here, count_ref[group * GROUP + tile], live)
        middles.append((middle_x, middle_y, live))

    for half in range(2):
        for channel in range(PROJ):
            put_parts(in_s, channel, half, layout.half(rows_ref, channel, half), PARTS)
    low_id = iota((slot_rows // 2, WIDE), 0)
    high_id = narrow(iota((WIDE, WIDE), 0))

    def pick_in(index, _):
        slots = jnp.concatenate([pos_ref[pl.ds(2 * index + one, 1), :] for one in range(2)], axis=1)

        def put(channel, value):
            for one in range(2):
                raw_s[pl.ds(channel * slot_rows + 2 * index + one, 1), :] = value[:, one * LANES : (one + 1) * LANES]

        pick_slots(in_s[...], slots, low_id, high_id, put)
        return 0

    lax.fori_loop(0, slot_rows // 2, pick_in, 0, unroll=True)
    for block in range(blocks):
        group = block * 8 // chunks
        middle_x, middle_y, live = middles[group]
        found = [
            raw_s[channel * slot_rows + 8 * block : channel * slot_rows + 8 * block + 8, :] for channel in range(PROJ)
        ]
        at_x = found[0] - middle_x
        at_y = found[1] - middle_y
        quad_a = -0.5 * found[2]
        quad_b = -found[3]
        quad_c = -0.5 * found[4]
        flat = quad_a * at_x * at_x + quad_c * at_y * at_y + quad_b * at_x * at_y + jnp.log(found[5])
        place = (8 * block - group * chunks + sub) * STEP + lane // GROUP
        terms = (
            quad_a * LOG2E,
            quad_b * LOG2E,
            quad_c * LOG2E,
            (-2.0 * quad_a * at_x - quad_b * at_y) * LOG2E,
            (-2.0 * quad_c * at_y - quad_b * at_x) * LOG2E,
            jnp.where(place < live, flat * LOG2E, -1e30),
        )
        for index, term in enumerate(terms):
            for part, value in enumerate(split_three(term)):
                coef_s[pl.ds(8 * block * 24 + 6 * part + index, 8, stride=24), :] = value
        for colour in range(3):
            for part, value in enumerate(split_two(found[6 + colour])):
                coef_s[pl.ds(8 * block * 24 + 18 + 3 * part + colour, 8, stride=24), :] = value

    pixel = iota((24, PIX), 1)
    row = iota((24, PIX), 0)
    pix_x = (pixel % 16).astype(f32) - 7.5
    pix_y = (pixel // 16).astype(f32) - 7.5
    kind = row % 6
    monomials = jnp.where(kind == 0, pix_x * pix_x, jnp.where(kind == 1, pix_x * pix_y, 1.0))
    monomials = jnp.where(kind == 2, pix_y * pix_y, monomials)
    monomials = jnp.where(kind == 3, pix_x, jnp.where(kind == 4, pix_y, monomials))
    moments = jnp.where(iota((8, PIX), 0) < 6, monomials[0:8], 0.0).astype(bf16)
    monomials = jnp.where(row < 18, monomials, 0.0)
    nothing = jnp.zeros((24, PIX), f32)
    for group in range(groups):
        for colour in range(3):
            for tile in range(GROUP):
                start = (group * GROUP + tile) * PIX
                cot_s[group * 24 + colour * GROUP + tile, :] = cot_ref[colour, start : start + PIX]
    cots = []
    spare = jnp.zeros((8, PIX), f32)
    for group in range(groups):
        first, second = split_two(cot_s[group * 24 : (group + 1) * 24, :])
        cots.append(jnp.concatenate([first, spare, second, spare], axis=0).astype(bf16))
        rhs_s[group] = jnp.concatenate(
            [
                jnp.concatenate([jnp.concatenate([nothing, monomials[8 * one : 8 * one + 8]], axis=0) for one in range(3)], axis=0),
                jnp.concatenate([first, spare, first, spare, second, spare], axis=0),
            ],
            axis=1,
        ).astype(bf16)

    own_tile = sub == tile_of
    own_pair = iota((8, WIDE), 0) == iota((8, WIDE), 1) % GROUP

    def evaluate(index):
        for group in range(groups):
            chunk = group * chunks + index
            coefs = coef_s[chunk * 24 : (chunk + 1) * 24, :]
            tints = [jnp.where(own_tile, coefs[18 + one : 19 + one], 0.0) for one in range(6)]
            lhs = jnp.concatenate(
                tints[:3] + [coefs[0:8]] + tints[3:] + [coefs[8:16]] + tints[:3] + [coefs[16:24]], axis=0
            ).astype(bf16)
            both = dot_tn(lhs, rhs_s[group])
            lanes = slice(chunk * LANES, (chunk + 1) * LANES)
            tint_s[:, lanes] = lhs[0:64]
            alpha_s[lanes, :] = jnp.exp2(both[:, :PIX])
            shade_s[lanes, :] = both[:, PIX:]

    def scan(index, trans):
        out = []
        for group in range(groups):
            one = trans[group]
            start = (group * chunks + index) * LANES
            for step in range(STEP):
                alpha = alpha_s[pl.ds(start + step * GROUP, GROUP), :]
                weight = one * alpha
                one = one - weight
                weight_s[pl.ds(start + step * GROUP, GROUP), :] = weight
            out.append(one)
        return tuple(out)

    def paint(index, images):
        out = []
        for group in range(groups):
            chunk = group * chunks + index
            both = slice(chunk * LANES, chunk * LANES + WIDE)
            first, second = split_two(weight_s[both, :])
            first = first.astype(bf16)
            second = second.astype(bf16)
            tints = tint_s[:, both]
            by_first = dot(tints, first)
            out.append(images[group] + by_first[0:24] + by_first[32:56] + dot(tints[0:32], second)[0:24])
            by_first = dot_nt(cots[group], first)
            tint_grad = by_first[0:24] + by_first[32:56] + dot_nt(cots[group][0:32], second)[0:24]
            for colour in range(3):
                own = jnp.where(own_pair, tint_grad[colour * GROUP : (colour + 1) * GROUP], 0.0)
                own = jnp.sum(own, axis=0, keepdims=True)
                for one in range(2):
                    sums_s[(chunk + one) * 16 + 8 + colour : (chunk + one) * 16 + 9 + colour, :] = own[:, one * LANES : (one + 1) * LANES]
        return tuple(out)

    trans = tuple(jnp.ones((GROUP, PIX), f32) for _ in range(groups))
    images = tuple(jnp.zeros((24, PIX), f32) for _ in range(groups))
    for pair in range(-AHEAD, chunks // 2 + 1):
        for one in range(2):
            if pair + AHEAD < chunks // 2:
                evaluate(2 * (pair + AHEAD) + one)
        for one in range(2):
            if 0 <= pair < chunks // 2:
                trans = scan(2 * pair + one, trans)
        if pair > 0:
            images = paint(2 * (pair - 1), images)
    for group in range(groups):
        for colour in range(3):
            for tile in range(GROUP):
                at = (group * GROUP + tile) * PIX
                image_ref[colour, at : at + PIX] = images[group][colour * GROUP + tile]

    def moment(index):
        for group in range(groups):
            chunk = group * chunks + index
            first, second = split_two(shade_s[slice(chunk * LANES, chunk * LANES + WIDE), :])
            found = dot_nt(moments, first.astype(bf16)) + dot_nt(moments, second.astype(bf16))
            for one in range(2):
                start = (chunk + one) * 16
                sums_s[start : start + 8, :] = found[:, one * LANES : (one + 1) * LANES]

    def rescan(index, behinds):
        out = []
        for group in range(groups):
            behind = behinds[group]
            start = (group * chunks + index) * LANES
            for step in reversed(range(STEP)):
                at = pl.ds(start + step * GROUP, GROUP)
                ahead = shade_s[at, :] - behind
                shade_s[at, :] = weight_s[at, :] * ahead
                behind = behind + alpha_s[at, :] * ahead
            out.append(behind)
        return tuple(out)

    behinds = tuple(jnp.zeros((GROUP, PIX), f32) for _ in range(groups))
    for pair in reversed(range(-1, chunks // 2)):
        for one in reversed(range(2)):
            if pair >= 0:
                behinds = rescan(2 * pair + one, behinds)
        if pair + 1 < chunks // 2:
            moment(2 * (pair + 1))

    slot_s = coef_s
    for block in range(blocks):
        middle_x, middle_y, _ = middles[block * 8 // chunks]
        at = slice(8 * block, 8 * block + 8)
        raw = [raw_s[channel * slot_rows + 8 * block : channel * slot_rows + 8 * block + 8, :] for channel in range(6)]
        (sum_xx, sum_xy, sum_yy, sum_x, sum_y, sum_one) = [
            sums_s[pl.ds(8 * block * 16 + index, 8, stride=16), :] for index in range(6)
        ]
        at_x = raw[0] - middle_x
        at_y = raw[1] - middle_y
        off_x = sum_x - at_x * sum_one
        off_y = sum_y - at_y * sum_one
        grads = [
            raw[2] * off_x + raw[3] * off_y,
            raw[4] * off_y + raw[3] * off_x,
            -0.5 * (sum_xx - at_x * (sum_x + off_x)),
            -(sum_xy - at_y * sum_x - at_x * off_y),
            -0.5 * (sum_yy - at_y * (sum_y + off_y)),
            sum_one / raw[5],
        ] + [sums_s[pl.ds(8 * block * 16 + 8 + colour, 8, stride=16), :] for colour in range(3)]
        for channel, value in enumerate(grads):
            slot_s[channel * slot_rows + 8 * block : channel * slot_rows + 8 * block + 8, :] = value

    for half in range(2):
        for channel in range(PROJ):
            value = slot_s[pl.ds(channel * slot_rows + half, slot_rows // 2, stride=2), :]
            put_parts(out_s, channel, half, value, (2,) * PROJ)
    minors = layout.minors()

    def pick_out(index, _):
        if layout.halves == 2:
            slots = back_ref[pl.ds(index, 1), :]
        else:
            slots = jnp.concatenate([back_ref[pl.ds(2 * index + one, 1), :] for one in range(2)], axis=1)

        def put(channel, value):
            for one in range(2):
                at = layout.row(channel, (2 * index + one) // minors, (2 * index + one) % minors)
                out_ref[pl.ds(at, 1), :] = value[:, one * LANES : (one + 1) * LANES]

        pick_slots(out_s[...], slots, low_id, high_id, put)
        return 0

    lax.fori_loop(0, layout.count // 2, pick_out, 0, unroll=True)


def collect_kernel(
    layout, camera_frame, angles_ref, dense_ref, asked_ref, terms_ref, grad_hbm, lhs_s, rhs_s, total_s, out_s, grad_ref, sems
):
    gauss = grad_ref.shape[1]
    rows = gauss // LANES
    lows = gauss // WIDE
    low_id = narrow(iota((lows, LANES), 0))
    high_id = narrow(iota((WIDE, LANES), 0))
    minors = layout.minors()

    for index in range(layout.count // 8):
        asked = asked_ref[8 * index : 8 * index + 8, :]
        low = asked // WIDE
        high = asked % WIDE
        for row in range(8):
            lanes = slice((8 * index + row) * LANES, (8 * index + row + 1) * LANES)
            mine = one_hot(low[row : row + 1], low_id)
            rhs_s[:, lanes] = one_hot(high[row : row + 1], high_id)
            for channel in range(PROJ):
                at = layout.row(channel, (8 * index + row) // minors, row % minors)
                put_terms(lhs_s, channel, lanes, terms_ref[at : at + 1, :], mine)
        lanes = slice(8 * index * LANES, 8 * (index + 1) * LANES)
        found = dot_nt(lhs_s[:, lanes], rhs_s[:, lanes])
        total_s[...] = found if index == 0 else total_s[...] + found
    rotation = view(angles_ref)
    basis = harmonics(*rotation[2])
    for part in range(rows // 8):
        half = part % 2
        low = part // 2 * 8
        lanes = slice(half * LANES, (half + 1) * LANES)
        sums = [
            total_s[channel * lows + low : channel * lows + low + 8, lanes]
            + total_s[(PROJ + channel) * lows + low : (PROJ + channel) * lows + low + 8, lanes]
            for channel in range(PROJ)
        ]
        columns = tuple(dense_ref[pl.ds(index * rows + 2 * low + half, 8, stride=2), :] for index in range(11))
        _, pullback = jax.vjp(lambda *values: shape_of(values, rotation, camera_frame), *columns)
        grads = pullback(tuple(sums[:6]))
        for index, value in enumerate(tuple(grads) + tuple(sums[6:])):
            out_s[pl.ds(index * rows + 2 * low + half, 8, stride=2), :] = value
    sub = iota((8, LANES), 0)
    patterns = [basis_rows(basis, eighth) for eighth in range(8)]
    copies = []
    pieces = sems.shape[0]
    wide = gauss // pieces
    for row in range(rows):
        lanes = slice(row * LANES, (row + 1) * LANES)
        grad_ref[0:8, lanes] = out_s[pl.ds(row, 8, stride=rows), :]
        tints = [out_s[(11 + colour) * rows + row : (11 + colour) * rows + row + 1, :] for colour in range(3)]
        for eighth in range(1, 8):
            value = None
            for colour in range(3):
                pattern = patterns[eighth][colour]
                if pattern is not None:
                    term = pattern * tints[colour]
                    value = term if value is None else value + term
            if eighth == 1:
                value = jnp.where(sub < 3, out_s[pl.ds(8 * rows + row, 8, stride=rows), :], value)
            if eighth == 7:
                grad_ref[56:59, lanes] = value[0:3]
            else:
                grad_ref[8 * eighth : 8 * eighth + 8, lanes] = value
        if (row + 1) * LANES % wide == 0:
            piece = len(copies)
            span = slice(piece * wide, (piece + 1) * wide)
            copies.append(pltpu.make_async_copy(grad_ref.at[:, span], grad_hbm.at[:, span], sems.at[piece]))
            copies[-1].start()
    for copy in copies:
        copy.wait()


VMEM = pl.BlockSpec(memory_space=pltpu.VMEM)
HBM = pl.BlockSpec(memory_space=pltpu.HBM)
SMEM = pl.BlockSpec(memory_space=pltpu.SMEM)


def call(kernel, specs, outs, scratch, flops, name, out_spec=VMEM, vmem=VMEM_BYTES):
    return pl.pallas_call(
        kernel,
        in_specs=specs,
        out_specs=[out_spec] * len(outs),
        out_shape=[jax.ShapeDtypeStruct(shape, dtype) for shape, dtype in outs],
        scratch_shapes=[pltpu.VMEM(*one) if isinstance(one, tuple) else one for one in scratch],
        compiler_params=pltpu.CompilerParams(vmem_limit_bytes=vmem),
        cost_estimate=pl.CostEstimate(flops=flops, bytes_accessed=4 << 20, transcendentals=0),
        name=name,
    )


def route(devices, owners, locals_):
    slots = owners.size
    per_owner = slots // devices
    rows = slots // LANES
    halves = per_owner // LANES if per_owner % LANES == 0 else 0
    asked = (devices * halves, LANES) if halves else (devices, per_owner)
    return call(
        partial(route_kernel, devices, per_owner),
        [HBM, HBM],
        [(asked, i32), ((devices, per_owner), i32), ((rows, LANES), i32)],
        [(owners.shape, i32)] * 2 + [((rows, LANES), i32)] * 3 + [pltpu.SemaphoreType.DMA((2,))],
        1 << 30,
        "route",
        vmem=63 << 20,
    )(owners, locals_)


def shade(camera_frame, view_angles, gaussians):
    rows = gaussians.shape[1] // LANES
    return call(
        partial(shade_kernel, camera_frame),
        [SMEM, VMEM],
        [((sum(PARTS) * rows // 2, WIDE), bf16), ((16 * rows, LANES), f32)],
        [((27 * rows, LANES), f32)],
        1 << 30,
        "shade",
    )(view_angles, gaussians)


def pick(layout, table, asked):
    return call(
        partial(pick_kernel, layout),
        [VMEM, VMEM],
        [((PROJ * layout.count, LANES), f32)],
        [],
        1 << 30,
        "pick",
    )(table, asked)[0]


def render(layout, list_counts, tile_order, rows, pos, back, cotangent):
    slot_rows = pos.shape[0]
    groups = tile_order.shape[0] // GROUP
    slots = slot_rows * LANES
    return call(
        partial(render_kernel, layout),
        [SMEM, SMEM, VMEM, VMEM, VMEM, VMEM],
        [(cotangent.shape, f32), ((PROJ * layout.count, LANES), f32)],
        [
            ((sum(PARTS) * slot_rows // 2, WIDE), bf16),
            ((2 * PROJ * slot_rows // 2, WIDE), bf16),
            ((PROJ * slot_rows, LANES), f32),
            ((24 * slot_rows, LANES), f32),
            ((24 * groups, PIX), f32),
            ((groups, 96, 2 * PIX), bf16),
            ((64, slots), bf16),
            ((slots, PIX), f32),
            ((slots, PIX), f32),
            ((slots, PIX), f32),
            ((16 * slot_rows, LANES), f32),
        ],
        1 << 34,
        "render",
    )(list_counts, tile_order, rows, pos, back, cotangent)


def collect(layout, camera_frame, view_angles, shape, dense, asked, terms):
    rows = shape[1] // LANES
    lows = shape[1] // WIDE
    return call(
        partial(collect_kernel, layout, camera_frame),
        [SMEM, VMEM, VMEM, VMEM],
        [(shape, f32)],
        [
            ((2 * PROJ * lows, layout.count * LANES), bf16),
            ((WIDE, layout.count * LANES), bf16),
            ((2 * PROJ * lows, WIDE), f32),
            ((16 * rows, LANES), f32),
            (shape, f32),
            pltpu.SemaphoreType.DMA((8,)),
        ],
        1 << 32,
        "collect",
        out_spec=HBM,
    )(view_angles, dense, asked, terms)[0]


def swap_requests(layout, devices, want):
    if layout.halves < 2:
        return lax.all_to_all(want, "dev", split_axis=0, concat_axis=0, tiled=True)
    planes = devices // PLANE
    in_plane = [[plane * PLANE + one for one in range(PLANE)] for plane in range(planes)]
    across = [[plane * PLANE + one for plane in range(planes)] for one in range(PLANE)]
    near = lax.all_to_all(want, "dev", split_axis=0, concat_axis=0, axis_index_groups=in_plane, tiled=True)
    near = near.reshape(PLANE, planes, layout.halves, LANES).transpose(1, 0, 2, 3).reshape(want.shape)
    return lax.all_to_all(near, "dev", split_axis=0, concat_axis=0, axis_index_groups=across, tiled=True)


def swap_rows(layout, devices, rows):
    if layout.halves:
        apart = rows.reshape(devices * PROJ, layout.halves, LANES)
        return lax.all_to_all(apart, "dev", split_axis=0, concat_axis=0, tiled=True).reshape(rows.shape)
    apart = rows.reshape(PROJ, devices, layout.count * LANES // devices)
    return lax.all_to_all(apart, "dev", split_axis=1, concat_axis=1, tiled=True).reshape(rows.shape)


def shards(gaussians, view_angles, tile_order, tile_owners, tile_locals, list_counts, image_cotangent):
    devices = lax.axis_size("dev")
    tiles_y = devices * tile_order.shape[0] // TX
    camera_frame = (4.0 * TX, 4.0 * tiles_y, 8.0 * TX, 8.0 * tiles_y)
    layout = Rows(devices, tile_owners.size // devices)
    want, back, pos = route(devices, tile_owners, tile_locals)
    asked = swap_requests(layout, devices, want)
    table, dense = shade(camera_frame, view_angles, gaussians)
    if not layout.halves:
        asked = asked.reshape(layout.count, LANES)
    if layout.halves != 2:
        back = back.reshape(layout.count, LANES)
    arrived = swap_rows(layout, devices, pick(layout, table, asked))
    rendered, slot_grads = render(layout, list_counts, tile_order, arrived, pos, back, image_cotangent)
    terms = swap_rows(layout, devices, slot_grads)
    gradients = collect(layout, camera_frame, view_angles, gaussians.shape, dense, asked, terms)
    return (rendered, gradients)


def solution(mesh):
    return jax.shard_map(
        shards,
        mesh=mesh,
        in_specs=(
            P(None, "dev"),
            P(),
            P("dev"),
            P("dev", None),
            P("dev", None),
            P("dev"),
            P(None, "dev"),
        ),
        out_specs=(P(None, "dev"), P(None, "dev")),
        check_vma=False,
    )
```

```python
from functools import partial

import jax
import jax.numpy as jnp
from jax import lax
from jax.experimental import pallas as pl
from jax.experimental.pallas import tpu as pltpu
from jax.sharding import PartitionSpec as P

PIX = 256
TX = 32
LANES = 128
PROJ = 9
GROUP = 8
WIDE = 2 * LANES
PARTS = (3, 3, 3, 3, 3, 2, 2, 2, 2)
STEP = LANES // GROUP
LOG2E = 1.4426950408889634
AHEAD = 2
VMEM_BYTES = 52 * 1024 * 1024

f32 = jnp.float32
bf16 = jnp.bfloat16
i32 = jnp.int32


def iota(shape, dim):
    return lax.broadcasted_iota(i32, shape, dim)


def lane_pick(row, lanes):
    source = jnp.broadcast_to(row, lanes.shape)
    return jnp.take_along_axis(source, lanes, axis=1, mode="promise_in_bounds")


def split_two(values):
    first = values.astype(bf16).astype(f32)
    return first, values - first


def split_three(values):
    first, rest = split_two(values)
    second, third = split_two(rest)
    return first, second, third


def dot(lhs, rhs):
    return lax.dot_general(lhs, rhs, (((1,), (0,)), ((), ())), preferred_element_type=f32)


def dot_nt(lhs, rhs):
    return lax.dot_general(lhs, rhs, (((1,), (1,)), ((), ())), preferred_element_type=f32)


def dot_tn(lhs, rhs):
    return lax.dot_general(lhs, rhs, (((0,), (0,)), ((), ())), preferred_element_type=f32)


class Rows:
    def __init__(self, devices, per_owner):
        self.halves = per_owner // LANES if per_owner % LANES == 0 else 0
        self.count = devices * per_owner // LANES

    def row(self, channel, major, minor):
        halves = self.halves
        if halves == 0:
            return channel * self.count + major
        return major * (PROJ * halves) + channel * halves + minor

    def half(self, ref, channel, half):
        halves = self.halves
        if halves == 0:
            return ref[pl.ds(channel * self.count + half, self.count // 2, stride=2), :]
        return jnp.concatenate(
            [ref[pl.ds(self.row(channel, one // halves, one % halves), 1), :] for one in range(half, self.count, 2)], axis=0
        ) if halves != 2 else ref[pl.ds(channel * 2 + half, self.count // 2, stride=2 * PROJ), :]

    def minors(self):
        return max(self.halves, 1)


def narrow(ids):
    return ids.astype(f32).astype(bf16)


def one_hot(ids, every):
    return jnp.where(narrow(ids) == every, jnp.ones((), bf16), jnp.zeros((), bf16))


def put_terms(lhs_s, channel, lanes, row, mine):
    lows = mine.shape[0]
    row = jnp.broadcast_to(row, (16, LANES))
    first = row.astype(bf16)
    second = (row - first.astype(f32)).astype(bf16)
    for part, value in enumerate((first, second)):
        for low in range(0, lows, 16):
            start = (part * PROJ + channel) * lows + low
            lhs_s[start : start + 16, lanes] = mine[low : low + 16] * value


def pick_slots(parts, hot, slots, low_id, put):
    found = dot(parts, hot)
    mine = slots // WIDE == low_id
    lows = low_id.shape[0]
    first = 0
    for channel, count in enumerate(PARTS if parts.shape[0] == sum(PARTS) * lows else (2,) * PROJ):
        value = found[first * lows : (first + 1) * lows]
        for part in range(1, count):
            value = value + found[(first + part) * lows : (first + part + 1) * lows]
        first += count
        put(channel, jnp.sum(jnp.where(mine, value, 0.0), axis=0, keepdims=True))


def put_parts(parts_ref, channel, half, value, counts, lows=None, low=0):
    lows = lows or value.shape[0]
    first = sum(counts[:channel])
    parts = split_three(value) if counts[channel] == 3 else split_two(value)
    for part, one in enumerate(parts):
        at = (first + part) * lows + low
        parts_ref[at : at + value.shape[0], half * LANES : (half + 1) * LANES] = one.astype(bf16)


def route_kernel(devices, per_owner, own_hbm, loc_hbm, want_ref, back_ref, pos_ref, own_ref, loc_ref, own_s, loc_s, rank_s, sems):
    copies = [pltpu.make_async_copy(own_hbm, own_ref, sems.at[0]), pltpu.make_async_copy(loc_hbm, loc_ref, sems.at[1])]
    for copy in copies:
        copy.start()
    for copy in copies:
        copy.wait()
    rows = own_s.shape[0]
    blocks = own_ref.shape[1] // LANES
    lane = iota((8, LANES), 1)
    from_slot = iota((8, LANES), 0) * STEP + lane // GROUP
    tile_of = lane % GROUP
    for group in range(own_ref.shape[0] // GROUP):
        for block in range(blocks):
            for source, target in ((own_ref, own_s), (loc_ref, loc_s)):
                part = source[group * GROUP : (group + 1) * GROUP, block * LANES : (block + 1) * LANES]
                out = jnp.zeros((8, LANES), i32)
                for tile in range(GROUP):
                    out = jnp.where(tile_of == tile, lane_pick(part[tile : tile + 1], from_slot), out)
                start = (group * blocks + block) * 8
                target[start : start + 8, :] = out
    owner = own_s[...]
    left = (iota((LANES, 2 * LANES), 0) < iota((LANES, 2 * LANES), 1)) | (iota((LANES, 2 * LANES), 1) >= LANES)
    above = iota((rows, rows), 1) < iota((rows, rows), 0)
    hits = jnp.concatenate([jnp.where(owner == one, 1.0, 0.0).astype(bf16) for one in range(devices)], axis=0)
    sums = dot(hits, jnp.where(left, 1.0, 0.0).astype(bf16))
    totals = jnp.concatenate(
        [sums[one * rows : (one + 1) * rows, LANES:].astype(bf16) for one in range(devices)], axis=1
    )
    base = dot(jnp.where(above, 1.0, 0.0).astype(bf16), totals)
    rank = jnp.zeros((rows, LANES), f32)
    for one in range(devices):
        here = sums[one * rows : (one + 1) * rows, :LANES] + base[:, one * LANES : (one + 1) * LANES]
        rank = jnp.where(owner == one, here, rank)
    rank = rank.astype(i32)
    pos_ref[...] = owner * per_owner + rank
    rank_s[...] = rank

    owner_id = iota((devices, LANES), 0)
    rank_id = narrow(iota((per_owner, LANES), 0))
    slot_lane = iota((devices, LANES), 1).astype(f32)

    def place(index, total):
        start = pl.multiple_of(index * 8, 8)
        own_rows = own_s[pl.ds(start, 8), :]
        loc_rows = loc_s[pl.ds(start, 8), :]
        rank_rows = rank_s[pl.ds(start, 8), :]
        high_rows = (loc_rows // LANES).astype(f32)
        low_rows = (loc_rows % LANES).astype(f32)
        lhs = []
        rhs = []
        for row in range(8):
            mine = own_rows[row : row + 1] == owner_id
            number = (start + row).astype(f32)
            lhs.append(
                jnp.concatenate(
                    [
                        jnp.where(mine, high_rows[row : row + 1], 0.0),
                        jnp.where(mine, low_rows[row : row + 1], 0.0),
                        jnp.where(mine, number, 0.0),
                        jnp.where(mine, slot_lane, 0.0),
                    ],
                    axis=0,
                ).astype(bf16)
            )
            rhs.append(one_hot(rank_rows[row : row + 1], rank_id))
        return total + dot_nt(jnp.concatenate(lhs, axis=1), jnp.concatenate(rhs, axis=1))

    total = lax.fori_loop(0, rows // 8, place, jnp.zeros((4 * devices, per_owner), f32), unroll=devices <= 32).astype(i32)
    want = total[:devices] * LANES + total[devices : 2 * devices]
    halves = per_owner // LANES
    if per_owner % LANES == 0 and halves > 1:
        for half in range(halves):
            want_ref[pl.ds(half, devices, stride=halves), :] = want[:, half * LANES : (half + 1) * LANES]
    else:
        want_ref[...] = want
    back_ref[...] = total[2 * devices : 3 * devices] * LANES + total[3 * devices :]


def view(angles_ref):
    angle = [jnp.full((1, LANES), angles_ref[index], f32) for index in range(3)]
    (cos_a, cos_b, cos_c) = [jnp.cos(one) for one in angle]
    (sin_a, sin_b, sin_c) = [jnp.sin(one) for one in angle]
    return [
        [cos_c * cos_b, cos_c * sin_b * sin_a - sin_c * cos_a, cos_c * sin_b * cos_a + sin_c * sin_a],
        [sin_c * cos_b, sin_c * sin_b * sin_a + cos_c * cos_a, sin_c * sin_b * cos_a - cos_c * sin_a],
        [-sin_b, cos_b * sin_a, cos_b * cos_a],
    ]


def harmonics(along_x, along_y, along_z):
    sq_x = along_x * along_x
    sq_y = along_y * along_y
    sq_z = along_z * along_z
    return [
        0.28209479177387814 + 0.0 * along_x,
        -0.4886025119029199 * along_y,
        0.4886025119029199 * along_z,
        -0.4886025119029199 * along_x,
        1.0925484305920792 * along_x * along_y,
        -1.0925484305920792 * along_y * along_z,
        0.31539156525252005 * (2.0 * sq_z - sq_x - sq_y),
        -1.0925484305920792 * along_x * along_z,
        0.5462742152960396 * (sq_x - sq_y),
        -0.5900435899266435 * along_y * (3.0 * sq_x - sq_y),
        2.890611442640554 * along_x * along_y * along_z,
        -0.4570457994644658 * along_y * (4.0 * sq_z - sq_x - sq_y),
        0.3731763325901154 * along_z * (2.0 * sq_z - 3.0 * sq_x - 3.0 * sq_y),
        -0.4570457994644658 * along_x * (4.0 * sq_z - sq_x - sq_y),
        1.445305721320277 * along_z * (sq_x - sq_y),
        -0.5900435899266435 * along_x * (sq_x - 3.0 * sq_y),
    ]


def basis_rows(basis, eighth):
    sub = iota((8, LANES), 0)
    found = []
    for colour in range(3):
        out = None
        for inner in range(8):
            index = 8 * eighth + inner - 11 - 16 * colour
            if 0 <= index < 16:
                out = jnp.zeros((8, LANES), f32) if out is None else out
                out = jnp.where(sub == inner, basis[index], out)
        found.append(out)
    return found


def shape_of(columns, rotation, camera_frame):
    focal_x, focal_y, centre_x, centre_y = camera_frame
    positions = columns[0:3]
    cam_first = rotation[0][0] * positions[0] + rotation[0][1] * positions[1] + rotation[0][2] * positions[2]
    cam_second = rotation[1][0] * positions[0] + rotation[1][1] * positions[1] + rotation[1][2] * positions[2]
    mean_x = centre_x + focal_x * cam_first
    mean_y = centre_y + focal_y * cam_second
    scales = [jnp.exp(one) for one in columns[3:6]]
    quat_w, quat_x, quat_y, quat_z = columns[6:10]
    norm_sq = jnp.maximum(quat_w * quat_w + quat_x * quat_x + quat_y * quat_y + quat_z * quat_z, 1.0)
    twice = 2.0 / norm_sq
    turned = [
        [
            1.0 - twice * (quat_y * quat_y + quat_z * quat_z),
            twice * (quat_x * quat_y - quat_w * quat_z),
            twice * (quat_x * quat_z + quat_w * quat_y),
        ],
        [
            twice * (quat_x * quat_y + quat_w * quat_z),
            1.0 - twice * (quat_x * quat_x + quat_z * quat_z),
            twice * (quat_y * quat_z - quat_w * quat_x),
        ],
        [
            twice * (quat_x * quat_z - quat_w * quat_y),
            twice * (quat_y * quat_z + quat_w * quat_x),
            1.0 - twice * (quat_x * quat_x + quat_y * quat_y),
        ],
    ]
    rows = []
    for focal, turn in ((focal_x, rotation[0]), (focal_y, rotation[1])):
        rows.append(
            [
                focal * (turn[0] * turned[0][k] + turn[1] * turned[1][k] + turn[2] * turned[2][k]) * scales[k]
                for k in range(3)
            ]
        )
    first, second = rows
    cov_a = first[0] * first[0] + first[1] * first[1] + first[2] * first[2] + 0.3
    cov_b = first[0] * second[0] + first[1] * second[1] + first[2] * second[2]
    cov_c = second[0] * second[0] + second[1] * second[1] + second[2] * second[2] + 0.3
    determinant = cov_a * cov_c - cov_b * cov_b
    opacity = 1.0 / (1.0 + jnp.exp(-columns[10]))
    return mean_x, mean_y, cov_c / determinant, -cov_b / determinant, cov_a / determinant, opacity


def spread_columns(gauss_ref, dense_s):
    rows = gauss_ref.shape[1] // LANES
    for row in range(rows):
        for eighth in range(2):
            dense_s[pl.ds(8 * eighth * rows + row, 8, stride=rows), :] = gauss_ref[
                8 * eighth : 8 * eighth + 8, row * LANES : (row + 1) * LANES
            ]


def shade_kernel(camera_frame, angles_ref, gauss_ref, parts_ref, dense_s, tint_s):
    rows = gauss_ref.shape[1] // LANES
    spread_columns(gauss_ref, dense_s)
    rotation = view(angles_ref)
    basis = harmonics(*rotation[2])
    patterns = [basis_rows(basis, eighth) for eighth in range(7)]
    for row in range(rows):
        lanes = slice(row * LANES, (row + 1) * LANES)
        tints = [None] * 3
        for eighth in range(1, 7):
            block = gauss_ref[8 * eighth : 8 * eighth + 8, lanes]
            for colour in range(3):
                pattern = patterns[eighth][colour]
                if pattern is not None:
                    term = block * pattern
                    tints[colour] = term if tints[colour] is None else tints[colour] + term
        for colour in range(3):
            tint_s[pl.ds(8 * colour * rows + row, 8, stride=rows), :] = tints[colour]
        tint_s[pl.ds(24 * rows + row, 3, stride=rows), :] = gauss_ref[56:59, lanes]
    for part in range(rows // 16):
        half = part % 2
        low = part // 2 * 16
        at = [pl.ds(index * rows + 2 * low + half, 16, stride=2) for index in range(27)]
        columns = [dense_s[one, :] for one in at[:11]]
        for index, value in enumerate(shape_of(columns, rotation, camera_frame)):
            put_parts(parts_ref, index, half, value, PARTS, rows // 2, low)
        for colour in range(3):
            total = 0.5
            for inner in range(8):
                total = total + tint_s[at[8 * colour + inner], :]
            if colour == 2:
                for inner in range(3):
                    total = total + basis[13 + inner] * tint_s[at[24 + inner], :]
            put_parts(parts_ref, 6 + colour, half, total, PARTS, rows // 2, low)


def pick_kernel(layout, parts_ref, asked_ref, out_ref):
    low_id = iota((parts_ref.shape[0] // sum(PARTS), WIDE), 0)
    high_id = narrow(iota((WIDE, WIDE), 0))
    minors = layout.minors()

    for index in range(layout.count // 2):
        slots = jnp.concatenate([asked_ref[2 * index + one : 2 * index + one + 1, :] for one in range(2)], axis=1)

        def put(channel, value):
            for one in range(2):
                at = layout.row(channel, (2 * index + one) // minors, (2 * index + one) % minors)
                out_ref[at : at + 1, :] = value[:, one * LANES : (one + 1) * LANES]

        pick_slots(parts_ref[...], one_hot(slots % WIDE, high_id), slots, low_id, put)


def render_kernel(
    layout,
    count_ref,
    order_ref,
    rows_ref,
    pos_ref,
    back_ref,
    cot_ref,
    image_hbm,
    out_ref,
    image_ref,
    image_sem,
    in_s,
    out_s,
    raw_s,
    coef_s,
    cot_s,
    rhs_s,
    tint_s,
    alpha_s,
    shade_s,
    weight_s,
    sums_s,
):
    slot_rows = pos_ref.shape[0]
    groups = cot_ref.shape[1] // (GROUP * PIX)
    chunks = slot_rows // groups
    sub = iota((8, LANES), 0)
    lane = iota((8, LANES), 1)
    tile_of = lane % GROUP
    blocks = slot_rows // 8
    middles = []
    for group in range(groups):
        middle_x = jnp.zeros((8, LANES), f32)
        middle_y = jnp.zeros((8, LANES), f32)
        live = jnp.zeros((8, LANES), i32)
        for tile in range(GROUP):
            shown = order_ref[group * GROUP + tile]
            here = tile_of == tile
            middle_x = jnp.where(here, (shown % TX * 16 + 8).astype(f32), middle_x)
            middle_y = jnp.where(here, (shown // TX * 16 + 8).astype(f32), middle_y)
            live = jnp.where(here, count_ref[group * GROUP + tile], live)
        middles.append((middle_x, middle_y, live))

    for half in range(2):
        for channel in range(PROJ):
            put_parts(in_s, channel, half, layout.half(rows_ref, channel, half), PARTS)
    low_id = iota((slot_rows // 2, WIDE), 0)
    high_id = narrow(iota((WIDE, WIDE), 0))

    def pick_in(row):
        slots = jnp.concatenate([pos_ref[row + one : row + one + 1, :] for one in range(2)], axis=1)

        def put(channel, value):
            for one in range(2):
                at = channel * slot_rows + row + one
                raw_s[at : at + 1, :] = value[:, one * LANES : (one + 1) * LANES]

        pick_slots(in_s[...], one_hot(slots % WIDE, high_id), slots, low_id, put)

    def quadratics(block):
        group = block * 8 // chunks
        middle_x, middle_y, live = middles[group]
        found = [
            raw_s[channel * slot_rows + 8 * block : channel * slot_rows + 8 * block + 8, :] for channel in range(PROJ)
        ]
        at_x = found[0] - middle_x
        at_y = found[1] - middle_y
        quad_a = -0.5 * found[2]
        quad_b = -found[3]
        quad_c = -0.5 * found[4]
        flat = quad_a * at_x * at_x + quad_c * at_y * at_y + quad_b * at_x * at_y + jnp.log(found[5])
        place = (8 * block - group * chunks + sub) * STEP + lane // GROUP
        terms = (
            quad_a * LOG2E,
            quad_b * LOG2E,
            quad_c * LOG2E,
            (-2.0 * quad_a * at_x - quad_b * at_y) * LOG2E,
            (-2.0 * quad_c * at_y - quad_b * at_x) * LOG2E,
            jnp.where(place < live, flat * LOG2E, -1e30),
        )
        for index, term in enumerate(terms):
            for part, value in enumerate(split_three(term)):
                coef_s[pl.ds(8 * block * 24 + 6 * part + index, 8, stride=24), :] = value
        for colour in range(3):
            for part, value in enumerate(split_two(found[6 + colour])):
                coef_s[pl.ds(8 * block * 24 + 18 + 3 * part + colour, 8, stride=24), :] = value

    pixel = iota((24, PIX), 1)
    row = iota((24, PIX), 0)
    pix_x = (pixel % 16).astype(f32) - 7.5
    pix_y = (pixel // 16).astype(f32) - 7.5
    kind = row % 6
    monomials = jnp.where(kind == 0, pix_x * pix_x, jnp.where(kind == 1, pix_x * pix_y, 1.0))
    monomials = jnp.where(kind == 2, pix_y * pix_y, monomials)
    monomials = jnp.where(kind == 3, pix_x, jnp.where(kind == 4, pix_y, monomials))
    moments = jnp.where(iota((8, PIX), 0) < 6, monomials[0:8], 0.0).astype(bf16)
    monomials = jnp.where(row < 18, monomials, 0.0)
    nothing = jnp.zeros((24, PIX), f32)
    for group in range(groups):
        for colour in range(3):
            for tile in range(GROUP):
                start = (group * GROUP + tile) * PIX
                cot_s[group * 24 + colour * GROUP + tile, :] = cot_ref[colour, start : start + PIX]
    cots = []
    spare = jnp.zeros((8, PIX), f32)
    for group in range(groups):
        first, second = split_two(cot_s[group * 24 : (group + 1) * 24, :])
        cots.append(jnp.concatenate([first, spare, second, spare], axis=0).astype(bf16))
        rhs_s[group] = jnp.concatenate(
            [
                jnp.concatenate([jnp.concatenate([nothing, monomials[8 * one : 8 * one + 8]], axis=0) for one in range(3)], axis=0),
                jnp.concatenate([first, spare, first, spare, second, spare], axis=0),
            ],
            axis=1,
        ).astype(bf16)

    own_tile = sub == tile_of
    own_pair = iota((8, WIDE), 0) == iota((8, WIDE), 1) % GROUP

    def evaluate(index):
        for group in range(groups):
            chunk = group * chunks + index
            coefs = coef_s[chunk * 24 : (chunk + 1) * 24, :]
            tints = [jnp.where(own_tile, coefs[18 + one : 19 + one], 0.0) for one in range(6)]
            lhs = jnp.concatenate(
                tints[:3] + [coefs[0:8]] + tints[3:] + [coefs[8:16]] + tints[:3] + [coefs[16:24]], axis=0
            ).astype(bf16)
            both = dot_tn(lhs, rhs_s[group])
            lanes = slice(chunk * LANES, (chunk + 1) * LANES)
            tint_s[:, lanes] = lhs[0:64]
            alpha_s[lanes, :] = jnp.exp2(both[:, :PIX])
            shade_s[lanes, :] = both[:, PIX:]

    def scan(index, trans):
        out = []
        for group in range(groups):
            one = trans[group]
            start = (group * chunks + index) * LANES
            for step in range(STEP):
                alpha = alpha_s[pl.ds(start + step * GROUP, GROUP), :]
                weight = one * alpha
                one = one - weight
                weight_s[pl.ds(start + step * GROUP, GROUP), :] = weight
            out.append(one)
        return tuple(out)

    def paint(index, images):
        out = []
        for group in range(groups):
            chunk = group * chunks + index
            both = slice(chunk * LANES, chunk * LANES + WIDE)
            first, second = split_two(weight_s[both, :])
            first = first.astype(bf16)
            second = second.astype(bf16)
            tints = tint_s[:, both]
            by_first = dot(tints, first)
            out.append(images[group] + by_first[0:24] + by_first[32:56] + dot(tints[0:32], second)[0:24])
            by_first = dot_nt(cots[group], first)
            tint_grad = by_first[0:24] + by_first[32:56] + dot_nt(cots[group][0:32], second)[0:24]
            for colour in range(3):
                own = jnp.where(own_pair, tint_grad[colour * GROUP : (colour + 1) * GROUP], 0.0)
                own = jnp.sum(own, axis=0, keepdims=True)
                for one in range(2):
                    sums_s[(chunk + one) * 16 + 8 + colour : (chunk + one) * 16 + 9 + colour, :] = own[:, one * LANES : (one + 1) * LANES]
        return tuple(out)

    trans = tuple(jnp.ones((GROUP, PIX), f32) for _ in range(groups))
    images = tuple(jnp.zeros((24, PIX), f32) for _ in range(groups))
    per_group = chunks // 8
    for block in range(0, blocks, per_group):
        for row in range(0, 8, 2):
            pick_in(8 * block + row)
        quadratics(block)
    for pair in range(-AHEAD, chunks // 2 + 1):
        step = pair + AHEAD + 4
        if 4 <= step < chunks // 2:
            for group in range(groups):
                block = group * per_group + step // 4
                pick_in(8 * block + step % 4 * 2)
                if step % 4 == 3:
                    quadratics(block)
        for one in range(2):
            if pair + AHEAD < chunks // 2:
                evaluate(2 * (pair + AHEAD) + one)
        for one in range(2):
            if 0 <= pair < chunks // 2:
                trans = scan(2 * pair + one, trans)
        if pair > 0:
            images = paint(2 * (pair - 1), images)
    for group in range(groups):
        for colour in range(3):
            for tile in range(GROUP):
                at = (group * GROUP + tile) * PIX
                image_ref[colour, at : at + PIX] = images[group][colour * GROUP + tile]
    image_copy = pltpu.make_async_copy(image_ref, image_hbm, image_sem)
    image_copy.start()

    def moment(index):
        for group in range(groups):
            chunk = group * chunks + index
            first, second = split_two(shade_s[slice(chunk * LANES, chunk * LANES + WIDE), :])
            found = dot_nt(moments, first.astype(bf16)) + dot_nt(moments, second.astype(bf16))
            for one in range(2):
                start = (chunk + one) * 16
                sums_s[start : start + 8, :] = found[:, one * LANES : (one + 1) * LANES]

    def rescan(index, behinds):
        out = []
        for group in range(groups):
            behind = behinds[group]
            start = (group * chunks + index) * LANES
            for step in reversed(range(STEP)):
                at = pl.ds(start + step * GROUP, GROUP)
                ahead = shade_s[at, :] - behind
                shade_s[at, :] = weight_s[at, :] * ahead
                behind = behind + alpha_s[at, :] * ahead
            out.append(behind)
        return tuple(out)

    behinds = tuple(jnp.zeros((GROUP, PIX), f32) for _ in range(groups))
    for pair in reversed(range(-1, chunks // 2)):
        for one in reversed(range(2)):
            if pair >= 0:
                behinds = rescan(2 * pair + one, behinds)
        if pair + 1 < chunks // 2:
            moment(2 * (pair + 1))

    slot_s = coef_s
    for block in range(blocks):
        middle_x, middle_y, _ = middles[block * 8 // chunks]
        at = slice(8 * block, 8 * block + 8)
        raw = [raw_s[channel * slot_rows + 8 * block : channel * slot_rows + 8 * block + 8, :] for channel in range(6)]
        (sum_xx, sum_xy, sum_yy, sum_x, sum_y, sum_one) = [
            sums_s[pl.ds(8 * block * 16 + index, 8, stride=16), :] for index in range(6)
        ]
        at_x = raw[0] - middle_x
        at_y = raw[1] - middle_y
        off_x = sum_x - at_x * sum_one
        off_y = sum_y - at_y * sum_one
        grads = [
            raw[2] * off_x + raw[3] * off_y,
            raw[4] * off_y + raw[3] * off_x,
            -0.5 * (sum_xx - at_x * (sum_x + off_x)),
            -(sum_xy - at_y * sum_x - at_x * off_y),
            -0.5 * (sum_yy - at_y * (sum_y + off_y)),
            sum_one / raw[5],
        ] + [sums_s[pl.ds(8 * block * 16 + 8 + colour, 8, stride=16), :] for colour in range(3)]
        for channel, value in enumerate(grads):
            slot_s[channel * slot_rows + 8 * block : channel * slot_rows + 8 * block + 8, :] = value

    for half in range(2):
        for channel in range(PROJ):
            value = slot_s[pl.ds(channel * slot_rows + half, slot_rows // 2, stride=2), :]
            put_parts(out_s, channel, half, value, (2,) * PROJ)
    minors = layout.minors()

    def pick_out(index, _):
        if layout.halves == 2:
            slots = back_ref[pl.ds(index, 1), :]
        else:
            slots = jnp.concatenate([back_ref[pl.ds(2 * index + one, 1), :] for one in range(2)], axis=1)

        def put(channel, value):
            for one in range(2):
                at = layout.row(channel, (2 * index + one) // minors, (2 * index + one) % minors)
                out_ref[pl.ds(at, 1), :] = value[:, one * LANES : (one + 1) * LANES]

        pick_slots(out_s[...], one_hot(slots % WIDE, high_id), slots, low_id, put)
        return 0

    lax.fori_loop(0, layout.count // 2, pick_out, 0, unroll=True)
    image_copy.wait()


def collect_kernel(
    layout, camera_frame, angles_ref, dense_ref, asked_ref, terms_ref, grad_hbm, lhs_s, rhs_s, total_s, out_s, grad_ref, sems
):
    gauss = grad_ref.shape[1]
    rows = gauss // LANES
    lows = gauss // WIDE
    low_id = narrow(iota((lows, LANES), 0))
    high_id = narrow(iota((WIDE, LANES), 0))
    minors = layout.minors()

    for index in range(layout.count // 8):
        asked = asked_ref[8 * index : 8 * index + 8, :]
        low = asked // WIDE
        high = asked % WIDE
        for row in range(8):
            lanes = slice((8 * index + row) * LANES, (8 * index + row + 1) * LANES)
            mine = one_hot(low[row : row + 1], low_id)
            rhs_s[:, lanes] = one_hot(high[row : row + 1], high_id)
            for channel in range(PROJ):
                at = layout.row(channel, (8 * index + row) // minors, row % minors)
                put_terms(lhs_s, channel, lanes, terms_ref[at : at + 1, :], mine)
        if index % 2 == 1:
            lanes = slice(8 * (index - 1) * LANES, 8 * (index + 1) * LANES)
            found = dot_nt(lhs_s[:, lanes], rhs_s[:, lanes])
            total_s[...] = found if index == 1 else total_s[...] + found
    rotation = view(angles_ref)
    basis = harmonics(*rotation[2])
    for part in range(rows // 8):
        half = part % 2
        low = part // 2 * 8
        lanes = slice(half * LANES, (half + 1) * LANES)
        sums = [
            total_s[channel * lows + low : channel * lows + low + 8, lanes]
            + total_s[(PROJ + channel) * lows + low : (PROJ + channel) * lows + low + 8, lanes]
            for channel in range(PROJ)
        ]
        columns = tuple(dense_ref[pl.ds(index * rows + 2 * low + half, 8, stride=2), :] for index in range(11))
        _, pullback = jax.vjp(lambda *values: shape_of(values, rotation, camera_frame), *columns)
        grads = pullback(tuple(sums[:6]))
        for index, value in enumerate(tuple(grads) + tuple(sums[6:])):
            out_s[pl.ds(index * rows + 2 * low + half, 8, stride=2), :] = value
    sub = iota((8, LANES), 0)
    patterns = [basis_rows(basis, eighth) for eighth in range(8)]
    copies = []
    pieces = sems.shape[0]
    wide = gauss // pieces
    for row in range(rows):
        lanes = slice(row * LANES, (row + 1) * LANES)
        grad_ref[0:8, lanes] = out_s[pl.ds(row, 8, stride=rows), :]
        tints = [out_s[(11 + colour) * rows + row : (11 + colour) * rows + row + 1, :] for colour in range(3)]
        for eighth in range(1, 8):
            value = None
            for colour in range(3):
                pattern = patterns[eighth][colour]
                if pattern is not None:
                    term = pattern * tints[colour]
                    value = term if value is None else value + term
            if eighth == 1:
                value = jnp.where(sub < 3, out_s[pl.ds(8 * rows + row, 8, stride=rows), :], value)
            if eighth == 7:
                grad_ref[56:59, lanes] = value[0:3]
            else:
                grad_ref[8 * eighth : 8 * eighth + 8, lanes] = value
        if (row + 1) * LANES % wide == 0:
            piece = len(copies)
            span = slice(piece * wide, (piece + 1) * wide)
            copies.append(pltpu.make_async_copy(grad_ref.at[:, span], grad_hbm.at[:, span], sems.at[piece]))
            copies[-1].start()
    for copy in copies:
        copy.wait()


VMEM = pl.BlockSpec(memory_space=pltpu.VMEM)
HBM = pl.BlockSpec(memory_space=pltpu.HBM)
SMEM = pl.BlockSpec(memory_space=pltpu.SMEM)


def call(kernel, specs, outs, scratch, flops, name, out_spec=VMEM, vmem=VMEM_BYTES):
    return pl.pallas_call(
        kernel,
        in_specs=specs,
        out_specs=list(out_spec) if isinstance(out_spec, tuple) else [out_spec] * len(outs),
        out_shape=[jax.ShapeDtypeStruct(shape, dtype) for shape, dtype in outs],
        scratch_shapes=[pltpu.VMEM(*one) if isinstance(one, tuple) else one for one in scratch],
        compiler_params=pltpu.CompilerParams(vmem_limit_bytes=vmem),
        cost_estimate=pl.CostEstimate(flops=flops, bytes_accessed=4 << 20, transcendentals=0),
        name=name,
    )


def route(devices, owners, locals_):
    slots = owners.size
    per_owner = slots // devices
    rows = slots // LANES
    halves = per_owner // LANES if per_owner % LANES == 0 else 0
    asked = (devices * halves, LANES) if halves else (devices, per_owner)
    return call(
        partial(route_kernel, devices, per_owner),
        [HBM, HBM],
        [(asked, i32), ((devices, per_owner), i32), ((rows, LANES), i32)],
        [(owners.shape, i32)] * 2 + [((rows, LANES), i32)] * 3 + [pltpu.SemaphoreType.DMA((2,))],
        1 << 30,
        "route",
        vmem=63 << 20,
    )(owners, locals_)


def shade(camera_frame, view_angles, gaussians):
    rows = gaussians.shape[1] // LANES
    return call(
        partial(shade_kernel, camera_frame),
        [SMEM, VMEM],
        [((sum(PARTS) * rows // 2, WIDE), bf16), ((16 * rows, LANES), f32)],
        [((27 * rows, LANES), f32)],
        1 << 30,
        "shade",
    )(view_angles, gaussians)


def pick(layout, table, asked):
    return call(
        partial(pick_kernel, layout),
        [VMEM, VMEM],
        [((PROJ * layout.count, LANES), f32)],
        [],
        1 << 30,
        "pick",
    )(table, asked)[0]


def render(layout, list_counts, tile_order, rows, pos, back, cotangent):
    slot_rows = pos.shape[0]
    groups = tile_order.shape[0] // GROUP
    slots = slot_rows * LANES
    return call(
        partial(render_kernel, layout),
        [SMEM, SMEM, VMEM, VMEM, VMEM, VMEM],
        [(cotangent.shape, f32), ((PROJ * layout.count, LANES), f32)],
        [
            (cotangent.shape, f32),
            pltpu.SemaphoreType.DMA,
            ((sum(PARTS) * slot_rows // 2, WIDE), bf16),
            ((2 * PROJ * slot_rows // 2, WIDE), bf16),
            ((PROJ * slot_rows, LANES), f32),
            ((24 * slot_rows, LANES), f32),
            ((24 * groups, PIX), f32),
            ((groups, 96, 2 * PIX), bf16),
            ((64, slots), bf16),
            ((slots, PIX), f32),
            ((slots, PIX), f32),
            ((slots, PIX), f32),
            ((16 * slot_rows, LANES), f32),
        ],
        1 << 34,
        "render",
        out_spec=(HBM, VMEM),
    )(list_counts, tile_order, rows, pos, back, cotangent)


def collect(layout, camera_frame, view_angles, shape, dense, asked, terms):
    rows = shape[1] // LANES
    lows = shape[1] // WIDE
    return call(
        partial(collect_kernel, layout, camera_frame),
        [SMEM, VMEM, VMEM, VMEM],
        [(shape, f32)],
        [
            ((2 * PROJ * lows, layout.count * LANES), bf16),
            ((WIDE, layout.count * LANES), bf16),
            ((2 * PROJ * lows, WIDE), f32),
            ((16 * rows, LANES), f32),
            (shape, f32),
            pltpu.SemaphoreType.DMA((8,)),
        ],
        1 << 32,
        "collect",
        out_spec=HBM,
    )(view_angles, dense, asked, terms)[0]


def swap_rows(layout, devices, rows):
    if layout.halves:
        apart = rows.reshape(devices * PROJ, layout.halves, LANES)
        return lax.all_to_all(apart, "dev", split_axis=0, concat_axis=0, tiled=True).reshape(rows.shape)
    apart = rows.reshape(PROJ, devices, layout.count * LANES // devices)
    return lax.all_to_all(apart, "dev", split_axis=1, concat_axis=1, tiled=True).reshape(rows.shape)


def shards(gaussians, view_angles, tile_order, tile_owners, tile_locals, list_counts, image_cotangent):
    devices = lax.axis_size("dev")
    tiles_y = devices * tile_order.shape[0] // TX
    camera_frame = (4.0 * TX, 4.0 * tiles_y, 8.0 * TX, 8.0 * tiles_y)
    layout = Rows(devices, tile_owners.size // devices)
    want, back, pos = route(devices, tile_owners, tile_locals)
    asked = lax.all_to_all(want, "dev", split_axis=0, concat_axis=0, tiled=True)
    table, dense = shade(camera_frame, view_angles, gaussians)
    if not layout.halves:
        asked = asked.reshape(layout.count, LANES)
    if layout.halves != 2:
        back = back.reshape(layout.count, LANES)
    arrived = swap_rows(layout, devices, pick(layout, table, asked))
    rendered, slot_grads = render(layout, list_counts, tile_order, arrived, pos, back, image_cotangent)
    terms = swap_rows(layout, devices, slot_grads)
    gradients = collect(layout, camera_frame, view_angles, gaussians.shape, dense, asked, terms)
    return (rendered, gradients)


def solution(mesh):
    return jax.shard_map(
        shards,
        mesh=mesh,
        in_specs=(
            P(None, "dev"),
            P(),
            P("dev"),
            P("dev", None),
            P("dev", None),
            P("dev"),
            P(None, "dev"),
        ),
        out_specs=(P(None, "dev"), P(None, "dev")),
        check_vma=False,
    )
```

```python
from functools import partial

import jax
import jax.numpy as jnp
from jax import lax
from jax.experimental import pallas as pl
from jax.experimental.pallas import tpu as pltpu
from jax.sharding import PartitionSpec as P

PIX = 256
TX = 32
LANES = 128
PROJ = 9
GROUP = 8
WIDE = 2 * LANES
PARTS = (3, 3, 3, 3, 3, 2, 2, 2, 2)
STEP = LANES // GROUP
LOG2E = 1.4426950408889634
AHEAD = 2
VMEM_BYTES = 52 * 1024 * 1024

f32 = jnp.float32
bf16 = jnp.bfloat16
i32 = jnp.int32


def iota(shape, dim):
    return lax.broadcasted_iota(i32, shape, dim)


def lane_pick(row, lanes):
    source = jnp.broadcast_to(row, lanes.shape)
    return jnp.take_along_axis(source, lanes, axis=1, mode="promise_in_bounds")


def split_two(values):
    first = values.astype(bf16).astype(f32)
    return first, values - first


def split_three(values):
    first, rest = split_two(values)
    second, third = split_two(rest)
    return first, second, third


def dot(lhs, rhs):
    return lax.dot_general(lhs, rhs, (((1,), (0,)), ((), ())), preferred_element_type=f32)


def dot_nt(lhs, rhs):
    return lax.dot_general(lhs, rhs, (((1,), (1,)), ((), ())), preferred_element_type=f32)


def dot_tn(lhs, rhs):
    return lax.dot_general(lhs, rhs, (((0,), (0,)), ((), ())), preferred_element_type=f32)


class Rows:
    def __init__(self, devices, per_owner):
        self.halves = per_owner // LANES if per_owner % LANES == 0 else 0
        self.count = devices * per_owner // LANES

    def row(self, channel, major, minor):
        halves = self.halves
        if halves == 0:
            return channel * self.count + major
        return major * (PROJ * halves) + channel * halves + minor

    def half(self, ref, channel, half):
        halves = self.halves
        if halves == 0:
            return ref[pl.ds(channel * self.count + half, self.count // 2, stride=2), :]
        return jnp.concatenate(
            [ref[pl.ds(self.row(channel, one // halves, one % halves), 1), :] for one in range(half, self.count, 2)], axis=0
        ) if halves != 2 else ref[pl.ds(channel * 2 + half, self.count // 2, stride=2 * PROJ), :]

    def minors(self):
        return max(self.halves, 1)


def narrow(ids):
    return ids.astype(f32).astype(bf16)


def one_hot(ids, every):
    return jnp.where(narrow(ids) == every, jnp.ones((), bf16), jnp.zeros((), bf16))


def put_terms(lhs_s, channel, lanes, row, mine):
    lows = mine.shape[0]
    row = jnp.broadcast_to(row, (16, LANES))
    first = row.astype(bf16)
    second = (row - first.astype(f32)).astype(bf16)
    for part, value in enumerate((first, second)):
        for low in range(0, lows, 16):
            start = (part * PROJ + channel) * lows + low
            lhs_s[start : start + 16, lanes] = mine[low : low + 16] * value


def pick_slots(parts, hot, slots, low_id, put):
    found = dot(parts, hot)
    mine = slots // WIDE == low_id
    lows = low_id.shape[0]
    first = 0
    for channel, count in enumerate(PARTS if parts.shape[0] == sum(PARTS) * lows else (2,) * PROJ):
        value = found[first * lows : (first + 1) * lows]
        for part in range(1, count):
            value = value + found[(first + part) * lows : (first + part + 1) * lows]
        first += count
        put(channel, jnp.sum(jnp.where(mine, value, 0.0), axis=0, keepdims=True))


def put_parts(parts_ref, channel, half, value, counts, lows=None, low=0):
    lows = lows or value.shape[0]
    first = sum(counts[:channel])
    parts = split_three(value) if counts[channel] == 3 else split_two(value)
    for part, one in enumerate(parts):
        at = (first + part) * lows + low
        parts_ref[at : at + value.shape[0], half * LANES : (half + 1) * LANES] = one.astype(bf16)


def route_kernel(devices, per_owner, own_hbm, loc_hbm, want_ref, place_ref, own_ref, loc_ref, own_s, loc_s, rank_s, sems):
    copies = [pltpu.make_async_copy(own_hbm, own_ref, sems.at[0]), pltpu.make_async_copy(loc_hbm, loc_ref, sems.at[1])]
    for copy in copies:
        copy.start()
    for copy in copies:
        copy.wait()
    tiles = own_ref.shape[0]
    rows = own_s.shape[0]
    for block in range(rows // tiles):
        own_s[block * tiles : (block + 1) * tiles, :] = own_ref[:, block * LANES : (block + 1) * LANES]
        loc_s[block * tiles : (block + 1) * tiles, :] = loc_ref[:, block * LANES : (block + 1) * LANES]
    owner = own_s[...]
    left = (iota((LANES, 2 * LANES), 0) < iota((LANES, 2 * LANES), 1)) | (iota((LANES, 2 * LANES), 1) >= LANES)
    above = iota((rows, rows), 1) < iota((rows, rows), 0)
    hits = jnp.concatenate([jnp.where(owner == one, 1.0, 0.0).astype(bf16) for one in range(devices)], axis=0)
    sums = dot(hits, jnp.where(left, 1.0, 0.0).astype(bf16))
    totals = jnp.concatenate(
        [sums[one * rows : (one + 1) * rows, LANES:].astype(bf16) for one in range(devices)], axis=1
    )
    base = dot(jnp.where(above, 1.0, 0.0).astype(bf16), totals)
    rank = jnp.zeros((rows, LANES), f32)
    for one in range(devices):
        here = sums[one * rows : (one + 1) * rows, :LANES] + base[:, one * LANES : (one + 1) * LANES]
        rank = jnp.where(owner == one, here, rank)
    rank = rank.astype(i32)
    place_ref[...] = owner * per_owner + rank
    rank_s[...] = rank

    owner_id = iota((devices, LANES), 0)
    rank_id = narrow(iota((per_owner, LANES), 0))

    def place(index, total):
        start = pl.multiple_of(index * 8, 8)
        own_rows = own_s[pl.ds(start, 8), :]
        loc_rows = loc_s[pl.ds(start, 8), :]
        rank_rows = rank_s[pl.ds(start, 8), :]
        high_rows = (loc_rows // LANES).astype(f32)
        low_rows = (loc_rows % LANES).astype(f32)
        lhs = []
        rhs = []
        for row in range(8):
            mine = own_rows[row : row + 1] == owner_id
            lhs.append(
                jnp.concatenate(
                    [
                        jnp.where(mine, high_rows[row : row + 1], 0.0),
                        jnp.where(mine, low_rows[row : row + 1], 0.0),
                    ],
                    axis=0,
                ).astype(bf16)
            )
            rhs.append(one_hot(rank_rows[row : row + 1], rank_id))
        return total + dot_nt(jnp.concatenate(lhs, axis=1), jnp.concatenate(rhs, axis=1))

    total = lax.fori_loop(0, rows // 8, place, jnp.zeros((2 * devices, per_owner), f32), unroll=devices <= 32).astype(i32)
    want = total[:devices] * LANES + total[devices:]
    halves = per_owner // LANES
    if per_owner % LANES == 0 and halves > 1:
        for half in range(halves):
            want_ref[pl.ds(half, devices, stride=halves), :] = want[:, half * LANES : (half + 1) * LANES]
    else:
        want_ref[...] = want


def order_kernel(tiles, place_ref, pos_ref, back_ref):
    rows = place_ref.shape[0]
    blocks = rows // tiles
    chunks = rows * GROUP // tiles
    lane = iota((8, LANES), 1)
    from_slot = iota((8, LANES), 0) * STEP + lane // GROUP
    tile_of = lane % GROUP
    for group in range(tiles // GROUP):
        for block in range(blocks):
            start = block * tiles + group * GROUP
            part = place_ref[start : start + GROUP, :]
            out = jnp.zeros((8, LANES), i32)
            for tile in range(GROUP):
                out = jnp.where(tile_of == tile, lane_pick(part[tile : tile + 1], from_slot), out)
            start = group * chunks + block * 8
            pos_ref[start : start + 8, :] = out
    lows = back_ref.shape[0]
    low_id = iota((lows, LANES), 0)
    high_id = narrow(iota((WIDE, LANES), 0))
    lane = iota((lows, LANES), 1)
    total = jnp.zeros((2 * lows, WIDE), f32)
    for start in range(0, rows, 8):
        lhs = []
        rhs = []
        for row in range(start, start + 8):
            place = place_ref[row : row + 1, :]
            mine = place // WIDE == low_id
            tile = row % tiles
            number = tile // GROUP * chunks + row // tiles * 8 + lane // STEP
            within = lane % STEP * GROUP + tile % GROUP
            lhs.append(
                jnp.concatenate(
                    [jnp.where(mine, number.astype(f32), 0.0), jnp.where(mine, within.astype(f32), 0.0)], axis=0
                ).astype(bf16)
            )
            rhs.append(one_hot(place % WIDE, high_id))
        total = total + dot_nt(jnp.concatenate(lhs, axis=1), jnp.concatenate(rhs, axis=1))
    total = total.astype(i32)
    back_ref[...] = total[:lows] * LANES + total[lows:]


def view(angles_ref):
    angle = [jnp.full((1, LANES), angles_ref[index], f32) for index in range(3)]
    (cos_a, cos_b, cos_c) = [jnp.cos(one) for one in angle]
    (sin_a, sin_b, sin_c) = [jnp.sin(one) for one in angle]
    return [
        [cos_c * cos_b, cos_c * sin_b * sin_a - sin_c * cos_a, cos_c * sin_b * cos_a + sin_c * sin_a],
        [sin_c * cos_b, sin_c * sin_b * sin_a + cos_c * cos_a, sin_c * sin_b * cos_a - cos_c * sin_a],
        [-sin_b, cos_b * sin_a, cos_b * cos_a],
    ]


def harmonics(along_x, along_y, along_z):
    sq_x = along_x * along_x
    sq_y = along_y * along_y
    sq_z = along_z * along_z
    return [
        0.28209479177387814 + 0.0 * along_x,
        -0.4886025119029199 * along_y,
        0.4886025119029199 * along_z,
        -0.4886025119029199 * along_x,
        1.0925484305920792 * along_x * along_y,
        -1.0925484305920792 * along_y * along_z,
        0.31539156525252005 * (2.0 * sq_z - sq_x - sq_y),
        -1.0925484305920792 * along_x * along_z,
        0.5462742152960396 * (sq_x - sq_y),
        -0.5900435899266435 * along_y * (3.0 * sq_x - sq_y),
        2.890611442640554 * along_x * along_y * along_z,
        -0.4570457994644658 * along_y * (4.0 * sq_z - sq_x - sq_y),
        0.3731763325901154 * along_z * (2.0 * sq_z - 3.0 * sq_x - 3.0 * sq_y),
        -0.4570457994644658 * along_x * (4.0 * sq_z - sq_x - sq_y),
        1.445305721320277 * along_z * (sq_x - sq_y),
        -0.5900435899266435 * along_x * (sq_x - 3.0 * sq_y),
    ]


def basis_rows(basis, eighth):
    sub = iota((8, LANES), 0)
    found = []
    for colour in range(3):
        out = None
        for inner in range(8):
            index = 8 * eighth + inner - 11 - 16 * colour
            if 0 <= index < 16:
                out = jnp.zeros((8, LANES), f32) if out is None else out
                out = jnp.where(sub == inner, basis[index], out)
        found.append(out)
    return found


def shape_of(columns, rotation, camera_frame):
    focal_x, focal_y, centre_x, centre_y = camera_frame
    positions = columns[0:3]
    cam_first = rotation[0][0] * positions[0] + rotation[0][1] * positions[1] + rotation[0][2] * positions[2]
    cam_second = rotation[1][0] * positions[0] + rotation[1][1] * positions[1] + rotation[1][2] * positions[2]
    mean_x = centre_x + focal_x * cam_first
    mean_y = centre_y + focal_y * cam_second
    scales = [jnp.exp(one) for one in columns[3:6]]
    quat_w, quat_x, quat_y, quat_z = columns[6:10]
    norm_sq = jnp.maximum(quat_w * quat_w + quat_x * quat_x + quat_y * quat_y + quat_z * quat_z, 1.0)
    twice = 2.0 / norm_sq
    turned = [
        [
            1.0 - twice * (quat_y * quat_y + quat_z * quat_z),
            twice * (quat_x * quat_y - quat_w * quat_z),
            twice * (quat_x * quat_z + quat_w * quat_y),
        ],
        [
            twice * (quat_x * quat_y + quat_w * quat_z),
            1.0 - twice * (quat_x * quat_x + quat_z * quat_z),
            twice * (quat_y * quat_z - quat_w * quat_x),
        ],
        [
            twice * (quat_x * quat_z - quat_w * quat_y),
            twice * (quat_y * quat_z + quat_w * quat_x),
            1.0 - twice * (quat_x * quat_x + quat_y * quat_y),
        ],
    ]
    rows = []
    for focal, turn in ((focal_x, rotation[0]), (focal_y, rotation[1])):
        rows.append(
            [
                focal * (turn[0] * turned[0][k] + turn[1] * turned[1][k] + turn[2] * turned[2][k]) * scales[k]
                for k in range(3)
            ]
        )
    first, second = rows
    cov_a = first[0] * first[0] + first[1] * first[1] + first[2] * first[2] + 0.3
    cov_b = first[0] * second[0] + first[1] * second[1] + first[2] * second[2]
    cov_c = second[0] * second[0] + second[1] * second[1] + second[2] * second[2] + 0.3
    determinant = cov_a * cov_c - cov_b * cov_b
    opacity = 1.0 / (1.0 + jnp.exp(-columns[10]))
    return mean_x, mean_y, cov_c / determinant, -cov_b / determinant, cov_a / determinant, opacity


def spread_columns(gauss_ref, dense_s):
    rows = gauss_ref.shape[1] // LANES
    for row in range(rows):
        for eighth in range(2):
            dense_s[pl.ds(8 * eighth * rows + row, 8, stride=rows), :] = gauss_ref[
                8 * eighth : 8 * eighth + 8, row * LANES : (row + 1) * LANES
            ]


def shade_kernel(camera_frame, angles_ref, gauss_ref, parts_ref, dense_s, tint_s):
    rows = gauss_ref.shape[1] // LANES
    spread_columns(gauss_ref, dense_s)
    rotation = view(angles_ref)
    basis = harmonics(*rotation[2])
    patterns = [basis_rows(basis, eighth) for eighth in range(7)]
    for row in range(rows):
        lanes = slice(row * LANES, (row + 1) * LANES)
        tints = [None] * 3
        for eighth in range(1, 7):
            block = gauss_ref[8 * eighth : 8 * eighth + 8, lanes]
            for colour in range(3):
                pattern = patterns[eighth][colour]
                if pattern is not None:
                    term = block * pattern
                    tints[colour] = term if tints[colour] is None else tints[colour] + term
        for colour in range(3):
            tint_s[pl.ds(8 * colour * rows + row, 8, stride=rows), :] = tints[colour]
        tint_s[pl.ds(24 * rows + row, 3, stride=rows), :] = gauss_ref[56:59, lanes]
    for part in range(rows // 16):
        half = part % 2
        low = part // 2 * 16
        at = [pl.ds(index * rows + 2 * low + half, 16, stride=2) for index in range(27)]
        columns = [dense_s[one, :] for one in at[:11]]
        for index, value in enumerate(shape_of(columns, rotation, camera_frame)):
            put_parts(parts_ref, index, half, value, PARTS, rows // 2, low)
        for colour in range(3):
            total = 0.5
            for inner in range(8):
                total = total + tint_s[at[8 * colour + inner], :]
            if colour == 2:
                for inner in range(3):
                    total = total + basis[13 + inner] * tint_s[at[24 + inner], :]
            put_parts(parts_ref, 6 + colour, half, total, PARTS, rows // 2, low)


def pick_kernel(layout, parts_ref, asked_ref, out_ref):
    low_id = iota((parts_ref.shape[0] // sum(PARTS), WIDE), 0)
    high_id = narrow(iota((WIDE, WIDE), 0))
    minors = layout.minors()

    for index in range(layout.count // 2):
        slots = jnp.concatenate([asked_ref[2 * index + one : 2 * index + one + 1, :] for one in range(2)], axis=1)

        def put(channel, value):
            for one in range(2):
                at = layout.row(channel, (2 * index + one) // minors, (2 * index + one) % minors)
                out_ref[at : at + 1, :] = value[:, one * LANES : (one + 1) * LANES]

        pick_slots(parts_ref[...], one_hot(slots % WIDE, high_id), slots, low_id, put)


def render_kernel(
    layout,
    count_ref,
    order_ref,
    rows_ref,
    pos_ref,
    back_ref,
    cot_ref,
    image_hbm,
    out_ref,
    image_ref,
    image_sem,
    in_s,
    out_s,
    raw_s,
    coef_s,
    cot_s,
    rhs_s,
    tint_s,
    alpha_s,
    shade_s,
    weight_s,
    sums_s,
):
    slot_rows = pos_ref.shape[0]
    groups = cot_ref.shape[1] // (GROUP * PIX)
    chunks = slot_rows // groups
    sub = iota((8, LANES), 0)
    lane = iota((8, LANES), 1)
    tile_of = lane % GROUP
    blocks = slot_rows // 8
    middles = []
    for group in range(groups):
        middle_x = jnp.zeros((8, LANES), f32)
        middle_y = jnp.zeros((8, LANES), f32)
        live = jnp.zeros((8, LANES), i32)
        for tile in range(GROUP):
            shown = order_ref[group * GROUP + tile]
            here = tile_of == tile
            middle_x = jnp.where(here, (shown % TX * 16 + 8).astype(f32), middle_x)
            middle_y = jnp.where(here, (shown // TX * 16 + 8).astype(f32), middle_y)
            live = jnp.where(here, count_ref[group * GROUP + tile], live)
        middles.append((middle_x, middle_y, live))

    for half in range(2):
        for channel in range(PROJ):
            put_parts(in_s, channel, half, layout.half(rows_ref, channel, half), PARTS)
    low_id = iota((slot_rows // 2, WIDE), 0)
    high_id = narrow(iota((WIDE, WIDE), 0))

    def pick_in(row):
        slots = jnp.concatenate([pos_ref[row + one : row + one + 1, :] for one in range(2)], axis=1)

        def put(channel, value):
            for one in range(2):
                at = channel * slot_rows + row + one
                raw_s[at : at + 1, :] = value[:, one * LANES : (one + 1) * LANES]

        pick_slots(in_s[...], one_hot(slots % WIDE, high_id), slots, low_id, put)

    def quadratics(block):
        group = block * 8 // chunks
        middle_x, middle_y, live = middles[group]
        found = [
            raw_s[channel * slot_rows + 8 * block : channel * slot_rows + 8 * block + 8, :] for channel in range(PROJ)
        ]
        at_x = found[0] - middle_x
        at_y = found[1] - middle_y
        quad_a = -0.5 * found[2]
        quad_b = -found[3]
        quad_c = -0.5 * found[4]
        flat = quad_a * at_x * at_x + quad_c * at_y * at_y + quad_b * at_x * at_y + jnp.log(found[5])
        place = (8 * block - group * chunks + sub) * STEP + lane // GROUP
        terms = (
            quad_a * LOG2E,
            quad_b * LOG2E,
            quad_c * LOG2E,
            (-2.0 * quad_a * at_x - quad_b * at_y) * LOG2E,
            (-2.0 * quad_c * at_y - quad_b * at_x) * LOG2E,
            jnp.where(place < live, flat * LOG2E, -1e30),
        )
        for index, term in enumerate(terms):
            for part, value in enumerate(split_three(term)):
                coef_s[pl.ds(8 * block * 24 + 6 * part + index, 8, stride=24), :] = value
        for colour in range(3):
            for part, value in enumerate(split_two(found[6 + colour])):
                coef_s[pl.ds(8 * block * 24 + 18 + 3 * part + colour, 8, stride=24), :] = value

    for row in range(0, slot_rows, 2):
        pick_in(row)
    for block in range(blocks):
        quadratics(block)

    pixel = iota((24, PIX), 1)
    row = iota((24, PIX), 0)
    pix_x = (pixel % 16).astype(f32) - 7.5
    pix_y = (pixel // 16).astype(f32) - 7.5
    kind = row % 6
    monomials = jnp.where(kind == 0, pix_x * pix_x, jnp.where(kind == 1, pix_x * pix_y, 1.0))
    monomials = jnp.where(kind == 2, pix_y * pix_y, monomials)
    monomials = jnp.where(kind == 3, pix_x, jnp.where(kind == 4, pix_y, monomials))
    moments = jnp.where(iota((8, PIX), 0) < 6, monomials[0:8], 0.0).astype(bf16)
    monomials = jnp.where(row < 18, monomials, 0.0)
    nothing = jnp.zeros((24, PIX), f32)
    for group in range(groups):
        for colour in range(3):
            for tile in range(GROUP):
                start = (group * GROUP + tile) * PIX
                cot_s[group * 24 + colour * GROUP + tile, :] = cot_ref[colour, start : start + PIX]
    cots = []
    spare = jnp.zeros((8, PIX), f32)
    for group in range(groups):
        first, second = split_two(cot_s[group * 24 : (group + 1) * 24, :])
        cots.append(jnp.concatenate([first, spare, second, spare], axis=0).astype(bf16))
        rhs_s[group] = jnp.concatenate(
            [
                jnp.concatenate([jnp.concatenate([nothing, monomials[8 * one : 8 * one + 8]], axis=0) for one in range(3)], axis=0),
                jnp.concatenate([first, spare, first, spare, second, spare], axis=0),
            ],
            axis=1,
        ).astype(bf16)

    own_tile = sub == tile_of
    own_pair = iota((8, WIDE), 0) == iota((8, WIDE), 1) % GROUP

    def evaluate(index):
        for group in range(groups):
            chunk = group * chunks + index
            coefs = coef_s[chunk * 24 : (chunk + 1) * 24, :]
            tints = [jnp.where(own_tile, coefs[18 + one : 19 + one], 0.0) for one in range(6)]
            lhs = jnp.concatenate(
                tints[:3] + [coefs[0:8]] + tints[3:] + [coefs[8:16]] + tints[:3] + [coefs[16:24]], axis=0
            ).astype(bf16)
            both = dot_tn(lhs, rhs_s[group])
            lanes = slice(chunk * LANES, (chunk + 1) * LANES)
            tint_s[:, lanes] = lhs[0:64]
            alpha_s[lanes, :] = jnp.exp2(both[:, :PIX])
            shade_s[lanes, :] = both[:, PIX:]

    def scan(index, trans):
        out = []
        for group in range(groups):
            one = trans[group]
            start = (group * chunks + index) * LANES
            for step in range(STEP):
                alpha = alpha_s[pl.ds(start + step * GROUP, GROUP), :]
                weight = one * alpha
                one = one - weight
                weight_s[pl.ds(start + step * GROUP, GROUP), :] = weight
            out.append(one)
        return tuple(out)

    def paint(index, images):
        out = []
        for group in range(groups):
            chunk = group * chunks + index
            both = slice(chunk * LANES, chunk * LANES + WIDE)
            first, second = split_two(weight_s[both, :])
            first = first.astype(bf16)
            second = second.astype(bf16)
            tints = tint_s[:, both]
            by_first = dot(tints, first)
            out.append(images[group] + by_first[0:24] + by_first[32:56] + dot(tints[0:32], second)[0:24])
            by_first = dot_nt(cots[group], first)
            tint_grad = by_first[0:24] + by_first[32:56] + dot_nt(cots[group][0:32], second)[0:24]
            for colour in range(3):
                own = jnp.where(own_pair, tint_grad[colour * GROUP : (colour + 1) * GROUP], 0.0)
                own = jnp.sum(own, axis=0, keepdims=True)
                for one in range(2):
                    sums_s[(chunk + one) * 16 + 8 + colour : (chunk + one) * 16 + 9 + colour, :] = own[:, one * LANES : (one + 1) * LANES]
        return tuple(out)

    trans = tuple(jnp.ones((GROUP, PIX), f32) for _ in range(groups))
    images = tuple(jnp.zeros((24, PIX), f32) for _ in range(groups))
    for pair in range(-AHEAD, chunks // 2 + 1):
        for one in range(2):
            if pair + AHEAD < chunks // 2:
                evaluate(2 * (pair + AHEAD) + one)
        for one in range(2):
            if 0 <= pair < chunks // 2:
                trans = scan(2 * pair + one, trans)
        if pair > 0:
            images = paint(2 * (pair - 1), images)
    for group in range(groups):
        for colour in range(3):
            for tile in range(GROUP):
                at = (group * GROUP + tile) * PIX
                image_ref[colour, at : at + PIX] = images[group][colour * GROUP + tile]
    image_copy = pltpu.make_async_copy(image_ref, image_hbm, image_sem)
    image_copy.start()

    def moment(index):
        for group in range(groups):
            chunk = group * chunks + index
            first, second = split_two(shade_s[slice(chunk * LANES, chunk * LANES + WIDE), :])
            found = dot_nt(moments, first.astype(bf16)) + dot_nt(moments, second.astype(bf16))
            for one in range(2):
                start = (chunk + one) * 16
                sums_s[start : start + 8, :] = found[:, one * LANES : (one + 1) * LANES]

    def rescan(index, behinds):
        out = []
        for group in range(groups):
            behind = behinds[group]
            start = (group * chunks + index) * LANES
            for step in reversed(range(STEP)):
                at = pl.ds(start + step * GROUP, GROUP)
                ahead = shade_s[at, :] - behind
                shade_s[at, :] = weight_s[at, :] * ahead
                behind = behind + alpha_s[at, :] * ahead
            out.append(behind)
        return tuple(out)

    behinds = tuple(jnp.zeros((GROUP, PIX), f32) for _ in range(groups))
    for pair in reversed(range(-1, chunks // 2)):
        for one in reversed(range(2)):
            if pair >= 0:
                behinds = rescan(2 * pair + one, behinds)
        if pair + 1 < chunks // 2:
            moment(2 * (pair + 1))

    slot_s = coef_s
    for block in range(blocks):
        middle_x, middle_y, _ = middles[block * 8 // chunks]
        at = slice(8 * block, 8 * block + 8)
        raw = [raw_s[channel * slot_rows + 8 * block : channel * slot_rows + 8 * block + 8, :] for channel in range(6)]
        (sum_xx, sum_xy, sum_yy, sum_x, sum_y, sum_one) = [
            sums_s[pl.ds(8 * block * 16 + index, 8, stride=16), :] for index in range(6)
        ]
        at_x = raw[0] - middle_x
        at_y = raw[1] - middle_y
        off_x = sum_x - at_x * sum_one
        off_y = sum_y - at_y * sum_one
        grads = [
            raw[2] * off_x + raw[3] * off_y,
            raw[4] * off_y + raw[3] * off_x,
            -0.5 * (sum_xx - at_x * (sum_x + off_x)),
            -(sum_xy - at_y * sum_x - at_x * off_y),
            -0.5 * (sum_yy - at_y * (sum_y + off_y)),
            sum_one / raw[5],
        ] + [sums_s[pl.ds(8 * block * 16 + 8 + colour, 8, stride=16), :] for colour in range(3)]
        for channel, value in enumerate(grads):
            slot_s[channel * slot_rows + 8 * block : channel * slot_rows + 8 * block + 8, :] = value

    for half in range(2):
        for channel in range(PROJ):
            value = slot_s[pl.ds(channel * slot_rows + half, slot_rows // 2, stride=2), :]
            put_parts(out_s, channel, half, value, (2,) * PROJ)
    minors = layout.minors()

    def pick_out(index, _):
        slots = back_ref[pl.ds(index, 1), :]

        def put(channel, value):
            for one in range(2):
                at = layout.row(channel, (2 * index + one) // minors, (2 * index + one) % minors)
                out_ref[pl.ds(at, 1), :] = value[:, one * LANES : (one + 1) * LANES]

        pick_slots(out_s[...], one_hot(slots % WIDE, high_id), slots, low_id, put)
        return 0

    lax.fori_loop(0, layout.count // 2, pick_out, 0, unroll=True)
    image_copy.wait()


def ready_kernel(camera_frame, angles_ref, dense_ref, asked_ref, hot_ref, mine_ref, slope_ref):
    rows = dense_ref.shape[0] // 16
    low_id = narrow(iota((mine_ref.shape[0], LANES), 0))
    high_id = narrow(iota((WIDE, LANES), 0))
    for row in range(asked_ref.shape[0]):
        lanes = slice(row * LANES, (row + 1) * LANES)
        asked = asked_ref[row : row + 1, :]
        mine_ref[:, lanes] = one_hot(asked // WIDE, low_id)
        hot_ref[:, lanes] = one_hot(asked % WIDE, high_id)
    rotation = view(angles_ref)
    for start in range(0, rows, 8):
        columns = [dense_ref[index * rows + start : index * rows + start + 8, :] for index in range(11)]

        def conics(*values):
            return shape_of(columns[0:3] + list(values) + columns[10:11], rotation, camera_frame)[2:5]

        _, pullback = jax.vjp(conics, *columns[3:10])
        for one in range(3):
            unit = tuple(jnp.full((8, LANES), 1.0 if one == other else 0.0, f32) for other in range(3))
            for index, slope in enumerate(pullback(unit)):
                at = (7 * one + index) * rows + start
                slope_ref[at : at + 8, :] = slope
        _, pullback = jax.vjp(lambda value: 1.0 / (1.0 + jnp.exp(-value)), columns[10])
        slope_ref[21 * rows + start : 21 * rows + start + 8, :] = pullback(jnp.ones((8, LANES), f32))[0]


def collect_kernel(
    layout, camera_frame, angles_ref, hot_ref, mine_ref, slope_ref, terms_ref, grad_hbm, lhs_s, total_s, out_s, grad_ref, sems
):
    gauss = grad_ref.shape[1]
    rows = gauss // LANES
    lows = gauss // WIDE
    minors = layout.minors()
    for index in range(layout.count // 8):
        for row in range(8 * index, 8 * index + 8):
            lanes = slice(row * LANES, (row + 1) * LANES)
            mine = mine_ref[:, lanes]
            for channel in range(PROJ):
                at = layout.row(channel, row // minors, row % minors)
                put_terms(lhs_s, channel, lanes, terms_ref[at : at + 1, :], mine)
        if index % 2 == 1:
            lanes = slice(8 * (index - 1) * LANES, 8 * (index + 1) * LANES)
            found = dot_nt(lhs_s[:, lanes], hot_ref[:, lanes])
            total_s[...] = found if index == 1 else total_s[...] + found
    rotation = view(angles_ref)
    basis = harmonics(*rotation[2])
    focal_x, focal_y, _, _ = camera_frame
    for part in range(rows // 8):
        half = part % 2
        low = part // 2 * 8
        lanes = slice(half * LANES, (half + 1) * LANES)
        sums = [
            total_s[channel * lows + low : channel * lows + low + 8, lanes]
            + total_s[(PROJ + channel) * lows + low : (PROJ + channel) * lows + low + 8, lanes]
            for channel in range(PROJ)
        ]
        slope = [slope_ref[pl.ds(index * rows + 2 * low + half, 8, stride=2), :] for index in range(22)]
        grads = [focal_x * rotation[0][k] * sums[0] + focal_y * rotation[1][k] * sums[1] for k in range(3)]
        grads += [slope[k] * sums[2] + slope[7 + k] * sums[3] + slope[14 + k] * sums[4] for k in range(7)]
        grads += [slope[21] * sums[5]]
        for index, value in enumerate(grads + sums[6:]):
            out_s[pl.ds(index * rows + 2 * low + half, 8, stride=2), :] = value
    sub = iota((8, LANES), 0)
    patterns = [basis_rows(basis, eighth) for eighth in range(8)]
    copies = []
    pieces = sems.shape[0]
    wide = gauss // pieces
    for row in range(rows):
        lanes = slice(row * LANES, (row + 1) * LANES)
        grad_ref[0:8, lanes] = out_s[pl.ds(row, 8, stride=rows), :]
        tints = [out_s[(11 + colour) * rows + row : (11 + colour) * rows + row + 1, :] for colour in range(3)]
        for eighth in range(1, 8):
            value = None
            for colour in range(3):
                pattern = patterns[eighth][colour]
                if pattern is not None:
                    term = pattern * tints[colour]
                    value = term if value is None else value + term
            if eighth == 1:
                value = jnp.where(sub < 3, out_s[pl.ds(8 * rows + row, 8, stride=rows), :], value)
            if eighth == 7:
                grad_ref[56:59, lanes] = value[0:3]
            else:
                grad_ref[8 * eighth : 8 * eighth + 8, lanes] = value
        if (row + 1) * LANES % wide == 0:
            piece = len(copies)
            span = slice(piece * wide, (piece + 1) * wide)
            copies.append(pltpu.make_async_copy(grad_ref.at[:, span], grad_hbm.at[:, span], sems.at[piece]))
            copies[-1].start()
    for copy in copies:
        copy.wait()


VMEM = pl.BlockSpec(memory_space=pltpu.VMEM)
HBM = pl.BlockSpec(memory_space=pltpu.HBM)
SMEM = pl.BlockSpec(memory_space=pltpu.SMEM)


def call(kernel, specs, outs, scratch, flops, name, out_spec=VMEM, vmem=VMEM_BYTES):
    return pl.pallas_call(
        kernel,
        in_specs=specs,
        out_specs=list(out_spec) if isinstance(out_spec, tuple) else [out_spec] * len(outs),
        out_shape=[jax.ShapeDtypeStruct(shape, dtype) for shape, dtype in outs],
        scratch_shapes=[pltpu.VMEM(*one) if isinstance(one, tuple) else one for one in scratch],
        compiler_params=pltpu.CompilerParams(vmem_limit_bytes=vmem),
        cost_estimate=pl.CostEstimate(flops=flops, bytes_accessed=4 << 20, transcendentals=0),
        name=name,
    )


def route(devices, owners, locals_):
    slots = owners.size
    per_owner = slots // devices
    rows = slots // LANES
    halves = per_owner // LANES if per_owner % LANES == 0 else 0
    asked = (devices * halves, LANES) if halves else (devices, per_owner)
    return call(
        partial(route_kernel, devices, per_owner),
        [HBM, HBM],
        [(asked, i32), ((rows, LANES), i32)],
        [(owners.shape, i32)] * 2 + [((rows, LANES), i32)] * 3 + [pltpu.SemaphoreType.DMA((2,))],
        1 << 30,
        "route",
        vmem=63 << 20,
    )(owners, locals_)


def order(tiles, place):
    rows = place.shape[0]
    return call(
        partial(order_kernel, tiles),
        [VMEM],
        [((rows, LANES), i32), ((rows // 2, WIDE), i32)],
        [],
        1 << 30,
        "order",
    )(place)


def shade(camera_frame, view_angles, gaussians):
    rows = gaussians.shape[1] // LANES
    return call(
        partial(shade_kernel, camera_frame),
        [SMEM, VMEM],
        [((sum(PARTS) * rows // 2, WIDE), bf16), ((16 * rows, LANES), f32)],
        [((27 * rows, LANES), f32)],
        1 << 30,
        "shade",
    )(view_angles, gaussians)


def pick(layout, table, asked):
    return call(
        partial(pick_kernel, layout),
        [VMEM, VMEM],
        [((PROJ * layout.count, LANES), f32)],
        [],
        1 << 30,
        "pick",
    )(table, asked)[0]


def render(layout, list_counts, tile_order, rows, pos, back, cotangent):
    slot_rows = pos.shape[0]
    groups = tile_order.shape[0] // GROUP
    slots = slot_rows * LANES
    return call(
        partial(render_kernel, layout),
        [SMEM, SMEM, VMEM, VMEM, VMEM, VMEM],
        [(cotangent.shape, f32), ((PROJ * layout.count, LANES), f32)],
        [
            (cotangent.shape, f32),
            pltpu.SemaphoreType.DMA,
            ((sum(PARTS) * slot_rows // 2, WIDE), bf16),
            ((2 * PROJ * slot_rows // 2, WIDE), bf16),
            ((PROJ * slot_rows, LANES), f32),
            ((24 * slot_rows, LANES), f32),
            ((24 * groups, PIX), f32),
            ((groups, 96, 2 * PIX), bf16),
            ((64, slots), bf16),
            ((slots, PIX), f32),
            ((slots, PIX), f32),
            ((slots, PIX), f32),
            ((16 * slot_rows, LANES), f32),
        ],
        1 << 34,
        "render",
        out_spec=(HBM, VMEM),
    )(list_counts, tile_order, rows, pos, back, cotangent)


def ready(camera_frame, view_angles, dense, asked):
    rows = dense.shape[0] // 16
    slots = asked.size
    return call(
        partial(ready_kernel, camera_frame),
        [SMEM, VMEM, VMEM],
        [((WIDE, slots), bf16), ((rows // 2, slots), bf16), ((22 * rows, LANES), f32)],
        [],
        1 << 30,
        "ready",
        vmem=24 << 20,
    )(view_angles, dense, asked)


def collect(layout, camera_frame, view_angles, shape, prepared, terms):
    rows = shape[1] // LANES
    lows = shape[1] // WIDE
    return call(
        partial(collect_kernel, layout, camera_frame),
        [SMEM, VMEM, VMEM, VMEM, VMEM],
        [(shape, f32)],
        [
            ((2 * PROJ * lows, layout.count * LANES), bf16),
            ((2 * PROJ * lows, WIDE), f32),
            ((16 * rows, LANES), f32),
            (shape, f32),
            pltpu.SemaphoreType.DMA((8,)),
        ],
        1 << 32,
        "collect",
        out_spec=HBM,
        vmem=32 << 20,
    )(view_angles, *prepared, terms)[0]


def swap_rows(layout, devices, rows):
    if layout.halves:
        apart = rows.reshape(devices * PROJ, layout.halves, LANES)
        return lax.all_to_all(apart, "dev", split_axis=0, concat_axis=0, tiled=True).reshape(rows.shape)
    apart = rows.reshape(PROJ, devices, layout.count * LANES // devices)
    return lax.all_to_all(apart, "dev", split_axis=1, concat_axis=1, tiled=True).reshape(rows.shape)


def shards(gaussians, view_angles, tile_order, tile_owners, tile_locals, list_counts, image_cotangent):
    devices = lax.axis_size("dev")
    tiles_y = devices * tile_order.shape[0] // TX
    camera_frame = (4.0 * TX, 4.0 * tiles_y, 8.0 * TX, 8.0 * tiles_y)
    layout = Rows(devices, tile_owners.size // devices)
    want, place = route(devices, tile_owners, tile_locals)
    asked = lax.all_to_all(want, "dev", split_axis=0, concat_axis=0, tiled=True)
    table, dense = shade(camera_frame, view_angles, gaussians)
    if not layout.halves:
        asked = asked.reshape(layout.count, LANES)
    picked, place = lax.optimization_barrier((pick(layout, table, asked), place))
    arrived = swap_rows(layout, devices, picked)
    pos, back = order(tile_owners.shape[0], place)
    rendered, slot_grads = render(layout, list_counts, tile_order, arrived, pos, back, image_cotangent)
    slot_grads, asked = lax.optimization_barrier((slot_grads, asked))
    terms = swap_rows(layout, devices, slot_grads)
    prepared = ready(camera_frame, view_angles, dense, asked)
    gradients = collect(layout, camera_frame, view_angles, gaussians.shape, prepared, terms)
    return (rendered, gradients)


def solution(mesh):
    return jax.shard_map(
        shards,
        mesh=mesh,
        in_specs=(
            P(None, "dev"),
            P(),
            P("dev"),
            P("dev", None),
            P("dev", None),
            P("dev"),
            P(None, "dev"),
        ),
        out_specs=(P(None, "dev"), P(None, "dev")),
        check_vma=False,
    )
```

```python
from functools import partial

import jax
import jax.numpy as jnp
from jax import lax
from jax.experimental import pallas as pl
from jax.experimental.pallas import tpu as pltpu
from jax.sharding import PartitionSpec as P

PIX = 256
TX = 32
LANES = 128
PROJ = 9
GROUP = 8
WIDE = 2 * LANES
PARTS = (3, 3, 3, 3, 3, 2, 2, 2, 2)
STEP = LANES // GROUP
LOG2E = 1.4426950408889634
AHEAD = 2
VMEM_BYTES = 52 * 1024 * 1024

f32 = jnp.float32
bf16 = jnp.bfloat16
i32 = jnp.int32


def iota(shape, dim):
    return lax.broadcasted_iota(i32, shape, dim)


def lane_pick(row, lanes):
    source = jnp.broadcast_to(row, lanes.shape)
    return jnp.take_along_axis(source, lanes, axis=1, mode="promise_in_bounds")


def split_two(values):
    first = values.astype(bf16).astype(f32)
    return first, values - first


def split_three(values):
    first, rest = split_two(values)
    second, third = split_two(rest)
    return first, second, third


def dot(lhs, rhs):
    return lax.dot_general(lhs, rhs, (((1,), (0,)), ((), ())), preferred_element_type=f32)


def dot_nt(lhs, rhs):
    return lax.dot_general(lhs, rhs, (((1,), (1,)), ((), ())), preferred_element_type=f32)


def dot_tn(lhs, rhs):
    return lax.dot_general(lhs, rhs, (((0,), (0,)), ((), ())), preferred_element_type=f32)


class Rows:
    def __init__(self, devices, per_owner):
        self.halves = per_owner // LANES if per_owner % LANES == 0 else 0
        self.count = devices * per_owner // LANES

    def row(self, channel, major, minor):
        halves = self.halves
        if halves == 0:
            return channel * self.count + major
        return major * (PROJ * halves) + channel * halves + minor

    def half(self, ref, channel, half):
        halves = self.halves
        if halves == 0:
            return ref[pl.ds(channel * self.count + half, self.count // 2, stride=2), :]
        return jnp.concatenate(
            [ref[pl.ds(self.row(channel, one // halves, one % halves), 1), :] for one in range(half, self.count, 2)], axis=0
        ) if halves != 2 else ref[pl.ds(channel * 2 + half, self.count // 2, stride=2 * PROJ), :]

    def minors(self):
        return max(self.halves, 1)


def narrow(ids):
    return ids.astype(f32).astype(bf16)


def one_hot(ids, every):
    return jnp.where(narrow(ids) == every, jnp.ones((), bf16), jnp.zeros((), bf16))


def put_terms(lhs_s, channel, lanes, row, mine):
    lows = mine.shape[0]
    row = jnp.broadcast_to(row, (16, LANES))
    first = row.astype(bf16)
    second = (row - first.astype(f32)).astype(bf16)
    for part, value in enumerate((first, second)):
        for low in range(0, lows, 16):
            start = (part * PROJ + channel) * lows + low
            lhs_s[start : start + 16, lanes] = mine[low : low + 16] * value


def pick_slots(parts, slots, low_id, high_id, put):
    found = dot(parts, one_hot(slots % WIDE, high_id))
    mine = slots // WIDE == low_id
    lows = low_id.shape[0]
    first = 0
    for channel, count in enumerate(PARTS if parts.shape[0] == sum(PARTS) * lows else (2,) * PROJ):
        value = found[first * lows : (first + 1) * lows]
        for part in range(1, count):
            value = value + found[(first + part) * lows : (first + part + 1) * lows]
        first += count
        put(channel, jnp.sum(jnp.where(mine, value, 0.0), axis=0, keepdims=True))


def put_parts(parts_ref, channel, half, value, counts, lows=None, low=0):
    lows = lows or value.shape[0]
    first = sum(counts[:channel])
    parts = split_three(value) if counts[channel] == 3 else split_two(value)
    for part, one in enumerate(parts):
        at = (first + part) * lows + low
        parts_ref[at : at + value.shape[0], half * LANES : (half + 1) * LANES] = one.astype(bf16)


def route_kernel(devices, per_owner, own_hbm, loc_hbm, want_ref, back_ref, pos_ref, own_ref, loc_ref, own_s, loc_s, rank_s, sems):
    copies = [pltpu.make_async_copy(own_hbm, own_ref, sems.at[0]), pltpu.make_async_copy(loc_hbm, loc_ref, sems.at[1])]
    for copy in copies:
        copy.start()
    for copy in copies:
        copy.wait()
    rows = own_s.shape[0]
    blocks = own_ref.shape[1] // LANES
    lane = iota((8, LANES), 1)
    from_slot = iota((8, LANES), 0) * STEP + lane // GROUP
    tile_of = lane % GROUP
    for group in range(own_ref.shape[0] // GROUP):
        for block in range(blocks):
            for source, target in ((own_ref, own_s), (loc_ref, loc_s)):
                part = source[group * GROUP : (group + 1) * GROUP, block * LANES : (block + 1) * LANES]
                out = jnp.zeros((8, LANES), i32)
                for tile in range(GROUP):
                    out = jnp.where(tile_of == tile, lane_pick(part[tile : tile + 1], from_slot), out)
                start = (group * blocks + block) * 8
                target[start : start + 8, :] = out
    owner = own_s[...]
    left = (iota((LANES, 2 * LANES), 0) < iota((LANES, 2 * LANES), 1)) | (iota((LANES, 2 * LANES), 1) >= LANES)
    above = iota((rows, rows), 1) < iota((rows, rows), 0)
    hits = jnp.concatenate([jnp.where(owner == one, 1.0, 0.0).astype(bf16) for one in range(devices)], axis=0)
    sums = dot(hits, jnp.where(left, 1.0, 0.0).astype(bf16))
    totals = jnp.concatenate(
        [sums[one * rows : (one + 1) * rows, LANES:].astype(bf16) for one in range(devices)], axis=1
    )
    base = dot(jnp.where(above, 1.0, 0.0).astype(bf16), totals)
    rank = jnp.zeros((rows, LANES), f32)
    for one in range(devices):
        here = sums[one * rows : (one + 1) * rows, :LANES] + base[:, one * LANES : (one + 1) * LANES]
        rank = jnp.where(owner == one, here, rank)
    rank = rank.astype(i32)
    pos_ref[...] = owner * per_owner + rank
    rank_s[...] = rank

    owner_id = iota((devices, LANES), 0)
    rank_id = narrow(iota((per_owner, LANES), 0))
    slot_lane = iota((devices, LANES), 1).astype(f32)

    def place(index, total):
        start = pl.multiple_of(index * 8, 8)
        own_rows = own_s[pl.ds(start, 8), :]
        loc_rows = loc_s[pl.ds(start, 8), :]
        rank_rows = rank_s[pl.ds(start, 8), :]
        high_rows = (loc_rows // LANES).astype(f32)
        low_rows = (loc_rows % LANES).astype(f32)
        lhs = []
        rhs = []
        for row in range(8):
            mine = own_rows[row : row + 1] == owner_id
            number = (start + row).astype(f32)
            lhs.append(
                jnp.concatenate(
                    [
                        jnp.where(mine, high_rows[row : row + 1], 0.0),
                        jnp.where(mine, low_rows[row : row + 1], 0.0),
                        jnp.where(mine, number, 0.0),
                        jnp.where(mine, slot_lane, 0.0),
                    ],
                    axis=0,
                ).astype(bf16)
            )
            rhs.append(one_hot(rank_rows[row : row + 1], rank_id))
        return total + dot_nt(jnp.concatenate(lhs, axis=1), jnp.concatenate(rhs, axis=1))

    total = lax.fori_loop(0, rows // 8, place, jnp.zeros((4 * devices, per_owner), f32), unroll=devices <= 32).astype(i32)
    want = total[:devices] * LANES + total[devices : 2 * devices]
    halves = per_owner // LANES
    if per_owner % LANES == 0 and halves > 1:
        for half in range(halves):
            want_ref[pl.ds(half, devices, stride=halves), :] = want[:, half * LANES : (half + 1) * LANES]
    else:
        want_ref[...] = want
    back_ref[...] = total[2 * devices : 3 * devices] * LANES + total[3 * devices :]


def view(angles_ref):
    angle = [jnp.full((1, LANES), angles_ref[index], f32) for index in range(3)]
    (cos_a, cos_b, cos_c) = [jnp.cos(one) for one in angle]
    (sin_a, sin_b, sin_c) = [jnp.sin(one) for one in angle]
    return [
        [cos_c * cos_b, cos_c * sin_b * sin_a - sin_c * cos_a, cos_c * sin_b * cos_a + sin_c * sin_a],
        [sin_c * cos_b, sin_c * sin_b * sin_a + cos_c * cos_a, sin_c * sin_b * cos_a - cos_c * sin_a],
        [-sin_b, cos_b * sin_a, cos_b * cos_a],
    ]


def harmonics(along_x, along_y, along_z):
    sq_x = along_x * along_x
    sq_y = along_y * along_y
    sq_z = along_z * along_z
    return [
        0.28209479177387814 + 0.0 * along_x,
        -0.4886025119029199 * along_y,
        0.4886025119029199 * along_z,
        -0.4886025119029199 * along_x,
        1.0925484305920792 * along_x * along_y,
        -1.0925484305920792 * along_y * along_z,
        0.31539156525252005 * (2.0 * sq_z - sq_x - sq_y),
        -1.0925484305920792 * along_x * along_z,
        0.5462742152960396 * (sq_x - sq_y),
        -0.5900435899266435 * along_y * (3.0 * sq_x - sq_y),
        2.890611442640554 * along_x * along_y * along_z,
        -0.4570457994644658 * along_y * (4.0 * sq_z - sq_x - sq_y),
        0.3731763325901154 * along_z * (2.0 * sq_z - 3.0 * sq_x - 3.0 * sq_y),
        -0.4570457994644658 * along_x * (4.0 * sq_z - sq_x - sq_y),
        1.445305721320277 * along_z * (sq_x - sq_y),
        -0.5900435899266435 * along_x * (sq_x - 3.0 * sq_y),
    ]


def basis_rows(basis, eighth):
    sub = iota((8, LANES), 0)
    found = []
    for colour in range(3):
        out = None
        for inner in range(8):
            index = 8 * eighth + inner - 11 - 16 * colour
            if 0 <= index < 16:
                out = jnp.zeros((8, LANES), f32) if out is None else out
                out = jnp.where(sub == inner, basis[index], out)
        found.append(out)
    return found


def shape_of(columns, rotation, camera_frame):
    focal_x, focal_y, centre_x, centre_y = camera_frame
    positions = columns[0:3]
    cam_first = rotation[0][0] * positions[0] + rotation[0][1] * positions[1] + rotation[0][2] * positions[2]
    cam_second = rotation[1][0] * positions[0] + rotation[1][1] * positions[1] + rotation[1][2] * positions[2]
    mean_x = centre_x + focal_x * cam_first
    mean_y = centre_y + focal_y * cam_second
    scales = [jnp.exp(one) for one in columns[3:6]]
    quat_w, quat_x, quat_y, quat_z = columns[6:10]
    norm_sq = jnp.maximum(quat_w * quat_w + quat_x * quat_x + quat_y * quat_y + quat_z * quat_z, 1.0)
    twice = 2.0 / norm_sq
    turned = [
        [
            1.0 - twice * (quat_y * quat_y + quat_z * quat_z),
            twice * (quat_x * quat_y - quat_w * quat_z),
            twice * (quat_x * quat_z + quat_w * quat_y),
        ],
        [
            twice * (quat_x * quat_y + quat_w * quat_z),
            1.0 - twice * (quat_x * quat_x + quat_z * quat_z),
            twice * (quat_y * quat_z - quat_w * quat_x),
        ],
        [
            twice * (quat_x * quat_z - quat_w * quat_y),
            twice * (quat_y * quat_z + quat_w * quat_x),
            1.0 - twice * (quat_x * quat_x + quat_y * quat_y),
        ],
    ]
    rows = []
    for focal, turn in ((focal_x, rotation[0]), (focal_y, rotation[1])):
        rows.append(
            [
                focal * (turn[0] * turned[0][k] + turn[1] * turned[1][k] + turn[2] * turned[2][k]) * scales[k]
                for k in range(3)
            ]
        )
    first, second = rows
    cov_a = first[0] * first[0] + first[1] * first[1] + first[2] * first[2] + 0.3
    cov_b = first[0] * second[0] + first[1] * second[1] + first[2] * second[2]
    cov_c = second[0] * second[0] + second[1] * second[1] + second[2] * second[2] + 0.3
    determinant = cov_a * cov_c - cov_b * cov_b
    opacity = 1.0 / (1.0 + jnp.exp(-columns[10]))
    return mean_x, mean_y, cov_c / determinant, -cov_b / determinant, cov_a / determinant, opacity


def spread_columns(gauss_ref, dense_s):
    rows = gauss_ref.shape[1] // LANES
    for row in range(rows):
        for eighth in range(2):
            dense_s[pl.ds(8 * eighth * rows + row, 8, stride=rows), :] = gauss_ref[
                8 * eighth : 8 * eighth + 8, row * LANES : (row + 1) * LANES
            ]


def shade_kernel(camera_frame, angles_ref, gauss_ref, parts_ref, dense_s, tint_s):
    rows = gauss_ref.shape[1] // LANES
    spread_columns(gauss_ref, dense_s)
    rotation = view(angles_ref)
    basis = harmonics(*rotation[2])
    patterns = [basis_rows(basis, eighth) for eighth in range(7)]
    for row in range(rows):
        lanes = slice(row * LANES, (row + 1) * LANES)
        tints = [None] * 3
        for eighth in range(1, 7):
            block = gauss_ref[8 * eighth : 8 * eighth + 8, lanes]
            for colour in range(3):
                pattern = patterns[eighth][colour]
                if pattern is not None:
                    term = block * pattern
                    tints[colour] = term if tints[colour] is None else tints[colour] + term
        for colour in range(3):
            tint_s[pl.ds(8 * colour * rows + row, 8, stride=rows), :] = tints[colour]
        tint_s[pl.ds(24 * rows + row, 3, stride=rows), :] = gauss_ref[56:59, lanes]
    for part in range(rows // 16):
        half = part % 2
        low = part // 2 * 16
        at = [pl.ds(index * rows + 2 * low + half, 16, stride=2) for index in range(27)]
        columns = [dense_s[one, :] for one in at[:11]]
        for index, value in enumerate(shape_of(columns, rotation, camera_frame)):
            put_parts(parts_ref, index, half, value, PARTS, rows // 2, low)
        for colour in range(3):
            total = 0.5
            for inner in range(8):
                total = total + tint_s[at[8 * colour + inner], :]
            if colour == 2:
                for inner in range(3):
                    total = total + basis[13 + inner] * tint_s[at[24 + inner], :]
            put_parts(parts_ref, 6 + colour, half, total, PARTS, rows // 2, low)


def pick_kernel(layout, parts_ref, asked_ref, out_ref):
    low_id = iota((parts_ref.shape[0] // sum(PARTS), WIDE), 0)
    high_id = narrow(iota((WIDE, WIDE), 0))
    minors = layout.minors()

    def pick_some(index, _):
        slots = jnp.concatenate([asked_ref[pl.ds(2 * index + one, 1), :] for one in range(2)], axis=1)

        def put(channel, value):
            for one in range(2):
                at = layout.row(channel, (2 * index + one) // minors, (2 * index + one) % minors)
                out_ref[pl.ds(at, 1), :] = value[:, one * LANES : (one + 1) * LANES]

        pick_slots(parts_ref[...], slots, low_id, high_id, put)
        return 0

    lax.fori_loop(0, layout.count // 2, pick_some, 0, unroll=True)


def render_kernel(
    layout,
    count_ref,
    order_ref,
    rows_ref,
    pos_ref,
    back_ref,
    cot_ref,
    image_ref,
    out_ref,
    in_s,
    out_s,
    raw_s,
    coef_s,
    cot_s,
    rhs_s,
    tint_s,
    alpha_s,
    shade_s,
    weight_s,
    sums_s,
):
    slot_rows = pos_ref.shape[0]
    groups = cot_ref.shape[1] // (GROUP * PIX)
    chunks = slot_rows // groups
    sub = iota((8, LANES), 0)
    lane = iota((8, LANES), 1)
    tile_of = lane % GROUP
    blocks = slot_rows // 8
    middles = []
    for group in range(groups):
        middle_x = jnp.zeros((8, LANES), f32)
        middle_y = jnp.zeros((8, LANES), f32)
        live = jnp.zeros((8, LANES), i32)
        for tile in range(GROUP):
            shown = order_ref[group * GROUP + tile]
            here = tile_of == tile
            middle_x = jnp.where(here, (shown % TX * 16 + 8).astype(f32), middle_x)
            middle_y = jnp.where(here, (shown // TX * 16 + 8).astype(f32), middle_y)
            live = jnp.where(here, count_ref[group * GROUP + tile], live)
        middles.append((middle_x, middle_y, live))

    for half in range(2):
        for channel in range(PROJ):
            put_parts(in_s, channel, half, layout.half(rows_ref, channel, half), PARTS)
    low_id = iota((slot_rows // 2, WIDE), 0)
    high_id = narrow(iota((WIDE, WIDE), 0))

    def pick_in(index, _):
        slots = jnp.concatenate([pos_ref[pl.ds(2 * index + one, 1), :] for one in range(2)], axis=1)

        def put(channel, value):
            for one in range(2):
                raw_s[pl.ds(channel * slot_rows + 2 * index + one, 1), :] = value[:, one * LANES : (one + 1) * LANES]

        pick_slots(in_s[...], slots, low_id, high_id, put)
        return 0

    lax.fori_loop(0, slot_rows // 2, pick_in, 0, unroll=True)
    for block in range(blocks):
        group = block * 8 // chunks
        middle_x, middle_y, live = middles[group]
        found = [
            raw_s[channel * slot_rows + 8 * block : channel * slot_rows + 8 * block + 8, :] for channel in range(PROJ)
        ]
        at_x = found[0] - middle_x
        at_y = found[1] - middle_y
        quad_a = -0.5 * found[2]
        quad_b = -found[3]
        quad_c = -0.5 * found[4]
        flat = quad_a * at_x * at_x + quad_c * at_y * at_y + quad_b * at_x * at_y + jnp.log(found[5])
        place = (8 * block - group * chunks + sub) * STEP + lane // GROUP
        terms = (
            quad_a * LOG2E,
            quad_b * LOG2E,
            quad_c * LOG2E,
            (-2.0 * quad_a * at_x - quad_b * at_y) * LOG2E,
            (-2.0 * quad_c * at_y - quad_b * at_x) * LOG2E,
            jnp.where(place < live, flat * LOG2E, -1e30),
        )
        for index, term in enumerate(terms):
            for part, value in enumerate(split_three(term)):
                coef_s[pl.ds(8 * block * 24 + 6 * part + index, 8, stride=24), :] = value
        for colour in range(3):
            for part, value in enumerate(split_two(found[6 + colour])):
                coef_s[pl.ds(8 * block * 24 + 18 + 3 * part + colour, 8, stride=24), :] = value

    pixel = iota((24, PIX), 1)
    row = iota((24, PIX), 0)
    pix_x = (pixel % 16).astype(f32) - 7.5
    pix_y = (pixel // 16).astype(f32) - 7.5
    kind = row % 6
    monomials = jnp.where(kind == 0, pix_x * pix_x, jnp.where(kind == 1, pix_x * pix_y, 1.0))
    monomials = jnp.where(kind == 2, pix_y * pix_y, monomials)
    monomials = jnp.where(kind == 3, pix_x, jnp.where(kind == 4, pix_y, monomials))
    moments = jnp.where(iota((8, PIX), 0) < 6, monomials[0:8], 0.0).astype(bf16)
    monomials = jnp.where(row < 18, monomials, 0.0)
    nothing = jnp.zeros((24, PIX), f32)
    for group in range(groups):
        for colour in range(3):
            for tile in range(GROUP):
                start = (group * GROUP + tile) * PIX
                cot_s[group * 24 + colour * GROUP + tile, :] = cot_ref[colour, start : start + PIX]
    cots = []
    spare = jnp.zeros((8, PIX), f32)
    for group in range(groups):
        first, second = split_two(cot_s[group * 24 : (group + 1) * 24, :])
        cots.append(jnp.concatenate([first, spare, second, spare], axis=0).astype(bf16))
        rhs_s[group] = jnp.concatenate(
            [
                jnp.concatenate([jnp.concatenate([nothing, monomials[8 * one : 8 * one + 8]], axis=0) for one in range(3)], axis=0),
                jnp.concatenate([first, spare, first, spare, second, spare], axis=0),
            ],
            axis=1,
        ).astype(bf16)

    own_tile = sub == tile_of
    own_pair = iota((8, WIDE), 0) == iota((8, WIDE), 1) % GROUP

    def evaluate(index):
        for group in range(groups):
            chunk = group * chunks + index
            coefs = coef_s[chunk * 24 : (chunk + 1) * 24, :]
            tints = [jnp.where(own_tile, coefs[18 + one : 19 + one], 0.0) for one in range(6)]
            lhs = jnp.concatenate(
                tints[:3] + [coefs[0:8]] + tints[3:] + [coefs[8:16]] + tints[:3] + [coefs[16:24]], axis=0
            ).astype(bf16)
            both = dot_tn(lhs, rhs_s[group])
            lanes = slice(chunk * LANES, (chunk + 1) * LANES)
            tint_s[:, lanes] = lhs[0:64]
            alpha_s[lanes, :] = jnp.exp2(both[:, :PIX])
            shade_s[lanes, :] = both[:, PIX:]

    def scan(index, trans):
        out = []
        for group in range(groups):
            one = trans[group]
            start = (group * chunks + index) * LANES
            for step in range(STEP):
                alpha = alpha_s[pl.ds(start + step * GROUP, GROUP), :]
                weight = one * alpha
                one = one - weight
                weight_s[pl.ds(start + step * GROUP, GROUP), :] = weight
            out.append(one)
        return tuple(out)

    def paint(index, images):
        out = []
        for group in range(groups):
            chunk = group * chunks + index
            both = slice(chunk * LANES, chunk * LANES + WIDE)
            first, second = split_two(weight_s[both, :])
            first = first.astype(bf16)
            second = second.astype(bf16)
            tints = tint_s[:, both]
            by_first = dot(tints, first)
            out.append(images[group] + by_first[0:24] + by_first[32:56] + dot(tints[0:32], second)[0:24])
            by_first = dot_nt(cots[group], first)
            tint_grad = by_first[0:24] + by_first[32:56] + dot_nt(cots[group][0:32], second)[0:24]
            for colour in range(3):
                own = jnp.where(own_pair, tint_grad[colour * GROUP : (colour + 1) * GROUP], 0.0)
                own = jnp.sum(own, axis=0, keepdims=True)
                for one in range(2):
                    sums_s[(chunk + one) * 16 + 8 + colour : (chunk + one) * 16 + 9 + colour, :] = own[:, one * LANES : (one + 1) * LANES]
        return tuple(out)

    trans = tuple(jnp.ones((GROUP, PIX), f32) for _ in range(groups))
    images = tuple(jnp.zeros((24, PIX), f32) for _ in range(groups))
    for pair in range(-AHEAD, chunks // 2 + 1):
        for one in range(2):
            if pair + AHEAD < chunks // 2:
                evaluate(2 * (pair + AHEAD) + one)
        for one in range(2):
            if 0 <= pair < chunks // 2:
                trans = scan(2 * pair + one, trans)
        if pair > 0:
            images = paint(2 * (pair - 1), images)
    for group in range(groups):
        for colour in range(3):
            for tile in range(GROUP):
                at = (group * GROUP + tile) * PIX
                image_ref[colour, at : at + PIX] = images[group][colour * GROUP + tile]

    def moment(index):
        for group in range(groups):
            chunk = group * chunks + index
            first, second = split_two(shade_s[slice(chunk * LANES, chunk * LANES + WIDE), :])
            found = dot_nt(moments, first.astype(bf16)) + dot_nt(moments, second.astype(bf16))
            for one in range(2):
                start = (chunk + one) * 16
                sums_s[start : start + 8, :] = found[:, one * LANES : (one + 1) * LANES]

    def rescan(index, behinds):
        out = []
        for group in range(groups):
            behind = behinds[group]
            start = (group * chunks + index) * LANES
            for step in reversed(range(STEP)):
                at = pl.ds(start + step * GROUP, GROUP)
                ahead = shade_s[at, :] - behind
                shade_s[at, :] = weight_s[at, :] * ahead
                behind = behind + alpha_s[at, :] * ahead
            out.append(behind)
        return tuple(out)

    behinds = tuple(jnp.zeros((GROUP, PIX), f32) for _ in range(groups))
    for pair in reversed(range(-1, chunks // 2)):
        for one in reversed(range(2)):
            if pair >= 0:
                behinds = rescan(2 * pair + one, behinds)
        if pair + 1 < chunks // 2:
            moment(2 * (pair + 1))

    slot_s = coef_s
    for block in range(blocks):
        middle_x, middle_y, _ = middles[block * 8 // chunks]
        at = slice(8 * block, 8 * block + 8)
        raw = [raw_s[channel * slot_rows + 8 * block : channel * slot_rows + 8 * block + 8, :] for channel in range(6)]
        (sum_xx, sum_xy, sum_yy, sum_x, sum_y, sum_one) = [
            sums_s[pl.ds(8 * block * 16 + index, 8, stride=16), :] for index in range(6)
        ]
        at_x = raw[0] - middle_x
        at_y = raw[1] - middle_y
        off_x = sum_x - at_x * sum_one
        off_y = sum_y - at_y * sum_one
        grads = [
            raw[2] * off_x + raw[3] * off_y,
            raw[4] * off_y + raw[3] * off_x,
            -0.5 * (sum_xx - at_x * (sum_x + off_x)),
            -(sum_xy - at_y * sum_x - at_x * off_y),
            -0.5 * (sum_yy - at_y * (sum_y + off_y)),
            sum_one / raw[5],
        ] + [sums_s[pl.ds(8 * block * 16 + 8 + colour, 8, stride=16), :] for colour in range(3)]
        for channel, value in enumerate(grads):
            slot_s[channel * slot_rows + 8 * block : channel * slot_rows + 8 * block + 8, :] = value

    for half in range(2):
        for channel in range(PROJ):
            value = slot_s[pl.ds(channel * slot_rows + half, slot_rows // 2, stride=2), :]
            put_parts(out_s, channel, half, value, (2,) * PROJ)
    minors = layout.minors()

    def pick_out(index, _):
        if layout.halves == 2:
            slots = back_ref[pl.ds(index, 1), :]
        else:
            slots = jnp.concatenate([back_ref[pl.ds(2 * index + one, 1), :] for one in range(2)], axis=1)

        def put(channel, value):
            for one in range(2):
                at = layout.row(channel, (2 * index + one) // minors, (2 * index + one) % minors)
                out_ref[pl.ds(at, 1), :] = value[:, one * LANES : (one + 1) * LANES]

        pick_slots(out_s[...], slots, low_id, high_id, put)
        return 0

    lax.fori_loop(0, layout.count // 2, pick_out, 0, unroll=True)


def collect_kernel(
    layout, camera_frame, angles_ref, dense_ref, asked_ref, terms_ref, grad_hbm, lhs_s, rhs_s, total_s, out_s, grad_ref, sems
):
    gauss = grad_ref.shape[1]
    rows = gauss // LANES
    lows = gauss // WIDE
    low_id = narrow(iota((lows, LANES), 0))
    high_id = narrow(iota((WIDE, LANES), 0))
    minors = layout.minors()

    for index in range(layout.count // 8):
        asked = asked_ref[8 * index : 8 * index + 8, :]
        low = asked // WIDE
        high = asked % WIDE
        for row in range(8):
            lanes = slice((8 * index + row) * LANES, (8 * index + row + 1) * LANES)
            mine = one_hot(low[row : row + 1], low_id)
            rhs_s[:, lanes] = one_hot(high[row : row + 1], high_id)
            for channel in range(PROJ):
                at = layout.row(channel, (8 * index + row) // minors, row % minors)
                put_terms(lhs_s, channel, lanes, terms_ref[at : at + 1, :], mine)
        lanes = slice(8 * index * LANES, 8 * (index + 1) * LANES)
        found = dot_nt(lhs_s[:, lanes], rhs_s[:, lanes])
        total_s[...] = found if index == 0 else total_s[...] + found
    rotation = view(angles_ref)
    basis = harmonics(*rotation[2])
    for part in range(rows // 8):
        half = part % 2
        low = part // 2 * 8
        lanes = slice(half * LANES, (half + 1) * LANES)
        sums = [
            total_s[channel * lows + low : channel * lows + low + 8, lanes]
            + total_s[(PROJ + channel) * lows + low : (PROJ + channel) * lows + low + 8, lanes]
            for channel in range(PROJ)
        ]
        columns = tuple(dense_ref[pl.ds(index * rows + 2 * low + half, 8, stride=2), :] for index in range(11))
        _, pullback = jax.vjp(lambda *values: shape_of(values, rotation, camera_frame), *columns)
        grads = pullback(tuple(sums[:6]))
        for index, value in enumerate(tuple(grads) + tuple(sums[6:])):
            out_s[pl.ds(index * rows + 2 * low + half, 8, stride=2), :] = value
    sub = iota((8, LANES), 0)
    patterns = [basis_rows(basis, eighth) for eighth in range(8)]
    copies = []
    pieces = sems.shape[0]
    wide = gauss // pieces
    for row in range(rows):
        lanes = slice(row * LANES, (row + 1) * LANES)
        grad_ref[0:8, lanes] = out_s[pl.ds(row, 8, stride=rows), :]
        tints = [out_s[(11 + colour) * rows + row : (11 + colour) * rows + row + 1, :] for colour in range(3)]
        for eighth in range(1, 8):
            value = None
            for colour in range(3):
                pattern = patterns[eighth][colour]
                if pattern is not None:
                    term = pattern * tints[colour]
                    value = term if value is None else value + term
            if eighth == 1:
                value = jnp.where(sub < 3, out_s[pl.ds(8 * rows + row, 8, stride=rows), :], value)
            if eighth == 7:
                grad_ref[56:59, lanes] = value[0:3]
            else:
                grad_ref[8 * eighth : 8 * eighth + 8, lanes] = value
        if (row + 1) * LANES % wide == 0:
            piece = len(copies)
            span = slice(piece * wide, (piece + 1) * wide)
            copies.append(pltpu.make_async_copy(grad_ref.at[:, span], grad_hbm.at[:, span], sems.at[piece]))
            copies[-1].start()
    for copy in copies:
        copy.wait()


VMEM = pl.BlockSpec(memory_space=pltpu.VMEM)
HBM = pl.BlockSpec(memory_space=pltpu.HBM)
SMEM = pl.BlockSpec(memory_space=pltpu.SMEM)


def call(kernel, specs, outs, scratch, flops, name, out_spec=VMEM, vmem=VMEM_BYTES):
    return pl.pallas_call(
        kernel,
        in_specs=specs,
        out_specs=[out_spec] * len(outs),
        out_shape=[jax.ShapeDtypeStruct(shape, dtype) for shape, dtype in outs],
        scratch_shapes=[pltpu.VMEM(*one) if isinstance(one, tuple) else one for one in scratch],
        compiler_params=pltpu.CompilerParams(vmem_limit_bytes=vmem),
        cost_estimate=pl.CostEstimate(flops=flops, bytes_accessed=4 << 20, transcendentals=0),
        name=name,
    )


def route(devices, owners, locals_):
    slots = owners.size
    per_owner = slots // devices
    rows = slots // LANES
    halves = per_owner // LANES if per_owner % LANES == 0 else 0
    asked = (devices * halves, LANES) if halves else (devices, per_owner)
    return call(
        partial(route_kernel, devices, per_owner),
        [HBM, HBM],
        [(asked, i32), ((devices, per_owner), i32), ((rows, LANES), i32)],
        [(owners.shape, i32)] * 2 + [((rows, LANES), i32)] * 3 + [pltpu.SemaphoreType.DMA((2,))],
        1 << 30,
        "route",
        vmem=63 << 20,
    )(owners, locals_)


def shade(camera_frame, view_angles, gaussians):
    rows = gaussians.shape[1] // LANES
    return call(
        partial(shade_kernel, camera_frame),
        [SMEM, VMEM],
        [((sum(PARTS) * rows // 2, WIDE), bf16), ((16 * rows, LANES), f32)],
        [((27 * rows, LANES), f32)],
        1 << 30,
        "shade",
    )(view_angles, gaussians)


def pick(layout, table, asked):
    return call(
        partial(pick_kernel, layout),
        [VMEM, VMEM],
        [((PROJ * layout.count, LANES), f32)],
        [],
        1 << 30,
        "pick",
    )(table, asked)[0]


def render(layout, list_counts, tile_order, rows, pos, back, cotangent):
    slot_rows = pos.shape[0]
    groups = tile_order.shape[0] // GROUP
    slots = slot_rows * LANES
    return call(
        partial(render_kernel, layout),
        [SMEM, SMEM, VMEM, VMEM, VMEM, VMEM],
        [(cotangent.shape, f32), ((PROJ * layout.count, LANES), f32)],
        [
            ((sum(PARTS) * slot_rows // 2, WIDE), bf16),
            ((2 * PROJ * slot_rows // 2, WIDE), bf16),
            ((PROJ * slot_rows, LANES), f32),
            ((24 * slot_rows, LANES), f32),
            ((24 * groups, PIX), f32),
            ((groups, 96, 2 * PIX), bf16),
            ((64, slots), bf16),
            ((slots, PIX), f32),
            ((slots, PIX), f32),
            ((slots, PIX), f32),
            ((16 * slot_rows, LANES), f32),
        ],
        1 << 34,
        "render",
    )(list_counts, tile_order, rows, pos, back, cotangent)


def collect(layout, camera_frame, view_angles, shape, dense, asked, terms):
    rows = shape[1] // LANES
    lows = shape[1] // WIDE
    return call(
        partial(collect_kernel, layout, camera_frame),
        [SMEM, VMEM, VMEM, VMEM],
        [(shape, f32)],
        [
            ((2 * PROJ * lows, layout.count * LANES), bf16),
            ((WIDE, layout.count * LANES), bf16),
            ((2 * PROJ * lows, WIDE), f32),
            ((16 * rows, LANES), f32),
            (shape, f32),
            pltpu.SemaphoreType.DMA((8,)),
        ],
        1 << 32,
        "collect",
        out_spec=HBM,
    )(view_angles, dense, asked, terms)[0]


def swap_rows(layout, devices, rows):
    if layout.halves:
        apart = rows.reshape(devices * PROJ, layout.halves, LANES)
        return lax.all_to_all(apart, "dev", split_axis=0, concat_axis=0, tiled=True).reshape(rows.shape)
    apart = rows.reshape(PROJ, devices, layout.count * LANES // devices)
    return lax.all_to_all(apart, "dev", split_axis=1, concat_axis=1, tiled=True).reshape(rows.shape)


def shards(gaussians, view_angles, tile_order, tile_owners, tile_locals, list_counts, image_cotangent):
    devices = lax.axis_size("dev")
    tiles_y = devices * tile_order.shape[0] // TX
    camera_frame = (4.0 * TX, 4.0 * tiles_y, 8.0 * TX, 8.0 * tiles_y)
    layout = Rows(devices, tile_owners.size // devices)
    want, back, pos = route(devices, tile_owners, tile_locals)
    asked = lax.all_to_all(want, "dev", split_axis=0, concat_axis=0, tiled=True)
    table, dense = shade(camera_frame, view_angles, gaussians)
    if not layout.halves:
        asked = asked.reshape(layout.count, LANES)
    if layout.halves != 2:
        back = back.reshape(layout.count, LANES)
    arrived = swap_rows(layout, devices, pick(layout, table, asked))
    rendered, slot_grads = render(layout, list_counts, tile_order, arrived, pos, back, image_cotangent)
    terms = swap_rows(layout, devices, slot_grads)
    gradients = collect(layout, camera_frame, view_angles, gaussians.shape, dense, asked, terms)
    return (rendered, gradients)


def solution(mesh):
    return jax.shard_map(
        shards,
        mesh=mesh,
        in_specs=(
            P(None, "dev"),
            P(),
            P("dev"),
            P("dev", None),
            P("dev", None),
            P("dev"),
            P(None, "dev"),
        ),
        out_specs=(P(None, "dev"), P(None, "dev")),
        check_vma=False,
    )
```
